128 devices in a mesh: slab: 32 (over z, x, y_lo), sec: 4 (over y_hi, core).
Axes of the slice: x: 4, y: 4 (y_hi: 2, y_lo: 2; y = y_hi * 2 + y_lo), z: 4, core: 2. Of those that a mesh axis runs over, the one named last changes fastest.
Arguments:
- fixed_image: float32 [2560, 80, 640], P('slab', 'sec'), may hold values from -16 to 16
- moving_image: float32 [2560, 80, 640], P('slab', 'sec'), may hold values from -16 to 16
- lattice_fine: float32 [3, 128, 5, 33], P(None, 'slab'), may hold values from -4 to 4
- lattice_mid: float32 [3, 33, 2, 9], replicated, may hold values from -4 to 4
- lattice_coarse: float32 [3, 9, 1, 3], replicated, may hold values from -4 to 4
- offset_fine: int32 [3, 128, 4], P(None, 'slab'), may hold values from -4 to 3
- offset_mid: int32 [3, 32, 1], P(None, 'slab'), may hold values from -4 to 3
- offset_coarse: int32 [3, 8, 1], replicated, may hold values from -4 to 3
Outputs:
- fine_step: float32 [3, 128, 5, 33], P(None, 'slab')
- mid_step: float32 [3, 33, 2, 9], replicated
- coarse_step: float32 [3, 9, 1, 3], replicated
The draws below stay inside these ranges and needn't reach their ends.
All inputs are finite; a program needn't handle non-finite values.
Results may differ from the reference program's by a relative error of at most 0.0003.
Values sent between devices are 32-bit elements; how exact they have to be, the bound alone decides.
A program may use at most 320 MiB of HBM per device.

```python
import jax
import jax.numpy as jnp
from jax import lax

SP = 20
OFF = 4
NX = 640
NZ = 2560
NY = 80
KZ0 = 128
KY0 = 5
KX0 = 33
KZ1 = 33
KY1 = 2
KX1 = 9
KZ2 = 9
KY2 = 1
KX2 = 3


TWO_PI = 6.283185307179586


def smooth_field(key):
    phases = jax.random.uniform(key, (3,), jnp.float32, 0.0, TWO_PI)
    depth = jnp.arange(NZ).astype(jnp.float32) / NZ
    rows = jnp.arange(NY).astype(jnp.float32) / NY
    across = jnp.arange(NX).astype(jnp.float32) / NX
    along_z = jnp.sin(TWO_PI * 2.0 * depth + phases[0])[:, None, None]
    along_y = jnp.sin(TWO_PI * rows + phases[1])[None, :, None]
    along_x = jnp.sin(TWO_PI * across + phases[2])[None, None, :]
    return 0.6 * along_z + 0.4 * along_y * along_x


def draw_fixed_image(key, part):
    key = jax.random.fold_in(key, 11)
    first_key = jax.random.fold_in(key, 0)
    third_key = jax.random.fold_in(key, 2)
    depth_ramp = jnp.exp(1.0986 * (jnp.arange(NZ).astype(jnp.float32) / NZ))[:, None, None]
    smooth = smooth_field(third_key)
    texture = jnp.clip(jax.random.normal(first_key, (NZ, NY, NX), jnp.float32), -3.5, 3.5)
    return (texture + smooth) * depth_ramp


def draw_moving_image(key, part):
    key = jax.random.fold_in(key, 12)
    first_key = jax.random.fold_in(key, 0)
    third_key = jax.random.fold_in(key, 2)
    depth_ramp = jnp.exp(1.0986 * (jnp.arange(NZ).astype(jnp.float32) / NZ))[:, None, None]
    smooth = smooth_field(third_key)
    texture = jnp.clip(jax.random.normal(first_key, (NZ, NY, NX), jnp.float32), -3.5, 3.5)
    return (texture + smooth) * depth_ramp


def with_ends(drawn, key, smallest, largest):
    extent = drawn.shape
    spot = [jax.random.randint(jax.random.fold_in(key, axis), (), 0, extent[axis]) for axis in range(len(extent))]
    drawn = drawn.at[tuple(spot)].set(smallest)
    longest = extent.index(max(extent))
    spot[longest] = (spot[longest] + 1) % extent[longest]
    return drawn.at[tuple(spot)].set(largest)


def level_of(rng, extent, cuts, low, largest):
    def one(dim, shards_of):
        steps = jax.random.uniform(jax.random.fold_in(jax.random.fold_in(rng, 6), dim), (shards_of,), jnp.float32, low / len(cuts), largest / len(cuts))
        return jnp.repeat(jnp.exp(steps), extent[dim] // shards_of).reshape((-1,) + (1,) * (len(extent) - dim - 1))

    level = one(*cuts[0])
    for cut in cuts[1:]:
        level = level * one(*cut)
    return level


def centred(own_key, shape, deviation, limit, cuts=(), dtype=jnp.bfloat16):
    values = deviation * jax.random.normal(own_key, shape, jnp.float32)
    if cuts:
        values = values * level_of(own_key, shape, cuts, -0.22, 0.18)
    return jnp.clip(values, -limit, limit).astype(dtype)


def setup_inputs(seed: int = 0) -> dict:
    arg_keys = jax.random.split(jax.random.key(seed), 9)
    fixed_image = draw_fixed_image(jax.random.fold_in(arg_keys[8], 71), 0)
    moving_image = draw_moving_image(jax.random.fold_in(arg_keys[8], 71), 0)
    lattice_fine = centred(arg_keys[2], (3, KZ0, KY0, KX0), 1.0, 4.0, ((1, 32),), jnp.float32)
    lattice_mid = centred(arg_keys[3], (3, KZ1, KY1, KX1), 1.0, 4.0, (), jnp.float32)
    lattice_coarse = centred(arg_keys[4], (3, KZ2, KY2, KX2), 1.0, 4.0, (), jnp.float32)
    offset_fine = with_ends(jax.random.randint(arg_keys[5], (3, NZ // SP, NY // SP), 0 - OFF, OFF), jax.random.fold_in(arg_keys[5], 1), 0 - OFF, OFF - 1).astype(jnp.int32)
    offset_mid = with_ends(jax.random.randint(arg_keys[6], (3, NZ // (4 * SP), NY // (4 * SP)), 0 - OFF, OFF), jax.random.fold_in(arg_keys[6], 1), 0 - OFF, OFF - 1).astype(jnp.int32)
    offset_coarse = with_ends(jax.random.randint(arg_keys[7], (3, NZ // (16 * SP), 1), 0 - OFF, OFF), jax.random.fold_in(arg_keys[7], 1), 0 - OFF, OFF - 1).astype(jnp.int32)
    return dict(fixed_image=fixed_image, moving_image=moving_image, lattice_fine=lattice_fine, lattice_mid=lattice_mid, lattice_coarse=lattice_coarse, offset_fine=offset_fine, offset_mid=offset_mid, offset_coarse=offset_coarse)


EPSILON = 1e-06
STEP_SIZE = 0.5
HIGHEST = lax.Precision.HIGHEST

def bspline(values):
    distance = jnp.abs(values)
    near_part = 2.0 / 3.0 - distance * distance + 0.5 * distance * distance * distance
    remain = jnp.maximum(2.0 - distance, 0.0)
    far_part = remain * remain * remain / 6.0
    return jnp.where(distance < 1.0, near_part, far_part)

def spline_basis(first_row, row_count, lattice, knot_first, factor, coarse):
    voxels = (jnp.arange(row_count) + first_row).astype(jnp.float32)
    knot_index = (jnp.arange(lattice) + knot_first).astype(jnp.float32)
    position = factor * voxels + 0.5 * (factor - 1)
    centre = SP * coarse * knot_index + 0.5 * (coarse - 1)
    return bspline((position[:, None] - centre[None, :]) / (SP * coarse))

def spline_field(lattice, along_z, along_y, along_x):
    result = jnp.einsum('dabc,xc->dabx', lattice, along_x, precision=HIGHEST)
    result = jnp.einsum('dabx,yb->dayx', result, along_y, precision=HIGHEST)
    return jnp.einsum('dayx,za->dzyx', result, along_z, precision=HIGHEST)

def spline_adjoint(values, along_z, along_y, along_x):
    result = jnp.einsum('dzyx,za->dayx', values, along_z, precision=HIGHEST)
    result = jnp.einsum('dayx,yb->dabx', result, along_y, precision=HIGHEST)
    return jnp.einsum('dabx,xc->dabc', result, along_x, precision=HIGHEST)

def linear_mix(lower, upper, weight):
    return lower + weight * (upper - lower)

def trilinear(window, frac_z, frac_y, frac_x):
    planes, height, breadth = frac_z.shape

    def corner(step_z, step_y, step_x):
        return window[step_z:step_z + planes, step_y:step_y + height, step_x:step_x + breadth]
    along_lines = {}
    span_diffs = {}
    for step_z in (0, 1):
        for step_y in (0, 1):
            lower_x = corner(step_z, step_y, 0)
            upper_x = corner(step_z, step_y, 1)
            along_lines[step_z, step_y] = linear_mix(lower_x, upper_x, frac_x)
            span_diffs[step_z, step_y] = upper_x - lower_x
    plane_low = linear_mix(along_lines[0, 0], along_lines[0, 1], frac_y)
    plane_high = linear_mix(along_lines[1, 0], along_lines[1, 1], frac_y)
    warped = linear_mix(plane_low, plane_high, frac_z)
    slope_z = plane_high - plane_low
    slope_y = linear_mix(along_lines[0, 1] - along_lines[0, 0], along_lines[1, 1] - along_lines[1, 0], frac_z)
    slope_x = linear_mix(linear_mix(span_diffs[0, 0], span_diffs[0, 1], frac_y), linear_mix(span_diffs[1, 0], span_diffs[1, 1], frac_y), frac_z)
    return (warped, jnp.stack([slope_z, slope_y, slope_x]))

def similarity_gradient(fixed, padded, offsets, contributions, block_y):
    planes, height, breadth = fixed.shape
    margin = (padded.shape[0] - planes) // 2
    blocks_z = planes // SP
    blocks_y = height // block_y
    own_lattice, own_z, own_y, own_x = contributions[0]
    columns = (jnp.arange(blocks_y) * block_y).astype(jnp.int32)

    def sample(start_z, start_y, shift_z, shift_y, shift_x, frac_z, frac_y, frac_x):
        window = lax.dynamic_slice(padded, (start_z + margin + shift_z, start_y + margin + shift_y, margin + shift_x), (SP + 1, block_y + 1, breadth + 1))
        return trilinear(window, frac_z, frac_y, frac_x)

    def one_block(running, block_index):
        start_z = (block_index * SP).astype(jnp.int32)
        control = jnp.zeros((3, SP, height, breadth), jnp.float32)
        for lattice, along_z, along_y, along_x in contributions:
            control = control + spline_field(lattice, lax.dynamic_slice_in_dim(along_z, start_z, SP, 0), along_y, along_x)
        fraction = jax.nn.sigmoid(control)
        pieces = jnp.moveaxis(fraction.reshape(3, SP, blocks_y, block_y, breadth), 2, 0)
        shifts = lax.dynamic_slice_in_dim(offsets, block_index, 1, 1)[:, 0]
        warped, slopes = jax.vmap(sample, in_axes=(None, 0, 0, 0, 0, 0, 0, 0))(start_z, columns, shifts[0], shifts[1], shifts[2], pieces[:, 0], pieces[:, 1], pieces[:, 2])
        warped = jnp.moveaxis(warped, 0, 1).reshape(SP, height, breadth)
        slopes = jnp.moveaxis(slopes, 0, 2).reshape(3, SP, height, breadth)
        residual = warped - lax.dynamic_slice_in_dim(fixed, start_z, SP, 0)
        weights = residual[None] * slopes * fraction * (1.0 - fraction)
        running = running + spline_adjoint(weights, lax.dynamic_slice_in_dim(own_z, start_z, SP, 0), own_y, own_x)
        return (running, None)
    running, _ = lax.scan(one_block, jnp.zeros(own_lattice.shape, jnp.float32), jnp.arange(blocks_z).astype(jnp.int32))
    return running

def normalized(gradient):
    return gradient / jnp.sqrt(jnp.mean(gradient * gradient) + EPSILON)

def pooled(volume):
    planes, height, breadth = volume.shape
    return volume.reshape(planes // 4, 4, height // 4, 4, breadth // 4, 4).mean(axis=(1, 3, 5))

def level_bases(factor, coarse, lattice):
    extents = (NZ // factor, NY // factor, NX // factor)
    return tuple((spline_basis(0, extents[dimension], lattice.shape[dimension + 1], 0, factor, coarse) for dimension in range(3)))

def reference(fixed_image, moving_image, lattice_fine, lattice_mid, lattice_coarse, offset_fine, offset_mid, offset_coarse):
    fixed_mid = pooled(fixed_image)
    moving_mid = pooled(moving_image)
    fixed_coarse = pooled(fixed_mid)
    moving_coarse = pooled(moving_mid)
    coarse_terms = [(lattice_coarse,) + level_bases(16, 16, lattice_coarse)]
    gradient_coarse = similarity_gradient(fixed_coarse, jnp.pad(moving_coarse, OFF), offset_coarse, coarse_terms, NY // 16)
    coarse_step = normalized(gradient_coarse)
    coarse_next = lattice_coarse - STEP_SIZE * coarse_step
    mid_terms = [(lattice_mid,) + level_bases(4, 4, lattice_mid), (coarse_next,) + level_bases(4, 16, coarse_next)]
    gradient_mid = similarity_gradient(fixed_mid, jnp.pad(moving_mid, OFF), offset_mid, mid_terms, SP)
    mid_step = normalized(gradient_mid)
    mid_next = lattice_mid - STEP_SIZE * mid_step
    fine_terms = [(lattice_fine,) + level_bases(1, 1, lattice_fine), (mid_next,) + level_bases(1, 4, mid_next), (coarse_next,) + level_bases(1, 16, coarse_next)]
    gradient_fine = similarity_gradient(fixed_image, jnp.pad(moving_image, OFF), offset_fine, fine_terms, SP)
    fine_step = normalized(gradient_fine)
    return (fine_step, mid_step, coarse_step)
```

```python
import functools

import jax
import jax.numpy as jnp
import ml_dtypes
import numpy as np
from jax import lax
from jax.experimental import pallas as pl
from jax.experimental.pallas import tpu as pltpu
from jax.sharding import PartitionSpec as P

SP = 20
EPSILON = 1e-06
STEP_SIZE = 0.5
HIGHEST = lax.Precision.HIGHEST
F32 = jnp.float32
BF16 = jnp.bfloat16
MESH = pl.DeviceIdType.MESH
SLABS = 32
SECS = 4
NZ, NY, NX = 80, 20, 640
CHUNKS = NX // 128
LOG2E = 1.4426950408889634
VMEM_LIMIT = 58 * 1024 * 1024


def basis(rows, knots, factor, coarse):
    rows, knots = np.asarray(rows, np.float64), np.asarray(knots, np.float64)
    position = factor * rows + 0.5 * (factor - 1)
    centre = SP * coarse * knots + 0.5 * (coarse - 1)
    distance = np.abs((position[:, None] - centre[None, :]) / (SP * coarse))
    near = 2.0 / 3.0 - distance**2 + 0.5 * distance**3
    far = np.maximum(2.0 - distance, 0.0) ** 3 / 6.0
    return np.where(distance < 1.0, near, far)


def two_parts(values):
    high = values.astype(ml_dtypes.bfloat16)
    low = (values - high.astype(np.float64)).astype(ml_dtypes.bfloat16)
    return high, low


@functools.cache
def tables():
    t = {}
    rz, ry = np.zeros((4, NZ, 64)), np.zeros((4, 24, 64))
    z, y, x = np.arange(NZ), np.arange(NY), np.arange(NX)
    for r in range(4):
        for a in range(7):
            rz[r, :, 5 * a : 5 * a + 5] = basis(z, [a - 1], 1, 1)
        for a in range(5):
            rz[r, :, 40 + 2 * a : 42 + 2 * a] = basis(z, [a - 2], 1, 4)
            rz[r, :, 56 + a : 57 + a] = basis(z + 80 * r, [a - 2], 1, 16)
    for s in range(4):
        for a in range(7):
            ry[s, :NY, 5 * a : 5 * a + 5] = basis(y + 20 * s, range(5), 1, 1)
        for a in range(5):
            ry[s, :NY, 40 + 2 * a : 42 + 2 * a] = basis(y + 20 * s, range(2), 1, 4)
            ry[s, :NY, 56 + a : 57 + a] = basis(y + 20 * s, [0], 1, 16)
    t["rz"] = np.tile(rz, (1, 1, 4)).astype(np.float32)
    t["ry"] = np.tile(ry, (1, 1, 4)).astype(np.float32)
    across = np.zeros((3, 128, NX))
    across[0, :33] = basis(x, range(33), 1, 1).T
    across[1, :9] = basis(x, range(9), 1, 4).T
    across[2, :3] = basis(x, range(3), 1, 16).T
    t["bt"] = (-LOG2E * across).astype(np.float32)
    spread = np.zeros((3, NX, 256), ml_dtypes.bfloat16)
    high, low = two_parts(basis(x, range(33), 1, 1))
    for d in range(3):
        spread[d, :, 40 * d : 40 * d + 33] = high
        spread[d, :, 128 + 40 * d : 128 + 40 * d + 33] = low
    t["bx"] = spread
    rz, ry = np.zeros((4, 24, 128)), np.zeros((4, 8, 128))
    z, y, x = np.arange(20), np.arange(5), np.arange(160)
    for r in range(4):
        for a in range(4):
            rz[r, :20, 2 * a : 2 * a + 2] = basis(z, [a - 1], 4, 4)
        for a in range(5):
            rz[r, :20, 8 + a : 9 + a] = basis(z + 20 * r, [a - 2], 4, 16)
    for s in range(4):
        for a in range(4):
            ry[s, :5, 2 * a : 2 * a + 2] = basis(y + 5 * s, range(2), 4, 4)
        for a in range(5):
            ry[s, :5, 8 + a : 9 + a] = basis(y + 5 * s, [0], 4, 16)
    t["mrz"], t["mry"] = rz.astype(np.float32), ry.astype(np.float32)
    across = np.zeros((2, 128, 256))
    across[0, :9, :160] = basis(x, range(9), 4, 4).T
    across[1, :3, :160] = basis(x, range(3), 4, 16).T
    t["mbt"] = (-LOG2E * across).astype(np.float32)
    spread = np.zeros((3, 256, 128), np.float32)
    for d in range(3):
        spread[d, :160, 16 * d : 16 * d + 9] = basis(x, range(9), 4, 4)
    t["mbx"] = spread
    rz, ry = np.zeros((4, 8, 128)), np.zeros((8, 128))
    z, y, x = np.arange(5), np.arange(5), np.arange(40)
    for r in range(4):
        for a in range(4):
            rz[r, :5, a : a + 1] = basis(z + 5 * r, [a - 1], 16, 16)
    ry[:5, :4] = basis(y, [0], 16, 16)
    t["crz"], t["cry"] = rz.astype(np.float32), ry.astype(np.float32)
    across = np.zeros((128, 128))
    across[:3, :40] = basis(x, range(3), 16, 16).T
    t["cbt"] = (-LOG2E * across).astype(np.float32)
    spread = np.zeros((3, 128, 128), np.float32)
    for d in range(3):
        spread[d, :40, 16 * d : 16 * d + 3] = basis(x, range(3), 16, 16)
    t["cbx"] = spread
    pool = np.zeros((NX, 256), ml_dtypes.bfloat16)
    pool[np.arange(NX), np.arange(NX) // 4] = 1
    t["px"] = pool
    pool = np.zeros((160, 480), ml_dtypes.bfloat16)
    for plane in range(20):
        for row in range(20):
            pool[8 * plane + row // 4, 24 * plane + row] = 1
    t["py"] = pool
    pool = np.zeros((2, 256, 128), np.float32)
    pool[0, np.arange(160), np.arange(160) // 4] = 1
    pool[1, np.arange(160), 64 + np.arange(160) // 4] = 1
    t["pc"] = pool
    return t


def dot(a, b):
    return jnp.dot(a, b, preferred_element_type=F32)


def dot_full(a, b):
    return jnp.dot(a, b, precision=HIGHEST, preferred_element_type=F32)


def dot_rows(a, b):
    return lax.dot_general(
        a, b, (((0,), (0,)), ((), ())), precision=HIGHEST, preferred_element_type=F32
    )


def parts(values):
    high = values.astype(BF16)
    return high, (values - high.astype(F32)).astype(BF16)


def shift_lanes(chunks, shift):
    amount = lax.rem(256 - shift, 128)
    rolled = [pltpu.roll(chunk, amount, 1) for chunk in chunks]
    lane = lax.broadcasted_iota(jnp.int32, chunks[0].shape, 1)
    first = lane < jnp.maximum(-shift, 0)
    last = lane >= 128 - jnp.maximum(shift, 0)
    zero = jnp.zeros_like(chunks[0])
    padded = [zero, *rolled, zero]
    return [
        jnp.where(first, padded[j], jnp.where(last, padded[j + 2], padded[j + 1]))
        for j in range(len(chunks))
    ]


def fraction(exponent):
    grown = jnp.exp2(exponent)
    total = 1.0 + grown
    frac = pl.reciprocal(total, approx=True)
    frac = frac * (2.0 - total * frac)
    return frac, frac * (grown * frac)


def weights(fixed, corner, step, exponents):
    (fz, gz), (fy, gy), (fx, gx) = (fraction(e) for e in exponents)
    line = [[corner[z][y] + fx * step[z][y] for y in (0, 1)] for z in (0, 1)]
    rise = [line[z][1] - line[z][0] for z in (0, 1)]
    plane = [line[z][0] + fy * rise[z] for z in (0, 1)]
    slope_z = plane[1] - plane[0]
    residual = (plane[0] + fz * slope_z) - fixed
    slope_y = rise[0] + fz * (rise[1] - rise[0])
    along = [step[z][0] + fy * (step[z][1] - step[z][0]) for z in (0, 1)]
    slope_x = along[0] + fz * (along[1] - along[0])
    return [
        (residual * slope_z) * gz,
        (residual * slope_y) * gy,
        (residual * slope_x) * gx,
    ]


def greet(k, s):
    barrier = pltpu.get_barrier_semaphore()

    def signal(slab, sec):
        pl.semaphore_signal(barrier, inc=1, device_id=(slab, sec), device_id_type=MESH)

    @pl.loop(1, SLABS)
    def _(i):
        signal(lax.rem(k + i, SLABS), s)

    for i in range(1, SECS):
        other = lax.rem(s + i, SECS)
        signal(k, other)
        signal(lax.rem(k + 1, SLABS), other)
        signal(lax.rem(k + SLABS - 1, SLABS), other)
    pl.semaphore_wait(barrier, SLABS - 1 + 3 * (SECS - 1))


def broadcast_start(k, s, tile, buffer, send_sem, recv_sem):
    @pl.loop(1, SLABS)
    def _(i):
        pltpu.make_async_remote_copy(
            src_ref=tile,
            dst_ref=buffer.at[k],
            send_sem=send_sem,
            recv_sem=recv_sem,
            device_id=(lax.rem(k + i, SLABS), s),
            device_id_type=MESH,
        ).start()


def broadcast_wait(buffer, send_sem, recv_sem):
    part = buffer.at[pl.ds(0, SLABS - 1)]
    pltpu.make_async_copy(part, part, recv_sem).wait()
    pltpu.make_async_copy(part, part, send_sem).wait()


def remote(src, dst, send_sem, recv_sem, device):
    return pltpu.make_async_remote_copy(
        src_ref=src,
        dst_ref=dst,
        send_sem=send_sem,
        recv_sem=recv_sem,
        device_id=device,
        device_id_type=MESH,
    )


def levels_kernel(
    moving, fixed, lat_fine, lat_mid, lat_coarse, off_mid, off_coarse,
    px, py, pc, mrz, mry, mbt, mbx, crz, cry, cbt, cbx,
    mid_out, coarse_out, lf, lm, lc, pad,
    mv, fx, sums, lo_pack, hi_pack, z_bef, z_aft, y_bef, y_aft, corners,
    lf_own, lf_prev, lf_next, lm_own, lc_own,
    pooled_m, pooled_f, pm_bef, pm_aft, pm_halo,
    piece, pieces, cv, mm, mr,
    c_tile, c_buf, m_part, m_parts, m_tile, m_buf,
    load_sem, send, recv, psend, precv, tsend, trecv, bsem,
):
    k, s = lax.axis_index("slab"), lax.axis_index("sec")
    nxt, prv = lax.rem(k + 1, SLABS), lax.rem(k + SLABS - 1, SLABS)
    q, r = k // 4, lax.rem(k, 4)
    has_prev, has_next = (k > 0).astype(F32), (k < SLABS - 1).astype(F32)

    loads = []
    for n, (src, dst) in enumerate(((moving, mv), (fixed, fx))):
        for part in range(4):
            rows = pl.ds(20 * part, 20)
            loads.append(pltpu.make_async_copy(src.at[rows], dst.at[rows], load_sem.at[4 * n + part]))
    for copy in loads:
        copy.start()

    lf_own[...] = jnp.zeros_like(lf_own)
    lm_own[...] = jnp.zeros_like(lm_own)
    lc_own[...] = jnp.zeros_like(lc_own)
    for d in range(3):
        for a in range(4):
            lf_own[d, 5 * a : 5 * a + 5, 0:33] = lat_fine[d, a]
        for a in range(33):
            lm_own[d, 2 * a + 4 : 2 * a + 6, 0:9] = lat_mid[d, a]
        for a in range(9):
            lc_own[d, a + 2 : a + 3, 0:3] = lat_coarse[d, a]
    sums[:, 20:24, :] = jnp.zeros((20, 4, NX), F32)
    cv[...] = jnp.zeros_like(cv)
    mm[...] = jnp.zeros_like(mm)
    pad[:, :, 28:32, :] = jnp.zeros((CHUNKS, NZ + 8, 4, 128), F32)

    greet(k, s)

    lat_to_next = remote(lf_own, lf_prev, send.at[0], recv.at[0], (nxt, s))
    lat_to_prev = remote(lf_own, lf_next, send.at[1], recv.at[1], (prv, s))
    z_to_next = remote(moving.at[pl.ds(76, 4)], z_bef, send.at[2], recv.at[2], (nxt, s))
    z_to_prev = remote(moving.at[pl.ds(0, 4)], z_aft, send.at[3], recv.at[3], (prv, s))
    for copy in (lat_to_next, lat_to_prev, z_to_next, z_to_prev):
        copy.start()

    def pool(source, n, halos):
        for part in range(4):
            loads[4 * n + part].wait()

            @pl.loop(5 * part, 5 * part + 5)
            def _(group):
                total = None
                for i in range(4):
                    plane = source[4 * group + i]
                    total = plane if total is None else total + plane
                    if halos:
                        lo_pack[2 * group + i // 2, 4 * (i % 2) : 4 * (i % 2) + 4, :] = plane[0:4]
                        hi_pack[2 * group + i // 2, 4 * (i % 2) : 4 * (i % 2) + 4, :] = plane[16:20]
                        for c in range(CHUNKS):
                            pad[c, 4 * group + i + 4, 4:24, :] = plane[:, 128 * c : 128 * c + 128]
                sums[group, 0:20, :] = total

        high, low = parts(sums[...].reshape(480, NX))
        table = py[...]
        high, low = parts(dot(table, high) + dot(table, low))
        table = px[...]
        return ((dot(high, table) + dot(low, table)) * (1.0 / 64.0)).reshape(20, 8, 256)

    pooled_m[...] = pool(mv, 0, True)

    to_bef = remote(hi_pack, y_bef, send.at[4], recv.at[4], (k, s + 1))
    to_aft = remote(lo_pack, y_aft, send.at[5], recv.at[5], (k, s - 1))
    first, last = pl.ds(0, 2), pl.ds(38, 2)
    corner_up = [
        remote(hi_pack.at[last], corners.at[0], send.at[6], recv.at[6], (nxt, s + 1)),
        remote(hi_pack.at[first], corners.at[1], send.at[7], recv.at[7], (prv, s + 1)),
    ]
    corner_down = [
        remote(lo_pack.at[last], corners.at[2], send.at[8], recv.at[8], (nxt, s - 1)),
        remote(lo_pack.at[first], corners.at[3], send.at[9], recv.at[9], (prv, s - 1)),
    ]
    head, tail = pl.ds(0, 4), pl.ds(16, 4)
    mid_same = [
        remote(pooled_m.at[tail], pm_halo.at[0, 1], send.at[10], recv.at[10], (nxt, s)),
        remote(pooled_m.at[head], pm_halo.at[1, 1], send.at[11], recv.at[11], (prv, s)),
    ]
    mid_up = [
        remote(pooled_m, pm_bef, send.at[12], recv.at[12], (k, s + 1)),
        remote(pooled_m.at[tail], pm_halo.at[0, 0], send.at[13], recv.at[13], (nxt, s + 1)),
        remote(pooled_m.at[head], pm_halo.at[1, 0], send.at[14], recv.at[14], (prv, s + 1)),
    ]
    mid_down = [
        remote(pooled_m, pm_aft, send.at[15], recv.at[15], (k, s - 1)),
        remote(pooled_m.at[tail], pm_halo.at[0, 2], send.at[16], recv.at[16], (nxt, s - 1)),
        remote(pooled_m.at[head], pm_halo.at[1, 2], send.at[17], recv.at[17], (prv, s - 1)),
    ]
    up, down = s < SECS - 1, s > 0

    for copy in mid_same:
        copy.start()

    @pl.when(up)
    def _():
        for copy in mid_up:
            copy.start()

    @pl.when(down)
    def _():
        for copy in mid_down:
            copy.start()

    pooled_f[...] = pool(fx, 1, False)

    row = lax.broadcasted_iota(jnp.int32, (5, 8, 256), 1)
    rows = []
    for pooled in (pooled_m, pooled_f):
        four = pooled[...].reshape(5, 4, 8, 256)
        four = (four[:, 0] + four[:, 1]) + (four[:, 2] + four[:, 3])
        upper = jnp.sum(jnp.where(row < 4 - s, four, 0.0), axis=1, keepdims=True)
        lower = jnp.sum(jnp.where(row < 4 - s, 0.0, four), axis=1, keepdims=True)
        rows.append(jnp.where(row == 0, upper, jnp.where(row == 1, lower, 0.0)).reshape(40, 256))
    both = (dot_full(rows[0], pc[0]) + dot_full(rows[1], pc[1])) * (1.0 / 64.0)
    piece[...] = both.reshape(5, 8, 128)
    pieces[1, s] = piece[...]

    def piece_copy(dk, other):
        slab = (prv, k, nxt)[dk]
        return remote(
            piece, pieces.at[2 - dk, s], psend.at[dk, other], precv.at[2 - dk, s], (slab, other)
        )

    for dk in range(3):
        for other in range(SECS):
            if dk == 1:

                @pl.when(s != other)
                def _():
                    piece_copy(dk, other).start()
            else:
                piece_copy(dk, other).start()

    @pl.when(up)
    def _():
        to_bef.start()
        for copy in corner_up:
            copy.start()

    @pl.when(down)
    def _():
        to_aft.start()
        for copy in corner_down:
            copy.start()

    for dk in range(3):
        for other in range(SECS):
            slot = pieces.at[dk, other]

            def arrived(dk=dk, other=other, slot=slot):
                remote(piece, slot, psend.at[dk, other], precv.at[dk, other], (k, other)).wait_recv()

            if dk == 1:
                pl.when(s != other)(arrived)
            else:
                arrived()

    lane = lax.broadcasted_iota(jnp.int32, (5, 1, 128), 2)
    for dk in range(3):
        keep = lane < 40
        scale = (has_prev, jnp.float32(1.0), has_next)[dk]
        for c in range(5):
            value = jnp.zeros((5, 1, 128), F32)
            if c < 4:
                value = value + pieces[dk, c, :, 0:1, :]
            if c > 0:
                value = value + pieces[dk, c - 1, :, 1:2, :]
            cv[5 * dk : 5 * dk + 5, 8 + c : 9 + c, :] = jnp.where(keep, value, 0.0) * scale
            if dk == 1:
                cv[15:20, 8 + c : 9 + c, :] = value
    fixed_c = pltpu.roll(cv[15:20, 8:16, :].reshape(40, 128), 64, 1)

    oz, oy, ox = off_coarse[0, q, 0], off_coarse[1, q, 0], off_coarse[2, q, 0]
    at, by = [], []
    for e in (0, 1):
        window = cv[pl.ds(5 + oz, 6), pl.ds(8 + oy + e, 8), :].reshape(48, 128)
        here, there = shift_lanes([window], ox)[0], shift_lanes([window], ox + 1)[0]
        at.append(here)
        by.append(there - here)
    corner = [[at[y][8 * z : 8 * z + 40] for y in (0, 1)] for z in (0, 1)]
    step = [[by[y][8 * z : 8 * z + 40] for y in (0, 1)] for z in (0, 1)]
    spread = jnp.concatenate([crz[r, pl.ds(z, 1), :] * cry[...] for z in range(5)], axis=0)
    filler = jnp.zeros((120, 128), F32)
    exponents = []
    for d in range(3):
        column = dot_full(lc_own[d, pl.ds(q + 1, 8), :], cbt[...])
        exponents.append(dot_full(spread, jnp.concatenate([column, filler], axis=0)))
    total = None
    for d, weight in enumerate(weights(fixed_c, corner, step, exponents)):
        term = dot_full(weight, cbx[d])
        total = term if total is None else total + term
    c_tile[...] = dot_rows(spread, total)[0:8]
    c_buf[k] = c_tile[...]
    broadcast_start(k, s, c_tile, c_buf, bsem.at[0], bsem.at[1])

    for z in range(20):
        mr[8 * z : 8 * z + 8, :] = mrz[r, z : z + 1, :] * mry[s]
    for copy in mid_same:
        copy.wait_recv()

    @pl.when(s > 0)
    def _():
        for copy in mid_up:
            copy.wait_recv()

    @pl.when(s < SECS - 1)
    def _():
        for copy in mid_down:
            copy.wait_recv()

    @pl.when(s == 0)
    def _():
        pm_bef[...] = jnp.zeros_like(pm_bef)
        pm_halo[:, 0] = jnp.zeros((2, 4, 8, 256), F32)

    @pl.when(s == SECS - 1)
    def _():
        pm_aft[...] = jnp.zeros_like(pm_aft)
        pm_halo[:, 2] = jnp.zeros((2, 4, 8, 256), F32)

    for c in range(2):
        lanes = slice(128 * c, 128 * c + 128)
        for e, (whole, where) in enumerate(((pm_bef, 3), (pooled_m, 8), (pm_aft, 13))):
            mm[c, 0:4, where : where + 5, :] = pm_halo[0, e, :, 0:5, lanes] * has_prev
            mm[c, 4:24, where : where + 5, :] = whole[:, 0:5, lanes]
            mm[c, 24:28, where : where + 5, :] = pm_halo[1, e, :, 0:5, lanes] * has_next

    oz, oy, ox = off_mid[0, 0, 0], off_mid[1, 0, 0], off_mid[2, 0, 0]
    at, by = [], []
    for e in (0, 1):
        window = [mm[c, pl.ds(4 + oz, 21), pl.ds(8 + oy + e, 8), :].reshape(168, 128) for c in range(2)]
        here, there = shift_lanes(window, ox), shift_lanes(window, ox + 1)
        at.append(here)
        by.append([there[c] - here[c] for c in range(2)])

    broadcast_wait(c_buf, bsem.at[0], bsem.at[1])
    pick_r = lax.broadcasted_iota(jnp.int32, (16, 256), 0)
    pick_c = lax.broadcasted_iota(jnp.int32, (16, 256), 1)
    low_bits = lax.rem(pick_c, 8)
    pick = (pick_r == pick_c // 32 + 1 + low_bits) & (low_bits < 4) & (pick_r >= 2) & (pick_r < 11)
    gradient = dot_full(jnp.where(pick, 1.0, 0.0), c_buf[...].reshape(256, 128))
    inverse = lax.rsqrt(jnp.sum(gradient * gradient) * (1.0 / 81.0) + EPSILON)
    gradient = gradient * inverse
    for d in range(3):
        own = gradient if d == 0 else pltpu.roll(gradient, 128 - 16 * d, 1)
        own = jnp.where(lax.broadcasted_iota(jnp.int32, (16, 128), 1) < 3, own, 0.0)
        lc[d] = lc_own[d] - STEP_SIZE * own
        for a in range(9):
            coarse_out[d, a] = own[a + 2 : a + 3, 0:3]

    filler = jnp.zeros((112, 256), F32)
    exponents = []
    for d in range(3):
        column = jnp.concatenate(
            [
                dot_full(lm_own[d, pl.ds(2 * k + 2, 8), :], mbt[0]),
                dot_full(lc[d, pl.ds(q, 8), :], mbt[1]),
                filler,
            ],
            axis=0,
        )
        exponents.append(dot_full(mr[...], column))
    fixed_m = pooled_f[...].reshape(160, 256)
    halves = []
    for c in range(2):
        lanes = slice(128 * c, 128 * c + 128)
        corner = [[at[y][c][8 * z : 8 * z + 160] for y in (0, 1)] for z in (0, 1)]
        step = [[by[y][c][8 * z : 8 * z + 160] for y in (0, 1)] for z in (0, 1)]
        halves.append(weights(fixed_m[:, lanes], corner, step, [e[:, lanes] for e in exponents]))
    total = None
    for d in range(3):
        for c in range(2):
            term = dot_full(halves[c][d], mbx[d, 128 * c : 128 * c + 128, :])
            total = term if total is None else total + term
    m_part[...] = dot_rows(mr[...], total)[0:8]
    m_parts[s] = m_part[...]

    def part_copy(other):
        return remote(m_part, m_parts.at[s], tsend.at[other], trecv.at[s], (k, other))

    for other in range(SECS):

        @pl.when(s != other)
        def _():
            part_copy(other).start()

    for other in range(SECS):

        @pl.when(s != other)
        def _():
            remote(m_part, m_parts.at[other], tsend.at[other], trecv.at[other], (k, other)).wait_recv()

    m_tile[...] = (m_parts[0] + m_parts[1]) + (m_parts[2] + m_parts[3])
    m_buf[k] = m_tile[...]
    broadcast_start(k, s, m_tile, m_buf, bsem.at[2], bsem.at[3])

    for copy in (lat_to_next, lat_to_prev, z_to_next, z_to_prev):
        copy.wait_recv()

    @pl.when(s > 0)
    def _():
        to_bef.wait_recv()
        for copy in corner_up:
            copy.wait_recv()

    @pl.when(s < SECS - 1)
    def _():
        to_aft.wait_recv()
        for copy in corner_down:
            copy.wait_recv()

    @pl.when(s == 0)
    def _():
        y_bef[...] = jnp.zeros_like(y_bef)
        corners[0:2] = jnp.zeros((2, 2, 8, NX), F32)

    @pl.when(s == SECS - 1)
    def _():
        y_aft[...] = jnp.zeros_like(y_aft)
        corners[2:4] = jnp.zeros((2, 2, 8, NX), F32)

    lf[...] = jnp.zeros_like(lf)
    for d in range(3):
        lf[d, 0:5, :] = lf_prev[d, 15:20, :] * has_prev
        lf[d, 5:25, :] = lf_own[d, 0:20, :]
        lf[d, 25:35, :] = lf_next[d, 0:10, :] * has_next

    @pl.loop(0, NZ // 2)
    def _(pair):
        for half in range(2):
            rows = slice(4 * half, 4 * half + 4)
            for c in range(CHUNKS):
                lanes = slice(128 * c, 128 * c + 128)
                pad[c, 2 * pair + half + 4, 0:4, :] = y_bef[pair, rows, lanes]
                pad[c, 2 * pair + half + 4, 24:28, :] = y_aft[pair, rows, lanes]

    for plane in range(4):
        pair, rows = plane // 2, slice(4 * (plane % 2), 4 * (plane % 2) + 4)
        for c in range(CHUNKS):
            lanes = slice(128 * c, 128 * c + 128)
            for base, keep, middle, n in ((0, has_prev, z_bef, 0), (NZ + 4, has_next, z_aft, 1)):
                pad[c, base + plane, 0:4, :] = corners[n, pair, rows, lanes] * keep
                pad[c, base + plane, 4:24, :] = middle[plane, :, lanes] * keep
                pad[c, base + plane, 24:28, :] = corners[2 + n, pair, rows, lanes] * keep

    broadcast_wait(m_buf, bsem.at[2], bsem.at[3])
    pick_r = lax.broadcasted_iota(jnp.int32, (80, 256), 0)
    pick_c = lax.broadcasted_iota(jnp.int32, (80, 256), 1)
    pick = (pick_r == 2 * (pick_c // 8) + 2 + lax.rem(pick_c, 8)) & (pick_r >= 4) & (pick_r < 70)
    gradient = dot_full(jnp.where(pick, 1.0, 0.0), m_buf[...].reshape(256, 128))
    inverse = lax.rsqrt(jnp.sum(gradient * gradient) * (1.0 / 1782.0) + EPSILON)
    gradient = gradient * inverse
    for d in range(3):
        own = gradient if d == 0 else pltpu.roll(gradient, 128 - 16 * d, 1)
        own = jnp.where(lax.broadcasted_iota(jnp.int32, (80, 128), 1) < 9, own, 0.0)
        lm[d] = lm_own[d] - STEP_SIZE * own
        for a in range(33):
            mid_out[d, a] = own[2 * a + 4 : 2 * a + 6, 0:9]

    for copy in (lat_to_next, lat_to_prev, z_to_next, z_to_prev, *mid_same):
        copy.wait_send()

    @pl.when(up)
    def _():
        for copy in (to_bef, *corner_up, *mid_up):
            copy.wait_send()

    @pl.when(down)
    def _():
        for copy in (to_aft, *corner_down, *mid_down):
            copy.wait_send()

    for dk in range(3):
        for other in range(SECS):

            def left(dk=dk, other=other):
                piece_copy(dk, other).wait_send()

            if dk == 1:
                pl.when(s != other)(left)
            else:
                left()
    for other in range(SECS):

        @pl.when(s != other)
        def _():
            part_copy(other).wait_send()


def run_levels(moving, fixed, lat_fine, lat_mid, lat_coarse, off_mid, off_coarse):
    t = tables()
    names = ("px", "py", "pc", "mrz", "mry", "mbt", "mbx", "crz", "cry", "cbt", "cbx")
    vmem, smem, hbm = (pl.BlockSpec(memory_space=m) for m in (pltpu.VMEM, pltpu.SMEM, pl.ANY))
    shape = lambda *dims: jax.ShapeDtypeStruct(dims, F32)
    buf = lambda *dims: pltpu.VMEM(dims, F32)
    dma = pltpu.SemaphoreType.DMA
    return pl.pallas_call(
        levels_kernel,
        out_shape=[
            shape(3, 33, 2, 9), shape(3, 9, 1, 3), shape(3, 40, 128), shape(3, 80, 128),
            shape(3, 16, 128), shape(CHUNKS, NZ + 8, 32, 128),
        ],
        in_specs=[hbm, hbm, vmem, vmem, vmem, smem, smem] + [vmem] * len(names),
        out_specs=[vmem] * 6,
        scratch_shapes=[
            buf(NZ, NY, NX), buf(NZ, NY, NX), buf(20, 24, NX),
            buf(40, 8, NX), buf(40, 8, NX), buf(4, NY, NX), buf(4, NY, NX),
            buf(40, 8, NX), buf(40, 8, NX), buf(4, 2, 8, NX),
            buf(3, 24, 128), buf(3, 24, 128), buf(3, 24, 128), buf(3, 80, 128), buf(3, 16, 128),
            buf(20, 8, 256), buf(20, 8, 256), buf(20, 8, 256), buf(20, 8, 256), buf(2, 3, 4, 8, 256),
            buf(5, 8, 128), buf(3, SECS, 5, 8, 128), buf(20, 24, 128), buf(2, 28, 24, 128), buf(160, 128),
            buf(8, 128), buf(SLABS, 8, 128), buf(8, 128), buf(SECS, 8, 128), buf(8, 128), buf(SLABS, 8, 128),
            dma((8,)), dma((18,)), dma((18,)), dma((3, SECS)), dma((3, SECS)), dma((SECS,)), dma((SECS,)), dma((4,)),
        ],
        compiler_params=pltpu.CompilerParams(
            collective_id=0, has_side_effects=True, vmem_limit_bytes=VMEM_LIMIT
        ),
        name="levels",
    )(moving, fixed, lat_fine, lat_mid, lat_coarse, off_mid, off_coarse, *(t[n] for n in names))


def fine_kernel(
    pad, fixed, lf, lm, lc, off, rz, ry, bt, bx,
    out,
    at, by, spread, field, high, low, mixed,
):
    k, s = lax.axis_index("slab"), lax.axis_index("sec")
    q, r = k // 4, lax.rem(k, 4)
    at[:, :, 24:32, :] = jnp.zeros((CHUNKS, 21, 8, 128), F32)
    by[:, :, 24:32, :] = jnp.zeros((CHUNKS, 21, 8, 128), F32)

    columns = []
    for d in range(3):
        column = jnp.concatenate(
            [
                dot_full(lf[d], bt[0]),
                dot_full(lm[d, pl.ds(2 * k, 16), :], bt[1]),
                dot_full(lc[d, pl.ds(q, 8), :], bt[2]),
            ],
            axis=0,
        )
        upper, lower = parts(column)
        columns.append(jnp.concatenate([upper, upper, lower, lower], axis=0))

    low_lane = (lax.broadcasted_iota(jnp.int32, (48, 256), 1) // 64) % 2 == 1

    @pl.loop(0, 4)
    def _(block):
        base = block * SP

        @pl.loop(0, SP // 2)
        def _(pair):
            z = base + 2 * pair
            both = [rz[r, pl.ds(z + h, 1), :] * ry[s] for h in range(2)]
            both = jnp.concatenate(both, axis=0)
            upper, lower = parts(both)
            spread[pl.ds(pl.multiple_of(48 * pair, 48), 48), :] = jnp.where(low_lane, lower.astype(F32), upper.astype(F32)).astype(BF16)
            mixed[0, pl.ds(pl.multiple_of(480 * block + 48 * pair, 48), 48), :] = both[:, 0:128]

        for d in range(3):
            field[d] = dot(spread[...], columns[d])

        oz, oy, ox = off[0, block, s], off[1, block, s], off[2, block, s]

        @pl.loop(0, SP + 1)
        def _(plane):
            window = [pad[c, base + 4 + oz + plane, pl.ds(4 + oy, 24), :] for c in range(CHUNKS)]
            here, there = shift_lanes(window, ox), shift_lanes(window, ox + 1)
            for c in range(CHUNKS):
                at[c, plane, 0:24, :] = here[c]
                by[c, plane, 0:24, :] = there[c] - here[c]

        rest = jnp.zeros((4, 128), F32)

        @pl.loop(0, SP // 2)
        def _(pair):
            for c in range(CHUNKS):
                lanes = slice(128 * c, 128 * c + 128)
                found = []
                for h in range(2):
                    plane = 2 * pair + h
                    corner = [[at[c, plane + z, y : y + 24, :] for y in (0, 1)] for z in (0, 1)]
                    step = [[by[c, plane + z, y : y + 24, :] for y in (0, 1)] for z in (0, 1)]
                    rows = pl.ds(pl.multiple_of(24 * plane, 8), 24)
                    exponents = [field[d, rows, lanes] for d in range(3)]
                    atlas = jnp.concatenate([fixed[base + plane, :, lanes], rest], axis=0)
                    found.append(weights(atlas, corner, step, exponents))
                rows = pl.ds(pl.multiple_of(48 * pair, 48), 48)
                for d in range(3):
                    upper, lower = parts(jnp.concatenate([found[0][d], found[1][d]], axis=0))
                    high[d, rows, lanes] = upper
                    low[d, rows, lanes] = lower

        total = None
        for d in range(3):
            wide = dot(high[d], bx[d])
            term = (wide[:, 0:128] + wide[:, 128:256]) + dot(low[d], bx[d, :, 0:128])
            total = term if total is None else total + term
        mixed[1, pl.ds(pl.multiple_of(480 * block, 480), 480), :] = total

    out[...] = dot_rows(mixed[0], mixed[1])[0:40]


def run_fine(pad, fixed, lf, lm, lc, off):
    t = tables()
    vmem, smem = (pl.BlockSpec(memory_space=m) for m in (pltpu.VMEM, pltpu.SMEM))
    buf = lambda *dims: pltpu.VMEM(dims, F32)
    return pl.pallas_call(
        fine_kernel,
        out_shape=jax.ShapeDtypeStruct((40, 128), F32),
        in_specs=[vmem] * 5 + [smem] + [vmem] * 4,
        out_specs=vmem,
        scratch_shapes=[
            buf(CHUNKS, 21, 32, 128), buf(CHUNKS, 21, 32, 128), pltpu.VMEM((480, 256), BF16),
            buf(3, 480, NX), pltpu.VMEM((3, 480, NX), BF16), pltpu.VMEM((3, 480, NX), BF16), buf(2, 1920, 128),
        ],
        compiler_params=pltpu.CompilerParams(vmem_limit_bytes=VMEM_LIMIT),
        name="fine",
    )(pad, fixed, lf, lm, lc, off, t["rz"], t["ry"], t["bt"], t["bx"])


def sums_kernel(
    part, out,
    mates, befores, afters, own, tile, tiles, send, recv, bsem,
):
    k, s = lax.axis_index("slab"), lax.axis_index("sec")
    nxt, prv = lax.rem(k + 1, SLABS), lax.rem(k + SLABS - 1, SLABS)
    greet(k, s)
    head, tail = part.at[pl.ds(0, 8)], part.at[pl.ds(24, 16)]

    def mate(other, slot):
        return remote(part, mates.at[slot], send.at[0, other], recv.at[0, slot], (k, other))

    def to_next(other, slot):
        return remote(tail, befores.at[slot], send.at[1, other], recv.at[1, slot], (nxt, other))

    def to_prev(other, slot):
        return remote(head, afters.at[slot], send.at[2, other], recv.at[2, slot], (prv, other))

    for other in range(SECS):
        pl.when(s != other)(lambda other=other: mate(other, s).start())
        to_next(other, s).start()
        to_prev(other, s).start()
    mates[s] = part[...]
    for other in range(SECS):
        pl.when(s != other)(lambda other=other: mate(other, other).wait_recv())
        to_next(other, other).wait_recv()
        to_prev(other, other).wait_recv()
    whole = (mates[0] + mates[1]) + (mates[2] + mates[3])
    before = ((befores[0] + befores[1]) + (befores[2] + befores[3])) * (k > 0).astype(F32)
    after = ((afters[0] + afters[1]) + (afters[2] + afters[3])) * (k < SLABS - 1).astype(F32)
    own[...] = jnp.zeros_like(own)
    own[0:20, :] = whole[5:25]
    own[0:10, :] = own[0:10, :] + before[1:11]
    own[15:20, :] = own[15:20, :] + after[0:5]
    gradient = own[...]
    tile[...] = jnp.full((8, 128), jnp.sum(gradient * gradient))
    tiles[k] = tile[...]
    broadcast_start(k, s, tile, tiles, bsem.at[0], bsem.at[1])
    broadcast_wait(tiles, bsem.at[0], bsem.at[1])
    squares = jnp.sum(tiles[...], axis=0)[0:1, :]
    gradient = gradient * lax.rsqrt(squares * (1.0 / 63360.0) + EPSILON)
    for d in range(3):
        mine = gradient if d == 0 else pltpu.roll(gradient, 128 - 40 * d, 1)
        for a in range(4):
            out[d, a] = mine[5 * a : 5 * a + 5, 0:33]
    for other in range(SECS):
        pl.when(s != other)(lambda other=other: mate(other, s).wait_send())
        to_next(other, s).wait_send()
        to_prev(other, s).wait_send()


def run_sums(part):
    vmem = pl.BlockSpec(memory_space=pltpu.VMEM)
    buf = lambda *dims: pltpu.VMEM(dims, F32)
    dma = pltpu.SemaphoreType.DMA
    return pl.pallas_call(
        sums_kernel,
        out_shape=jax.ShapeDtypeStruct((3, 4, 5, 33), F32),
        in_specs=[vmem],
        out_specs=vmem,
        scratch_shapes=[
            buf(SECS, 40, 128), buf(SECS, 16, 128), buf(SECS, 8, 128), buf(24, 128), buf(8, 128), buf(SLABS, 8, 128),
            dma((3, SECS)), dma((3, SECS)), dma((2,)),
        ],
        compiler_params=pltpu.CompilerParams(
            collective_id=1, has_side_effects=True, vmem_limit_bytes=VMEM_LIMIT
        ),
        name="sums",
    )(part)


def body(
    fixed_image,
    moving_image,
    lattice_fine,
    lattice_mid,
    lattice_coarse,
    offset_fine,
    offset_mid,
    offset_coarse,
):
    mid_step, coarse_step, lf, lm, lc, pad = run_levels(
        moving_image, fixed_image, lattice_fine, lattice_mid, lattice_coarse, offset_mid, offset_coarse
    )
    part = run_fine(pad, fixed_image, lf, lm, lc, offset_fine)
    return (run_sums(part), mid_step, coarse_step)


def solution(mesh):
    placed = (
        P("slab", "sec", None),
        P("slab", "sec", None),
        P(None, "slab", None, None),
        P(),
        P(),
        P(None, "slab", None),
        P(None, "slab", None),
        P(),
    )
    return jax.shard_map(
        body,
        mesh=mesh,
        in_specs=placed,
        out_specs=(P(None, "slab", None, None), P(), P()),
        check_vma=False,
    )
```

```python
import functools

import jax
import jax.numpy as jnp
import ml_dtypes
import numpy as np
from jax import lax
from jax.experimental import pallas as pl
from jax.experimental.pallas import tpu as pltpu
from jax.sharding import PartitionSpec as P

SP = 20
EPSILON = 1e-06
STEP_SIZE = 0.5
HIGHEST = lax.Precision.HIGHEST
F32 = jnp.float32
BF16 = jnp.bfloat16
MESH = pl.DeviceIdType.MESH
SLABS = 32
SECS = 4
NZ, NY, NX = 80, 20, 640
CHUNKS = NX // 128
LOG2E = 1.4426950408889634
VMEM_LIMIT = 58 * 1024 * 1024


def basis(rows, knots, factor, coarse):
    rows, knots = np.asarray(rows, np.float64), np.asarray(knots, np.float64)
    position = factor * rows + 0.5 * (factor - 1)
    centre = SP * coarse * knots + 0.5 * (coarse - 1)
    distance = np.abs((position[:, None] - centre[None, :]) / (SP * coarse))
    near = 2.0 / 3.0 - distance**2 + 0.5 * distance**3
    far = np.maximum(2.0 - distance, 0.0) ** 3 / 6.0
    return np.where(distance < 1.0, near, far)


@functools.cache
def tables():
    t = {}
    rz, ry = np.zeros((4, 4, 24, 64)), np.zeros((4, 24, 64))
    z, y, x = np.arange(NZ), np.arange(NY), np.arange(NX)
    for r in range(4):
        for block in range(4):
            rows = z[20 * block : 20 * block + 20]
            for a in range(7):
                rz[r, block, :20, a:40:8] = basis(rows, [a - 1], 1, 1)
            for a in range(5):
                rz[r, block, :20, 40 + a : 56 : 8] = basis(rows, [a - 2], 1, 4)
                rz[r, block, :20, 56 + a : 57 + a] = basis(rows + 80 * r, [a - 2], 1, 16)
    for s in range(4):
        for a in range(7):
            ry[s, :NY, a:40:8] = basis(y + 20 * s, range(5), 1, 1)
        for a in range(5):
            ry[s, :NY, 40 + a : 56 : 8] = basis(y + 20 * s, range(2), 1, 4)
            ry[s, :NY, 56 + a : 57 + a] = basis(y + 20 * s, [0], 1, 16)
    t["rz"] = np.tile(rz, (1, 1, 1, 4)).astype(np.float32)
    t["ry"] = np.tile(ry, (1, 1, 4)).astype(np.float32)
    across = np.zeros((3, 128, NX))
    across[0, :33] = basis(x, range(33), 1, 1).T
    across[1, :9] = basis(x, range(9), 1, 4).T
    across[2, :3] = basis(x, range(3), 1, 16).T
    t["bt"] = (-LOG2E * across).astype(np.float32)
    along = np.zeros((NX, 128), np.float32)
    along[:, :33] = basis(x, range(33), 1, 1)
    t["bx"] = along
    rz, ry = np.zeros((4, 24, 128)), np.zeros((4, 8, 128))
    z, y, x = np.arange(20), np.arange(5), np.arange(160)
    for r in range(4):
        for a in range(4):
            rz[r, :20, a:16:8] = basis(z, [a - 1], 4, 4)
        for a in range(5):
            rz[r, :20, 16 + a : 17 + a] = basis(z + 20 * r, [a - 2], 4, 16)
    for s in range(4):
        for a in range(4):
            ry[s, :5, a:16:8] = basis(y + 5 * s, range(2), 4, 4)
        for a in range(5):
            ry[s, :5, 16 + a : 17 + a] = basis(y + 5 * s, [0], 4, 16)
    t["mrz"], t["mry"] = rz.astype(np.float32), ry.astype(np.float32)
    across = np.zeros((2, 128, 256))
    across[0, :9, :160] = basis(x, range(9), 4, 4).T
    across[1, :3, :160] = basis(x, range(3), 4, 16).T
    t["mbt"] = (-LOG2E * across).astype(np.float32)
    spread = np.zeros((3, 256, 128), np.float32)
    for d in range(3):
        spread[d, :160, 16 * d : 16 * d + 9] = basis(x, range(9), 4, 4)
    t["mbx"] = spread
    rz, ry = np.zeros((4, 8, 128)), np.zeros((8, 128))
    z, y, x = np.arange(5), np.arange(5), np.arange(40)
    for r in range(4):
        for a in range(4):
            rz[r, :5, a : a + 1] = basis(z + 5 * r, [a - 1], 16, 16)
    ry[:5, :4] = basis(y, [0], 16, 16)
    t["crz"], t["cry"] = rz.astype(np.float32), ry.astype(np.float32)
    across = np.zeros((128, 128))
    across[:3, :40] = basis(x, range(3), 16, 16).T
    t["cbt"] = (-LOG2E * across).astype(np.float32)
    spread = np.zeros((3, 128, 128), np.float32)
    for d in range(3):
        spread[d, :40, 16 * d : 16 * d + 3] = basis(x, range(3), 16, 16)
    t["cbx"] = spread
    pool = np.zeros((120, 400), ml_dtypes.bfloat16)
    for row in range(5):
        for plane in range(80):
            pool[24 * row + plane // 4, 80 * row + plane] = 1
    t["pz"] = pool
    pool = np.zeros((2, 256, 128), np.float32)
    pool[0, np.arange(160), np.arange(160) // 4] = 1
    pool[1, np.arange(160), 64 + np.arange(160) // 4] = 1
    t["pcx"] = pool
    pool = np.zeros((16, 48), np.float32)
    for part in range(2):
        for plane in range(20):
            pool[8 * part + plane // 4, 24 * part + plane] = 1
    t["pcz"] = pool
    return t


def dot(a, b):
    return jnp.dot(a, b, preferred_element_type=F32)


def dot_full(a, b):
    return jnp.dot(a, b, precision=HIGHEST, preferred_element_type=F32)


def dot_rows(a, b):
    return lax.dot_general(
        a, b, (((0,), (0,)), ((), ())), precision=HIGHEST, preferred_element_type=F32
    )


def parts(values):
    high = values.astype(BF16)
    return high, (values - high.astype(F32)).astype(BF16)


def shift_lanes(chunks, shift):
    amount = lax.rem(256 - shift, 128)
    rolled = [pltpu.roll(chunk, amount, 1) for chunk in chunks]
    lane = lax.broadcasted_iota(jnp.int32, chunks[0].shape, 1)
    first = lane < jnp.maximum(-shift, 0)
    last = lane >= 128 - jnp.maximum(shift, 0)
    zero = jnp.zeros_like(chunks[0])
    padded = [zero, *rolled, zero]
    return [
        jnp.where(first, padded[j], jnp.where(last, padded[j + 2], padded[j + 1]))
        for j in range(len(chunks))
    ]


def fraction(exponent):
    grown = jnp.exp2(exponent)
    total = 1.0 + grown
    frac = pl.reciprocal(total, approx=True)
    frac = frac * (2.0 - total * frac)
    return frac, frac * (grown * frac)


def weights(fixed, corner, step, exponents):
    (fz, gz), (fy, gy), (fx, gx) = (fraction(e) for e in exponents)
    line = [[corner[z][y] + fx * step[z][y] for y in (0, 1)] for z in (0, 1)]
    rise = [line[z][1] - line[z][0] for z in (0, 1)]
    plane = [line[z][0] + fy * rise[z] for z in (0, 1)]
    slope_z = plane[1] - plane[0]
    residual = (plane[0] + fz * slope_z) - fixed
    slope_y = rise[0] + fz * (rise[1] - rise[0])
    along = [step[z][0] + fy * (step[z][1] - step[z][0]) for z in (0, 1)]
    slope_x = along[0] + fz * (along[1] - along[0])
    return [
        (residual * slope_z) * gz,
        (residual * slope_y) * gy,
        (residual * slope_x) * gx,
    ]


def greet(k, s):
    barrier = pltpu.get_barrier_semaphore()

    def signal(slab, sec):
        pl.semaphore_signal(barrier, inc=1, device_id=(slab, sec), device_id_type=MESH)

    @pl.loop(1, SLABS)
    def _(i):
        signal(lax.rem(k + i, SLABS), s)

    for i in range(1, SECS):
        other = lax.rem(s + i, SECS)
        signal(k, other)
        signal(lax.rem(k + 1, SLABS), other)
        signal(lax.rem(k + SLABS - 1, SLABS), other)
    return lambda: pl.semaphore_wait(barrier, SLABS - 1 + 3 * (SECS - 1))


def broadcast_start(k, s, tile, buffer, send_sem, recv_sem):
    @pl.loop(1, SLABS)
    def _(i):
        pltpu.make_async_remote_copy(
            src_ref=tile,
            dst_ref=buffer.at[k],
            send_sem=send_sem,
            recv_sem=recv_sem,
            device_id=(lax.rem(k + i, SLABS), s),
            device_id_type=MESH,
        ).start()


def broadcast_wait(buffer, send_sem, recv_sem):
    part = buffer.at[pl.ds(0, SLABS - 1)]
    pltpu.make_async_copy(part, part, recv_sem).wait()
    pltpu.make_async_copy(part, part, send_sem).wait()


def remote(src, dst, send_sem, recv_sem, device):
    return pltpu.make_async_remote_copy(
        src_ref=src,
        dst_ref=dst,
        send_sem=send_sem,
        recv_sem=recv_sem,
        device_id=device,
        device_id_type=MESH,
    )


def around(k, s, source, buffer, send, recv, act):
    slabs = (lax.rem(k + SLABS - 1, SLABS), k, lax.rem(k + 1, SLABS))

    def one(dk, other):
        if act == "wait_recv":
            copy = remote(source, buffer.at[dk, other], send.at[dk, other], recv.at[dk, other], (k, other))
        else:
            copy = remote(
                source, buffer.at[2 - dk, s], send.at[dk, other], recv.at[2 - dk, s], (slabs[dk], other)
            )
        getattr(copy, act)()

    for dk in range(3):
        for other in range(SECS):
            if dk == 1:
                pl.when(s != other)(functools.partial(one, dk, other))
            else:
                one(dk, other)


def kernel(
    moving, fixed, lat_fine, lat_mid, lat_coarse, off_fine, off_mid, off_coarse,
    rz_hbm, bt_hbm, bx_hbm, ry, pz, pcx, pcz, mrz, mry, mbt, mbx, crz, cry, cbt, cbx,
    fine_out, mid_out, coarse_out,
    rz, bt, bf, bx, pad, fx, sums, zlo, zhi, z_bef, z_aft, corners,
    lf_own, lf_prev, lf_next, lf, mt, lm_own, lc_own, lm, lc,
    pooled_m, pooled_f, pm_bef, pm_aft, pm_halo,
    piece, pieces, cv, cf, mm, mr,
    c_tile, c_buf, m_part, m_parts, m_tile, m_buf,
    at, by, spread, field, high, low, mixed,
    f_part, f_parts, f_tile, f_buf,
    load_sem, send, recv, psend, precv, fsend, frecv, tsend, trecv, bsem,
):
    k, s = lax.axis_index("slab"), lax.axis_index("sec")
    nxt, prv = lax.rem(k + 1, SLABS), lax.rem(k + SLABS - 1, SLABS)
    q, r = k // 4, lax.rem(k, 4)
    has_prev, has_next = (k > 0).astype(F32), (k < SLABS - 1).astype(F32)
    up, down = s < SECS - 1, s > 0
    own_y, own_z = pl.ds(4, NY), pl.ds(8, NZ)

    load_moving = [
        pltpu.make_async_copy(
            moving.at[:, :, pl.ds(128 * c, 128)], pad.at[c, own_y, own_z], load_sem.at[c]
        )
        for c in range(CHUNKS)
    ]
    load_fixed = [
        pltpu.make_async_copy(
            fixed.at[:, :, pl.ds(128 * c, 128)], fx.at[c, :, pl.ds(0, NZ)], load_sem.at[CHUNKS + c]
        )
        for c in range(CHUNKS)
    ]
    load_tables = [
        pltpu.make_async_copy(src, dst, load_sem.at[2 * CHUNKS + n])
        for n, (src, dst) in enumerate(((rz_hbm, rz), (bt_hbm, bt), (bx_hbm, bf)))
    ]
    for copy in (*load_moving, *load_fixed, *load_tables):
        copy.start()
    all_here = greet(k, s)

    for ref in (lf_own, mt, lm_own, lc_own, cv, mm):
        ref[...] = jnp.zeros_like(ref)
    eye = lax.broadcasted_iota(jnp.int32, (16, 128), 0) == lax.broadcasted_iota(jnp.int32, (16, 128), 1)
    eye = jnp.where(eye, 1.0, 0.0)
    for d in range(3):
        for b in range(5):
            lf_own[d, b, 0:4, 0:33] = lat_fine[d, b]
        for a in range(9):
            for b in range(2):
                mt[d, b, a : a + 1, 0:33] = lat_mid[d, a, b : b + 1]
        for a in range(3):
            mt[d, 2, a : a + 1, 0:9] = lat_coarse[d, a]
    for d in range(3):
        for b in range(2):
            lm_own[d, b, 2:42, :] = dot_rows(mt[d, b], eye)[0:40]
        lc_own[d, 2:16, :] = dot_rows(mt[d, 2], eye)[0:14]
    for c in range(CHUNKS):
        pad[c, :, 0:8, :] = jnp.zeros((28, 8, 128), F32)
        pad[c, :, 88:96, :] = jnp.zeros((28, 8, 128), F32)
        fx[c, :, 80:88, :] = jnp.zeros((NY, 8, 128), F32)

    @pl.when(s == 0)
    def _():
        pad[:, 0:4, 8:88, :] = jnp.zeros((CHUNKS, 4, NZ, 128), F32)
        corners[0:2] = jnp.zeros((2, CHUNKS, 2, 8, 128), F32)
        pm_bef[...] = jnp.zeros_like(pm_bef)
        pm_halo[:, 0] = jnp.zeros((2, 5, 8, 256), F32)

    @pl.when(s == SECS - 1)
    def _():
        pad[:, 24:28, 8:88, :] = jnp.zeros((CHUNKS, 4, NZ, 128), F32)
        corners[2:4] = jnp.zeros((2, CHUNKS, 2, 8, 128), F32)
        pm_aft[...] = jnp.zeros_like(pm_aft)
        pm_halo[:, 2] = jnp.zeros((2, 5, 8, 256), F32)

    four_x = lax.broadcasted_iota(jnp.int32, (NX, 256), 0) // 4
    four_x = jnp.where(four_x == lax.broadcasted_iota(jnp.int32, (NX, 256), 1), 1.0, 0.0).astype(BF16)

    def pooled():
        high, low = parts(sums[...].reshape(400, NX))
        table = four_x
        high, low = parts(dot(high, table) + dot(low, table))
        table = pz[...]
        return ((dot(table, high) + dot(table, low)) * (1.0 / 64.0)).reshape(5, 24, 256)

    for copy in load_moving:
        copy.wait()
    for c in range(CHUNKS):
        lanes = slice(128 * c, 128 * c + 128)

        @pl.loop(0, 5)
        def _(group):
            four = [pad[c, 4 * group + 4 + i, 8:88, :] for i in range(4)]
            sums[group, :, lanes] = (four[0] + four[1]) + (four[2] + four[3])

        @pl.loop(0, NY // 2)
        def _(pair):
            for half in range(2):
                rows = slice(4 * half, 4 * half + 4)
                zlo[c, pair, rows, :] = pad[c, 2 * pair + half + 4, 8:12, :]
                zhi[c, pair, rows, :] = pad[c, 2 * pair + half + 4, 84:88, :]

    pooled_m[...] = pooled()
    all_here()

    lat_to_next = remote(lf_own, lf_prev, send.at[0], recv.at[0], (nxt, s))
    lat_to_prev = remote(lf_own, lf_next, send.at[1], recv.at[1], (prv, s))
    z_to_next = remote(zhi, z_bef, send.at[2], recv.at[2], (nxt, s))
    z_to_prev = remote(zlo, z_aft, send.at[3], recv.at[3], (prv, s))
    to_bef = remote(
        pad.at[:, pl.ds(20, 4), own_z], pad.at[:, pl.ds(0, 4), own_z], send.at[4], recv.at[4], (k, s + 1)
    )
    to_aft = remote(
        pad.at[:, pl.ds(4, 4), own_z], pad.at[:, pl.ds(24, 4), own_z], send.at[5], recv.at[5], (k, s - 1)
    )
    first, last = pl.ds(0, 2), pl.ds(8, 2)
    corner_up = [
        remote(zhi.at[:, last], corners.at[0], send.at[6], recv.at[6], (nxt, s + 1)),
        remote(zlo.at[:, last], corners.at[1], send.at[7], recv.at[7], (prv, s + 1)),
    ]
    corner_down = [
        remote(zhi.at[:, first], corners.at[2], send.at[8], recv.at[8], (nxt, s - 1)),
        remote(zlo.at[:, first], corners.at[3], send.at[9], recv.at[9], (prv, s - 1)),
    ]
    head, tail = pl.ds(0, 8), pl.ds(16, 8)
    mid_same = [
        remote(pooled_m.at[:, tail], pm_halo.at[0, 1], send.at[10], recv.at[10], (nxt, s)),
        remote(pooled_m.at[:, head], pm_halo.at[1, 1], send.at[11], recv.at[11], (prv, s)),
    ]
    mid_up = [
        remote(pooled_m, pm_bef, send.at[12], recv.at[12], (k, s + 1)),
        remote(pooled_m.at[:, tail], pm_halo.at[0, 0], send.at[13], recv.at[13], (nxt, s + 1)),
        remote(pooled_m.at[:, head], pm_halo.at[1, 0], send.at[14], recv.at[14], (prv, s + 1)),
    ]
    mid_down = [
        remote(pooled_m, pm_aft, send.at[15], recv.at[15], (k, s - 1)),
        remote(pooled_m.at[:, tail], pm_halo.at[0, 2], send.at[16], recv.at[16], (nxt, s - 1)),
        remote(pooled_m.at[:, head], pm_halo.at[1, 2], send.at[17], recv.at[17], (prv, s - 1)),
    ]
    for copy in mid_same:
        copy.start()

    @pl.when(up)
    def _():
        for copy in mid_up:
            copy.start()

    @pl.when(down)
    def _():
        for copy in mid_down:
            copy.start()

    for copy in load_fixed:
        copy.wait()

    @pl.loop(0, 5)
    def _(group):
        for c in range(CHUNKS):
            lanes = slice(128 * c, 128 * c + 128)
            four = [fx[c, 4 * group + i, 0:80, :] for i in range(4)]
            sums[group, :, lanes] = (four[0] + four[1]) + (four[2] + four[3])

    pooled_f[...] = pooled()

    both = None
    for n, ref in enumerate((pooled_m, pooled_f)):
        upper, lower = jnp.zeros((24, 256), F32), jnp.zeros((24, 256), F32)
        for i in range(5):
            keep = (i + s < 4).astype(F32)
            upper = upper + ref[i] * keep
            lower = lower + ref[i] * (1.0 - keep)
        term = dot_full(jnp.concatenate([upper, lower], axis=0), pcx[n])
        both = term if both is None else both + term
    piece[...] = (dot_full(pcz[...], both) * (1.0 / 64.0)).reshape(2, 8, 128)
    pieces[1, s] = piece[...]
    around(k, s, piece, pieces, psend, precv, "start")

    for copy in (lat_to_next, lat_to_prev):
        copy.start()

    @pl.when(up)
    def _():
        to_bef.start()

    @pl.when(down)
    def _():
        to_aft.start()

    for copy in (z_to_next, z_to_prev):
        copy.start()

    @pl.when(up)
    def _():
        for copy in corner_up:
            copy.start()

    @pl.when(down)
    def _():
        for copy in corner_down:
            copy.start()

    around(k, s, piece, pieces, psend, precv, "wait_recv")

    lane = lax.broadcasted_iota(jnp.int32, (5, 128), 1)
    for dk in range(3):
        scale = (has_prev, jnp.float32(1.0), has_next)[dk]
        rows = (slice(3, 8), slice(8, 13), slice(13, 18))[dk]
        for c in range(5):
            value = jnp.zeros((8, 128), F32)
            if c < 4:
                value = value + pieces[dk, c, 0]
            if c > 0:
                value = value + pieces[dk, c - 1, 1]
            cv[4 + c, rows, :] = jnp.where(lane < 40, value[0:5], 0.0) * scale
            if dk == 1:
                cf[c] = value
    fixed_c = pltpu.roll(cf[...].reshape(40, 128), 64, 1)

    oz, oy, ox = off_coarse[0, 0, q], off_coarse[1, 0, q], off_coarse[2, 0, q]
    a_z, b_z = [], []
    for e in (0, 1):
        window = cv[pl.ds(4 + oy, 6), pl.ds(8 + oz + e, 8), :].reshape(48, 128)
        here, there = shift_lanes([window], ox)[0], shift_lanes([window], ox + 1)[0]
        a_z.append(here)
        b_z.append(there - here)
    corner = [[a_z[z][8 * y : 8 * y + 40] for y in (0, 1)] for z in (0, 1)]
    step = [[b_z[z][8 * y : 8 * y + 40] for y in (0, 1)] for z in (0, 1)]
    cr = jnp.concatenate([crz[r] * cry[y : y + 1, :] for y in range(5)], axis=0)
    filler = jnp.zeros((120, 128), F32)
    exponents = []
    for d in range(3):
        column = dot_full(lc_own[d, pl.ds(q + 1, 8), :], cbt[...])
        exponents.append(dot_full(cr, jnp.concatenate([column, filler], axis=0)))
    total = None
    for d, weight in enumerate(weights(fixed_c, corner, step, exponents)):
        term = dot_full(weight, cbx[d])
        total = term if total is None else total + term
    c_tile[...] = dot_rows(cr, total)[0:8]
    c_buf[k] = c_tile[...]
    broadcast_start(k, s, c_tile, c_buf, bsem.at[0], bsem.at[1])

    for y in range(5):
        mr[24 * y : 24 * y + 24, :] = mrz[r] * mry[s, y : y + 1, :]
    for copy in mid_same:
        copy.wait_recv()

    @pl.when(s > 0)
    def _():
        for copy in mid_up:
            copy.wait_recv()

    @pl.when(s < SECS - 1)
    def _():
        for copy in mid_down:
            copy.wait_recv()

    for c in range(2):
        lanes = slice(128 * c, 128 * c + 128)
        for e, whole in enumerate((pm_bef, pooled_m, pm_aft)):
            for y in range(5):
                mm[c, 5 * e + y, 4:8, :] = pm_halo[0, e, y, 0:4, lanes] * has_prev
                mm[c, 5 * e + y, 8:28, :] = whole[y, 0:20, lanes]
                mm[c, 5 * e + y, 28:32, :] = pm_halo[1, e, y, 0:4, lanes] * has_next

    oz, oy, ox = off_mid[0, 0, 0], off_mid[0, 0, 1], off_mid[0, 0, 2]
    a_z, b_z = [], []
    for e in (0, 1):
        window = [mm[c, pl.ds(5 + oy, 6), pl.ds(8 + oz + e, 24), :].reshape(144, 128) for c in range(2)]
        here, there = shift_lanes(window, ox), shift_lanes(window, ox + 1)
        a_z.append(here)
        b_z.append([there[c] - here[c] for c in range(2)])

    load_tables[0].wait()
    low_lane = (lax.broadcasted_iota(jnp.int32, (48, 256), 1) // 64) % 2 == 1

    @pl.loop(0, 4)
    def _(block):
        @pl.loop(0, NY // 2)
        def _(pair):
            two = [rz[r, block] * ry[s, pl.ds(2 * pair + h, 1), :] for h in range(2)]
            two = jnp.concatenate(two, axis=0)
            upper, lower = parts(two)
            rows = pl.ds(pl.multiple_of(480 * block + 48 * pair, 48), 48)
            spread[rows, :] = jnp.where(low_lane, lower.astype(F32), upper.astype(F32)).astype(BF16)
            mixed[0, rows, :] = two[:, 0:128]

    load_tables[2].wait()
    for d in range(3):
        upper, lower = parts(bf[...] if d == 0 else pltpu.roll(bf[...], 40 * d, 1))
        bx[d, :, 0:128] = upper
        bx[d, :, 128:256] = lower

    broadcast_wait(c_buf, bsem.at[0], bsem.at[1])
    pick_r = lax.broadcasted_iota(jnp.int32, (16, 256), 0)
    pick_c = lax.broadcasted_iota(jnp.int32, (16, 256), 1)
    low_bits = lax.rem(pick_c, 8)
    pick = (pick_r == pick_c // 32 + 1 + low_bits) & (low_bits < 4) & (pick_r >= 2) & (pick_r < 11)
    gradient = dot_full(jnp.where(pick, 1.0, 0.0), c_buf[...].reshape(256, 128))
    gradient = gradient * lax.rsqrt(jnp.sum(gradient * gradient) * (1.0 / 81.0) + EPSILON)
    for d in range(3):
        own = gradient if d == 0 else pltpu.roll(gradient, 128 - 16 * d, 1)
        own = jnp.where(lax.broadcasted_iota(jnp.int32, (16, 128), 1) < 3, own, 0.0)
        lc[d] = lc_own[d] - STEP_SIZE * own
    mt[0, 0] = gradient

    filler = jnp.zeros((104, 256), F32)
    exponents = []
    for d in range(3):
        column = jnp.concatenate(
            [
                dot_full(lm_own[d, 0, pl.ds(k + 1, 8), :], mbt[0]),
                dot_full(lm_own[d, 1, pl.ds(k + 1, 8), :], mbt[0]),
                dot_full(lc[d, pl.ds(q, 8), :], mbt[1]),
                filler,
            ],
            axis=0,
        )
        exponents.append(dot_full(mr[...], column))
    fixed_m = pooled_f[...].reshape(120, 256)
    halves = []
    for c in range(2):
        lanes = slice(128 * c, 128 * c + 128)
        corner = [[a_z[z][c][24 * y : 24 * y + 120] for y in (0, 1)] for z in (0, 1)]
        step = [[b_z[z][c][24 * y : 24 * y + 120] for y in (0, 1)] for z in (0, 1)]
        halves.append(weights(fixed_m[:, lanes], corner, step, [e[:, lanes] for e in exponents]))
    total = None
    for d in range(3):
        for c in range(2):
            term = dot_full(halves[c][d], mbx[d, 128 * c : 128 * c + 128, :])
            total = term if total is None else total + term
    m_part[...] = dot_rows(mr[...], total)[0:16]
    m_parts[s] = m_part[...]

    def part_copies(act):
        for other in range(SECS):

            @pl.when(s != other)
            def _():
                slot = other if act == "wait_recv" else s
                getattr(remote(m_part, m_parts.at[slot], tsend.at[other], trecv.at[slot], (k, other)), act)()

    part_copies("start")
    part_copies("wait_recv")
    m_tile[...] = (m_parts[0] + m_parts[1]) + (m_parts[2] + m_parts[3])
    m_buf[k] = m_tile[...]
    broadcast_start(k, s, m_tile, m_buf, bsem.at[2], bsem.at[3])

    turn_r = lax.broadcasted_iota(jnp.int32, (48, 128), 0)
    turn = jnp.where(turn_r == lax.broadcasted_iota(jnp.int32, (48, 128), 1) + 2, 1.0, 0.0)
    turned = dot_rows(mt[0, 0], turn[0:16])
    for d in range(3):
        for a in range(3):
            coarse_out[d, a] = turned[16 * d + a : 16 * d + a + 1, 0:9]

    for copy in (lat_to_next, lat_to_prev, z_to_next, z_to_prev):
        copy.wait_recv()

    @pl.when(s > 0)
    def _():
        for copy in (to_bef, *corner_up):
            copy.wait_recv()

    @pl.when(s < SECS - 1)
    def _():
        for copy in (to_aft, *corner_down):
            copy.wait_recv()

    for d in range(3):
        for b in range(5):
            lf[d, 8 * b : 8 * b + 1, :] = lf_prev[d, b, 3:4, :] * has_prev
            lf[d, 8 * b + 1 : 8 * b + 5, :] = lf_own[d, b, 0:4, :]
            lf[d, 8 * b + 5 : 8 * b + 7, :] = lf_next[d, b, 0:2, :] * has_next
            lf[d, 8 * b + 7 : 8 * b + 8, :] = jnp.zeros((1, 128), F32)

    @pl.loop(0, NY // 2)
    def _(pair):
        for half in range(2):
            rows = slice(4 * half, 4 * half + 4)
            for c in range(CHUNKS):
                pad[c, 2 * pair + half + 4, 4:8, :] = z_bef[c, pair, rows, :] * has_prev
                pad[c, 2 * pair + half + 4, 88:92, :] = z_aft[c, pair, rows, :] * has_next

    for y in range(4):
        rows = slice(4 * (y % 2), 4 * (y % 2) + 4)
        for c in range(CHUNKS):
            for n in range(2):
                where = slice(4, 8) if n == 0 else slice(88, 92)
                keep = has_prev if n == 0 else has_next
                pad[c, y, where, :] = corners[n, c, y // 2, rows, :] * keep
                pad[c, 24 + y, where, :] = corners[2 + n, c, y // 2, rows, :] * keep

    for c in range(CHUNKS):
        for block in range(4):
            at[block, c, :, 24:32, :] = jnp.zeros((21, 8, 128), F32)
            by[block, c, :, 24:32, :] = jnp.zeros((21, 8, 128), F32)

    @pl.loop(0, 4)
    def _(block):
        oz, oy, ox = off_fine[0, block, s], off_fine[1, block, s], off_fine[2, block, s]

        @pl.loop(0, NY + 1)
        def _(y):
            window = [pad[c, 4 + oy + y, pl.ds(20 * block + 8 + oz, 24), :] for c in range(CHUNKS)]
            here, there = shift_lanes(window, ox), shift_lanes(window, ox + 1)
            for c in range(CHUNKS):
                at[block, c, y, 0:24, :] = here[c]
                by[block, c, y, 0:24, :] = there[c] - here[c]

    load_tables[1].wait()
    columns = [dot_full(lf[d], bt[0]) for d in range(3)]

    broadcast_wait(m_buf, bsem.at[2], bsem.at[3])
    pick_r = lax.broadcasted_iota(jnp.int32, (48, 512), 0)
    pick_c = lax.broadcasted_iota(jnp.int32, (48, 512), 1)
    sites = m_buf[...].reshape(512, 128)
    gradients = []
    for b in range(2):
        pick = (pick_r == pick_c // 16 + 1 + lax.rem(pick_c, 8)) & ((pick_c // 8) % 2 == b)
        pick = pick & (pick_r >= 2) & (pick_r < 35)
        gradients.append(dot_full(jnp.where(pick, 1.0, 0.0), sites))
    squares = jnp.sum(gradients[0] * gradients[0] + gradients[1] * gradients[1])
    inverse = lax.rsqrt(squares * (1.0 / 1782.0) + EPSILON)
    gradients = [gradient * inverse for gradient in gradients]
    for d in range(3):
        for b in range(2):
            own = gradients[b] if d == 0 else pltpu.roll(gradients[b], 128 - 16 * d, 1)
            own = jnp.where(lax.broadcasted_iota(jnp.int32, (48, 128), 1) < 9, own, 0.0)
            lm[d, b] = lm_own[d, b] - STEP_SIZE * own

    for d in range(3):
        column = jnp.concatenate(
            [
                columns[d],
                dot_full(lm[d, 0, pl.ds(k, 8), :], bt[1]),
                dot_full(lm[d, 1, pl.ds(k, 8), :], bt[1]),
                dot_full(lc[d, pl.ds(q, 8), :], bt[2]),
            ],
            axis=0,
        )
        upper, lower = parts(column)
        columns[d] = jnp.concatenate([upper, upper, lower, lower], axis=0)

    @pl.loop(0, 4)
    def _(block):
        whole = pl.ds(pl.multiple_of(480 * block, 480), 480)
        for d in range(3):
            field[d] = dot(spread[whole, :], columns[d])

        @pl.loop(0, NY // 2)
        def _(pair):
            for c in range(CHUNKS):
                lanes = slice(128 * c, 128 * c + 128)
                found = []
                for h in range(2):
                    y = 2 * pair + h
                    corner = [[at[block, c, y + e, z : z + 24, :] for e in (0, 1)] for z in (0, 1)]
                    step = [[by[block, c, y + e, z : z + 24, :] for e in (0, 1)] for z in (0, 1)]
                    rows = pl.ds(pl.multiple_of(24 * y, 8), 24)
                    exponents = [field[d, rows, lanes] for d in range(3)]
                    atlas = fx[c, y, pl.ds(20 * block, 24), :]
                    found.append(weights(atlas, corner, step, exponents))
                rows = pl.ds(pl.multiple_of(48 * pair, 48), 48)
                for d in range(3):
                    upper, lower = parts(jnp.concatenate([found[0][d], found[1][d]], axis=0))
                    high[d, rows, lanes] = upper
                    low[d, rows, lanes] = lower

        total = None
        for d in range(3):
            wide = dot(high[d], bx[d])
            term = (wide[:, 0:128] + wide[:, 128:256]) + dot(low[d], bx[d, :, 0:128])
            total = term if total is None else total + term
        mixed[1, whole, :] = total

    f_part[...] = dot_rows(mixed[0], mixed[1])[0:40]
    f_parts[1, s] = f_part[...]
    around(k, s, f_part, f_parts, fsend, frecv, "start")

    for b in range(2):
        turned = dot_rows(gradients[b], turn)
        for d in range(3):
            for a in range(9):
                mid_out[d, a, b : b + 1, :] = turned[16 * d + a : 16 * d + a + 1, 0:33]

    around(k, s, f_part, f_parts, fsend, frecv, "wait_recv")
    before, middle, after = ((f_parts[i, 0] + f_parts[i, 1]) + (f_parts[i, 2] + f_parts[i, 3]) for i in range(3))
    row = lax.rem(lax.broadcasted_iota(jnp.int32, (40, 128), 0), 8)
    middle = middle + jnp.where((row == 1) | (row == 2), pltpu.roll(before * has_prev, 36, 0), 0.0)
    middle = middle + jnp.where(row == 4, pltpu.roll(after * has_next, 4, 0), 0.0)
    middle = jnp.where((row >= 1) & (row <= 4), middle, 0.0)
    f_tile[...] = jnp.full((8, 128), jnp.sum(middle * middle))
    f_buf[k] = f_tile[...]
    broadcast_start(k, s, f_tile, f_buf, bsem.at[4], bsem.at[5])

    for copy in (lat_to_next, lat_to_prev, z_to_next, z_to_prev, *mid_same):
        copy.wait_send()

    @pl.when(up)
    def _():
        for copy in (to_bef, *corner_up, *mid_up):
            copy.wait_send()

    @pl.when(down)
    def _():
        for copy in (to_aft, *corner_down, *mid_down):
            copy.wait_send()

    around(k, s, piece, pieces, psend, precv, "wait_send")
    around(k, s, f_part, f_parts, fsend, frecv, "wait_send")
    part_copies("wait_send")
    middle = pltpu.roll(middle, 39, 0)
    thirds = [middle if d == 0 else pltpu.roll(middle, 128 - 40 * d, 1) for d in range(3)]

    broadcast_wait(f_buf, bsem.at[4], bsem.at[5])
    squares = jnp.sum(f_buf[...], axis=0)[0:1, :]
    inverse = lax.rsqrt(squares * (1.0 / 63360.0) + EPSILON)
    for d in range(3):
        scaled = thirds[d] * inverse
        for b in range(5):
            fine_out[d, b] = scaled[8 * b : 8 * b + 4, 0:33]


def body(
    fixed_image,
    moving_image,
    lattice_fine,
    lattice_mid,
    lattice_coarse,
    offset_fine,
    offset_mid,
    offset_coarse,
):
    t = tables()
    names = ("rz", "bt", "bx", "ry", "pz", "pcx", "pcz", "mrz", "mry", "mbt", "mbx", "crz", "cry", "cbt", "cbx")
    vmem, smem, hbm = (pl.BlockSpec(memory_space=m) for m in (pltpu.VMEM, pltpu.SMEM, pl.ANY))
    shape = lambda *dims: jax.ShapeDtypeStruct(dims, F32)
    buf = lambda *dims: pltpu.VMEM(dims, F32)
    half = lambda *dims: pltpu.VMEM(dims, BF16)
    dma = lambda *dims: pltpu.SemaphoreType.DMA(dims)
    fine, mid, coarse = pl.pallas_call(
        kernel,
        out_shape=[shape(3, 5, 4, 33), shape(3, 9, 2, 33), shape(3, 3, 1, 9)],
        in_specs=[hbm, hbm, vmem, vmem, vmem, smem, smem, smem, hbm, hbm, hbm] + [vmem] * (len(names) - 3),
        out_specs=[vmem] * 3,
        scratch_shapes=[
            buf(4, 4, 24, 256), buf(3, 128, NX), buf(NX, 128), half(3, NX, 256),
            buf(CHUNKS, 28, 96, 128), buf(CHUNKS, NY, 88, 128), buf(5, NZ, NX),
            *[buf(CHUNKS, 10, 8, 128)] * 4, buf(4, CHUNKS, 2, 8, 128),
            *[buf(3, 5, 8, 128)] * 3, buf(3, 40, 128), buf(3, 3, 16, 128),
            buf(3, 2, 48, 128), buf(3, 16, 128), buf(3, 2, 48, 128), buf(3, 16, 128),
            *[buf(5, 24, 256)] * 4, buf(2, 3, 5, 8, 256),
            buf(2, 8, 128), buf(3, SECS, 2, 8, 128), buf(14, 32, 128), buf(5, 8, 128), buf(2, 15, 40, 128), buf(120, 128),
            buf(8, 128), buf(SLABS, 8, 128), buf(16, 128), buf(SECS, 16, 128), buf(16, 128), buf(SLABS, 16, 128),
            *[buf(4, CHUNKS, 21, 32, 128)] * 2, half(1920, 256), buf(3, 480, NX),
            half(3, 480, NX), half(3, 480, NX), buf(2, 1920, 128),
            buf(40, 128), buf(3, SECS, 40, 128), buf(8, 128), buf(SLABS, 8, 128),
            dma(13), dma(18), dma(18), *[dma(3, SECS)] * 4, dma(SECS), dma(SECS), dma(6),
        ],
        compiler_params=pltpu.CompilerParams(
            collective_id=0, has_side_effects=True, vmem_limit_bytes=VMEM_LIMIT
        ),
        name="mega",
    )(
        jnp.transpose(moving_image, (1, 0, 2)),
        jnp.transpose(fixed_image, (1, 0, 2)),
        jnp.transpose(lattice_fine, (0, 2, 1, 3)),
        jnp.transpose(lattice_mid, (0, 3, 2, 1)),
        jnp.transpose(lattice_coarse, (0, 3, 2, 1)),
        offset_fine,
        jnp.transpose(offset_mid, (1, 2, 0)),
        jnp.transpose(offset_coarse, (0, 2, 1)),
        *(t[n] for n in names),
    )
    return (
        jnp.transpose(fine, (0, 2, 1, 3)),
        jnp.transpose(mid, (0, 3, 2, 1)),
        jnp.transpose(coarse, (0, 3, 2, 1)),
    )


def solution(mesh):
    placed = (
        P("slab", "sec", None),
        P("slab", "sec", None),
        P(None, "slab", None, None),
        P(),
        P(),
        P(None, "slab", None),
        P(None, "slab", None),
        P(),
    )
    return jax.shard_map(
        body,
        mesh=mesh,
        in_specs=placed,
        out_specs=(P(None, "slab", None, None), P(), P()),
        check_vma=False,
    )
```

```python
import functools

import jax
import jax.numpy as jnp
import ml_dtypes
import numpy as np
from jax import lax
from jax.experimental import pallas as pl
from jax.experimental.pallas import tpu as pltpu
from jax.sharding import PartitionSpec as P

SP = 20
EPSILON = 1e-06
STEP_SIZE = 0.5
HIGHEST = lax.Precision.HIGHEST
F32 = jnp.float32
BF16 = jnp.bfloat16
MESH = pl.DeviceIdType.MESH
SLABS = 32
SECS = 4
NZ, NY, NX = 80, 20, 640
CHUNKS = NX // 128
LOG2E = 1.4426950408889634
VMEM_LIMIT = 58 * 1024 * 1024


def basis(rows, knots, factor, coarse):
    rows, knots = np.asarray(rows, np.float64), np.asarray(knots, np.float64)
    position = factor * rows + 0.5 * (factor - 1)
    centre = SP * coarse * knots + 0.5 * (coarse - 1)
    distance = np.abs((position[:, None] - centre[None, :]) / (SP * coarse))
    near = 2.0 / 3.0 - distance**2 + 0.5 * distance**3
    far = np.maximum(2.0 - distance, 0.0) ** 3 / 6.0
    return np.where(distance < 1.0, near, far)


@functools.cache
def tables():
    t = {}
    rz, ry = np.zeros((4, 4, 24, 64)), np.zeros((4, 24, 64))
    z, y, x = np.arange(NZ), np.arange(NY), np.arange(NX)
    for r in range(4):
        for block in range(4):
            rows = z[20 * block : 20 * block + 20]
            for a in range(7):
                rz[r, block, :20, a:40:8] = basis(rows, [a - 1], 1, 1)
            for a in range(5):
                rz[r, block, :20, 40 + a : 56 : 8] = basis(rows, [a - 2], 1, 4)
                rz[r, block, :20, 56 + a : 57 + a] = basis(rows + 80 * r, [a - 2], 1, 16)
    for s in range(4):
        for a in range(7):
            ry[s, :NY, a:40:8] = basis(y + 20 * s, range(5), 1, 1)
        for a in range(5):
            ry[s, :NY, 40 + a : 56 : 8] = basis(y + 20 * s, range(2), 1, 4)
            ry[s, :NY, 56 + a : 57 + a] = basis(y + 20 * s, [0], 1, 16)
    t["rz"] = np.tile(rz, (1, 1, 1, 4)).astype(np.float32)
    t["ry"] = np.tile(ry, (1, 1, 4)).astype(np.float32)
    across = np.zeros((3, 128, NX))
    across[0, :33] = basis(x, range(33), 1, 1).T
    across[1, :9] = basis(x, range(9), 1, 4).T
    across[2, :3] = basis(x, range(3), 1, 16).T
    t["bt"] = (-LOG2E * across).astype(np.float32)
    along = np.zeros((NX, 128), np.float32)
    along[:, :33] = basis(x, range(33), 1, 1)
    t["bx"] = along
    rz, ry = np.zeros((4, 24, 128)), np.zeros((4, 8, 128))
    z, y, x = np.arange(20), np.arange(5), np.arange(160)
    for r in range(4):
        for a in range(4):
            rz[r, :20, a:16:8] = basis(z, [a - 1], 4, 4)
        for a in range(5):
            rz[r, :20, 16 + a : 17 + a] = basis(z + 20 * r, [a - 2], 4, 16)
    for s in range(4):
        for a in range(4):
            ry[s, :5, a:16:8] = basis(y + 5 * s, range(2), 4, 4)
        for a in range(5):
            ry[s, :5, 16 + a : 17 + a] = basis(y + 5 * s, [0], 4, 16)
    t["mrz"], t["mry"] = rz.astype(np.float32), ry.astype(np.float32)
    across = np.zeros((2, 128, 256))
    across[0, :9, :160] = basis(x, range(9), 4, 4).T
    across[1, :3, :160] = basis(x, range(3), 4, 16).T
    t["mbt"] = (-LOG2E * across).astype(np.float32)
    spread = np.zeros((3, 256, 128), np.float32)
    for d in range(3):
        spread[d, :160, 16 * d : 16 * d + 9] = basis(x, range(9), 4, 4)
    t["mbx"] = spread.reshape(768, 128)
    rz, ry = np.zeros((4, 8, 128)), np.zeros((8, 128))
    z, y, x = np.arange(5), np.arange(5), np.arange(40)
    for r in range(4):
        for a in range(4):
            rz[r, :5, a : a + 1] = basis(z + 5 * r, [a - 1], 16, 16)
    ry[:5, :4] = basis(y, [0], 16, 16)
    t["crz"], t["cry"] = rz.astype(np.float32), ry.astype(np.float32)
    across = np.zeros((128, 128))
    across[:3, :40] = basis(x, range(3), 16, 16).T
    t["cbt"] = (-LOG2E * across).astype(np.float32)
    spread = np.zeros((3, 128, 128), np.float32)
    for d in range(3):
        spread[d, :40, 16 * d : 16 * d + 3] = basis(x, range(3), 16, 16)
    t["cbx"] = spread.reshape(384, 128)
    pool = np.zeros((120, 400), ml_dtypes.bfloat16)
    for row in range(5):
        for plane in range(80):
            pool[24 * row + plane // 4, 80 * row + plane] = 1
    t["pz"] = pool
    pool = np.zeros((2, 256, 128), np.float32)
    pool[0, np.arange(160), np.arange(160) // 4] = 1
    pool[1, np.arange(160), 64 + np.arange(160) // 4] = 1
    t["pcx"] = pool
    pool = np.zeros((16, 48), np.float32)
    for part in range(2):
        for plane in range(20):
            pool[8 * part + plane // 4, 24 * part + plane] = 1
    t["pcz"] = pool
    return t


def dot(a, b):
    return jnp.dot(a, b, preferred_element_type=F32)


def dot_full(a, b):
    return jnp.dot(a, b, precision=HIGHEST, preferred_element_type=F32)


def dot_rows(a, b):
    return lax.dot_general(
        a, b, (((0,), (0,)), ((), ())), precision=HIGHEST, preferred_element_type=F32
    )


def parts(values):
    high = values.astype(BF16)
    return high, (values - high.astype(F32)).astype(BF16)


def shift_lanes(chunks, shift):
    amount = lax.rem(256 - shift, 128)
    rolled = [pltpu.roll(chunk, amount, 1) for chunk in chunks]
    lane = lax.broadcasted_iota(jnp.int32, chunks[0].shape, 1)
    first = lane < jnp.maximum(-shift, 0)
    last = lane >= 128 - jnp.maximum(shift, 0)
    zero = jnp.zeros_like(chunks[0])
    padded = [zero, *rolled, zero]
    return [
        jnp.where(first, padded[j], jnp.where(last, padded[j + 2], padded[j + 1]))
        for j in range(len(chunks))
    ]


def fraction(exponent):
    grown = jnp.exp2(exponent)
    frac = pl.reciprocal(1.0 + grown, approx=True)
    return frac, frac * (grown * frac)


def weights(fixed, corner, step, fractions):
    (fz, gz), (fy, gy), (fx, gx) = fractions
    line = [[corner[z][y] + fx * step[z][y] for y in (0, 1)] for z in (0, 1)]
    rise = [line[z][1] - line[z][0] for z in (0, 1)]
    plane = [line[z][0] + fy * rise[z] for z in (0, 1)]
    slope_z = plane[1] - plane[0]
    residual = (plane[0] + fz * slope_z) - fixed
    slope_y = rise[0] + fz * (rise[1] - rise[0])
    along = [step[z][0] + fy * (step[z][1] - step[z][0]) for z in (0, 1)]
    slope_x = along[0] + fz * (along[1] - along[0])
    return [
        (residual * slope_z) * gz,
        (residual * slope_y) * gy,
        (residual * slope_x) * gx,
    ]


def greet(k, s):
    barrier = pltpu.get_barrier_semaphore()

    def signal(slab, sec):
        pl.semaphore_signal(barrier, inc=1, device_id=(slab, sec), device_id_type=MESH)

    @pl.loop(1, SLABS)
    def _(i):
        signal(lax.rem(k + i, SLABS), s)

    for i in range(1, SECS):
        other = lax.rem(s + i, SECS)
        signal(k, other)
        signal(lax.rem(k + 1, SLABS), other)
        signal(lax.rem(k + SLABS - 1, SLABS), other)
    return lambda: pl.semaphore_wait(barrier, SLABS - 1 + 3 * (SECS - 1))


def broadcast_start(k, s, tile, buffer, send_sem, recv_sem):
    @pl.loop(0, SLABS - 1)
    def _(i):
        pltpu.make_async_remote_copy(
            src_ref=tile,
            dst_ref=buffer.at[k],
            send_sem=send_sem,
            recv_sem=recv_sem,
            device_id=(lax.rem(k + 1 + lax.rem(i + 15, SLABS - 1), SLABS), s),
            device_id_type=MESH,
        ).start()


def broadcast_wait(buffer, send_sem, recv_sem):
    part = buffer.at[pl.ds(0, SLABS - 1)]
    pltpu.make_async_copy(part, part, recv_sem).wait()
    pltpu.make_async_copy(part, part, send_sem).wait()


def remote(src, dst, send_sem, recv_sem, device):
    return pltpu.make_async_remote_copy(
        src_ref=src,
        dst_ref=dst,
        send_sem=send_sem,
        recv_sem=recv_sem,
        device_id=device,
        device_id_type=MESH,
    )


def around(k, s, source, buffer, send, recv, act):
    slabs = (lax.rem(k + SLABS - 1, SLABS), k, lax.rem(k + 1, SLABS))

    def one(dk, other):
        if act == "wait_recv":
            copy = remote(source, buffer.at[dk, other], send.at[dk, other], recv.at[dk, other], (k, other))
        else:
            copy = remote(
                source, buffer.at[2 - dk, s], send.at[dk, other], recv.at[2 - dk, s], (slabs[dk], other)
            )
        getattr(copy, act)()

    for dk in range(3):
        for other in range(SECS):
            if dk == 1:
                pl.when(s != other)(functools.partial(one, dk, other))
            else:
                one(dk, other)


NAMES = ("rz", "bt", "bx", "ry", "pz", "pcx", "pcz", "mrz", "mry", "mbt", "mbx", "crz", "cry", "cbt", "cbx")


def finish(*refs):
    copies = [pltpu.make_async_copy(refs[i], refs[i + 3], refs[6].at[i]) for i in range(3)]
    for copy in copies:
        copy.start()
    for copy in copies:
        copy.wait()


def kernel(
    moving, fixed, lat_fine, lat_mid, lat_coarse, off_fine, off_mid, off_coarse, *refs
):
    n = len(NAMES)
    stored, refs = refs[:n], refs[n:]
    fine_out, mid_out, coarse_out, *refs = refs
    rz, bt, bf, ry, pz, pcx, pcz, mrz, mry, mbt, mbx, crz, cry, cbt, cbx = refs[:n]
    (
        bx, pad, fx, sums, zlo, zhi, z_bef, z_aft, y_bef, y_aft, corners,
        lf_own, lf_prev, lf_next, lf, mt, lm_own, lc_own, lc,
        pooled_m, pooled_f, pm_bef, pm_aft, pm_halo,
        piece, pieces, cv, cf, mm, mr,
        c_tile, c_buf, m_part, m_parts, m_tile, m_buf,
        at, by, spread, columns, field_a, field_b, split_a, split_b, adjoint, mixed,
        f_part, f_parts, f_tile, f_buf,
        load_sem, table_sem, send, recv, psend, precv, fsend, frecv, tsend, trecv, bsem,
    ) = refs[n:]
    k, s = lax.axis_index("slab"), lax.axis_index("sec")
    nxt, prv = lax.rem(k + 1, SLABS), lax.rem(k + SLABS - 1, SLABS)
    q, r = k // 4, lax.rem(k, 4)
    has_prev, has_next = (k > 0).astype(F32), (k < SLABS - 1).astype(F32)
    up, down = s < SECS - 1, s > 0
    own_y, own_z = pl.ds(4, NY), pl.ds(8, NZ)

    load_moving = [
        pltpu.make_async_copy(
            moving.at[:, :, pl.ds(128 * c, 128)], pad.at[c, own_y, own_z], load_sem.at[c]
        )
        for c in range(CHUNKS)
    ]
    load_fixed = [
        pltpu.make_async_copy(
            fixed.at[:, :, pl.ds(128 * c, 128)], fx.at[c, :, pl.ds(0, NZ)], load_sem.at[CHUNKS + c]
        )
        for c in range(CHUNKS)
    ]
    load_tables = [
        pltpu.make_async_copy(src, dst, table_sem.at[i])
        for i, (src, dst) in enumerate(zip(stored, refs[:n]))
    ]
    for copy in (*load_moving, *load_fixed, *load_tables):
        copy.start()
    all_here = greet(k, s)

    for ref in (lf_own, mt, lm_own, lc_own, cv, mm):
        ref[...] = jnp.zeros_like(ref)
    eye = lax.broadcasted_iota(jnp.int32, (16, 128), 0) == lax.broadcasted_iota(jnp.int32, (16, 128), 1)
    eye = jnp.where(eye, 1.0, 0.0)
    for d in range(3):
        for b in range(5):
            lf_own[d, b, 0:4, 0:33] = lat_fine[d, b]
        for a in range(9):
            for b in range(2):
                mt[d, b, a : a + 1, 0:33] = lat_mid[d, a, b : b + 1]
        for a in range(3):
            mt[d, 2, a : a + 1, 0:9] = lat_coarse[d, a]
    for d in range(3):
        for b in range(2):
            lm_own[d, b, 2:42, :] = dot_rows(mt[d, b], eye)[0:40]
        lc_own[d, 2:16, :] = dot_rows(mt[d, 2], eye)[0:14]
    for copy in load_tables:
        copy.wait()
    cr = jnp.concatenate([crz[r] * cry[y : y + 1, :] for y in range(5)], axis=0)
    column = [dot_full(lc_own[d, pl.ds(q + 1, 8), :], cbt[...]) for d in range(3)]
    column = jnp.concatenate([jnp.concatenate(column, axis=1), jnp.zeros((120, 384), F32)], axis=0)
    exponent = dot_full(cr, column)
    fractions_c = [fraction(exponent[:, 128 * d : 128 * d + 128]) for d in range(3)]

    for c in range(CHUNKS):
        pad[c, :, 0:8, :] = jnp.zeros((28, 8, 128), F32)
        pad[c, :, 88:96, :] = jnp.zeros((28, 8, 128), F32)
        fx[c, :, 80:88, :] = jnp.zeros((NY, 8, 128), F32)

    @pl.when(s == 0)
    def _():
        y_bef[...] = jnp.zeros_like(y_bef)
        corners[0:2] = jnp.zeros((2, CHUNKS, 2, 8, 128), F32)
        pm_bef[...] = jnp.zeros_like(pm_bef)
        pm_halo[:, 0] = jnp.zeros((2, 5, 8, 256), F32)

    @pl.when(s == SECS - 1)
    def _():
        y_aft[...] = jnp.zeros_like(y_aft)
        corners[2:4] = jnp.zeros((2, CHUNKS, 2, 8, 128), F32)
        pm_aft[...] = jnp.zeros_like(pm_aft)
        pm_halo[:, 2] = jnp.zeros((2, 5, 8, 256), F32)

    four_x = lax.broadcasted_iota(jnp.int32, (NX, 256), 0) // 4
    four_x = jnp.where(four_x == lax.broadcasted_iota(jnp.int32, (NX, 256), 1), 1.0, 0.0).astype(BF16)

    def pooled():
        high, low = parts(sums[...].reshape(400, NX))
        table = four_x
        high, low = parts(dot(high, table) + dot(low, table))
        table = pz[...]
        return ((dot(table, high) + dot(table, low)) * (1.0 / 64.0)).reshape(5, 24, 256)

    for copy in load_moving:
        copy.wait()
    for c in range(CHUNKS):
        lanes = slice(128 * c, 128 * c + 128)

        @pl.loop(0, 5, unroll=5)
        def _(group):
            four = [pad[c, 4 * group + 4 + i, 8:88, :] for i in range(4)]
            sums[group, :, lanes] = (four[0] + four[1]) + (four[2] + four[3])

        @pl.loop(0, NY // 2, unroll=5)
        def _(pair):
            for half in range(2):
                rows = slice(4 * half, 4 * half + 4)
                zlo[c, pair, rows, :] = pad[c, 2 * pair + half + 4, 8:12, :]
                zhi[c, pair, rows, :] = pad[c, 2 * pair + half + 4, 84:88, :]

    pooled_m[...] = pooled()
    all_here()

    lat_to_next = remote(lf_own, lf_prev, send.at[0], recv.at[0], (nxt, s))
    lat_to_prev = remote(lf_own, lf_next, send.at[1], recv.at[1], (prv, s))
    z_to_next = remote(zhi, z_bef, send.at[2], recv.at[2], (nxt, s))
    z_to_prev = remote(zlo, z_aft, send.at[3], recv.at[3], (prv, s))
    to_bef = remote(pad.at[:, pl.ds(20, 4), own_z], y_bef, send.at[4], recv.at[4], (k, s + 1))
    to_aft = remote(pad.at[:, pl.ds(4, 4), own_z], y_aft, send.at[5], recv.at[5], (k, s - 1))
    first, last = pl.ds(0, 2), pl.ds(8, 2)
    corner_up = [
        remote(zhi.at[:, last], corners.at[0], send.at[6], recv.at[6], (nxt, s + 1)),
        remote(zlo.at[:, last], corners.at[1], send.at[7], recv.at[7], (prv, s + 1)),
    ]
    corner_down = [
        remote(zhi.at[:, first], corners.at[2], send.at[8], recv.at[8], (nxt, s - 1)),
        remote(zlo.at[:, first], corners.at[3], send.at[9], recv.at[9], (prv, s - 1)),
    ]
    head, tail = pl.ds(0, 8), pl.ds(16, 8)
    mid_same = [
        remote(pooled_m.at[:, tail], pm_halo.at[0, 1], send.at[10], recv.at[10], (nxt, s)),
        remote(pooled_m.at[:, head], pm_halo.at[1, 1], send.at[11], recv.at[11], (prv, s)),
    ]
    mid_up = [
        remote(pooled_m, pm_bef, send.at[12], recv.at[12], (k, s + 1)),
        remote(pooled_m.at[:, tail], pm_halo.at[0, 0], send.at[13], recv.at[13], (nxt, s + 1)),
        remote(pooled_m.at[:, head], pm_halo.at[1, 0], send.at[14], recv.at[14], (prv, s + 1)),
    ]
    mid_down = [
        remote(pooled_m, pm_aft, send.at[15], recv.at[15], (k, s - 1)),
        remote(pooled_m.at[:, tail], pm_halo.at[0, 2], send.at[16], recv.at[16], (nxt, s - 1)),
        remote(pooled_m.at[:, head], pm_halo.at[1, 2], send.at[17], recv.at[17], (prv, s - 1)),
    ]
    for copy in mid_same:
        copy.start()

    @pl.when(up)
    def _():
        for copy in mid_up:
            copy.start()

    @pl.when(down)
    def _():
        for copy in mid_down:
            copy.start()

    for copy in load_fixed:
        copy.wait()

    @pl.loop(0, 5, unroll=5)
    def _(group):
        for c in range(CHUNKS):
            lanes = slice(128 * c, 128 * c + 128)
            four = [fx[c, 4 * group + i, 0:80, :] for i in range(4)]
            sums[group, :, lanes] = (four[0] + four[1]) + (four[2] + four[3])

    pooled_f[...] = pooled()

    both = None
    for n, ref in enumerate((pooled_m, pooled_f)):
        upper, lower = jnp.zeros((24, 256), F32), jnp.zeros((24, 256), F32)
        for i in range(5):
            keep = (i + s < 4).astype(F32)
            upper = upper + ref[i] * keep
            lower = lower + ref[i] * (1.0 - keep)
        term = dot_full(jnp.concatenate([upper, lower], axis=0), pcx[n])
        both = term if both is None else both + term
    piece[...] = (dot_full(pcz[...], both) * (1.0 / 64.0)).reshape(2, 8, 128)
    pieces[1, s] = piece[...]
    around(k, s, piece, pieces, psend, precv, "start")

    for copy in (lat_to_next, lat_to_prev):
        copy.start()

    @pl.when(up)
    def _():
        to_bef.start()

    @pl.when(down)
    def _():
        to_aft.start()

    for copy in (z_to_next, z_to_prev):
        copy.start()

    @pl.when(up)
    def _():
        for copy in corner_up:
            copy.start()

    @pl.when(down)
    def _():
        for copy in corner_down:
            copy.start()

    low_lane = (lax.broadcasted_iota(jnp.int32, (48, 256), 1) // 64) % 2 == 1

    @pl.loop(0, 4)
    def _(block):
        @pl.loop(0, NY // 2, unroll=5)
        def _(pair):
            two = [rz[r, block] * ry[s, pl.ds(2 * pair + h, 1), :] for h in range(2)]
            two = jnp.concatenate(two, axis=0)
            upper, lower = parts(two)
            rows = pl.ds(pl.multiple_of(480 * block + 48 * pair, 48), 48)
            spread[rows, :] = jnp.where(low_lane, lower.astype(F32), upper.astype(F32)).astype(BF16)
            mixed[0, rows, :] = two[:, 0:128]

    for y in range(5):
        mr[24 * y : 24 * y + 24, :] = mrz[r] * mry[s, y : y + 1, :]
    for d in range(3):
        upper, lower = parts(bf[...] if d == 0 else pltpu.roll(bf[...], 40 * d, 1))
        row = 2 * NX * d
        bx[row : row + NX, 0:128] = upper
        bx[row : row + NX, 128:256] = lower
        bx[row + NX : row + 2 * NX, 0:128] = upper
        bx[row + NX : row + 2 * NX, 128:256] = jnp.zeros((NX, 128), BF16)
    column = []
    for d in range(3):
        three = [dot_full(lm_own[d, b, pl.ds(k + 1, 8), :], mbt[0]) for b in range(2)]
        three.append(dot_full(lc_own[d, pl.ds(q, 8), :], mbt[1]))
        column.append(jnp.concatenate(three, axis=0))
    column = jnp.concatenate([jnp.concatenate(column, axis=1), jnp.zeros((104, 768), F32)], axis=0)
    base_m = dot_full(mr[...], column)
    around(k, s, piece, pieces, psend, precv, "wait_recv")

    lane = lax.broadcasted_iota(jnp.int32, (5, 128), 1)
    for dk in range(3):
        scale = (has_prev, jnp.float32(1.0), has_next)[dk]
        rows = (slice(3, 8), slice(8, 13), slice(13, 18))[dk]
        for c in range(5):
            value = jnp.zeros((8, 128), F32)
            if c < 4:
                value = value + pieces[dk, c, 0]
            if c > 0:
                value = value + pieces[dk, c - 1, 1]
            cv[4 + c, rows, :] = jnp.where(lane < 40, value[0:5], 0.0) * scale
            if dk == 1:
                cf[c] = value
    fixed_c = pltpu.roll(cf[...].reshape(40, 128), 64, 1)

    oz, oy, ox = off_coarse[0, 0, q], off_coarse[1, 0, q], off_coarse[2, 0, q]
    a_z, b_z = [], []
    for e in (0, 1):
        window = cv[pl.ds(4 + oy, 6), pl.ds(8 + oz + e, 8), :].reshape(48, 128)
        here, there = shift_lanes([window], ox)[0], shift_lanes([window], ox + 1)[0]
        a_z.append(here)
        b_z.append(there - here)
    corner = [[a_z[z][8 * y : 8 * y + 40] for y in (0, 1)] for z in (0, 1)]
    step = [[b_z[z][8 * y : 8 * y + 40] for y in (0, 1)] for z in (0, 1)]
    total = dot_full(jnp.concatenate(weights(fixed_c, corner, step, fractions_c), axis=1), cbx[...])
    c_tile[...] = dot_rows(cr, total)[0:8]
    c_buf[k] = c_tile[...]
    broadcast_start(k, s, c_tile, c_buf, bsem.at[0], bsem.at[1])

    for copy in mid_same:
        copy.wait_recv()

    @pl.when(s > 0)
    def _():
        for copy in mid_up:
            copy.wait_recv()

    @pl.when(s < SECS - 1)
    def _():
        for copy in mid_down:
            copy.wait_recv()

    for c in range(2):
        lanes = slice(128 * c, 128 * c + 128)
        for e, whole in enumerate((pm_bef, pooled_m, pm_aft)):
            for y in range(5):
                mm[c, 5 * e + y, 4:8, :] = pm_halo[0, e, y, 0:4, lanes] * has_prev
                mm[c, 5 * e + y, 8:28, :] = whole[y, 0:20, lanes]
                mm[c, 5 * e + y, 28:32, :] = pm_halo[1, e, y, 0:4, lanes] * has_next

    oz, oy, ox = off_mid[0, 0, 0], off_mid[0, 0, 1], off_mid[0, 0, 2]
    a_z, b_z = [], []
    for e in (0, 1):
        window = [mm[c, pl.ds(5 + oy, 6), pl.ds(8 + oz + e, 24), :].reshape(144, 128) for c in range(2)]
        here, there = shift_lanes(window, ox), shift_lanes(window, ox + 1)
        a_z.append(here)
        b_z.append([there[c] - here[c] for c in range(2)])

    def make_window(block, oz, oy, ox, y):
        window = [pad[c, 4 + oy + y, pl.ds(20 * block + 8 + oz, 24), :] for c in range(CHUNKS)]
        here, there = shift_lanes(window, ox), shift_lanes(window, ox + 1)
        for c in range(CHUNKS):
            at[block, c, y, 0:24, :] = here[c]
            by[block, c, y, 0:24, :] = there[c] - here[c]

    def make_windows(blocks, ranges):
        @pl.loop(*blocks)
        def _(block):
            offsets = [off_fine[d, block, s] for d in range(3)]
            for first_y, last_y, unroll in ranges:
                pl.loop(first_y, last_y, unroll=unroll)(functools.partial(make_window, block, *offsets))

    make_windows((1, 3), ((4, 16, 3),))

    broadcast_wait(c_buf, bsem.at[0], bsem.at[1])
    pick_r = lax.broadcasted_iota(jnp.int32, (24, 256), 0)
    pick_r = jnp.where(pick_r < 16, pick_r, pick_r - 16 + q)
    pick_c = lax.broadcasted_iota(jnp.int32, (24, 256), 1)
    low_bits = lax.rem(pick_c, 8)
    pick = (pick_r == pick_c // 32 + 1 + low_bits) & (low_bits < 4) & (pick_r >= 2) & (pick_r < 11)
    gradient = dot_full(jnp.where(pick, 1.0, 0.0), c_buf[...].reshape(256, 128))
    near = gradient[16:24]
    gradient = gradient[0:16]
    inverse = lax.rsqrt(jnp.sum(gradient * gradient) * (1.0 / 81.0) + EPSILON)

    near = jnp.concatenate([near, pltpu.roll(near, 112, 1), pltpu.roll(near, 96, 1)], axis=0)
    near = dot_full(near, mbt[1])
    near = jnp.concatenate([near[8 * d : 8 * d + 8] for d in range(3)], axis=1)
    blank = jnp.zeros((16, 768), F32)
    near = dot_full(mr[...], jnp.concatenate([blank, near, jnp.zeros((104, 768), F32)], axis=0))
    exponent = base_m - (STEP_SIZE * inverse) * near
    fixed_m = pooled_f[...].reshape(120, 256)
    found = []
    for c in range(2):
        lanes = slice(128 * c, 128 * c + 128)
        corner = [[a_z[z][c][24 * y : 24 * y + 120] for y in (0, 1)] for z in (0, 1)]
        step = [[b_z[z][c][24 * y : 24 * y + 120] for y in (0, 1)] for z in (0, 1)]
        fractions = [fraction(exponent[:, 256 * d + 128 * c : 256 * d + 128 * c + 128]) for d in range(3)]
        found.append(weights(fixed_m[:, lanes], corner, step, fractions))
    total = jnp.concatenate([found[c][d] for d in range(3) for c in range(2)], axis=1)
    total = dot_full(total, mbx[...])
    m_part[...] = dot_rows(mr[...], total)[0:16]
    m_parts[s] = m_part[...]

    def part_copies(act):
        for other in range(SECS):

            @pl.when(s != other)
            def _():
                slot = other if act == "wait_recv" else s
                getattr(remote(m_part, m_parts.at[slot], tsend.at[other], trecv.at[slot], (k, other)), act)()

    part_copies("start")
    part_copies("wait_recv")
    m_tile[...] = (m_parts[0] + m_parts[1]) + (m_parts[2] + m_parts[3])
    m_buf[k] = m_tile[...]
    broadcast_start(k, s, m_tile, m_buf, bsem.at[2], bsem.at[3])

    gradient = gradient * inverse
    for d in range(3):
        own = gradient if d == 0 else pltpu.roll(gradient, 128 - 16 * d, 1)
        own = jnp.where(lax.broadcasted_iota(jnp.int32, (16, 128), 1) < 3, own, 0.0)
        lc[d] = lc_own[d] - STEP_SIZE * own
    turn_r = lax.broadcasted_iota(jnp.int32, (48, 128), 0)
    turn = jnp.where(turn_r == lax.broadcasted_iota(jnp.int32, (48, 128), 1) + 2, 1.0, 0.0)
    turned = dot_rows(gradient, turn[0:16])
    for d in range(3):
        for a in range(3):
            coarse_out[d, a] = turned[16 * d + a : 16 * d + a + 1, 0:9]

    for copy in (lat_to_next, lat_to_prev, z_to_next, z_to_prev):
        copy.wait_recv()

    @pl.when(s > 0)
    def _():
        for copy in (to_bef, *corner_up):
            copy.wait_recv()

    @pl.when(s < SECS - 1)
    def _():
        for copy in (to_aft, *corner_down):
            copy.wait_recv()

    for d in range(3):
        for b in range(5):
            lf[d, 8 * b : 8 * b + 1, :] = lf_prev[d, b, 3:4, :] * has_prev
            lf[d, 8 * b + 1 : 8 * b + 5, :] = lf_own[d, b, 0:4, :]
            lf[d, 8 * b + 5 : 8 * b + 7, :] = lf_next[d, b, 0:2, :] * has_next
            lf[d, 8 * b + 7 : 8 * b + 8, :] = jnp.zeros((1, 128), F32)

    pad[:, 0:4, 8:88, :] = y_bef[...]
    pad[:, 24:28, 8:88, :] = y_aft[...]

    @pl.loop(0, NY // 2, unroll=2)
    def _(pair):
        for half in range(2):
            rows = slice(4 * half, 4 * half + 4)
            for c in range(CHUNKS):
                pad[c, 2 * pair + half + 4, 4:8, :] = z_bef[c, pair, rows, :] * has_prev
                pad[c, 2 * pair + half + 4, 88:92, :] = z_aft[c, pair, rows, :] * has_next

    for y in range(4):
        rows = slice(4 * (y % 2), 4 * (y % 2) + 4)
        for c in range(CHUNKS):
            for n in range(2):
                where = slice(4, 8) if n == 0 else slice(88, 92)
                keep = has_prev if n == 0 else has_next
                pad[c, y, where, :] = corners[n, c, y // 2, rows, :] * keep
                pad[c, 24 + y, where, :] = corners[2 + n, c, y // 2, rows, :] * keep

    for c in range(CHUNKS):
        for block in range(4):
            at[block, c, :, 24:32, :] = jnp.zeros((21, 8, 128), F32)
            by[block, c, :, 24:32, :] = jnp.zeros((21, 8, 128), F32)

    make_windows((1, 3), ((0, 4, 2), (16, 21, 5)))
    make_windows((0, 1), ((0, 21, 3),))
    make_windows((3, 4), ((0, 21, 3),))

    base_f = []
    for d in range(3):
        four = [dot_full(lf[d], bt[0])]
        four += [dot_full(lm_own[d, b, pl.ds(k, 8), :], bt[1]) for b in range(2)]
        four.append(dot_full(lc[d, pl.ds(q, 8), :], bt[2]))
        base_f.append(jnp.concatenate(four, axis=0))
    base_f = jnp.concatenate(base_f, axis=1)

    broadcast_wait(m_buf, bsem.at[2], bsem.at[3])
    pick_r = lax.broadcasted_iota(jnp.int32, (112, 512), 0)
    pick_c = lax.broadcasted_iota(jnp.int32, (112, 512), 1)
    pick_b = jnp.where(pick_r < 96, pick_r // 48, (pick_r - 96) // 8)
    pick_r = jnp.where(pick_r < 96, lax.rem(pick_r, 48), lax.rem(pick_r, 8) + k)
    pick = (pick_r == pick_c // 16 + 1 + lax.rem(pick_c, 8)) & (lax.rem(pick_c // 8, 2) == pick_b)
    pick = pick & (pick_r >= 2) & (pick_r < 35)
    gradient = dot_full(jnp.where(pick, 1.0, 0.0), m_buf[...].reshape(512, 128))
    near = gradient[96:112]
    gradient = gradient[0:96]
    inverse = lax.rsqrt(jnp.sum(gradient * gradient) * (1.0 / 1782.0) + EPSILON)

    near = jnp.concatenate([near, pltpu.roll(near, 112, 1), pltpu.roll(near, 96, 1)], axis=0)
    near = dot_full(near, bt[1])
    near = jnp.concatenate([near[16 * d : 16 * d + 16] for d in range(3)], axis=1)
    near = jnp.concatenate([jnp.zeros((40, 3 * NX), F32), near, jnp.zeros((8, 3 * NX), F32)], axis=0)
    upper, lower = parts(base_f - (STEP_SIZE * inverse) * near)
    columns[0:64, :] = upper
    columns[64:128, :] = upper
    columns[128:192, :] = lower
    columns[192:256, :] = lower
    field_a[...] = dot(spread[0:480, :], columns[...])

    def fine_block(block, split, split_before, field, field_after):
        adjoint[...] = jnp.zeros_like(adjoint)
        after = pl.ds(pl.multiple_of(480 * jnp.minimum(block + 1, 3), 480), 480)

        @pl.loop(0, 5)
        def _(i):
            lanes = pl.ds(pl.multiple_of(384 * i, 384), 384)
            field_after[:, lanes] = dot(spread[after, :], columns[:, lanes])
            lanes = pl.ds(pl.multiple_of(768 * i, 768), 768)
            adjoint[...] += dot(split_before[:, lanes], bx[lanes, :])
            for pair in range(2):
                for c in range(CHUNKS):
                    found = []
                    for h in range(2):
                        y = 4 * i + 2 * pair + h
                        corner = [[at[block, c, y + e, z : z + 24, :] for e in (0, 1)] for z in (0, 1)]
                        step = [[by[block, c, y + e, z : z + 24, :] for e in (0, 1)] for z in (0, 1)]
                        rows = pl.ds(pl.multiple_of(24 * y, 8), 24)
                        fractions = [
                            fraction(field[rows, NX * d + 128 * c : NX * d + 128 * c + 128]) for d in range(3)
                        ]
                        atlas = fx[c, y, pl.ds(20 * block, 24), :]
                        found.append(weights(atlas, corner, step, fractions))
                    rows = pl.ds(pl.multiple_of(96 * i + 48 * pair, 48), 48)
                    for d in range(3):
                        upper, lower = parts(jnp.concatenate([found[0][d], found[1][d]], axis=0))
                        lane = 2 * NX * d + 128 * c
                        split[rows, lane : lane + 128] = upper
                        split[rows, lane + NX : lane + NX + 128] = lower

        before = pl.ds(pl.multiple_of(480 * jnp.maximum(block - 1, 0), 480), 480)
        mixed[1, before, :] = adjoint[:, 0:128] + adjoint[:, 128:256]

    @pl.loop(0, 2)
    def _(two):
        fine_block(2 * two, split_a, split_b, field_a, field_b)
        fine_block(2 * two + 1, split_b, split_a, field_b, field_a)

    wide = dot(split_b[...], bx[...])
    mixed[1, 1440:1920, :] = wide[:, 0:128] + wide[:, 128:256]
    f_part[...] = dot_rows(mixed[0], mixed[1])[0:40]
    f_parts[1, s] = f_part[...]
    around(k, s, f_part, f_parts, fsend, frecv, "start")

    for b in range(2):
        turned = dot_rows(gradient[48 * b : 48 * b + 48] * inverse, turn)
        for d in range(3):
            for a in range(9):
                mid_out[d, a, b : b + 1, :] = turned[16 * d + a : 16 * d + a + 1, 0:33]

    around(k, s, f_part, f_parts, fsend, frecv, "wait_recv")
    before, middle, after = ((f_parts[i, 0] + f_parts[i, 1]) + (f_parts[i, 2] + f_parts[i, 3]) for i in range(3))
    row = lax.rem(lax.broadcasted_iota(jnp.int32, (40, 128), 0), 8)
    middle = middle + jnp.where((row == 1) | (row == 2), pltpu.roll(before * has_prev, 36, 0), 0.0)
    middle = middle + jnp.where(row == 4, pltpu.roll(after * has_next, 4, 0), 0.0)
    middle = jnp.where((row >= 1) & (row <= 4), middle, 0.0)
    f_tile[...] = jnp.full((8, 128), jnp.sum(middle * middle))
    f_buf[k] = f_tile[...]
    broadcast_start(k, s, f_tile, f_buf, bsem.at[4], bsem.at[5])

    for copy in (lat_to_next, lat_to_prev, z_to_next, z_to_prev, *mid_same):
        copy.wait_send()

    @pl.when(up)
    def _():
        for copy in (to_bef, *corner_up, *mid_up):
            copy.wait_send()

    @pl.when(down)
    def _():
        for copy in (to_aft, *corner_down, *mid_down):
            copy.wait_send()

    around(k, s, piece, pieces, psend, precv, "wait_send")
    around(k, s, f_part, f_parts, fsend, frecv, "wait_send")
    part_copies("wait_send")
    middle = pltpu.roll(middle, 39, 0)
    thirds = [middle if d == 0 else pltpu.roll(middle, 128 - 40 * d, 1) for d in range(3)]

    broadcast_wait(f_buf, bsem.at[4], bsem.at[5])
    squares = jnp.sum(f_buf[...], axis=0)[0:1, :]
    inverse = lax.rsqrt(squares * (1.0 / 63360.0) + EPSILON)
    for d in range(3):
        scaled = thirds[d] * inverse
        for b in range(5):
            fine_out[d, b] = scaled[8 * b : 8 * b + 4, 0:33]


def body(
    fixed_image,
    moving_image,
    lattice_fine,
    lattice_mid,
    lattice_coarse,
    offset_fine,
    offset_mid,
    offset_coarse,
):
    t = tables()
    vmem, smem, hbm = (pl.BlockSpec(memory_space=m) for m in (pltpu.VMEM, pltpu.SMEM, pl.ANY))
    shape = lambda *dims: jax.ShapeDtypeStruct(dims, F32)
    buf = lambda *dims: pltpu.VMEM(dims, F32)
    half = lambda *dims: pltpu.VMEM(dims, BF16)
    dma = lambda *dims: pltpu.SemaphoreType.DMA(dims)
    fine, mid, coarse = pl.pallas_call(
        kernel,
        out_shape=[shape(3, 5, 4, 33), shape(3, 9, 2, 33), shape(3, 3, 1, 9)],
        in_specs=[hbm, hbm, vmem, vmem, vmem, smem, smem, smem] + [hbm] * len(NAMES),
        out_specs=[vmem] * 3,
        scratch_shapes=[
            *[pltpu.VMEM(t[n].shape, t[n].dtype) for n in NAMES],
            half(6 * NX, 256), buf(CHUNKS, 28, 96, 128), buf(CHUNKS, NY, 88, 128), buf(5, NZ, NX),
            *[buf(CHUNKS, 10, 8, 128)] * 4, *[buf(CHUNKS, 4, NZ, 128)] * 2, buf(4, CHUNKS, 2, 8, 128),
            *[buf(3, 5, 8, 128)] * 3, buf(3, 40, 128), buf(3, 3, 16, 128),
            buf(3, 2, 48, 128), buf(3, 16, 128), buf(3, 16, 128),
            *[buf(5, 24, 256)] * 4, buf(2, 3, 5, 8, 256),
            buf(2, 8, 128), buf(3, SECS, 2, 8, 128), buf(14, 32, 128), buf(5, 8, 128), buf(2, 15, 40, 128), buf(120, 128),
            buf(8, 128), buf(SLABS, 8, 128), buf(16, 128), buf(SECS, 16, 128), buf(16, 128), buf(SLABS, 16, 128),
            *[buf(4, CHUNKS, 21, 32, 128)] * 2, half(1920, 256), half(256, 3 * NX),
            *[buf(480, 3 * NX)] * 2, *[half(480, 6 * NX)] * 2, buf(480, 256), buf(2, 1920, 128),
            buf(40, 128), buf(3, SECS, 40, 128), buf(8, 128), buf(SLABS, 8, 128),
            dma(10), dma(len(NAMES)), dma(18), dma(18), *[dma(3, SECS)] * 4, dma(SECS), dma(SECS), dma(6),
        ],
        compiler_params=pltpu.CompilerParams(
            collective_id=0, has_side_effects=True, vmem_limit_bytes=VMEM_LIMIT
        ),
        name="mega",
    )(
        jnp.transpose(moving_image, (1, 0, 2)),
        jnp.transpose(fixed_image, (1, 0, 2)),
        jnp.transpose(lattice_fine, (0, 2, 1, 3)),
        jnp.transpose(lattice_mid, (0, 3, 2, 1)),
        jnp.transpose(lattice_coarse, (0, 3, 2, 1)),
        offset_fine,
        jnp.transpose(offset_mid, (1, 2, 0)),
        jnp.transpose(offset_coarse, (0, 2, 1)),
        *(t[n] for n in NAMES),
    )
    results = (fine, mid, coarse)
    fine, mid, coarse = pl.pallas_call(
        finish,
        out_shape=[jax.ShapeDtypeStruct(a.shape, F32) for a in results],
        in_specs=[hbm] * 3,
        out_specs=[hbm] * 3,
        scratch_shapes=[dma(3)],
        name="finish",
    )(*results)
    return (
        jnp.transpose(fine, (0, 2, 1, 3)),
        jnp.transpose(mid, (0, 3, 2, 1)),
        jnp.transpose(coarse, (0, 3, 2, 1)),
    )


def solution(mesh):
    placed = (
        P("slab", "sec", None),
        P("slab", "sec", None),
        P(None, "slab", None, None),
        P(),
        P(),
        P(None, "slab", None),
        P(None, "slab", None),
        P(),
    )
    return jax.shard_map(
        body,
        mesh=mesh,
        in_specs=placed,
        out_specs=(P(None, "slab", None, None), P(), P()),
        check_vma=False,
    )
```

```python
import functools

import jax
import jax.numpy as jnp
import ml_dtypes
import numpy as np
from jax import lax
from jax.experimental import pallas as pl
from jax.experimental.pallas import tpu as pltpu
from jax.sharding import PartitionSpec as P

SP = 20
EPSILON = 1e-06
STEP_SIZE = 0.5
HIGHEST = lax.Precision.HIGHEST
F32 = jnp.float32
BF16 = jnp.bfloat16
MESH = pl.DeviceIdType.MESH
SLABS = 32
SECS = 4
NZ, NY, NX = 80, 20, 640
CHUNKS = NX // 128
LOG2E = 1.4426950408889634
VMEM_LIMIT = 58 * 1024 * 1024


def basis(rows, knots, factor, coarse):
    rows, knots = np.asarray(rows, np.float64), np.asarray(knots, np.float64)
    position = factor * rows + 0.5 * (factor - 1)
    centre = SP * coarse * knots + 0.5 * (coarse - 1)
    distance = np.abs((position[:, None] - centre[None, :]) / (SP * coarse))
    near = 2.0 / 3.0 - distance**2 + 0.5 * distance**3
    far = np.maximum(2.0 - distance, 0.0) ** 3 / 6.0
    return np.where(distance < 1.0, near, far)


def two_parts(values):
    high = values.astype(ml_dtypes.bfloat16)
    low = (values - high.astype(np.float64)).astype(ml_dtypes.bfloat16)
    return high, low


def right_parts(values):
    high, low = two_parts(values)
    return np.concatenate([high, low, high], axis=-2)


def wide_parts(values):
    high, low = two_parts(values)
    zero = np.zeros_like(high)
    return np.concatenate([np.concatenate([high, low], 1), np.concatenate([high, zero], 1)], 0)


def one_hot(condition):
    return condition.astype(ml_dtypes.bfloat16)


@functools.cache
def tables():
    t = {}
    rz, ry = np.zeros((4, 4, 24, 64)), np.zeros((4, NY, 64))
    z, y, x = np.arange(NZ), np.arange(NY), np.arange(NX)
    for r in range(4):
        for block in range(4):
            rows = z[20 * block : 20 * block + 20]
            for a in range(7):
                rz[r, block, :20, a:40:8] = basis(rows, [a - 1], 1, 1)
            for a in range(5):
                rz[r, block, :20, 40 + a : 56 : 8] = basis(rows, [a - 2], 1, 4)
                rz[r, block, :20, 56 + a : 57 + a] = basis(rows + 80 * r, [a - 2], 1, 16)
    for s in range(4):
        for a in range(7):
            ry[s, :, a:40:8] = basis(y + 20 * s, range(5), 1, 1)
        for a in range(5):
            ry[s, :, 40 + a : 56 : 8] = basis(y + 20 * s, range(2), 1, 4)
            ry[s, :, 56 + a : 57 + a] = basis(y + 20 * s, [0], 1, 16)
    whole = rz[:, None, :, None] * ry[None, :, None, :, None, :]
    high, low = two_parts(whole.reshape(16, 1920, 64))
    t["spread"] = np.concatenate([high, low, high, low], axis=2)
    t["gather"] = np.concatenate([high[:4, :, :40], low[:4, :, :40]], axis=2).transpose(0, 2, 1)
    across = np.zeros((3, 128, NX))
    across[0, :33] = basis(x, range(33), 1, 1).T
    across[1, :9] = basis(x, range(9), 1, 4).T
    across[2, :3] = basis(x, range(3), 1, 16).T
    t["bt"] = right_parts(-LOG2E * across)
    along = np.zeros((3, NX, 128))
    for d in range(3):
        along[d, :, 40 * d : 40 * d + 33] = basis(x, range(33), 1, 1)
    t["bx"] = np.concatenate([wide_parts(along[d]) for d in range(3)], axis=0)
    rz, ry = np.zeros((4, 24, 32)), np.zeros((4, 5, 32))
    z, y, x = np.arange(20), np.arange(5), np.arange(160)
    for r in range(4):
        for a in range(4):
            rz[r, :20, a:16:8] = basis(z, [a - 1], 4, 4)
        for a in range(5):
            rz[r, :20, 16 + a : 17 + a] = basis(z + 20 * r, [a - 2], 4, 16)
    for s in range(4):
        for a in range(4):
            ry[s, :, a:16:8] = basis(y + 5 * s, range(2), 4, 4)
        for a in range(5):
            ry[s, :, 16 + a : 17 + a] = basis(y + 5 * s, [0], 4, 16)
    whole = np.zeros((16, 128, 32))
    whole[:, :120] = (rz[:, None, None] * ry[None, :, :, None]).reshape(16, 120, 32)
    high, low = two_parts(whole)
    t["mspread"] = np.concatenate([high, high, low, np.zeros_like(low)], axis=2)
    t["mgather"] = np.concatenate([high[:, :, :16], low[:, :, :16]], axis=2).transpose(0, 2, 1)
    across = np.zeros((2, 128, 256))
    across[0, :9, :160] = basis(x, range(9), 4, 4).T
    across[1, :3, :160] = basis(x, range(3), 4, 16).T
    t["mbt"] = right_parts(-LOG2E * across)
    along = np.zeros((3, 256, 128))
    for d in range(3):
        along[d, :160, 16 * d : 16 * d + 9] = basis(x, range(9), 4, 4)
    t["mbx"] = wide_parts(along.reshape(768, 128))
    rz = np.zeros((4, 8, 32))
    z, y, x = np.arange(5), np.arange(5), np.arange(40)
    for r in range(4):
        for a in range(4):
            rz[r, :5, a : a + 1] = basis(z + 5 * r, [a - 1], 16, 16)
    whole = np.zeros((4, 128, 32))
    whole[:, :40] = (rz[:, None] * basis(y, [0], 16, 16)[None, :, None]).reshape(4, 40, 32)
    high, low = two_parts(whole)
    t["cspread"] = np.concatenate([high, high, low, np.zeros_like(low)], axis=2)
    t["cgather"] = np.concatenate([high[:, :, :16], low[:, :, :16]], axis=2).transpose(0, 2, 1)
    across = np.zeros((128, 128))
    across[:3, :40] = basis(x, range(3), 16, 16).T
    t["cbt"] = right_parts(-LOG2E * across)
    along = np.zeros((3, 128, 128))
    for d in range(3):
        along[d, :40, 16 * d : 16 * d + 3] = basis(x, range(3), 16, 16)
    t["cbx"] = wide_parts(along.reshape(384, 128))
    row, column = np.arange(NX)[:, None], np.arange(256)[None, :]
    t["px"] = one_hot(row // 4 == column)
    row, column = np.arange(120)[:, None], np.arange(400)[None, :]
    t["pz"] = one_hot((row // 24 == column // 80) & (row % 24 == column % 80 // 4))
    row, column = np.arange(512)[:, None], np.arange(128)[None, :]
    t["pcx"] = one_hot((row % 256 < 160) & (row // 256 * 64 + row % 256 // 4 == column))
    row, column = np.arange(16)[:, None], np.arange(48)[None, :]
    t["pcz"] = one_hot((row // 8 == column // 24) & (column % 24 < 20) & (row % 8 == column % 24 // 4))
    row, column, place = np.arange(16)[:, None], np.arange(128)[None, :], np.arange(32)[:, None, None]
    knot = place - 1 - row // 8 + row % 8
    t["rows_m"] = one_hot((knot == column) & (column < 33))
    t["rows_c"] = one_hot((knot == column) & (column < 9))[:8]
    row, column, place = np.arange(24)[:, None], np.arange(256)[None, :], np.arange(8)[:, None, None]
    knot = np.where(row < 16, row - 2, row - 16 + place - 2)
    found = (knot == column // 32 - 1 + column % 8) & (column % 8 < 4) & (knot >= 0) & (knot < 9)
    t["sum_c"] = one_hot(found)
    row, column, place = np.arange(112)[:, None], np.arange(512)[None, :], np.arange(32)[:, None, None]
    knot = np.where(row < 96, row % 48 - 2, row % 8 + place - 2)
    b = np.where(row < 96, row // 48, (row - 96) // 8)
    found = (knot == column // 16 - 1 + column % 8) & (column % 8 < 4) & (column // 8 % 2 == b)
    t["sum_m"] = one_hot(found & (knot >= 0) & (knot < 33))
    return t


def dot(a, b):
    return jnp.dot(a, b, preferred_element_type=F32)


def dot_rows(a, b):
    return lax.dot_general(
        a, b, (((0,), (0,)), ((), ())), precision=HIGHEST, preferred_element_type=F32
    )


def parts(values):
    high = values.astype(BF16)
    return high, (values - high.astype(F32)).astype(BF16)


def dot3(a, right):
    high, low = parts(a)
    return dot(jnp.concatenate([high, high, low], axis=1), right)


def dot_wide(a, table):
    wide = dot(jnp.concatenate(parts(a), axis=1), table)
    return wide[:, 0:128] + wide[:, 128:256]


def dot_exact(table, b):
    wide = dot(table, jnp.concatenate(parts(b), axis=1))
    return wide[:, 0:128] + wide[:, 128:256]


def dot_gather(table, b):
    n = table.shape[0] // 2
    wide = dot(table, jnp.concatenate(parts(b), axis=1))
    return (wide[0:n, 0:128] + wide[0:n, 128:256]) + wide[n:, 0:128]


def stacked(column, n):
    high, low = parts(jnp.concatenate([column, jnp.zeros((32 - n, column.shape[1]), F32)], axis=0))
    return jnp.concatenate([high, low, high, jnp.zeros_like(low)], axis=0)


def from_lane(values, lane):
    return values if lane == 0 else pltpu.roll(values, 128 - lane, 1)


def shift_lanes(chunks, shift):
    amount = (128 - shift) & 127
    rolled = [pltpu.roll(chunk, amount, 1) for chunk in chunks]
    lane = lax.broadcasted_iota(jnp.int32, chunks[0].shape, 1)
    first = lane < jnp.maximum(-shift, 0)
    last = lane >= 128 - jnp.maximum(shift, 0)
    zero = jnp.zeros_like(chunks[0])
    padded = [zero, *rolled, zero]
    return [
        jnp.where(first, padded[j], jnp.where(last, padded[j + 2], padded[j + 1]))
        for j in range(len(chunks))
    ]


def fraction(exponent):
    grown = jnp.exp2(exponent)
    frac = pl.reciprocal(1.0 + grown, approx=True)
    return frac, frac * (grown * frac)


def weights(fixed, corner, step, fractions):
    (fz, gz), (fy, gy), (fx, gx) = fractions
    line = [[corner[z][y] + fx * step[z][y] for y in (0, 1)] for z in (0, 1)]
    rise = [line[z][1] - line[z][0] for z in (0, 1)]
    plane = [line[z][0] + fy * rise[z] for z in (0, 1)]
    slope_z = plane[1] - plane[0]
    residual = (plane[0] + fz * slope_z) - fixed
    slope_y = rise[0] + fz * (rise[1] - rise[0])
    along = [step[z][0] + fy * (step[z][1] - step[z][0]) for z in (0, 1)]
    slope_x = along[0] + fz * (along[1] - along[0])
    return [
        (residual * slope_z) * gz,
        (residual * slope_y) * gy,
        (residual * slope_x) * gx,
    ]


def greet(k, s):
    barrier = pltpu.get_barrier_semaphore()

    def signal(slab, sec):
        pl.semaphore_signal(barrier, inc=1, device_id=(slab, sec), device_id_type=MESH)

    @pl.loop(1, SLABS)
    def _(i):
        signal((k + i) & (SLABS - 1), s)

    for i in range(1, SECS):
        other = (s + i) & (SECS - 1)
        signal(k, other)
        signal((k + 1) & (SLABS - 1), other)
        signal((k + SLABS - 1) & (SLABS - 1), other)
    return lambda: pl.semaphore_wait(barrier, SLABS - 1 + 3 * (SECS - 1))


def broadcast_start(k, s, tile, buffer, send_sem, recv_sem):
    @pl.loop(0, SLABS - 1)
    def _(i):
        pltpu.make_async_remote_copy(
            src_ref=tile,
            dst_ref=buffer.at[k],
            send_sem=send_sem,
            recv_sem=recv_sem,
            device_id=((k + 16 + i + (i > 15).astype(jnp.int32)) & (SLABS - 1), s),
            device_id_type=MESH,
        ).start()


def broadcast_wait(buffer, send_sem, recv_sem):
    part = buffer.at[pl.ds(0, SLABS - 1)]
    pltpu.make_async_copy(part, part, recv_sem).wait()
    pltpu.make_async_copy(part, part, send_sem).wait()


def remote(src, dst, send_sem, recv_sem, device):
    return pltpu.make_async_remote_copy(
        src_ref=src,
        dst_ref=dst,
        send_sem=send_sem,
        recv_sem=recv_sem,
        device_id=device,
        device_id_type=MESH,
    )


def around(k, s, source, buffer, send, recv, act):
    slabs = ((k + SLABS - 1) & (SLABS - 1), k, (k + 1) & (SLABS - 1))

    def one(dk, other):
        if act == "wait_recv":
            copy = remote(source, buffer.at[dk, other], send.at[dk, other], recv.at[dk, other], (k, other))
        else:
            copy = remote(
                source, buffer.at[2 - dk, s], send.at[dk, other], recv.at[2 - dk, s], (slabs[dk], other)
            )
        getattr(copy, act)()

    for dk in range(3):
        for other in range(SECS):
            if dk == 1:
                pl.when(s != other)(functools.partial(one, dk, other))
            else:
                one(dk, other)


TABLES = {
    "px": None, "pz": None, "pcx": None, "pcz": None,
    "rows_m": "k", "rows_c": "q", "cspread": "r", "cgather": "r", "cbt": None, "cbx": None,
    "sum_c": "q", "mspread": "rs", "mgather": "rs", "mbt": None, "mbx": None,
    "spread": "rs", "gather": "s", "bt": None, "bx": None, "sum_m": "k",
}


def finish(*refs):
    copies = [pltpu.make_async_copy(refs[i], refs[i + 3], refs[6].at[i]) for i in range(3)]
    for copy in copies:
        copy.start()
    for copy in copies:
        copy.wait()


def kernel(
    moving, fixed, lat_fine, lat_mid, lat_coarse, off_fine, off_mid, off_coarse, *refs
):
    n = len(TABLES)
    stored, refs = refs[:n], refs[n:]
    fine_out, mid_out, coarse_out, *refs = refs
    t = dict(zip(TABLES, refs[:n]))
    (
        pad, fx, sums, zlo, zhi, z_bef, z_aft, y_bef, y_aft, corners,
        lf_own, lf_prev, lf_next, lf, mt, ct,
        pooled_m, pooled_f, pm_bef, pm_aft, pm_halo,
        piece, pieces, cv, cf, mm,
        c_tile, c_buf, m_part, m_parts, m_tile, m_buf,
        at, by, columns, field_a, field_b, split_a, split_b, adjoint, mixed,
        f_part, f_parts, f_tile, f_buf,
        load_sem, table_sem, send, recv, psend, precv, fsend, frecv, tsend, trecv, bsem,
    ) = refs[n:]
    k, s = lax.axis_index("slab"), lax.axis_index("sec")
    nxt, prv = (k + 1) & (SLABS - 1), (k + SLABS - 1) & (SLABS - 1)
    q, r = k >> 2, k & 3
    has_prev, has_next = (k > 0).astype(F32), (k < SLABS - 1).astype(F32)
    up, down = s < SECS - 1, s > 0
    own_y, own_z = pl.ds(4, NY), pl.ds(8, NZ)

    load_moving = [
        pltpu.make_async_copy(
            moving.at[:, :, pl.ds(128 * c, 128)], pad.at[c, own_y, own_z], load_sem.at[c]
        )
        for c in range(CHUNKS)
    ]
    load_fixed = [
        pltpu.make_async_copy(
            fixed.at[:, :, pl.ds(128 * c, 128)], fx.at[c, :, pl.ds(0, NZ)], load_sem.at[CHUNKS + c]
        )
        for c in range(CHUNKS)
    ]
    place = {"k": k, "q": q, "r": r, "s": s, "rs": 4 * r + s}
    load_table = {}
    for i, (name, which) in enumerate(TABLES.items()):
        source = stored[i] if which is None else stored[i].at[place[which]]
        load_table[name] = pltpu.make_async_copy(source, t[name], table_sem.at[i])
    for copy in load_moving:
        copy.start()
    all_here = greet(k, s)
    for copy in (*load_fixed, *load_table.values()):
        copy.start()

    def table(name):
        load_table[name].wait()
        return t[name]

    px, pz = table("px"), table("pz")

    def pooled():
        high, low = parts(sums[...].reshape(400, NX))
        high, low = parts(dot(high, px[...]) + dot(low, px[...]))
        return ((dot(pz[...], high) + dot(pz[...], low)) * (1.0 / 64.0)).reshape(5, 24, 256)

    for c in range(CHUNKS):
        load_moving[c].wait()
        lanes = slice(128 * c, 128 * c + 128)

        @pl.loop(0, 5, unroll=5)
        def _(group):
            four = [pad[c, 4 * group + 4 + i, 8:88, :] for i in range(4)]
            sums[group, :, lanes] = (four[0] + four[1]) + (four[2] + four[3])

    pooled_m[...] = pooled()
    all_here()

    lat_to_next = remote(lf_own, lf_prev, send.at[0], recv.at[0], (nxt, s))
    lat_to_prev = remote(lf_own, lf_next, send.at[1], recv.at[1], (prv, s))
    z_to_next = remote(zhi, z_bef, send.at[2], recv.at[2], (nxt, s))
    z_to_prev = remote(zlo, z_aft, send.at[3], recv.at[3], (prv, s))
    to_bef = remote(pad.at[:, pl.ds(20, 4), own_z], y_bef, send.at[4], recv.at[4], (k, s + 1))
    to_aft = remote(pad.at[:, pl.ds(4, 4), own_z], y_aft, send.at[5], recv.at[5], (k, s - 1))
    first, last = pl.ds(0, 2), pl.ds(8, 2)
    corner_up = [
        remote(zhi.at[:, last], corners.at[0], send.at[6], recv.at[6], (nxt, s + 1)),
        remote(zlo.at[:, last], corners.at[1], send.at[7], recv.at[7], (prv, s + 1)),
    ]
    corner_down = [
        remote(zhi.at[:, first], corners.at[2], send.at[8], recv.at[8], (nxt, s - 1)),
        remote(zlo.at[:, first], corners.at[3], send.at[9], recv.at[9], (prv, s - 1)),
    ]
    head, tail = pl.ds(0, 8), pl.ds(16, 8)
    mid_same = [
        remote(pooled_m.at[:, tail], pm_halo.at[0, 1], send.at[10], recv.at[10], (nxt, s)),
        remote(pooled_m.at[:, head], pm_halo.at[1, 1], send.at[11], recv.at[11], (prv, s)),
    ]
    mid_up = [
        remote(pooled_m, pm_bef, send.at[12], recv.at[12], (k, s + 1)),
        remote(pooled_m.at[:, tail], pm_halo.at[0, 0], send.at[13], recv.at[13], (nxt, s + 1)),
        remote(pooled_m.at[:, head], pm_halo.at[1, 0], send.at[14], recv.at[14], (prv, s + 1)),
    ]
    mid_down = [
        remote(pooled_m, pm_aft, send.at[15], recv.at[15], (k, s - 1)),
        remote(pooled_m.at[:, tail], pm_halo.at[0, 2], send.at[16], recv.at[16], (nxt, s - 1)),
        remote(pooled_m.at[:, head], pm_halo.at[1, 2], send.at[17], recv.at[17], (prv, s - 1)),
    ]

    def start(*copies):
        for copy in copies:
            copy.start()

    def start_if(condition, *copies):
        @pl.when(condition)
        def _():
            start(*copies)

    for c in range(CHUNKS):
        load_fixed[c].wait()
        lanes = slice(128 * c, 128 * c + 128)

        @pl.loop(0, 5, unroll=5)
        def _(group):
            four = [fx[c, 4 * group + i, 0:80, :] for i in range(4)]
            sums[group, :, lanes] = (four[0] + four[1]) + (four[2] + four[3])

    pooled_f[...] = pooled()

    halves = []
    for ref in (pooled_m, pooled_f):
        upper, lower = jnp.zeros((24, 256), F32), jnp.zeros((24, 256), F32)
        for i in range(5):
            keep = (i + s < 4).astype(F32)
            upper = upper + ref[i] * keep
            lower = lower + ref[i] * (1.0 - keep)
        halves.append(jnp.concatenate([upper, lower], axis=0))
    high, low = parts(jnp.concatenate(halves, axis=1))
    pcx, pcz = table("pcx")[...], table("pcz")[...]
    both = dot(high, pcx) + dot(low, pcx)
    piece[...] = (dot_exact(pcz, both) * (1.0 / 64.0)).reshape(2, 8, 128)
    around(k, s, piece, pieces, psend, precv, "start")
    pieces[1, s] = piece[...]
    start(*mid_same)
    start_if(up, *mid_up)
    start_if(down, *mid_down)

    for ref in (lf_own, mt, ct, cv, mm):
        ref[...] = jnp.zeros_like(ref)
    for d in range(3):
        for b in range(5):
            lf_own[d, b, 0:4, 0:33] = lat_fine[d, b]
        for a in range(9):
            for b in range(2):
                row = 32 * d + 16 * b + a
                mt[row : row + 1, 0:33] = lat_mid[d, a, b : b + 1]
        for a in range(3):
            ct[16 * d + a : 16 * d + a + 1, 0:9] = lat_coarse[d, a]
    for c in range(CHUNKS):

        @pl.loop(0, NY // 2, unroll=5)
        def _(pair):
            for half in range(2):
                rows = slice(4 * half, 4 * half + 4)
                zlo[c, pair, rows, :] = pad[c, 2 * pair + half + 4, 8:12, :]
                zhi[c, pair, rows, :] = pad[c, 2 * pair + half + 4, 84:88, :]

    start(lat_to_next, lat_to_prev)
    start_if(up, to_bef)
    start_if(down, to_aft)
    start(z_to_next, z_to_prev)
    start_if(up, *corner_up)
    start_if(down, *corner_down)

    def pick_rows(name, ref):
        rows = table(name)[...]
        contract = (((1,), (1,)), ((), ()))
        high, low = parts(ref[...])
        return lax.dot_general(rows, high, contract, preferred_element_type=F32) + lax.dot_general(
            rows, low, contract, preferred_element_type=F32
        )

    rows_m, rows_c = pick_rows("rows_m", mt), pick_rows("rows_c", ct)
    cbt, cspread = table("cbt")[...], table("cspread")[...]
    column = dot3(jnp.concatenate([from_lane(rows_c[0:8], 16 * d) for d in range(3)], axis=0), cbt)
    column = jnp.concatenate([column[8 * d : 8 * d + 8] for d in range(3)], axis=1)
    exponent = dot(cspread, stacked(column, 8))[0:40]
    fractions_c = [fraction(exponent[:, 128 * d : 128 * d + 128]) for d in range(3)]
    cbx, cgather = table("cbx"), table("cgather")

    around(k, s, piece, pieces, psend, precv, "wait_recv")

    lane = lax.broadcasted_iota(jnp.int32, (5, 128), 1)
    for dk in range(3):
        scale = (has_prev, jnp.float32(1.0), has_next)[dk]
        rows = (slice(3, 8), slice(8, 13), slice(13, 18))[dk]
        for c in range(5):
            value = jnp.zeros((8, 128), F32)
            if c < 4:
                value = value + pieces[dk, c, 0]
            if c > 0:
                value = value + pieces[dk, c - 1, 1]
            cv[4 + c, rows, :] = jnp.where(lane < 40, value[0:5], 0.0) * scale
            if dk == 1:
                cf[c] = value
    fixed_c = pltpu.roll(cf[...].reshape(40, 128), 64, 1)

    oz, oy, ox = off_coarse[0, 0, q], off_coarse[1, 0, q], off_coarse[2, 0, q]
    a_z, b_z = [], []
    for e in (0, 1):
        window = cv[pl.ds(4 + oy, 6), pl.ds(8 + oz + e, 8), :].reshape(48, 128)
        here, there = shift_lanes([window], ox)[0], shift_lanes([window], ox + 1)[0]
        a_z.append(here)
        b_z.append(there - here)
    corner = [[a_z[z][8 * y : 8 * y + 40] for y in (0, 1)] for z in (0, 1)]
    step = [[b_z[z][8 * y : 8 * y + 40] for y in (0, 1)] for z in (0, 1)]
    total = jnp.concatenate(weights(fixed_c, corner, step, fractions_c), axis=1)
    total = dot_wide(jnp.concatenate([total, jnp.zeros((8, 384), F32)], axis=0), cbx[...])
    total = jnp.concatenate([total, jnp.zeros((80, 128), F32)], axis=0)
    c_tile[...] = dot_gather(cgather[...], total)[0:8]
    broadcast_start(k, s, c_tile, c_buf, bsem.at[0], bsem.at[1])
    c_buf[k] = c_tile[...]

    @pl.when(s == 0)
    def _():
        y_bef[...] = jnp.zeros_like(y_bef)
        corners[0:2] = jnp.zeros((2, CHUNKS, 2, 8, 128), F32)
        pm_bef[...] = jnp.zeros_like(pm_bef)
        pm_halo[:, 0] = jnp.zeros((2, 5, 8, 256), F32)

    @pl.when(s == SECS - 1)
    def _():
        y_aft[...] = jnp.zeros_like(y_aft)
        corners[2:4] = jnp.zeros((2, CHUNKS, 2, 8, 128), F32)
        pm_aft[...] = jnp.zeros_like(pm_aft)
        pm_halo[:, 2] = jnp.zeros((2, 5, 8, 256), F32)

    for copy in mid_same:
        copy.wait_recv()

    @pl.when(s > 0)
    def _():
        for copy in mid_up:
            copy.wait_recv()

    @pl.when(s < SECS - 1)
    def _():
        for copy in mid_down:
            copy.wait_recv()

    for c in range(2):
        lanes = slice(128 * c, 128 * c + 128)
        for e, whole in enumerate((pm_bef, pooled_m, pm_aft)):
            for y in range(5):
                mm[c, 5 * e + y, 4:8, :] = pm_halo[0, e, y, 0:4, lanes] * has_prev
                mm[c, 5 * e + y, 8:28, :] = whole[y, 0:20, lanes]
                mm[c, 5 * e + y, 28:32, :] = pm_halo[1, e, y, 0:4, lanes] * has_next

    oz, oy, ox = off_mid[0, 0, 0], off_mid[0, 0, 1], off_mid[0, 0, 2]
    a_z, b_z = [], []
    for e in (0, 1):
        window = [mm[c, pl.ds(5 + oy, 6), pl.ds(8 + oz + e, 24), :].reshape(144, 128) for c in range(2)]
        here, there = shift_lanes(window, ox), shift_lanes(window, ox + 1)
        a_z.append(here)
        b_z.append([there[c] - here[c] for c in range(2)])

    mbt, mspread, mbx, mgather = table("mbt"), table("mspread"), table("mbx"), table("mgather")
    own = [from_lane(rows_m[0:8], 32 * d + 16 * b) for d in range(3) for b in range(2)]
    own = dot3(jnp.concatenate(own, axis=0), mbt[0])
    coarse = dot3(jnp.concatenate([from_lane(rows_c[8:16], 16 * d) for d in range(3)], axis=0), mbt[1])
    column = [
        jnp.concatenate([own[16 * d : 16 * d + 16], coarse[8 * d : 8 * d + 8]], axis=0) for d in range(3)
    ]
    base_m = dot(mspread[...], stacked(jnp.concatenate(column, axis=1), 24))[0:120]
    sum_c = table("sum_c")

    def make_window(block, oz, oy, ox, y):
        window = [pad[c, 4 + oy + y, pl.ds(20 * block + 8 + oz, 24), :] for c in range(CHUNKS)]
        here, there = shift_lanes(window, ox), shift_lanes(window, ox + 1)
        for c in range(CHUNKS):
            at[block, c, y, 0:24, :] = here[c]
            by[block, c, y, 0:24, :] = there[c] - here[c]

    def make_windows(blocks, ranges):
        @pl.loop(*blocks)
        def _(block):
            offsets = [off_fine[d, block, s] for d in range(3)]
            for first_y, last_y, unroll in ranges:
                pl.loop(first_y, last_y, unroll=unroll)(functools.partial(make_window, block, *offsets))

    make_windows((1, 3), ((4, 16, 3),))

    broadcast_wait(c_buf, bsem.at[0], bsem.at[1])
    gradient = dot_exact(sum_c[...], c_buf[...].reshape(256, 128))
    near_c = gradient[16:24]
    gradient = gradient[0:16]
    inverse = lax.rsqrt(jnp.sum(gradient * gradient) * (1.0 / 81.0) + EPSILON)

    near = dot3(jnp.concatenate([from_lane(near_c, 16 * d) for d in range(3)], axis=0), mbt[1])
    near = jnp.concatenate([near[8 * d : 8 * d + 8] for d in range(3)], axis=1)
    near = dot(mspread[...], stacked(jnp.concatenate([jnp.zeros((16, 768), F32), near], axis=0), 24))
    exponent = base_m - (STEP_SIZE * inverse) * near[0:120]
    fixed_m = pooled_f[...].reshape(120, 256)
    found = []
    for c in range(2):
        lanes = slice(128 * c, 128 * c + 128)
        corner = [[a_z[z][c][24 * y : 24 * y + 120] for y in (0, 1)] for z in (0, 1)]
        step = [[b_z[z][c][24 * y : 24 * y + 120] for y in (0, 1)] for z in (0, 1)]
        fractions = [fraction(exponent[:, 256 * d + 128 * c : 256 * d + 128 * c + 128]) for d in range(3)]
        found.append(weights(fixed_m[:, lanes], corner, step, fractions))
    total = jnp.concatenate([found[c][d] for d in range(3) for c in range(2)], axis=1)
    total = dot_wide(jnp.concatenate([total, jnp.zeros((8, 768), F32)], axis=0), mbx[...])
    m_part[...] = dot_gather(mgather[...], total)

    def part_copies(act):
        for other in range(SECS):

            @pl.when(s != other)
            def _():
                slot = other if act == "wait_recv" else s
                getattr(remote(m_part, m_parts.at[slot], tsend.at[other], trecv.at[slot], (k, other)), act)()

    part_copies("start")
    m_parts[s] = m_part[...]
    part_copies("wait_recv")
    m_tile[...] = (m_parts[0] + m_parts[1]) + (m_parts[2] + m_parts[3])
    broadcast_start(k, s, m_tile, m_buf, bsem.at[2], bsem.at[3])
    m_buf[k] = m_tile[...]

    gradient = gradient * inverse
    next_c = [
        from_lane(rows_c[8:16], 16 * d) - (STEP_SIZE * inverse) * from_lane(near_c, 16 * d) for d in range(3)
    ]
    turn_r = lax.broadcasted_iota(jnp.int32, (48, 128), 0)
    turn = jnp.where(turn_r == lax.broadcasted_iota(jnp.int32, (48, 128), 1) + 2, 1.0, 0.0)
    turned = dot_rows(gradient, turn[0:16])
    for d in range(3):
        for a in range(3):
            coarse_out[d, a] = turned[16 * d + a : 16 * d + a + 1, 0:9]
    for c in range(CHUNKS):
        pad[c, :, 0:8, :] = jnp.zeros((28, 8, 128), F32)
        pad[c, :, 88:96, :] = jnp.zeros((28, 8, 128), F32)
        fx[c, :, 80:88, :] = jnp.zeros((NY, 8, 128), F32)
        for block in range(4):
            at[block, c, :, 24:32, :] = jnp.zeros((21, 8, 128), F32)
            by[block, c, :, 24:32, :] = jnp.zeros((21, 8, 128), F32)

    for copy in (lat_to_next, lat_to_prev, z_to_next, z_to_prev):
        copy.wait_recv()

    @pl.when(s > 0)
    def _():
        for copy in (to_bef, *corner_up):
            copy.wait_recv()

    @pl.when(s < SECS - 1)
    def _():
        for copy in (to_aft, *corner_down):
            copy.wait_recv()

    pad[:, 0:4, 8:88, :] = y_bef[...]
    pad[:, 24:28, 8:88, :] = y_aft[...]

    @pl.loop(0, NY // 2, unroll=2)
    def _(pair):
        for half in range(2):
            rows = slice(4 * half, 4 * half + 4)
            for c in range(CHUNKS):
                pad[c, 2 * pair + half + 4, 4:8, :] = z_bef[c, pair, rows, :] * has_prev
                pad[c, 2 * pair + half + 4, 88:92, :] = z_aft[c, pair, rows, :] * has_next

    for y in range(4):
        rows = slice(4 * (y % 2), 4 * (y % 2) + 4)
        for c in range(CHUNKS):
            for n in range(2):
                where = slice(4, 8) if n == 0 else slice(88, 92)
                keep = has_prev if n == 0 else has_next
                pad[c, y, where, :] = corners[n, c, y // 2, rows, :] * keep
                pad[c, 24 + y, where, :] = corners[2 + n, c, y // 2, rows, :] * keep

    make_windows((1, 3), ((0, 4, 2), (16, 21, 5)))
    make_windows((0, 1), ((0, 21, 3),))
    make_windows((3, 4), ((0, 21, 3),))

    for d in range(3):
        for b in range(5):
            lf[d, 8 * b : 8 * b + 1, :] = lf_prev[d, b, 3:4, :] * has_prev
            lf[d, 8 * b + 1 : 8 * b + 5, :] = lf_own[d, b, 0:4, :]
            lf[d, 8 * b + 5 : 8 * b + 7, :] = lf_next[d, b, 0:2, :] * has_next
            lf[d, 8 * b + 7 : 8 * b + 8, :] = jnp.zeros((1, 128), F32)
    bt = table("bt")
    own = dot3(lf[...].reshape(120, 128), bt[0])
    mid = [from_lane(rows_m[8:16], 32 * d + 16 * b) for d in range(3) for b in range(2)]
    mid = dot3(jnp.concatenate(mid, axis=0), bt[1])
    coarse = dot3(jnp.concatenate(next_c, axis=0), bt[2])
    base_f = [
        jnp.concatenate(
            [own[40 * d : 40 * d + 40], mid[16 * d : 16 * d + 16], coarse[8 * d : 8 * d + 8]], axis=0
        )
        for d in range(3)
    ]
    base_f = jnp.concatenate(base_f, axis=1)
    spread, gather, bx, sum_m = table("spread"), table("gather"), table("bx"), table("sum_m")

    broadcast_wait(m_buf, bsem.at[2], bsem.at[3])
    gradient = dot_exact(sum_m[...], m_buf[...].reshape(512, 128))
    near = gradient[96:112]
    gradient = gradient[0:96]
    inverse = lax.rsqrt(jnp.sum(gradient * gradient) * (1.0 / 1782.0) + EPSILON)

    near = dot3(jnp.concatenate([from_lane(near, 16 * d) for d in range(3)], axis=0), bt[1])
    near = jnp.concatenate([near[16 * d : 16 * d + 16] for d in range(3)], axis=1)
    near = jnp.concatenate([jnp.zeros((40, 3 * NX), F32), near, jnp.zeros((8, 3 * NX), F32)], axis=0)
    upper, lower = parts(base_f - (STEP_SIZE * inverse) * near)
    columns[0:64, :] = upper
    columns[64:128, :] = upper
    columns[128:192, :] = lower
    columns[192:256, :] = lower
    field_a[...] = dot(spread[0:480, :], columns[...])

    def fine_block(block, split, split_before, field, field_after):
        adjoint[...] = jnp.zeros_like(adjoint)
        after = pl.ds(pl.multiple_of(480 * jnp.minimum(block + 1, 3), 480), 480)

        @pl.loop(0, 5)
        def _(i):
            lanes = pl.ds(pl.multiple_of(384 * i, 384), 384)
            field_after[:, lanes] = dot(spread[after, :], columns[:, lanes])
            lanes = pl.ds(pl.multiple_of(768 * i, 768), 768)
            adjoint[...] += dot(split_before[:, lanes], bx[lanes, :])
            for pair in range(2):
                for c in range(CHUNKS):
                    found = []
                    for h in range(2):
                        y = 4 * i + 2 * pair + h
                        corner = [[at[block, c, y + e, z : z + 24, :] for e in (0, 1)] for z in (0, 1)]
                        step = [[by[block, c, y + e, z : z + 24, :] for e in (0, 1)] for z in (0, 1)]
                        rows = pl.ds(pl.multiple_of(24 * y, 8), 24)
                        fractions = [
                            fraction(field[rows, NX * d + 128 * c : NX * d + 128 * c + 128]) for d in range(3)
                        ]
                        atlas = fx[c, y, pl.ds(20 * block, 24), :]
                        found.append(weights(atlas, corner, step, fractions))
                    rows = pl.ds(pl.multiple_of(96 * i + 48 * pair, 48), 48)
                    for d in range(3):
                        upper, lower = parts(jnp.concatenate([found[0][d], found[1][d]], axis=0))
                        lane = 2 * NX * d + 128 * c
                        split[rows, lane : lane + 128] = upper
                        split[rows, lane + NX : lane + NX + 128] = lower

        before = pl.ds(pl.multiple_of(480 * jnp.maximum(block - 1, 0), 480), 480)
        mixed[before, :] = adjoint[:, 0:128] + adjoint[:, 128:256]

    @pl.loop(0, 2)
    def _(two):
        fine_block(2 * two, split_a, split_b, field_a, field_b)
        fine_block(2 * two + 1, split_b, split_a, field_b, field_a)

    wide = dot(split_b[...], bx[...])
    mixed[1440:1920, :] = wide[:, 0:128] + wide[:, 128:256]
    f_part[...] = dot_gather(gather[...], mixed[...])
    around(k, s, f_part, f_parts, fsend, frecv, "start")
    f_parts[1, s] = f_part[...]

    for b in range(2):
        turned = dot_rows(gradient[48 * b : 48 * b + 48] * inverse, turn)
        for d in range(3):
            for a in range(9):
                mid_out[d, a, b : b + 1, :] = turned[16 * d + a : 16 * d + a + 1, 0:33]
    row = lax.broadcasted_iota(jnp.int32, (40, 128), 0) & 7

    around(k, s, f_part, f_parts, fsend, frecv, "wait_recv")
    before, middle, after = ((f_parts[i, 0] + f_parts[i, 1]) + (f_parts[i, 2] + f_parts[i, 3]) for i in range(3))
    middle = middle + jnp.where((row == 1) | (row == 2), pltpu.roll(before * has_prev, 36, 0), 0.0)
    middle = middle + jnp.where(row == 4, pltpu.roll(after * has_next, 4, 0), 0.0)
    middle = jnp.where((row >= 1) & (row <= 4), middle, 0.0)
    f_tile[...] = jnp.full((8, 128), jnp.sum(middle * middle))
    broadcast_start(k, s, f_tile, f_buf, bsem.at[4], bsem.at[5])
    f_buf[k] = f_tile[...]

    for copy in (lat_to_next, lat_to_prev, z_to_next, z_to_prev, *mid_same):
        copy.wait_send()

    @pl.when(up)
    def _():
        for copy in (to_bef, *corner_up, *mid_up):
            copy.wait_send()

    @pl.when(down)
    def _():
        for copy in (to_aft, *corner_down, *mid_down):
            copy.wait_send()

    around(k, s, piece, pieces, psend, precv, "wait_send")
    around(k, s, f_part, f_parts, fsend, frecv, "wait_send")
    part_copies("wait_send")
    middle = pltpu.roll(middle, 39, 0)
    thirds = [from_lane(middle, 40 * d) for d in range(3)]

    broadcast_wait(f_buf, bsem.at[4], bsem.at[5])
    squares = jnp.sum(f_buf[...], axis=0)[0:1, :]
    inverse = lax.rsqrt(squares * (1.0 / 63360.0) + EPSILON)
    for d in range(3):
        scaled = thirds[d] * inverse
        for b in range(5):
            fine_out[d, b] = scaled[8 * b : 8 * b + 4, 0:33]


def body(
    fixed_image,
    moving_image,
    lattice_fine,
    lattice_mid,
    lattice_coarse,
    offset_fine,
    offset_mid,
    offset_coarse,
):
    t = tables()
    vmem, smem, hbm = (pl.BlockSpec(memory_space=m) for m in (pltpu.VMEM, pltpu.SMEM, pl.ANY))
    shape = lambda *dims: jax.ShapeDtypeStruct(dims, F32)
    buf = lambda *dims: pltpu.VMEM(dims, F32)
    half = lambda *dims: pltpu.VMEM(dims, BF16)
    dma = lambda *dims: pltpu.SemaphoreType.DMA(dims)
    fine, mid, coarse = pl.pallas_call(
        kernel,
        out_shape=[shape(3, 5, 4, 33), shape(3, 9, 2, 33), shape(3, 3, 1, 9)],
        in_specs=[hbm, hbm, vmem, vmem, vmem, smem, smem, smem] + [hbm] * len(TABLES),
        out_specs=[vmem] * 3,
        scratch_shapes=[
            *[pltpu.VMEM(t[n].shape[which is not None :], t[n].dtype) for n, which in TABLES.items()],
            buf(CHUNKS, 28, 96, 128), buf(CHUNKS, NY, 88, 128), buf(5, NZ, NX),
            *[buf(CHUNKS, 10, 8, 128)] * 4, *[buf(CHUNKS, 4, NZ, 128)] * 2, buf(4, CHUNKS, 2, 8, 128),
            *[buf(3, 5, 8, 128)] * 3, buf(3, 40, 128), buf(128, 128), buf(128, 128),
            *[buf(5, 24, 256)] * 4, buf(2, 3, 5, 8, 256),
            buf(2, 8, 128), buf(3, SECS, 2, 8, 128), buf(14, 32, 128), buf(5, 8, 128), buf(2, 15, 40, 128),
            buf(8, 128), buf(SLABS, 8, 128), buf(16, 128), buf(SECS, 16, 128), buf(16, 128), buf(SLABS, 16, 128),
            *[buf(4, CHUNKS, 21, 32, 128)] * 2, half(256, 3 * NX),
            *[buf(480, 3 * NX)] * 2, *[half(480, 6 * NX)] * 2, buf(480, 256), buf(1920, 128),
            buf(40, 128), buf(3, SECS, 40, 128), buf(8, 128), buf(SLABS, 8, 128),
            dma(10), dma(len(TABLES)), dma(18), dma(18), *[dma(3, SECS)] * 4, dma(SECS), dma(SECS), dma(6),
        ],
        compiler_params=pltpu.CompilerParams(
            collective_id=0, has_side_effects=True, vmem_limit_bytes=VMEM_LIMIT
        ),
        name="mega",
    )(
        jnp.transpose(moving_image, (1, 0, 2)),
        jnp.transpose(fixed_image, (1, 0, 2)),
        jnp.transpose(lattice_fine, (0, 2, 1, 3)),
        jnp.transpose(lattice_mid, (0, 3, 2, 1)),
        jnp.transpose(lattice_coarse, (0, 3, 2, 1)),
        offset_fine,
        jnp.transpose(offset_mid, (1, 2, 0)),
        jnp.transpose(offset_coarse, (0, 2, 1)),
        *(t[n] for n in TABLES),
    )
    results = (fine, mid, coarse)
    fine, mid, coarse = pl.pallas_call(
        finish,
        out_shape=[jax.ShapeDtypeStruct(a.shape, F32) for a in results],
        in_specs=[hbm] * 3,
        out_specs=[hbm] * 3,
        scratch_shapes=[dma(3)],
        name="finish",
    )(*results)
    return (
        jnp.transpose(fine, (0, 2, 1, 3)),
        jnp.transpose(mid, (0, 3, 2, 1)),
        jnp.transpose(coarse, (0, 3, 2, 1)),
    )


def solution(mesh):
    placed = (
        P("slab", "sec", None),
        P("slab", "sec", None),
        P(None, "slab", None, None),
        P(),
        P(),
        P(None, "slab", None),
        P(None, "slab", None),
        P(),
    )
    return jax.shard_map(
        body,
        mesh=mesh,
        in_specs=placed,
        out_specs=(P(None, "slab", None, None), P(), P()),
        check_vma=False,
    )
```

```python
import functools

import jax
import jax.numpy as jnp
import ml_dtypes
import numpy as np
from jax import lax
from jax.experimental import pallas as pl
from jax.experimental.pallas import tpu as pltpu
from jax.sharding import PartitionSpec as P

SP = 20
EPSILON = 1e-06
STEP_SIZE = 0.5
HIGHEST = lax.Precision.HIGHEST
F32 = jnp.float32
BF16 = jnp.bfloat16
MESH = pl.DeviceIdType.MESH
SLABS = 32
SECS = 4
NZ, NY, NX = 80, 20, 640
CHUNKS = NX // 128
LOG2E = 1.4426950408889634
VMEM_LIMIT = 58 * 1024 * 1024


def basis(rows, knots, factor, coarse):
    rows, knots = np.asarray(rows, np.float64), np.asarray(knots, np.float64)
    position = factor * rows + 0.5 * (factor - 1)
    centre = SP * coarse * knots + 0.5 * (coarse - 1)
    distance = np.abs((position[:, None] - centre[None, :]) / (SP * coarse))
    near = 2.0 / 3.0 - distance**2 + 0.5 * distance**3
    far = np.maximum(2.0 - distance, 0.0) ** 3 / 6.0
    return np.where(distance < 1.0, near, far)


def two_parts(values):
    high = values.astype(ml_dtypes.bfloat16)
    low = (values - high.astype(np.float64)).astype(ml_dtypes.bfloat16)
    return high, low


def right_parts(values):
    high, low = two_parts(values)
    return np.concatenate([high, low, high], axis=-2)


def wide_parts(values):
    high, low = two_parts(values)
    zero = np.zeros_like(high)
    return np.concatenate([np.concatenate([high, low], 1), np.concatenate([high, zero], 1)], 0)


def one_hot(condition):
    return condition.astype(ml_dtypes.bfloat16)


@functools.cache
def tables():
    t = {}
    rz, ry = np.zeros((4, 4, 24, 64)), np.zeros((4, NY, 64))
    z, y, x = np.arange(NZ), np.arange(NY), np.arange(NX)
    for r in range(4):
        for block in range(4):
            rows = z[20 * block : 20 * block + 20]
            for a in range(7):
                rz[r, block, :20, a:40:8] = basis(rows, [a - 1], 1, 1)
            for a in range(5):
                rz[r, block, :20, 40 + a : 56 : 8] = basis(rows, [a - 2], 1, 4)
                rz[r, block, :20, 56 + a : 57 + a] = basis(rows + 80 * r, [a - 2], 1, 16)
    for s in range(4):
        for a in range(7):
            ry[s, :, a:40:8] = basis(y + 20 * s, range(5), 1, 1)
        for a in range(5):
            ry[s, :, 40 + a : 56 : 8] = basis(y + 20 * s, range(2), 1, 4)
            ry[s, :, 56 + a : 57 + a] = basis(y + 20 * s, [0], 1, 16)
    whole = rz[:, None, :, None] * ry[None, :, None, :, None, :]
    high, low = two_parts(whole.reshape(16, 1920, 64))
    t["spread"] = np.concatenate([high, low, high, low], axis=2)
    t["gather"] = np.concatenate([high[:4, :, :40], low[:4, :, :40]], axis=2).transpose(0, 2, 1)
    across = np.zeros((3, 128, NX))
    across[0, :33] = basis(x, range(33), 1, 1).T
    across[1, :9] = basis(x, range(9), 1, 4).T
    across[2, :3] = basis(x, range(3), 1, 16).T
    t["bt"] = right_parts(-LOG2E * across)
    along = np.zeros((3, NX, 128))
    for d in range(3):
        along[d, :, 40 * d : 40 * d + 33] = basis(x, range(33), 1, 1)
    t["bx"] = np.concatenate([wide_parts(along[d]) for d in range(3)], axis=0)
    rz, ry = np.zeros((4, 24, 32)), np.zeros((4, 5, 32))
    z, y, x = np.arange(20), np.arange(5), np.arange(160)
    for r in range(4):
        for a in range(4):
            rz[r, :20, a:16:8] = basis(z, [a - 1], 4, 4)
        for a in range(5):
            rz[r, :20, 16 + a : 17 + a] = basis(z + 20 * r, [a - 2], 4, 16)
    for s in range(4):
        for a in range(4):
            ry[s, :, a:16:8] = basis(y + 5 * s, range(2), 4, 4)
        for a in range(5):
            ry[s, :, 16 + a : 17 + a] = basis(y + 5 * s, [0], 4, 16)
    whole = np.zeros((16, 128, 32))
    whole[:, :120] = (rz[:, None, None] * ry[None, :, :, None]).reshape(16, 120, 32)
    high, low = two_parts(whole)
    t["mspread"] = np.concatenate([high, high, low, np.zeros_like(low)], axis=2)
    t["mgather"] = np.concatenate([high[:, :, :16], low[:, :, :16]], axis=2).transpose(0, 2, 1)
    across = np.zeros((2, 128, 256))
    across[0, :9, :160] = basis(x, range(9), 4, 4).T
    across[1, :3, :160] = basis(x, range(3), 4, 16).T
    t["mbt"] = right_parts(-LOG2E * across)
    along = np.zeros((3, 256, 128))
    for d in range(3):
        along[d, :160, 16 * d : 16 * d + 9] = basis(x, range(9), 4, 4)
    t["mbx"] = wide_parts(along.reshape(768, 128))
    rz = np.zeros((4, 8, 32))
    z, y, x = np.arange(5), np.arange(5), np.arange(40)
    for r in range(4):
        for a in range(4):
            rz[r, :5, a : a + 1] = basis(z + 5 * r, [a - 1], 16, 16)
    whole = np.zeros((4, 128, 32))
    whole[:, :40] = (rz[:, None] * basis(y, [0], 16, 16)[None, :, None]).reshape(4, 40, 32)
    high, low = two_parts(whole)
    t["cspread"] = np.concatenate([high, high, low, np.zeros_like(low)], axis=2)
    t["cgather"] = np.concatenate([high[:, :, :16], low[:, :, :16]], axis=2).transpose(0, 2, 1)
    across = np.zeros((128, 128))
    across[:3, :40] = basis(x, range(3), 16, 16).T
    t["cbt"] = right_parts(-LOG2E * across)
    along = np.zeros((3, 128, 128))
    for d in range(3):
        along[d, :40, 16 * d : 16 * d + 3] = basis(x, range(3), 16, 16)
    t["cbx"] = wide_parts(along.reshape(384, 128))
    row, column = np.arange(NX)[:, None], np.arange(256)[None, :]
    t["px"] = one_hot(row // 4 == column)
    row, column = np.arange(120)[:, None], np.arange(400)[None, :]
    t["pz"] = one_hot((row // 24 == column // 80) & (row % 24 == column % 80 // 4))
    row, column = np.arange(512)[:, None], np.arange(128)[None, :]
    t["pcx"] = one_hot((row % 256 < 160) & (row // 256 * 64 + row % 256 // 4 == column))
    row, column = np.arange(16)[:, None], np.arange(48)[None, :]
    t["pcz"] = one_hot((row // 8 == column // 24) & (column % 24 < 20) & (row % 8 == column % 24 // 4))
    row, column, place = np.arange(16)[:, None], np.arange(128)[None, :], np.arange(32)[:, None, None]
    knot = place - 1 - row // 8 + row % 8
    t["rows_m"] = one_hot((knot == column) & (column < 33))
    t["rows_c"] = one_hot((knot == column) & (column < 9))[:8]
    row, column, place = np.arange(24)[:, None], np.arange(256)[None, :], np.arange(8)[:, None, None]
    knot = np.where(row < 16, row - 2, row - 16 + place - 2)
    found = (knot == column // 32 - 1 + column % 8) & (column % 8 < 4) & (knot >= 0) & (knot < 9)
    t["sum_c"] = one_hot(found)
    row, column, place = np.arange(112)[:, None], np.arange(512)[None, :], np.arange(32)[:, None, None]
    knot = np.where(row < 96, row % 48 - 2, row % 8 + place - 2)
    b = np.where(row < 96, row // 48, (row - 96) // 8)
    found = (knot == column // 16 - 1 + column % 8) & (column % 8 < 4) & (column // 8 % 2 == b)
    t["sum_m"] = one_hot(found & (knot >= 0) & (knot < 33))
    return t


def dot(a, b):
    return jnp.dot(a, b, preferred_element_type=F32)


def dot_rows(a, b):
    return lax.dot_general(
        a, b, (((0,), (0,)), ((), ())), precision=HIGHEST, preferred_element_type=F32
    )


def parts(values):
    high = values.astype(BF16)
    return high, (values - high.astype(F32)).astype(BF16)


def dot3(a, right):
    high, low = parts(a)
    return dot(jnp.concatenate([high, high, low], axis=1), right)


def dot_wide(a, table):
    wide = dot(jnp.concatenate(parts(a), axis=1), table)
    return wide[:, 0:128] + wide[:, 128:256]


def dot_exact(table, b):
    wide = dot(table, jnp.concatenate(parts(b), axis=1))
    return wide[:, 0:128] + wide[:, 128:256]


def dot_gather(table, b):
    n = table.shape[0] // 2
    wide = dot(table, jnp.concatenate(parts(b), axis=1))
    return (wide[0:n, 0:128] + wide[0:n, 128:256]) + wide[n:, 0:128]


def stacked(column, n):
    high, low = parts(jnp.concatenate([column, jnp.zeros((32 - n, column.shape[1]), F32)], axis=0))
    return jnp.concatenate([high, low, high, jnp.zeros_like(low)], axis=0)


def from_lane(values, lane):
    return values if lane == 0 else pltpu.roll(values, 128 - lane, 1)


def shift_lanes(chunks, shift):
    amount = (128 - shift) & 127
    rolled = [pltpu.roll(chunk, amount, 1) for chunk in chunks]
    lane = lax.broadcasted_iota(jnp.int32, chunks[0].shape, 1)
    first = lane < jnp.maximum(-shift, 0)
    last = lane >= 128 - jnp.maximum(shift, 0)
    zero = jnp.zeros_like(chunks[0])
    padded = [zero, *rolled, zero]
    return [
        jnp.where(first, padded[j], jnp.where(last, padded[j + 2], padded[j + 1]))
        for j in range(len(chunks))
    ]


def fraction(exponent):
    grown = jnp.exp2(exponent)
    frac = pl.reciprocal(1.0 + grown, approx=True)
    return frac, frac * (grown * frac)


def weights(fixed, corner, step, fractions):
    (fz, gz), (fy, gy), (fx, gx) = fractions
    line = [[corner[z][y] + fx * step[z][y] for y in (0, 1)] for z in (0, 1)]
    rise = [line[z][1] - line[z][0] for z in (0, 1)]
    plane = [line[z][0] + fy * rise[z] for z in (0, 1)]
    slope_z = plane[1] - plane[0]
    residual = (plane[0] + fz * slope_z) - fixed
    slope_y = rise[0] + fz * (rise[1] - rise[0])
    along = [step[z][0] + fy * (step[z][1] - step[z][0]) for z in (0, 1)]
    slope_x = along[0] + fz * (along[1] - along[0])
    return [
        (residual * slope_z) * gz,
        (residual * slope_y) * gy,
        (residual * slope_x) * gx,
    ]


def greet(k, s):
    barrier = pltpu.get_barrier_semaphore()

    def signal(slab, sec):
        pl.semaphore_signal(barrier, inc=1, device_id=(slab, sec), device_id_type=MESH)

    @pl.loop(1, SLABS)
    def _(i):
        signal((k + i) & (SLABS - 1), s)

    for i in range(1, SECS):
        other = (s + i) & (SECS - 1)
        signal(k, other)
        signal((k + 1) & (SLABS - 1), other)
        signal((k + SLABS - 1) & (SLABS - 1), other)
    return lambda: pl.semaphore_wait(barrier, SLABS - 1 + 3 * (SECS - 1))


def broadcast_start(k, s, tile, buffer, send_sem, recv_sem):
    @pl.loop(0, SLABS - 1)
    def _(i):
        pltpu.make_async_remote_copy(
            src_ref=tile,
            dst_ref=buffer.at[k],
            send_sem=send_sem,
            recv_sem=recv_sem,
            device_id=((k + 16 + i + (i > 15).astype(jnp.int32)) & (SLABS - 1), s),
            device_id_type=MESH,
        ).start()


def broadcast_wait(buffer, send_sem, recv_sem):
    part = buffer.at[pl.ds(0, SLABS - 1)]
    pltpu.make_async_copy(part, part, recv_sem).wait()
    pltpu.make_async_copy(part, part, send_sem).wait()


def remote(src, dst, send_sem, recv_sem, device):
    return pltpu.make_async_remote_copy(
        src_ref=src,
        dst_ref=dst,
        send_sem=send_sem,
        recv_sem=recv_sem,
        device_id=device,
        device_id_type=MESH,
    )


def around(k, s, source, buffer, send, recv, act):
    slabs = ((k + SLABS - 1) & (SLABS - 1), k, (k + 1) & (SLABS - 1))

    def one(dk, other):
        if act == "wait_recv":
            copy = remote(source, buffer.at[dk, other], send.at[dk, other], recv.at[dk, other], (k, other))
        else:
            copy = remote(
                source, buffer.at[2 - dk, s], send.at[dk, other], recv.at[2 - dk, s], (slabs[dk], other)
            )
        getattr(copy, act)()

    for dk in range(3):
        for other in range(SECS):
            if dk == 1:
                pl.when(s != other)(functools.partial(one, dk, other))
            else:
                one(dk, other)


TABLES = {
    "px": None, "pz": None, "pcx": None, "pcz": None,
    "rows_m": "k", "rows_c": "q", "cspread": "r", "cgather": "r", "cbt": None, "cbx": None,
    "sum_c": "q", "mspread": "rs", "mgather": "rs", "mbt": None, "mbx": None,
    "spread": "rs", "gather": "s", "bt": None, "bx": None, "sum_m": "k",
}


def finish(*refs):
    copies = [pltpu.make_async_copy(refs[i], refs[i + 3], refs[6].at[i]) for i in range(3)]
    for copy in copies:
        copy.start()
    for copy in copies:
        copy.wait()


def kernel(
    moving, fixed, lat_fine, lat_mid, lat_coarse, off_fine, off_mid, off_coarse, *refs
):
    n = len(TABLES)
    stored, refs = refs[:n], refs[n:]
    fine_out, mid_out, coarse_out, *refs = refs
    t = dict(zip(TABLES, refs[:n]))
    (
        pad, fx, sums, zlo, zhi, z_bef, z_aft, y_bef, y_aft, corners,
        lf_own, lf_prev, lf_next, lf, mt, ct,
        pooled_m, pooled_f, pm_bef, pm_aft, pm_halo,
        piece, pieces, cv, cf, mm,
        c_tile, c_buf, m_part, m_parts, m_tile, m_buf,
        at, by, columns, field_a, field_b, split_a, split_b, adjoint, mixed,
        f_part, f_parts, f_tile, f_buf,
        load_sem, table_sem, send, recv, psend, precv, fsend, frecv, tsend, trecv, bsem,
    ) = refs[n:]
    k, s = lax.axis_index("slab"), lax.axis_index("sec")
    nxt, prv = (k + 1) & (SLABS - 1), (k + SLABS - 1) & (SLABS - 1)
    q, r = k >> 2, k & 3
    has_prev, has_next = (k > 0).astype(F32), (k < SLABS - 1).astype(F32)
    up, down = s < SECS - 1, s > 0
    own_y, own_z = pl.ds(4, NY), pl.ds(8, NZ)

    load_moving = [
        pltpu.make_async_copy(
            moving.at[:, :, pl.ds(128 * c, 128)], pad.at[c, own_y, own_z], load_sem.at[c]
        )
        for c in range(CHUNKS)
    ]
    load_fixed = [
        pltpu.make_async_copy(
            fixed.at[:, :, pl.ds(128 * c, 128)], fx.at[c, :, pl.ds(0, NZ)], load_sem.at[CHUNKS + c]
        )
        for c in range(CHUNKS)
    ]
    place = {"k": k, "q": q, "r": r, "s": s, "rs": 4 * r + s}
    load_table = {}
    for i, (name, which) in enumerate(TABLES.items()):
        source = stored[i] if which is None else stored[i].at[place[which]]
        load_table[name] = pltpu.make_async_copy(source, t[name], table_sem.at[i])
    for copy in load_moving:
        copy.start()
    all_here = greet(k, s)
    for copy in (*load_fixed, *load_table.values()):
        copy.start()

    def table(name):
        load_table[name].wait()
        return t[name]

    lat_to_next = remote(lf_own, lf_prev, send.at[0], recv.at[0], (nxt, s))
    lat_to_prev = remote(lf_own, lf_next, send.at[1], recv.at[1], (prv, s))
    z_to_next = remote(zhi, z_bef, send.at[2], recv.at[2], (nxt, s))
    z_to_prev = remote(zlo, z_aft, send.at[3], recv.at[3], (prv, s))
    to_bef = remote(moving.at[pl.ds(16, 4)], y_bef, send.at[4], recv.at[4], (k, s + 1))
    to_aft = remote(moving.at[pl.ds(0, 4)], y_aft, send.at[5], recv.at[5], (k, s - 1))
    first, last = pl.ds(0, 2), pl.ds(8, 2)
    corner_up = [
        remote(zhi.at[:, last], corners.at[0], send.at[6], recv.at[6], (nxt, s + 1)),
        remote(zlo.at[:, last], corners.at[1], send.at[7], recv.at[7], (prv, s + 1)),
    ]
    corner_down = [
        remote(zhi.at[:, first], corners.at[2], send.at[8], recv.at[8], (nxt, s - 1)),
        remote(zlo.at[:, first], corners.at[3], send.at[9], recv.at[9], (prv, s - 1)),
    ]
    head, tail = pl.ds(0, 8), pl.ds(16, 8)
    mid_same = [
        remote(pooled_m.at[:, tail], pm_halo.at[0, 1], send.at[10], recv.at[10], (nxt, s)),
        remote(pooled_m.at[:, head], pm_halo.at[1, 1], send.at[11], recv.at[11], (prv, s)),
    ]
    mid_up = [
        remote(pooled_m, pm_bef, send.at[12], recv.at[12], (k, s + 1)),
        remote(pooled_m.at[:, tail], pm_halo.at[0, 0], send.at[13], recv.at[13], (nxt, s + 1)),
        remote(pooled_m.at[:, head], pm_halo.at[1, 0], send.at[14], recv.at[14], (prv, s + 1)),
    ]
    mid_down = [
        remote(pooled_m, pm_aft, send.at[15], recv.at[15], (k, s - 1)),
        remote(pooled_m.at[:, tail], pm_halo.at[0, 2], send.at[16], recv.at[16], (nxt, s - 1)),
        remote(pooled_m.at[:, head], pm_halo.at[1, 2], send.at[17], recv.at[17], (prv, s - 1)),
    ]

    def start(*copies):
        for copy in copies:
            copy.start()

    def start_if(condition, *copies):
        @pl.when(condition)
        def _():
            start(*copies)

    all_here()
    start_if(up, to_bef)
    start_if(down, to_aft)
    for c in range(CHUNKS):
        load_moving[c].wait()

        @pl.loop(0, NY // 2, unroll=5)
        def _(pair):
            for half in range(2):
                rows = slice(4 * half, 4 * half + 4)
                zlo[c, pair, rows, :] = pad[c, 2 * pair + half + 4, 8:12, :]
                zhi[c, pair, rows, :] = pad[c, 2 * pair + half + 4, 84:88, :]

    start(z_to_next, z_to_prev)
    start_if(up, *corner_up)
    start_if(down, *corner_down)

    px, pz = table("px"), table("pz")

    def pooled():
        high, low = parts(sums[...].reshape(400, NX))
        high, low = parts(dot(high, px[...]) + dot(low, px[...]))
        return ((dot(pz[...], high) + dot(pz[...], low)) * (1.0 / 64.0)).reshape(5, 24, 256)

    for c in range(CHUNKS):
        lanes = slice(128 * c, 128 * c + 128)

        @pl.loop(0, 5, unroll=5)
        def _(group):
            four = [pad[c, 4 * group + 4 + i, 8:88, :] for i in range(4)]
            sums[group, :, lanes] = (four[0] + four[1]) + (four[2] + four[3])

    pooled_m[...] = pooled()

    for c in range(CHUNKS):
        load_fixed[c].wait()
        lanes = slice(128 * c, 128 * c + 128)

        @pl.loop(0, 5, unroll=5)
        def _(group):
            four = [fx[c, 4 * group + i, 0:80, :] for i in range(4)]
            sums[group, :, lanes] = (four[0] + four[1]) + (four[2] + four[3])

    pooled_f[...] = pooled()

    halves = []
    for ref in (pooled_m, pooled_f):
        upper, lower = jnp.zeros((24, 256), F32), jnp.zeros((24, 256), F32)
        for i in range(5):
            keep = (i + s < 4).astype(F32)
            upper = upper + ref[i] * keep
            lower = lower + ref[i] * (1.0 - keep)
        halves.append(jnp.concatenate([upper, lower], axis=0))
    high, low = parts(jnp.concatenate(halves, axis=1))
    pcx, pcz = table("pcx")[...], table("pcz")[...]
    both = dot(high, pcx) + dot(low, pcx)
    piece[...] = (dot_exact(pcz, both) * (1.0 / 64.0)).reshape(2, 8, 128)
    around(k, s, piece, pieces, psend, precv, "start")
    pieces[1, s] = piece[...]
    start(*mid_same)
    start_if(up, *mid_up)
    start_if(down, *mid_down)

    for ref in (lf_own, mt, ct, cv, mm):
        ref[...] = jnp.zeros_like(ref)
    for d in range(3):
        for b in range(5):
            lf_own[d, b, 0:4, 0:33] = lat_fine[d, b]
        for a in range(9):
            for b in range(2):
                row = 32 * d + 16 * b + a
                mt[row : row + 1, 0:33] = lat_mid[d, a, b : b + 1]
        for a in range(3):
            ct[16 * d + a : 16 * d + a + 1, 0:9] = lat_coarse[d, a]
    start(lat_to_next, lat_to_prev)

    def pick_rows(name, ref):
        rows = table(name)[...]
        contract = (((1,), (1,)), ((), ()))
        high, low = parts(ref[...])
        return lax.dot_general(rows, high, contract, preferred_element_type=F32) + lax.dot_general(
            rows, low, contract, preferred_element_type=F32
        )

    rows_m, rows_c = pick_rows("rows_m", mt), pick_rows("rows_c", ct)
    cbt, cspread = table("cbt")[...], table("cspread")[...]
    column = dot3(jnp.concatenate([from_lane(rows_c[0:8], 16 * d) for d in range(3)], axis=0), cbt)
    column = jnp.concatenate([column[8 * d : 8 * d + 8] for d in range(3)], axis=1)
    exponent = dot(cspread, stacked(column, 8))[0:40]
    fractions_c = [fraction(exponent[:, 128 * d : 128 * d + 128]) for d in range(3)]
    cbx, cgather = table("cbx"), table("cgather")

    around(k, s, piece, pieces, psend, precv, "wait_recv")

    lane = lax.broadcasted_iota(jnp.int32, (5, 128), 1)
    for dk in range(3):
        scale = (has_prev, jnp.float32(1.0), has_next)[dk]
        rows = (slice(3, 8), slice(8, 13), slice(13, 18))[dk]
        for c in range(5):
            value = jnp.zeros((8, 128), F32)
            if c < 4:
                value = value + pieces[dk, c, 0]
            if c > 0:
                value = value + pieces[dk, c - 1, 1]
            cv[4 + c, rows, :] = jnp.where(lane < 40, value[0:5], 0.0) * scale
            if dk == 1:
                cf[c] = value
    fixed_c = pltpu.roll(cf[...].reshape(40, 128), 64, 1)

    oz, oy, ox = off_coarse[0, 0, q], off_coarse[1, 0, q], off_coarse[2, 0, q]
    a_z, b_z = [], []
    for e in (0, 1):
        window = cv[pl.ds(4 + oy, 6), pl.ds(8 + oz + e, 8), :].reshape(48, 128)
        here, there = shift_lanes([window], ox)[0], shift_lanes([window], ox + 1)[0]
        a_z.append(here)
        b_z.append(there - here)
    corner = [[a_z[z][8 * y : 8 * y + 40] for y in (0, 1)] for z in (0, 1)]
    step = [[b_z[z][8 * y : 8 * y + 40] for y in (0, 1)] for z in (0, 1)]
    total = jnp.concatenate(weights(fixed_c, corner, step, fractions_c), axis=1)
    total = dot_wide(jnp.concatenate([total, jnp.zeros((8, 384), F32)], axis=0), cbx[...])
    total = jnp.concatenate([total, jnp.zeros((80, 128), F32)], axis=0)
    c_tile[...] = dot_gather(cgather[...], total)[0:8]
    broadcast_start(k, s, c_tile, c_buf, bsem.at[0], bsem.at[1])
    c_buf[k] = c_tile[...]

    @pl.when(s == 0)
    def _():
        y_bef[...] = jnp.zeros_like(y_bef)
        corners[0:2] = jnp.zeros((2, CHUNKS, 2, 8, 128), F32)
        pm_bef[...] = jnp.zeros_like(pm_bef)
        pm_halo[:, 0] = jnp.zeros((2, 5, 8, 256), F32)

    @pl.when(s == SECS - 1)
    def _():
        y_aft[...] = jnp.zeros_like(y_aft)
        corners[2:4] = jnp.zeros((2, CHUNKS, 2, 8, 128), F32)
        pm_aft[...] = jnp.zeros_like(pm_aft)
        pm_halo[:, 2] = jnp.zeros((2, 5, 8, 256), F32)

    for copy in mid_same:
        copy.wait_recv()

    @pl.when(s > 0)
    def _():
        for copy in mid_up:
            copy.wait_recv()

    @pl.when(s < SECS - 1)
    def _():
        for copy in mid_down:
            copy.wait_recv()

    for c in range(2):
        lanes = slice(128 * c, 128 * c + 128)
        for e, whole in enumerate((pm_bef, pooled_m, pm_aft)):
            for y in range(5):
                mm[c, 5 * e + y, 4:8, :] = pm_halo[0, e, y, 0:4, lanes] * has_prev
                mm[c, 5 * e + y, 8:28, :] = whole[y, 0:20, lanes]
                mm[c, 5 * e + y, 28:32, :] = pm_halo[1, e, y, 0:4, lanes] * has_next

    oz, oy, ox = off_mid[0, 0, 0], off_mid[0, 0, 1], off_mid[0, 0, 2]
    a_z, b_z = [], []
    for e in (0, 1):
        window = [mm[c, pl.ds(5 + oy, 6), pl.ds(8 + oz + e, 24), :].reshape(144, 128) for c in range(2)]
        here, there = shift_lanes(window, ox), shift_lanes(window, ox + 1)
        a_z.append(here)
        b_z.append([there[c] - here[c] for c in range(2)])

    mbt, mspread, mbx, mgather = table("mbt"), table("mspread"), table("mbx"), table("mgather")
    own = [from_lane(rows_m[0:8], 32 * d + 16 * b) for d in range(3) for b in range(2)]
    own = dot3(jnp.concatenate(own, axis=0), mbt[0])
    coarse = dot3(jnp.concatenate([from_lane(rows_c[8:16], 16 * d) for d in range(3)], axis=0), mbt[1])
    column = [
        jnp.concatenate([own[16 * d : 16 * d + 16], coarse[8 * d : 8 * d + 8]], axis=0) for d in range(3)
    ]
    base_m = dot(mspread[...], stacked(jnp.concatenate(column, axis=1), 24))[0:120]
    sum_c = table("sum_c")

    def make_window(block, oz, oy, ox, y):
        window = [pad[c, 4 + oy + y, pl.ds(20 * block + 8 + oz, 24), :] for c in range(CHUNKS)]
        here, there = shift_lanes(window, ox), shift_lanes(window, ox + 1)
        for c in range(CHUNKS):
            at[block, c, y, 0:24, :] = here[c]
            by[block, c, y, 0:24, :] = there[c] - here[c]

    def make_windows(blocks, ranges):
        @pl.loop(*blocks)
        def _(block):
            offsets = [off_fine[d, block, s] for d in range(3)]
            for first_y, last_y, unroll in ranges:
                pl.loop(first_y, last_y, unroll=unroll)(functools.partial(make_window, block, *offsets))

    make_windows((1, 3), ((4, 16, 3),))

    broadcast_wait(c_buf, bsem.at[0], bsem.at[1])
    gradient = dot_exact(sum_c[...], c_buf[...].reshape(256, 128))
    near_c = gradient[16:24]
    gradient = gradient[0:16]
    inverse = lax.rsqrt(jnp.sum(gradient * gradient) * (1.0 / 81.0) + EPSILON)

    near = dot3(jnp.concatenate([from_lane(near_c, 16 * d) for d in range(3)], axis=0), mbt[1])
    near = jnp.concatenate([near[8 * d : 8 * d + 8] for d in range(3)], axis=1)
    near = dot(mspread[...], stacked(jnp.concatenate([jnp.zeros((16, 768), F32), near], axis=0), 24))
    exponent = base_m - (STEP_SIZE * inverse) * near[0:120]
    fixed_m = pooled_f[...].reshape(120, 256)
    found = []
    for c in range(2):
        lanes = slice(128 * c, 128 * c + 128)
        corner = [[a_z[z][c][24 * y : 24 * y + 120] for y in (0, 1)] for z in (0, 1)]
        step = [[b_z[z][c][24 * y : 24 * y + 120] for y in (0, 1)] for z in (0, 1)]
        fractions = [fraction(exponent[:, 256 * d + 128 * c : 256 * d + 128 * c + 128]) for d in range(3)]
        found.append(weights(fixed_m[:, lanes], corner, step, fractions))
    total = jnp.concatenate([found[c][d] for d in range(3) for c in range(2)], axis=1)
    total = dot_wide(jnp.concatenate([total, jnp.zeros((8, 768), F32)], axis=0), mbx[...])
    m_part[...] = dot_gather(mgather[...], total)

    def part_copies(act):
        for other in range(SECS):

            @pl.when(s != other)
            def _():
                slot = other if act == "wait_recv" else s
                getattr(remote(m_part, m_parts.at[slot], tsend.at[other], trecv.at[slot], (k, other)), act)()

    part_copies("start")
    m_parts[s] = m_part[...]
    part_copies("wait_recv")
    m_tile[...] = (m_parts[0] + m_parts[1]) + (m_parts[2] + m_parts[3])
    broadcast_start(k, s, m_tile, m_buf, bsem.at[2], bsem.at[3])
    m_buf[k] = m_tile[...]

    gradient = gradient * inverse
    next_c = [
        from_lane(rows_c[8:16], 16 * d) - (STEP_SIZE * inverse) * from_lane(near_c, 16 * d) for d in range(3)
    ]
    turn_r = lax.broadcasted_iota(jnp.int32, (48, 128), 0)
    turn = jnp.where(turn_r == lax.broadcasted_iota(jnp.int32, (48, 128), 1) + 2, 1.0, 0.0)
    turned = dot_rows(gradient, turn[0:16])
    for d in range(3):
        for a in range(3):
            coarse_out[d, a] = turned[16 * d + a : 16 * d + a + 1, 0:9]
    for c in range(CHUNKS):
        pad[c, :, 0:8, :] = jnp.zeros((28, 8, 128), F32)
        pad[c, :, 88:96, :] = jnp.zeros((28, 8, 128), F32)
        fx[c, :, 80:88, :] = jnp.zeros((NY, 8, 128), F32)
        for block in range(4):
            at[block, c, :, 24:32, :] = jnp.zeros((21, 8, 128), F32)
            by[block, c, :, 24:32, :] = jnp.zeros((21, 8, 128), F32)

    for copy in (lat_to_next, lat_to_prev, z_to_next, z_to_prev):
        copy.wait_recv()

    @pl.when(s > 0)
    def _():
        for copy in (to_bef, *corner_up):
            copy.wait_recv()

    @pl.when(s < SECS - 1)
    def _():
        for copy in (to_aft, *corner_down):
            copy.wait_recv()

    for c in range(CHUNKS):
        lanes = slice(128 * c, 128 * c + 128)
        pad[c, 0:4, 8:88, :] = y_bef[:, :, lanes]
        pad[c, 24:28, 8:88, :] = y_aft[:, :, lanes]

    @pl.loop(0, NY // 2, unroll=2)
    def _(pair):
        for half in range(2):
            rows = slice(4 * half, 4 * half + 4)
            for c in range(CHUNKS):
                pad[c, 2 * pair + half + 4, 4:8, :] = z_bef[c, pair, rows, :] * has_prev
                pad[c, 2 * pair + half + 4, 88:92, :] = z_aft[c, pair, rows, :] * has_next

    for y in range(4):
        rows = slice(4 * (y % 2), 4 * (y % 2) + 4)
        for c in range(CHUNKS):
            for n in range(2):
                where = slice(4, 8) if n == 0 else slice(88, 92)
                keep = has_prev if n == 0 else has_next
                pad[c, y, where, :] = corners[n, c, y // 2, rows, :] * keep
                pad[c, 24 + y, where, :] = corners[2 + n, c, y // 2, rows, :] * keep

    make_windows((1, 3), ((0, 4, 2), (16, 21, 5)))
    make_windows((0, 1), ((0, 21, 3),))
    make_windows((3, 4), ((0, 21, 3),))

    for d in range(3):
        for b in range(5):
            lf[d, 8 * b : 8 * b + 1, :] = lf_prev[d, b, 3:4, :] * has_prev
            lf[d, 8 * b + 1 : 8 * b + 5, :] = lf_own[d, b, 0:4, :]
            lf[d, 8 * b + 5 : 8 * b + 7, :] = lf_next[d, b, 0:2, :] * has_next
            lf[d, 8 * b + 7 : 8 * b + 8, :] = jnp.zeros((1, 128), F32)
    bt = table("bt")
    own = dot3(lf[...].reshape(120, 128), bt[0])
    mid = [from_lane(rows_m[8:16], 32 * d + 16 * b) for d in range(3) for b in range(2)]
    mid = dot3(jnp.concatenate(mid, axis=0), bt[1])
    coarse = dot3(jnp.concatenate(next_c, axis=0), bt[2])
    base_f = [
        jnp.concatenate(
            [own[40 * d : 40 * d + 40], mid[16 * d : 16 * d + 16], coarse[8 * d : 8 * d + 8]], axis=0
        )
        for d in range(3)
    ]
    base_f = jnp.concatenate(base_f, axis=1)
    spread, gather, bx, sum_m = table("spread"), table("gather"), table("bx"), table("sum_m")

    broadcast_wait(m_buf, bsem.at[2], bsem.at[3])
    gradient = dot_exact(sum_m[...], m_buf[...].reshape(512, 128))
    near = gradient[96:112]
    gradient = gradient[0:96]
    inverse = lax.rsqrt(jnp.sum(gradient * gradient) * (1.0 / 1782.0) + EPSILON)

    near = dot3(jnp.concatenate([from_lane(near, 16 * d) for d in range(3)], axis=0), bt[1])
    near = jnp.concatenate([near[16 * d : 16 * d + 16] for d in range(3)], axis=1)
    near = jnp.concatenate([jnp.zeros((40, 3 * NX), F32), near, jnp.zeros((8, 3 * NX), F32)], axis=0)
    upper, lower = parts(base_f - (STEP_SIZE * inverse) * near)
    columns[0:64, :] = upper
    columns[64:128, :] = upper
    columns[128:192, :] = lower
    columns[192:256, :] = lower
    field_a[...] = dot(spread[0:480, :], columns[...])

    def fine_block(block, split, split_before, field, field_after):
        adjoint[...] = jnp.zeros_like(adjoint)
        after = pl.ds(pl.multiple_of(480 * jnp.minimum(block + 1, 3), 480), 480)

        @pl.loop(0, 5)
        def _(i):
            lanes = pl.ds(pl.multiple_of(384 * i, 384), 384)
            field_after[:, lanes] = dot(spread[after, :], columns[:, lanes])
            lanes = pl.ds(pl.multiple_of(768 * i, 768), 768)
            adjoint[...] += dot(split_before[:, lanes], bx[lanes, :])
            for pair in range(2):
                for c in range(CHUNKS):
                    found = []
                    for h in range(2):
                        y = 4 * i + 2 * pair + h
                        corner = [[at[block, c, y + e, z : z + 24, :] for e in (0, 1)] for z in (0, 1)]
                        step = [[by[block, c, y + e, z : z + 24, :] for e in (0, 1)] for z in (0, 1)]
                        rows = pl.ds(pl.multiple_of(24 * y, 8), 24)
                        fractions = [
                            fraction(field[rows, NX * d + 128 * c : NX * d + 128 * c + 128]) for d in range(3)
                        ]
                        atlas = fx[c, y, pl.ds(20 * block, 24), :]
                        found.append(weights(atlas, corner, step, fractions))
                    rows = pl.ds(pl.multiple_of(96 * i + 48 * pair, 48), 48)
                    for d in range(3):
                        upper, lower = parts(jnp.concatenate([found[0][d], found[1][d]], axis=0))
                        lane = 2 * NX * d + 128 * c
                        split[rows, lane : lane + 128] = upper
                        split[rows, lane + NX : lane + NX + 128] = lower

        before = pl.ds(pl.multiple_of(480 * jnp.maximum(block - 1, 0), 480), 480)
        mixed[before, :] = adjoint[:, 0:128] + adjoint[:, 128:256]

    @pl.loop(0, 2)
    def _(two):
        fine_block(2 * two, split_a, split_b, field_a, field_b)
        fine_block(2 * two + 1, split_b, split_a, field_b, field_a)

    wide = dot(split_b[...], bx[...])
    mixed[1440:1920, :] = wide[:, 0:128] + wide[:, 128:256]
    f_part[...] = dot_gather(gather[...], mixed[...])
    around(k, s, f_part, f_parts, fsend, frecv, "start")
    f_parts[1, s] = f_part[...]

    for b in range(2):
        turned = dot_rows(gradient[48 * b : 48 * b + 48] * inverse, turn)
        for d in range(3):
            for a in range(9):
                mid_out[d, a, b : b + 1, :] = turned[16 * d + a : 16 * d + a + 1, 0:33]
    row = lax.broadcasted_iota(jnp.int32, (40, 128), 0) & 7

    around(k, s, f_part, f_parts, fsend, frecv, "wait_recv")
    before, middle, after = ((f_parts[i, 0] + f_parts[i, 1]) + (f_parts[i, 2] + f_parts[i, 3]) for i in range(3))
    middle = middle + jnp.where((row == 1) | (row == 2), pltpu.roll(before * has_prev, 36, 0), 0.0)
    middle = middle + jnp.where(row == 4, pltpu.roll(after * has_next, 4, 0), 0.0)
    middle = jnp.where((row >= 1) & (row <= 4), middle, 0.0)
    f_tile[...] = jnp.full((8, 128), jnp.sum(middle * middle))
    broadcast_start(k, s, f_tile, f_buf, bsem.at[4], bsem.at[5])
    f_buf[k] = f_tile[...]

    for copy in (lat_to_next, lat_to_prev, z_to_next, z_to_prev, *mid_same):
        copy.wait_send()

    @pl.when(up)
    def _():
        for copy in (to_bef, *corner_up, *mid_up):
            copy.wait_send()

    @pl.when(down)
    def _():
        for copy in (to_aft, *corner_down, *mid_down):
            copy.wait_send()

    around(k, s, piece, pieces, psend, precv, "wait_send")
    around(k, s, f_part, f_parts, fsend, frecv, "wait_send")
    part_copies("wait_send")
    middle = pltpu.roll(middle, 39, 0)
    thirds = [from_lane(middle, 40 * d) for d in range(3)]

    broadcast_wait(f_buf, bsem.at[4], bsem.at[5])
    squares = jnp.sum(f_buf[...], axis=0)[0:1, :]
    inverse = lax.rsqrt(squares * (1.0 / 63360.0) + EPSILON)
    for d in range(3):
        scaled = thirds[d] * inverse
        for b in range(5):
            fine_out[d, b] = scaled[8 * b : 8 * b + 4, 0:33]


def body(
    fixed_image,
    moving_image,
    lattice_fine,
    lattice_mid,
    lattice_coarse,
    offset_fine,
    offset_mid,
    offset_coarse,
):
    t = tables()
    vmem, smem, hbm = (pl.BlockSpec(memory_space=m) for m in (pltpu.VMEM, pltpu.SMEM, pl.ANY))
    shape = lambda *dims: jax.ShapeDtypeStruct(dims, F32)
    buf = lambda *dims: pltpu.VMEM(dims, F32)
    half = lambda *dims: pltpu.VMEM(dims, BF16)
    dma = lambda *dims: pltpu.SemaphoreType.DMA(dims)
    fine, mid, coarse = pl.pallas_call(
        kernel,
        out_shape=[shape(3, 5, 4, 33), shape(3, 9, 2, 33), shape(3, 3, 1, 9)],
        in_specs=[hbm, hbm, vmem, vmem, vmem, smem, smem, smem] + [hbm] * len(TABLES),
        out_specs=[vmem] * 3,
        scratch_shapes=[
            *[pltpu.VMEM(t[n].shape[which is not None :], t[n].dtype) for n, which in TABLES.items()],
            buf(CHUNKS, 28, 96, 128), buf(CHUNKS, NY, 88, 128), buf(5, NZ, NX),
            *[buf(CHUNKS, 10, 8, 128)] * 4, *[buf(4, NZ, NX)] * 2, buf(4, CHUNKS, 2, 8, 128),
            *[buf(3, 5, 8, 128)] * 3, buf(3, 40, 128), buf(128, 128), buf(128, 128),
            *[buf(5, 24, 256)] * 4, buf(2, 3, 5, 8, 256),
            buf(2, 8, 128), buf(3, SECS, 2, 8, 128), buf(14, 32, 128), buf(5, 8, 128), buf(2, 15, 40, 128),
            buf(8, 128), buf(SLABS, 8, 128), buf(16, 128), buf(SECS, 16, 128), buf(16, 128), buf(SLABS, 16, 128),
            *[buf(4, CHUNKS, 21, 32, 128)] * 2, half(256, 3 * NX),
            *[buf(480, 3 * NX)] * 2, *[half(480, 6 * NX)] * 2, buf(480, 256), buf(1920, 128),
            buf(40, 128), buf(3, SECS, 40, 128), buf(8, 128), buf(SLABS, 8, 128),
            dma(10), dma(len(TABLES)), dma(18), dma(18), *[dma(3, SECS)] * 4, dma(SECS), dma(SECS), dma(6),
        ],
        compiler_params=pltpu.CompilerParams(
            collective_id=0, has_side_effects=True, vmem_limit_bytes=VMEM_LIMIT
        ),
        name="mega",
    )(
        jnp.transpose(moving_image, (1, 0, 2)),
        jnp.transpose(fixed_image, (1, 0, 2)),
        jnp.transpose(lattice_fine, (0, 2, 1, 3)),
        jnp.transpose(lattice_mid, (0, 3, 2, 1)),
        jnp.transpose(lattice_coarse, (0, 3, 2, 1)),
        offset_fine,
        jnp.transpose(offset_mid, (1, 2, 0)),
        jnp.transpose(offset_coarse, (0, 2, 1)),
        *(t[n] for n in TABLES),
    )
    results = (fine, mid, coarse)
    fine, mid, coarse = pl.pallas_call(
        finish,
        out_shape=[jax.ShapeDtypeStruct(a.shape, F32) for a in results],
        in_specs=[hbm] * 3,
        out_specs=[hbm] * 3,
        scratch_shapes=[dma(3)],
        name="finish",
    )(*results)
    return (
        jnp.transpose(fine, (0, 2, 1, 3)),
        jnp.transpose(mid, (0, 3, 2, 1)),
        jnp.transpose(coarse, (0, 3, 2, 1)),
    )


def solution(mesh):
    placed = (
        P("slab", "sec", None),
        P("slab", "sec", None),
        P(None, "slab", None, None),
        P(),
        P(),
        P(None, "slab", None),
        P(None, "slab", None),
        P(),
    )
    return jax.shard_map(
        body,
        mesh=mesh,
        in_specs=placed,
        out_specs=(P(None, "slab", None, None), P(), P()),
        check_vma=False,
    )
```

```python
import functools

import jax
import jax.numpy as jnp
import ml_dtypes
import numpy as np
from jax import lax
from jax.experimental import pallas as pl
from jax.experimental.pallas import tpu as pltpu
from jax.sharding import PartitionSpec as P

SP = 20
EPSILON = 1e-06
STEP_SIZE = 0.5
HIGHEST = lax.Precision.HIGHEST
F32 = jnp.float32
BF16 = jnp.bfloat16
MESH = pl.DeviceIdType.MESH
SLABS = 32
SECS = 4
NZ, NY, NX = 80, 20, 640
CHUNKS = NX // 128
LOG2E = 1.4426950408889634
VMEM_LIMIT = 58 * 1024 * 1024


def basis(rows, knots, factor, coarse):
    rows, knots = np.asarray(rows, np.float64), np.asarray(knots, np.float64)
    position = factor * rows + 0.5 * (factor - 1)
    centre = SP * coarse * knots + 0.5 * (coarse - 1)
    distance = np.abs((position[:, None] - centre[None, :]) / (SP * coarse))
    near = 2.0 / 3.0 - distance**2 + 0.5 * distance**3
    far = np.maximum(2.0 - distance, 0.0) ** 3 / 6.0
    return np.where(distance < 1.0, near, far)


def two_parts(values):
    high = values.astype(ml_dtypes.bfloat16)
    low = (values - high.astype(np.float64)).astype(ml_dtypes.bfloat16)
    return high, low


def right_parts(values):
    high, low = two_parts(values)
    return np.concatenate([high, low, high], axis=-2)


def wide_parts(values):
    high, low = two_parts(values)
    zero = np.zeros_like(high)
    return np.concatenate([np.concatenate([high, low], 1), np.concatenate([high, zero], 1)], 0)


def one_hot(condition):
    return condition.astype(ml_dtypes.bfloat16)


@functools.cache
def tables():
    t = {}
    rz, ry = np.zeros((4, 4, 24, 64)), np.zeros((4, NY, 64))
    z, y, x = np.arange(NZ), np.arange(NY), np.arange(NX)
    for r in range(4):
        for block in range(4):
            rows = z[20 * block : 20 * block + 20]
            for a in range(7):
                rz[r, block, :20, a:40:8] = basis(rows, [a - 1], 1, 1)
            for a in range(5):
                rz[r, block, :20, 40 + a : 56 : 8] = basis(rows, [a - 2], 1, 4)
                rz[r, block, :20, 56 + a : 57 + a] = basis(rows + 80 * r, [a - 2], 1, 16)
    for s in range(4):
        for a in range(7):
            ry[s, :, a:40:8] = basis(y + 20 * s, range(5), 1, 1)
        for a in range(5):
            ry[s, :, 40 + a : 56 : 8] = basis(y + 20 * s, range(2), 1, 4)
            ry[s, :, 56 + a : 57 + a] = basis(y + 20 * s, [0], 1, 16)
    whole = rz[:, None, :, None] * ry[None, :, None, :, None, :]
    high, low = two_parts(whole.reshape(16, 1920, 64))
    t["spread"] = np.concatenate([high, low, high, low], axis=2)
    t["gather"] = np.concatenate([high[:4, :, :40], low[:4, :, :40]], axis=2).transpose(0, 2, 1)
    across = np.zeros((3, 128, NX))
    across[0, :33] = basis(x, range(33), 1, 1).T
    across[1, :9] = basis(x, range(9), 1, 4).T
    across[2, :3] = basis(x, range(3), 1, 16).T
    t["bt"] = right_parts(-LOG2E * across)
    along = np.zeros((3, NX, 128))
    for d in range(3):
        along[d, :, 40 * d : 40 * d + 33] = basis(x, range(33), 1, 1)
    t["bx"] = np.concatenate([wide_parts(along[d]) for d in range(3)], axis=0)
    rz, ry = np.zeros((4, 24, 32)), np.zeros((4, 5, 32))
    z, y, x = np.arange(20), np.arange(5), np.arange(160)
    for r in range(4):
        for a in range(4):
            rz[r, :20, a:16:8] = basis(z, [a - 1], 4, 4)
        for a in range(5):
            rz[r, :20, 16 + a : 17 + a] = basis(z + 20 * r, [a - 2], 4, 16)
    for s in range(4):
        for a in range(4):
            ry[s, :, a:16:8] = basis(y + 5 * s, range(2), 4, 4)
        for a in range(5):
            ry[s, :, 16 + a : 17 + a] = basis(y + 5 * s, [0], 4, 16)
    whole = np.zeros((16, 128, 32))
    whole[:, :120] = (rz[:, None, None] * ry[None, :, :, None]).reshape(16, 120, 32)
    high, low = two_parts(whole)
    t["mspread"] = np.concatenate([high, high, low, np.zeros_like(low)], axis=2)
    t["mgather"] = np.concatenate([high[:, :, :16], low[:, :, :16]], axis=2).transpose(0, 2, 1)
    across = np.zeros((2, 128, 256))
    across[0, :9, :160] = basis(x, range(9), 4, 4).T
    across[1, :3, :160] = basis(x, range(3), 4, 16).T
    t["mbt"] = right_parts(-LOG2E * across)
    along = np.zeros((3, 256, 128))
    for d in range(3):
        along[d, :160, 16 * d : 16 * d + 9] = basis(x, range(9), 4, 4)
    t["mbx"] = wide_parts(along.reshape(768, 128))
    rz = np.zeros((4, 8, 32))
    z, y, x = np.arange(5), np.arange(5), np.arange(40)
    for r in range(4):
        for a in range(4):
            rz[r, :5, a : a + 1] = basis(z + 5 * r, [a - 1], 16, 16)
    whole = np.zeros((4, 128, 32))
    whole[:, :40] = (rz[:, None] * basis(y, [0], 16, 16)[None, :, None]).reshape(4, 40, 32)
    high, low = two_parts(whole)
    t["cspread"] = np.concatenate([high, high, low, np.zeros_like(low)], axis=2)
    t["cgather"] = np.concatenate([high[:, :, :16], low[:, :, :16]], axis=2).transpose(0, 2, 1)
    across = np.zeros((128, 128))
    across[:3, :40] = basis(x, range(3), 16, 16).T
    t["cbt"] = right_parts(-LOG2E * across)
    along = np.zeros((3, 128, 128))
    for d in range(3):
        along[d, :40, 16 * d : 16 * d + 3] = basis(x, range(3), 16, 16)
    t["cbx"] = wide_parts(along.reshape(384, 128))
    row, column = np.arange(NX)[:, None], np.arange(256)[None, :]
    t["px"] = one_hot(row // 4 == column)
    row, column = np.arange(120)[:, None], np.arange(400)[None, :]
    t["pz"] = one_hot((row // 24 == column // 80) & (row % 24 == column % 80 // 4))
    row, column = np.arange(512)[:, None], np.arange(128)[None, :]
    t["pcx"] = one_hot((row % 256 < 160) & (row // 256 * 64 + row % 256 // 4 == column))
    row, column = np.arange(16)[:, None], np.arange(48)[None, :]
    t["pcz"] = one_hot((row // 8 == column // 24) & (column % 24 < 20) & (row % 8 == column % 24 // 4))
    row, column, place = np.arange(16)[:, None], np.arange(128)[None, :], np.arange(32)[:, None, None]
    knot = place - 1 - row // 8 + row % 8
    t["rows_m"] = one_hot((knot == column) & (column < 33))
    t["rows_c"] = one_hot((knot == column) & (column < 9))[:8]
    row, column, place = np.arange(24)[:, None], np.arange(256)[None, :], np.arange(8)[:, None, None]
    knot = np.where(row < 16, row - 2, row - 16 + place - 2)
    found = (knot == column // 32 - 1 + column % 8) & (column % 8 < 4) & (knot >= 0) & (knot < 9)
    t["sum_c"] = one_hot(found)
    row, column, place = np.arange(112)[:, None], np.arange(512)[None, :], np.arange(32)[:, None, None]
    knot = np.where(row < 96, row % 48 - 2, row % 8 + place - 2)
    b = np.where(row < 96, row // 48, (row - 96) // 8)
    found = (knot == column // 16 - 1 + column % 8) & (column % 8 < 4) & (column // 8 % 2 == b)
    t["sum_m"] = one_hot(found & (knot >= 0) & (knot < 33))
    return t


def dot(a, b):
    return jnp.dot(a, b, preferred_element_type=F32)


def dot_rows(a, b):
    return lax.dot_general(
        a, b, (((0,), (0,)), ((), ())), precision=HIGHEST, preferred_element_type=F32
    )


def parts(values):
    high = values.astype(BF16)
    return high, (values - high.astype(F32)).astype(BF16)


def dot3(a, right):
    high, low = parts(a)
    return dot(jnp.concatenate([high, high, low], axis=1), right)


def dot_wide(a, table):
    wide = dot(jnp.concatenate(parts(a), axis=1), table)
    return wide[:, 0:128] + wide[:, 128:256]


def dot_exact(table, b):
    wide = dot(table, jnp.concatenate(parts(b), axis=1))
    return wide[:, 0:128] + wide[:, 128:256]


def dot_gather(table, b):
    n = table.shape[0] // 2
    wide = dot(table, jnp.concatenate(parts(b), axis=1))
    return (wide[0:n, 0:128] + wide[0:n, 128:256]) + wide[n:, 0:128]


def stacked(column, n):
    high, low = parts(jnp.concatenate([column, jnp.zeros((32 - n, column.shape[1]), F32)], axis=0))
    return jnp.concatenate([high, low, high, jnp.zeros_like(low)], axis=0)


def from_lane(values, lane):
    return values if lane == 0 else pltpu.roll(values, 128 - lane, 1)


def shift_lanes(chunks, shift):
    amount = (128 - shift) & 127
    rolled = [pltpu.roll(chunk, amount, 1) for chunk in chunks]
    lane = lax.broadcasted_iota(jnp.int32, chunks[0].shape, 1)
    first = lane < jnp.maximum(-shift, 0)
    last = lane >= 128 - jnp.maximum(shift, 0)
    zero = jnp.zeros_like(chunks[0])
    padded = [zero, *rolled, zero]
    return [
        jnp.where(first, padded[j], jnp.where(last, padded[j + 2], padded[j + 1]))
        for j in range(len(chunks))
    ]


def fraction(exponent):
    grown = jnp.exp2(exponent)
    frac = pl.reciprocal(1.0 + grown, approx=True)
    return frac, frac * (grown * frac)


def weights(fixed, corner, step, fractions):
    (fz, gz), (fy, gy), (fx, gx) = fractions
    line = [[corner[z][y] + fx * step[z][y] for y in (0, 1)] for z in (0, 1)]
    rise = [line[z][1] - line[z][0] for z in (0, 1)]
    plane = [line[z][0] + fy * rise[z] for z in (0, 1)]
    slope_z = plane[1] - plane[0]
    residual = (plane[0] + fz * slope_z) - fixed
    slope_y = rise[0] + fz * (rise[1] - rise[0])
    along = [step[z][0] + fy * (step[z][1] - step[z][0]) for z in (0, 1)]
    slope_x = along[0] + fz * (along[1] - along[0])
    return [
        (residual * slope_z) * gz,
        (residual * slope_y) * gy,
        (residual * slope_x) * gx,
    ]


def greet(k, s):
    barrier = pltpu.get_barrier_semaphore()

    def signal(slab, sec):
        pl.semaphore_signal(barrier, inc=1, device_id=(slab, sec), device_id_type=MESH)

    @pl.loop(1, SLABS)
    def _(i):
        signal((k + i) & (SLABS - 1), s)

    for i in range(1, SECS):
        other = (s + i) & (SECS - 1)
        signal(k, other)
        signal((k + 1) & (SLABS - 1), other)
        signal((k + SLABS - 1) & (SLABS - 1), other)
    return lambda: pl.semaphore_wait(barrier, SLABS - 1 + 3 * (SECS - 1))


def broadcast_start(k, s, tile, buffer, send_sem, recv_sem):
    @pl.loop(0, SLABS - 1)
    def _(i):
        pltpu.make_async_remote_copy(
            src_ref=tile,
            dst_ref=buffer.at[k],
            send_sem=send_sem,
            recv_sem=recv_sem,
            device_id=((k + 16 + i + (i > 15).astype(jnp.int32)) & (SLABS - 1), s),
            device_id_type=MESH,
        ).start()


def broadcast_wait(buffer, send_sem, recv_sem):
    part = buffer.at[pl.ds(0, SLABS - 1)]
    pltpu.make_async_copy(part, part, recv_sem).wait()
    pltpu.make_async_copy(part, part, send_sem).wait()


def remote(src, dst, send_sem, recv_sem, device):
    return pltpu.make_async_remote_copy(
        src_ref=src,
        dst_ref=dst,
        send_sem=send_sem,
        recv_sem=recv_sem,
        device_id=device,
        device_id_type=MESH,
    )


def around(k, s, source, buffer, send, recv, act):
    slabs = ((k + SLABS - 1) & (SLABS - 1), k, (k + 1) & (SLABS - 1))

    def one(dk, other):
        if act == "wait_recv":
            copy = remote(source, buffer.at[dk, other], send.at[dk, other], recv.at[dk, other], (k, other))
        else:
            copy = remote(
                source, buffer.at[2 - dk, s], send.at[dk, other], recv.at[2 - dk, s], (slabs[dk], other)
            )
        getattr(copy, act)()

    for dk in (0, 2):
        for other in range(SECS):
            one(dk, other)
    for i in range(1, SECS):
        one(1, (s + i) & (SECS - 1))


TABLES = {
    "px": None, "pz": None, "pcx": None, "pcz": None,
    "rows_m": "k", "rows_c": "q", "cspread": "r", "cgather": "r", "cbt": None, "cbx": None,
    "sum_c": "q", "mspread": "rs", "mgather": "rs", "mbt": None, "mbx": None,
    "spread": "rs", "gather": "s", "bt": None, "bx": None, "sum_m": "k",
}


def finish(*refs):
    copies = [pltpu.make_async_copy(refs[i], refs[i + 3], refs[6].at[i]) for i in range(3)]
    for copy in copies:
        copy.start()
    for copy in copies:
        copy.wait()


def kernel(
    moving, fixed, lat_fine, lat_mid, lat_coarse, off_fine, off_mid, off_coarse, *refs
):
    n = len(TABLES)
    stored, refs = refs[:n], refs[n:]
    fine_out, mid_out, coarse_out, *refs = refs
    t = dict(zip(TABLES, refs[:n]))
    (
        pad, fx, sums, zlo, zhi, z_bef, z_aft, y_bef, y_aft, corners,
        lf_own, lf_prev, lf_next, lf, mt, ct,
        pooled_m, pooled_f, pm_bef, pm_aft, pm_halo,
        piece, pieces, cv, cf, mm,
        c_tile, c_buf, m_part, m_parts, m_tile, m_buf,
        at, by, columns, field_a, field_b, split_a, split_b, adjoint, mixed,
        f_part, f_parts, f_tile, f_buf,
        load_sem, table_sem, send, recv, psend, precv, fsend, frecv, tsend, trecv, bsem,
    ) = refs[n:]
    k, s = lax.axis_index("slab"), lax.axis_index("sec")
    nxt, prv = (k + 1) & (SLABS - 1), (k + SLABS - 1) & (SLABS - 1)
    q, r = k >> 2, k & 3
    has_prev, has_next = (k > 0).astype(F32), (k < SLABS - 1).astype(F32)
    up, down = s < SECS - 1, s > 0
    own_y, own_z = pl.ds(4, NY), pl.ds(8, NZ)

    load_moving = [
        pltpu.make_async_copy(
            moving.at[:, :, pl.ds(128 * c, 128)], pad.at[c, own_y, own_z], load_sem.at[c]
        )
        for c in range(CHUNKS)
    ]
    load_fixed = [
        pltpu.make_async_copy(
            fixed.at[:, :, pl.ds(128 * c, 128)], fx.at[c, :, pl.ds(0, NZ)], load_sem.at[CHUNKS + c]
        )
        for c in range(CHUNKS)
    ]
    place = {"k": k, "q": q, "r": r, "s": s, "rs": 4 * r + s}
    load_table = {}
    for i, (name, which) in enumerate(TABLES.items()):
        source = stored[i] if which is None else stored[i].at[place[which]]
        load_table[name] = pltpu.make_async_copy(source, t[name], table_sem.at[i])
    for copy in load_moving:
        copy.start()
    all_here = greet(k, s)
    for copy in (*load_fixed, *load_table.values()):
        copy.start()

    def table(name):
        load_table[name].wait()
        return t[name]

    lat_to_next = remote(lf_own, lf_prev, send.at[0], recv.at[0], (nxt, s))
    lat_to_prev = remote(lf_own, lf_next, send.at[1], recv.at[1], (prv, s))
    z_to_next = remote(zhi, z_bef, send.at[2], recv.at[2], (nxt, s))
    z_to_prev = remote(zlo, z_aft, send.at[3], recv.at[3], (prv, s))
    to_bef = remote(moving.at[pl.ds(16, 4)], y_bef, send.at[4], recv.at[4], (k, s + 1))
    to_aft = remote(moving.at[pl.ds(0, 4)], y_aft, send.at[5], recv.at[5], (k, s - 1))
    first, last = pl.ds(0, 2), pl.ds(8, 2)
    corner_up = [
        remote(zhi.at[:, last], corners.at[0], send.at[6], recv.at[6], (nxt, s + 1)),
        remote(zlo.at[:, last], corners.at[1], send.at[7], recv.at[7], (prv, s + 1)),
    ]
    corner_down = [
        remote(zhi.at[:, first], corners.at[2], send.at[8], recv.at[8], (nxt, s - 1)),
        remote(zlo.at[:, first], corners.at[3], send.at[9], recv.at[9], (prv, s - 1)),
    ]
    head, tail = pl.ds(0, 8), pl.ds(16, 8)
    mid_same = [
        remote(pooled_m.at[:, tail], pm_halo.at[0, 1], send.at[10], recv.at[10], (nxt, s)),
        remote(pooled_m.at[:, head], pm_halo.at[1, 1], send.at[11], recv.at[11], (prv, s)),
    ]
    mid_up = [
        remote(pooled_m, pm_bef, send.at[12], recv.at[12], (k, s + 1)),
        remote(pooled_m.at[:, tail], pm_halo.at[0, 0], send.at[13], recv.at[13], (nxt, s + 1)),
        remote(pooled_m.at[:, head], pm_halo.at[1, 0], send.at[14], recv.at[14], (prv, s + 1)),
    ]
    mid_down = [
        remote(pooled_m, pm_aft, send.at[15], recv.at[15], (k, s - 1)),
        remote(pooled_m.at[:, tail], pm_halo.at[0, 2], send.at[16], recv.at[16], (nxt, s - 1)),
        remote(pooled_m.at[:, head], pm_halo.at[1, 2], send.at[17], recv.at[17], (prv, s - 1)),
    ]

    def start(*copies):
        for copy in copies:
            copy.start()

    def start_if(condition, *copies):
        @pl.when(condition)
        def _():
            start(*copies)

    all_here()
    start_if(up, to_bef)
    start_if(down, to_aft)
    for c in range(CHUNKS):
        load_moving[c].wait()

        @pl.loop(0, NY // 2, unroll=5)
        def _(pair):
            for half in range(2):
                rows = slice(4 * half, 4 * half + 4)
                zlo[c, pair, rows, :] = pad[c, 2 * pair + half + 4, 8:12, :]
                zhi[c, pair, rows, :] = pad[c, 2 * pair + half + 4, 84:88, :]

    start(z_to_next, z_to_prev)
    start_if(up, *corner_up)
    start_if(down, *corner_down)

    px, pz = table("px"), table("pz")

    def pooled():
        high, low = parts(sums[...].reshape(400, NX))
        high, low = parts(dot(high, px[...]) + dot(low, px[...]))
        return ((dot(pz[...], high) + dot(pz[...], low)) * (1.0 / 64.0)).reshape(5, 24, 256)

    for c in range(CHUNKS):
        lanes = slice(128 * c, 128 * c + 128)

        @pl.loop(0, 5, unroll=5)
        def _(group):
            four = [pad[c, 4 * group + 4 + i, 8:88, :] for i in range(4)]
            sums[group, :, lanes] = (four[0] + four[1]) + (four[2] + four[3])

    pooled_m[...] = pooled()

    for c in range(CHUNKS):
        load_fixed[c].wait()
        lanes = slice(128 * c, 128 * c + 128)

        @pl.loop(0, 5, unroll=5)
        def _(group):
            four = [fx[c, 4 * group + i, 0:80, :] for i in range(4)]
            sums[group, :, lanes] = (four[0] + four[1]) + (four[2] + four[3])

    pooled_f[...] = pooled()

    halves = []
    for ref in (pooled_m, pooled_f):
        upper, lower = jnp.zeros((24, 256), F32), jnp.zeros((24, 256), F32)
        for i in range(5):
            keep = (i + s < 4).astype(F32)
            upper = upper + ref[i] * keep
            lower = lower + ref[i] * (1.0 - keep)
        halves.append(jnp.concatenate([upper, lower], axis=0))
    high, low = parts(jnp.concatenate(halves, axis=1))
    pcx, pcz = table("pcx")[...], table("pcz")[...]
    both = dot(high, pcx) + dot(low, pcx)
    piece[...] = (dot_exact(pcz, both) * (1.0 / 64.0)).reshape(2, 8, 128)
    around(k, s, piece, pieces, psend, precv, "start")
    pieces[1, s] = piece[...]
    start(*mid_same)
    start_if(up, *mid_up)
    start_if(down, *mid_down)

    for ref in (lf_own, mt, ct, cv, mm):
        ref[...] = jnp.zeros_like(ref)
    for d in range(3):
        for b in range(5):
            lf_own[d, b, 0:4, 0:33] = lat_fine[d, b]
        for a in range(9):
            for b in range(2):
                row = 32 * d + 16 * b + a
                mt[row : row + 1, 0:33] = lat_mid[d, a, b : b + 1]
        for a in range(3):
            ct[16 * d + a : 16 * d + a + 1, 0:9] = lat_coarse[d, a]
    start(lat_to_next, lat_to_prev)

    def pick_rows(name, ref):
        rows = table(name)[...]
        contract = (((1,), (1,)), ((), ()))
        high, low = parts(ref[...])
        return lax.dot_general(rows, high, contract, preferred_element_type=F32) + lax.dot_general(
            rows, low, contract, preferred_element_type=F32
        )

    rows_m, rows_c = pick_rows("rows_m", mt), pick_rows("rows_c", ct)
    cbt, cspread = table("cbt")[...], table("cspread")[...]
    column = dot3(jnp.concatenate([from_lane(rows_c[0:8], 16 * d) for d in range(3)], axis=0), cbt)
    column = jnp.concatenate([column[8 * d : 8 * d + 8] for d in range(3)], axis=1)
    exponent = dot(cspread, stacked(column, 8))[0:40]
    fractions_c = [fraction(exponent[:, 128 * d : 128 * d + 128]) for d in range(3)]
    cbx, cgather = table("cbx"), table("cgather")

    around(k, s, piece, pieces, psend, precv, "wait_recv")

    lane = lax.broadcasted_iota(jnp.int32, (5, 128), 1)
    for dk in range(3):
        scale = (has_prev, jnp.float32(1.0), has_next)[dk]
        rows = (slice(3, 8), slice(8, 13), slice(13, 18))[dk]
        for c in range(5):
            value = jnp.zeros((8, 128), F32)
            if c < 4:
                value = value + pieces[dk, c, 0]
            if c > 0:
                value = value + pieces[dk, c - 1, 1]
            cv[4 + c, rows, :] = jnp.where(lane < 40, value[0:5], 0.0) * scale
            if dk == 1:
                cf[c] = value
    fixed_c = pltpu.roll(cf[...].reshape(40, 128), 64, 1)

    oz, oy, ox = off_coarse[0, 0, q], off_coarse[1, 0, q], off_coarse[2, 0, q]
    a_z, b_z = [], []
    for e in (0, 1):
        window = cv[pl.ds(4 + oy, 6), pl.ds(8 + oz + e, 8), :].reshape(48, 128)
        here, there = shift_lanes([window], ox)[0], shift_lanes([window], ox + 1)[0]
        a_z.append(here)
        b_z.append(there - here)
    corner = [[a_z[z][8 * y : 8 * y + 40] for y in (0, 1)] for z in (0, 1)]
    step = [[b_z[z][8 * y : 8 * y + 40] for y in (0, 1)] for z in (0, 1)]
    total = jnp.concatenate(weights(fixed_c, corner, step, fractions_c), axis=1)
    total = dot_wide(jnp.concatenate([total, jnp.zeros((8, 384), F32)], axis=0), cbx[...])
    total = jnp.concatenate([total, jnp.zeros((80, 128), F32)], axis=0)
    c_tile[...] = dot_gather(cgather[...], total)[0:8]
    broadcast_start(k, s, c_tile, c_buf, bsem.at[0], bsem.at[1])
    c_buf[k] = c_tile[...]

    @pl.when(s == 0)
    def _():
        y_bef[...] = jnp.zeros_like(y_bef)
        corners[0:2] = jnp.zeros((2, CHUNKS, 2, 8, 128), F32)
        pm_bef[...] = jnp.zeros_like(pm_bef)
        pm_halo[:, 0] = jnp.zeros((2, 5, 8, 256), F32)

    @pl.when(s == SECS - 1)
    def _():
        y_aft[...] = jnp.zeros_like(y_aft)
        corners[2:4] = jnp.zeros((2, CHUNKS, 2, 8, 128), F32)
        pm_aft[...] = jnp.zeros_like(pm_aft)
        pm_halo[:, 2] = jnp.zeros((2, 5, 8, 256), F32)

    for copy in mid_same:
        copy.wait_recv()

    @pl.when(s > 0)
    def _():
        for copy in mid_up:
            copy.wait_recv()

    @pl.when(s < SECS - 1)
    def _():
        for copy in mid_down:
            copy.wait_recv()

    for c in range(2):
        lanes = slice(128 * c, 128 * c + 128)
        for e, whole in enumerate((pm_bef, pooled_m, pm_aft)):
            for y in range(5):
                mm[c, 5 * e + y, 4:8, :] = pm_halo[0, e, y, 0:4, lanes] * has_prev
                mm[c, 5 * e + y, 8:28, :] = whole[y, 0:20, lanes]
                mm[c, 5 * e + y, 28:32, :] = pm_halo[1, e, y, 0:4, lanes] * has_next

    oz, oy, ox = off_mid[0, 0, 0], off_mid[0, 0, 1], off_mid[0, 0, 2]
    a_z, b_z = [], []
    for e in (0, 1):
        window = [mm[c, pl.ds(5 + oy, 6), pl.ds(8 + oz + e, 24), :].reshape(144, 128) for c in range(2)]
        here, there = shift_lanes(window, ox), shift_lanes(window, ox + 1)
        a_z.append(here)
        b_z.append([there[c] - here[c] for c in range(2)])

    mbt, mspread, mbx, mgather = table("mbt"), table("mspread"), table("mbx"), table("mgather")
    own = [from_lane(rows_m[0:8], 32 * d + 16 * b) for d in range(3) for b in range(2)]
    own = dot3(jnp.concatenate(own, axis=0), mbt[0])
    coarse = dot3(jnp.concatenate([from_lane(rows_c[8:16], 16 * d) for d in range(3)], axis=0), mbt[1])
    column = [
        jnp.concatenate([own[16 * d : 16 * d + 16], coarse[8 * d : 8 * d + 8]], axis=0) for d in range(3)
    ]
    base_m = dot(mspread[...], stacked(jnp.concatenate(column, axis=1), 24))[0:120]
    sum_c = table("sum_c")

    def make_window(block, oz, oy, ox, y):
        window = [pad[c, 4 + oy + y, pl.ds(20 * block + 8 + oz, 24), :] for c in range(CHUNKS)]
        here, there = shift_lanes(window, ox), shift_lanes(window, ox + 1)
        for c in range(CHUNKS):
            at[block, c, y, 0:24, :] = here[c]
            by[block, c, y, 0:24, :] = there[c] - here[c]

    def make_windows(blocks, ranges):
        @pl.loop(*blocks)
        def _(block):
            offsets = [off_fine[d, block, s] for d in range(3)]
            for first_y, last_y, unroll in ranges:
                pl.loop(first_y, last_y, unroll=unroll)(functools.partial(make_window, block, *offsets))

    make_windows((1, 3), ((4, 16, 3),))

    broadcast_wait(c_buf, bsem.at[0], bsem.at[1])
    gradient = dot_exact(sum_c[...], c_buf[...].reshape(256, 128))
    near_c = gradient[16:24]
    gradient = gradient[0:16]
    inverse = lax.rsqrt(jnp.sum(gradient * gradient) * (1.0 / 81.0) + EPSILON)

    near = dot3(jnp.concatenate([from_lane(near_c, 16 * d) for d in range(3)], axis=0), mbt[1])
    near = jnp.concatenate([near[8 * d : 8 * d + 8] for d in range(3)], axis=1)
    near = dot(mspread[...], stacked(jnp.concatenate([jnp.zeros((16, 768), F32), near], axis=0), 24))
    exponent = base_m - (STEP_SIZE * inverse) * near[0:120]
    fixed_m = pooled_f[...].reshape(120, 256)
    found = []
    for c in range(2):
        lanes = slice(128 * c, 128 * c + 128)
        corner = [[a_z[z][c][24 * y : 24 * y + 120] for y in (0, 1)] for z in (0, 1)]
        step = [[b_z[z][c][24 * y : 24 * y + 120] for y in (0, 1)] for z in (0, 1)]
        fractions = [fraction(exponent[:, 256 * d + 128 * c : 256 * d + 128 * c + 128]) for d in range(3)]
        found.append(weights(fixed_m[:, lanes], corner, step, fractions))
    total = jnp.concatenate([found[c][d] for d in range(3) for c in range(2)], axis=1)
    total = dot_wide(jnp.concatenate([total, jnp.zeros((8, 768), F32)], axis=0), mbx[...])
    m_part[...] = dot_gather(mgather[...], total)

    def part_copies(act):
        for i in range(1, SECS):
            other = (s + i) & (SECS - 1)
            slot = other if act == "wait_recv" else s
            getattr(remote(m_part, m_parts.at[slot], tsend.at[other], trecv.at[slot], (k, other)), act)()

    part_copies("start")
    m_parts[s] = m_part[...]
    part_copies("wait_recv")
    m_tile[...] = (m_parts[0] + m_parts[1]) + (m_parts[2] + m_parts[3])
    broadcast_start(k, s, m_tile, m_buf, bsem.at[2], bsem.at[3])
    m_buf[k] = m_tile[...]

    gradient = gradient * inverse
    next_c = [
        from_lane(rows_c[8:16], 16 * d) - (STEP_SIZE * inverse) * from_lane(near_c, 16 * d) for d in range(3)
    ]
    turn_r = lax.broadcasted_iota(jnp.int32, (48, 128), 0)
    turn = jnp.where(turn_r == lax.broadcasted_iota(jnp.int32, (48, 128), 1) + 2, 1.0, 0.0)
    turned = dot_rows(gradient, turn[0:16])
    for d in range(3):
        for a in range(3):
            coarse_out[d, a] = turned[16 * d + a : 16 * d + a + 1, 0:9]
    for c in range(CHUNKS):
        pad[c, :, 0:8, :] = jnp.zeros((28, 8, 128), F32)
        pad[c, :, 88:96, :] = jnp.zeros((28, 8, 128), F32)
        fx[c, :, 80:88, :] = jnp.zeros((NY, 8, 128), F32)
        for block in range(4):
            at[block, c, :, 24:32, :] = jnp.zeros((21, 8, 128), F32)
            by[block, c, :, 24:32, :] = jnp.zeros((21, 8, 128), F32)

    for copy in (lat_to_next, lat_to_prev, z_to_next, z_to_prev):
        copy.wait_recv()

    @pl.when(s > 0)
    def _():
        for copy in (to_bef, *corner_up):
            copy.wait_recv()

    @pl.when(s < SECS - 1)
    def _():
        for copy in (to_aft, *corner_down):
            copy.wait_recv()

    for c in range(CHUNKS):
        lanes = slice(128 * c, 128 * c + 128)
        pad[c, 0:4, 8:88, :] = y_bef[:, :, lanes]
        pad[c, 24:28, 8:88, :] = y_aft[:, :, lanes]

    @pl.loop(0, NY // 2, unroll=2)
    def _(pair):
        for half in range(2):
            rows = slice(4 * half, 4 * half + 4)
            for c in range(CHUNKS):
                pad[c, 2 * pair + half + 4, 4:8, :] = z_bef[c, pair, rows, :] * has_prev
                pad[c, 2 * pair + half + 4, 88:92, :] = z_aft[c, pair, rows, :] * has_next

    for y in range(4):
        rows = slice(4 * (y % 2), 4 * (y % 2) + 4)
        for c in range(CHUNKS):
            for n in range(2):
                where = slice(4, 8) if n == 0 else slice(88, 92)
                keep = has_prev if n == 0 else has_next
                pad[c, y, where, :] = corners[n, c, y // 2, rows, :] * keep
                pad[c, 24 + y, where, :] = corners[2 + n, c, y // 2, rows, :] * keep

    make_windows((1, 3), ((0, 4, 2), (16, 21, 5)))
    make_windows((0, 1), ((0, 21, 3),))
    make_windows((3, 4), ((0, 21, 3),))

    for d in range(3):
        for b in range(5):
            lf[d, 8 * b : 8 * b + 1, :] = lf_prev[d, b, 3:4, :] * has_prev
            lf[d, 8 * b + 1 : 8 * b + 5, :] = lf_own[d, b, 0:4, :]
            lf[d, 8 * b + 5 : 8 * b + 7, :] = lf_next[d, b, 0:2, :] * has_next
            lf[d, 8 * b + 7 : 8 * b + 8, :] = jnp.zeros((1, 128), F32)
    bt = table("bt")
    own = dot3(lf[...].reshape(120, 128), bt[0])
    mid = [from_lane(rows_m[8:16], 32 * d + 16 * b) for d in range(3) for b in range(2)]
    mid = dot3(jnp.concatenate(mid, axis=0), bt[1])
    coarse = dot3(jnp.concatenate(next_c, axis=0), bt[2])
    base_f = [
        jnp.concatenate(
            [own[40 * d : 40 * d + 40], mid[16 * d : 16 * d + 16], coarse[8 * d : 8 * d + 8]], axis=0
        )
        for d in range(3)
    ]
    base_f = jnp.concatenate(base_f, axis=1)
    spread, gather, bx, sum_m = table("spread"), table("gather"), table("bx"), table("sum_m")

    broadcast_wait(m_buf, bsem.at[2], bsem.at[3])
    gradient = dot_exact(sum_m[...], m_buf[...].reshape(512, 128))
    near = gradient[96:112]
    gradient = gradient[0:96]
    inverse = lax.rsqrt(jnp.sum(gradient * gradient) * (1.0 / 1782.0) + EPSILON)

    near = dot3(jnp.concatenate([from_lane(near, 16 * d) for d in range(3)], axis=0), bt[1])
    near = jnp.concatenate([near[16 * d : 16 * d + 16] for d in range(3)], axis=1)
    near = jnp.concatenate([jnp.zeros((40, 3 * NX), F32), near, jnp.zeros((8, 3 * NX), F32)], axis=0)
    upper, lower = parts(base_f - (STEP_SIZE * inverse) * near)
    columns[0:64, :] = upper
    columns[64:128, :] = upper
    columns[128:192, :] = lower
    columns[192:256, :] = lower
    field_a[...] = dot(spread[0:480, :], columns[...])

    rows_z = (pl.ds(0, 24), pl.ds(jnp.minimum(k + 1, 1), 24))

    def fine_block(block, split, split_before, field, field_after):
        adjoint[...] = jnp.zeros_like(adjoint)
        after = pl.ds(pl.multiple_of(480 * jnp.minimum(block + 1, 3), 480), 480)

        @pl.loop(0, 5)
        def _(i):
            lanes = pl.ds(pl.multiple_of(384 * i, 384), 384)
            field_after[:, lanes] = dot(spread[after, :], columns[:, lanes])
            lanes = pl.ds(pl.multiple_of(768 * i, 768), 768)
            adjoint[...] += dot(split_before[:, lanes], bx[lanes, :])
            for pair in range(2):
                for c in range(CHUNKS):
                    found = []
                    for h in range(2):
                        y = 4 * i + 2 * pair + h
                        corner = [[at[block, c, y + e, z, :] for e in (0, 1)] for z in rows_z]
                        step = [[by[block, c, y + e, z, :] for e in (0, 1)] for z in rows_z]
                        rows = pl.ds(pl.multiple_of(24 * y, 8), 24)
                        fractions = [
                            fraction(field[rows, NX * d + 128 * c : NX * d + 128 * c + 128]) for d in range(3)
                        ]
                        atlas = fx[c, y, pl.ds(20 * block, 24), :]
                        found.append(weights(atlas, corner, step, fractions))
                    rows = pl.ds(pl.multiple_of(96 * i + 48 * pair, 48), 48)
                    for d in range(3):
                        upper, lower = parts(jnp.concatenate([found[0][d], found[1][d]], axis=0))
                        lane = 2 * NX * d + 128 * c
                        split[rows, lane : lane + 128] = upper
                        split[rows, lane + NX : lane + NX + 128] = lower

        before = pl.ds(pl.multiple_of(480 * jnp.maximum(block - 1, 0), 480), 480)
        mixed[before, :] = adjoint[:, 0:128] + adjoint[:, 128:256]

    @pl.loop(0, 2)
    def _(two):
        fine_block(2 * two, split_a, split_b, field_a, field_b)
        fine_block(2 * two + 1, split_b, split_a, field_b, field_a)

    wide = dot(split_b[...], bx[...])
    mixed[1440:1920, :] = wide[:, 0:128] + wide[:, 128:256]
    f_part[...] = dot_gather(gather[...], mixed[...])
    around(k, s, f_part, f_parts, fsend, frecv, "start")
    f_parts[1, s] = f_part[...]

    for b in range(2):
        turned = dot_rows(gradient[48 * b : 48 * b + 48] * inverse, turn)
        for d in range(3):
            for a in range(9):
                mid_out[d, a, b : b + 1, :] = turned[16 * d + a : 16 * d + a + 1, 0:33]
    row = lax.broadcasted_iota(jnp.int32, (40, 128), 0) & 7

    around(k, s, f_part, f_parts, fsend, frecv, "wait_recv")
    before, middle, after = ((f_parts[i, 0] + f_parts[i, 1]) + (f_parts[i, 2] + f_parts[i, 3]) for i in range(3))
    middle = middle + jnp.where((row == 1) | (row == 2), pltpu.roll(before * has_prev, 36, 0), 0.0)
    middle = middle + jnp.where(row == 4, pltpu.roll(after * has_next, 4, 0), 0.0)
    middle = jnp.where((row >= 1) & (row <= 4), middle, 0.0)
    f_tile[...] = jnp.full((8, 128), jnp.sum(middle * middle))
    broadcast_start(k, s, f_tile, f_buf, bsem.at[4], bsem.at[5])
    f_buf[k] = f_tile[...]

    for copy in (lat_to_next, lat_to_prev, z_to_next, z_to_prev, *mid_same):
        copy.wait_send()

    @pl.when(up)
    def _():
        for copy in (to_bef, *corner_up, *mid_up):
            copy.wait_send()

    @pl.when(down)
    def _():
        for copy in (to_aft, *corner_down, *mid_down):
            copy.wait_send()

    around(k, s, piece, pieces, psend, precv, "wait_send")
    around(k, s, f_part, f_parts, fsend, frecv, "wait_send")
    part_copies("wait_send")
    middle = pltpu.roll(middle, 39, 0)
    thirds = [from_lane(middle, 40 * d) for d in range(3)]

    broadcast_wait(f_buf, bsem.at[4], bsem.at[5])
    squares = jnp.sum(f_buf[...], axis=0)[0:1, :]
    inverse = lax.rsqrt(squares * (1.0 / 63360.0) + EPSILON)
    for d in range(3):
        scaled = thirds[d] * inverse
        for b in range(5):
            fine_out[d, b] = scaled[8 * b : 8 * b + 4, 0:33]


def body(
    fixed_image,
    moving_image,
    lattice_fine,
    lattice_mid,
    lattice_coarse,
    offset_fine,
    offset_mid,
    offset_coarse,
):
    t = tables()
    vmem, smem, hbm = (pl.BlockSpec(memory_space=m) for m in (pltpu.VMEM, pltpu.SMEM, pl.ANY))
    shape = lambda *dims: jax.ShapeDtypeStruct(dims, F32)
    buf = lambda *dims: pltpu.VMEM(dims, F32)
    half = lambda *dims: pltpu.VMEM(dims, BF16)
    dma = lambda *dims: pltpu.SemaphoreType.DMA(dims)
    fine, mid, coarse = pl.pallas_call(
        kernel,
        out_shape=[shape(3, 5, 4, 33), shape(3, 9, 2, 33), shape(3, 3, 1, 9)],
        in_specs=[hbm, hbm, vmem, vmem, vmem, smem, smem, smem] + [hbm] * len(TABLES),
        out_specs=[vmem] * 3,
        scratch_shapes=[
            *[pltpu.VMEM(t[n].shape[which is not None :], t[n].dtype) for n, which in TABLES.items()],
            buf(CHUNKS, 28, 96, 128), buf(CHUNKS, NY, 88, 128), buf(5, NZ, NX),
            *[buf(CHUNKS, 10, 8, 128)] * 4, *[buf(4, NZ, NX)] * 2, buf(4, CHUNKS, 2, 8, 128),
            *[buf(3, 5, 8, 128)] * 3, buf(3, 40, 128), buf(128, 128), buf(128, 128),
            *[buf(5, 24, 256)] * 4, buf(2, 3, 5, 8, 256),
            buf(2, 8, 128), buf(3, SECS, 2, 8, 128), buf(14, 32, 128), buf(5, 8, 128), buf(2, 15, 40, 128),
            buf(8, 128), buf(SLABS, 8, 128), buf(16, 128), buf(SECS, 16, 128), buf(16, 128), buf(SLABS, 16, 128),
            *[buf(4, CHUNKS, 21, 32, 128)] * 2, half(256, 3 * NX),
            *[buf(480, 3 * NX)] * 2, *[half(480, 6 * NX)] * 2, buf(480, 256), buf(1920, 128),
            buf(40, 128), buf(3, SECS, 40, 128), buf(8, 128), buf(SLABS, 8, 128),
            dma(10), dma(len(TABLES)), dma(18), dma(18), *[dma(3, SECS)] * 4, dma(SECS), dma(SECS), dma(6),
        ],
        compiler_params=pltpu.CompilerParams(
            collective_id=0, has_side_effects=True, vmem_limit_bytes=VMEM_LIMIT
        ),
        name="mega",
    )(
        jnp.transpose(moving_image, (1, 0, 2)),
        jnp.transpose(fixed_image, (1, 0, 2)),
        jnp.transpose(lattice_fine, (0, 2, 1, 3)),
        jnp.transpose(lattice_mid, (0, 3, 2, 1)),
        jnp.transpose(lattice_coarse, (0, 3, 2, 1)),
        offset_fine,
        jnp.transpose(offset_mid, (1, 2, 0)),
        jnp.transpose(offset_coarse, (0, 2, 1)),
        *(t[n] for n in TABLES),
    )
    results = (fine, mid, coarse)
    fine, mid, coarse = pl.pallas_call(
        finish,
        out_shape=[jax.ShapeDtypeStruct(a.shape, F32) for a in results],
        in_specs=[hbm] * 3,
        out_specs=[hbm] * 3,
        scratch_shapes=[dma(3)],
        name="finish",
    )(*results)
    return (
        jnp.transpose(fine, (0, 2, 1, 3)),
        jnp.transpose(mid, (0, 3, 2, 1)),
        jnp.transpose(coarse, (0, 3, 2, 1)),
    )


def solution(mesh):
    placed = (
        P("slab", "sec", None),
        P("slab", "sec", None),
        P(None, "slab", None, None),
        P(),
        P(),
        P(None, "slab", None),
        P(None, "slab", None),
        P(),
    )
    return jax.shard_map(
        body,
        mesh=mesh,
        in_specs=placed,
        out_specs=(P(None, "slab", None, None), P(), P()),
        check_vma=False,
    )
```

```python
import functools

import jax
import jax.numpy as jnp
import ml_dtypes
import numpy as np
from jax import lax
from jax.experimental import pallas as pl
from jax.experimental.pallas import tpu as pltpu
from jax.sharding import PartitionSpec as P

SP = 20
EPSILON = 1e-06
STEP_SIZE = 0.5
HIGHEST = lax.Precision.HIGHEST
F32 = jnp.float32
BF16 = jnp.bfloat16
MESH = pl.DeviceIdType.MESH
SLABS = 32
SECS = 4
NZ, NY, NX = 80, 20, 640
CHUNKS = NX // 128
LOG2E = 1.4426950408889634
VMEM_LIMIT = 58 * 1024 * 1024


def basis(rows, knots, factor, coarse):
    rows, knots = np.asarray(rows, np.float64), np.asarray(knots, np.float64)
    position = factor * rows + 0.5 * (factor - 1)
    centre = SP * coarse * knots + 0.5 * (coarse - 1)
    distance = np.abs((position[:, None] - centre[None, :]) / (SP * coarse))
    near = 2.0 / 3.0 - distance**2 + 0.5 * distance**3
    far = np.maximum(2.0 - distance, 0.0) ** 3 / 6.0
    return np.where(distance < 1.0, near, far)


def two_parts(values):
    high = values.astype(ml_dtypes.bfloat16)
    low = (values - high.astype(np.float64)).astype(ml_dtypes.bfloat16)
    return high, low


def right_parts(values):
    high, low = two_parts(values)
    return np.concatenate([high, low, high], axis=-2)


def wide_parts(values):
    high, low = two_parts(values)
    zero = np.zeros_like(high)
    return np.concatenate([np.concatenate([high, low], 1), np.concatenate([high, zero], 1)], 0)


def one_hot(condition):
    return condition.astype(ml_dtypes.bfloat16)


@functools.cache
def tables():
    t = {}
    rz, ry = np.zeros((4, 4, 24, 64)), np.zeros((4, NY, 64))
    z, y, x = np.arange(NZ), np.arange(NY), np.arange(NX)
    for r in range(4):
        for block in range(4):
            rows = z[20 * block : 20 * block + 20]
            for a in range(7):
                rz[r, block, :20, a:40:8] = basis(rows, [a - 1], 1, 1)
            for a in range(5):
                rz[r, block, :20, 40 + a : 56 : 8] = basis(rows, [a - 2], 1, 4)
                rz[r, block, :20, 56 + a : 57 + a] = basis(rows + 80 * r, [a - 2], 1, 16)
    for s in range(4):
        for a in range(7):
            ry[s, :, a:40:8] = basis(y + 20 * s, range(5), 1, 1)
        for a in range(5):
            ry[s, :, 40 + a : 56 : 8] = basis(y + 20 * s, range(2), 1, 4)
            ry[s, :, 56 + a : 57 + a] = basis(y + 20 * s, [0], 1, 16)
    whole = rz[:, None, :, None] * ry[None, :, None, :, None, :]
    high, low = two_parts(whole.reshape(16, 1920, 64))
    t["spread"] = np.concatenate([high, low, high, low], axis=2)
    t["gather"] = np.concatenate([high[:4, :, :40], low[:4, :, :40]], axis=2).transpose(0, 2, 1)
    across = np.zeros((3, 128, NX))
    across[0, :33] = basis(x, range(33), 1, 1).T
    across[1, :9] = basis(x, range(9), 1, 4).T
    across[2, :3] = basis(x, range(3), 1, 16).T
    t["bt"] = right_parts(-LOG2E * across)
    along = np.zeros((3, NX, 128))
    for d in range(3):
        along[d, :, 40 * d : 40 * d + 33] = basis(x, range(33), 1, 1)
    t["bx"] = np.concatenate([wide_parts(along[d]) for d in range(3)], axis=0)
    rz, ry = np.zeros((4, 24, 32)), np.zeros((4, 5, 32))
    z, y, x = np.arange(20), np.arange(5), np.arange(160)
    for r in range(4):
        for a in range(4):
            rz[r, :20, a:16:8] = basis(z, [a - 1], 4, 4)
        for a in range(5):
            rz[r, :20, 16 + a : 17 + a] = basis(z + 20 * r, [a - 2], 4, 16)
    for s in range(4):
        for a in range(4):
            ry[s, :, a:16:8] = basis(y + 5 * s, range(2), 4, 4)
        for a in range(5):
            ry[s, :, 16 + a : 17 + a] = basis(y + 5 * s, [0], 4, 16)
    whole = np.zeros((16, 128, 32))
    whole[:, :120] = (rz[:, None, None] * ry[None, :, :, None]).reshape(16, 120, 32)
    high, low = two_parts(whole)
    t["mspread"] = np.concatenate([high, high, low, np.zeros_like(low)], axis=2)
    t["mgather"] = np.concatenate([high[:, :, :16], low[:, :, :16]], axis=2).transpose(0, 2, 1)
    across = np.zeros((2, 128, 256))
    across[0, :9, :160] = basis(x, range(9), 4, 4).T
    across[1, :3, :160] = basis(x, range(3), 4, 16).T
    t["mbt"] = right_parts(-LOG2E * across)
    along = np.zeros((3, 256, 128))
    for d in range(3):
        along[d, :160, 16 * d : 16 * d + 9] = basis(x, range(9), 4, 4)
    t["mbx"] = wide_parts(along.reshape(768, 128))
    rz = np.zeros((4, 8, 32))
    z, y, x = np.arange(5), np.arange(5), np.arange(40)
    for r in range(4):
        for a in range(4):
            rz[r, :5, a : a + 1] = basis(z + 5 * r, [a - 1], 16, 16)
    whole = np.zeros((4, 128, 32))
    whole[:, :40] = (rz[:, None] * basis(y, [0], 16, 16)[None, :, None]).reshape(4, 40, 32)
    high, low = two_parts(whole)
    t["cspread"] = np.concatenate([high, high, low, np.zeros_like(low)], axis=2)
    t["cgather"] = np.concatenate([high[:, :, :16], low[:, :, :16]], axis=2).transpose(0, 2, 1)
    across = np.zeros((128, 128))
    across[:3, :40] = basis(x, range(3), 16, 16).T
    t["cbt"] = right_parts(-LOG2E * across)
    along = np.zeros((3, 128, 128))
    for d in range(3):
        along[d, :40, 16 * d : 16 * d + 3] = basis(x, range(3), 16, 16)
    t["cbx"] = wide_parts(along.reshape(384, 128))
    row, column = np.arange(NX)[:, None], np.arange(256)[None, :]
    t["px"] = one_hot(row // 4 == column)
    row, column = np.arange(120)[:, None], np.arange(400)[None, :]
    t["pz"] = one_hot((row // 24 == column // 80) & (row % 24 == column % 80 // 4))
    row, column = np.arange(512)[:, None], np.arange(128)[None, :]
    t["pcx"] = one_hot((row % 256 < 160) & (row // 256 * 64 + row % 256 // 4 == column))
    row, column = np.arange(16)[:, None], np.arange(48)[None, :]
    t["pcz"] = one_hot((row // 8 == column // 24) & (column % 24 < 20) & (row % 8 == column % 24 // 4))
    row, column, place = np.arange(16)[:, None], np.arange(128)[None, :], np.arange(32)[:, None, None]
    knot = place - 1 - row // 8 + row % 8
    t["rows_m"] = one_hot((knot == column) & (column < 33))
    t["rows_c"] = one_hot((knot == column) & (column < 9))[:8]
    row, column, place = np.arange(24)[:, None], np.arange(256)[None, :], np.arange(8)[:, None, None]
    knot = np.where(row < 16, row - 2, row - 16 + place - 2)
    slab = column // 8 % 4 * 8 + column // 32
    found = (knot == slab // 4 - 1 + column % 8) & (column % 8 < 4) & (knot >= 0) & (knot < 9)
    t["sum_c"] = one_hot(found)
    row, column, place = np.arange(112)[:, None], np.arange(512)[None, :], np.arange(32)[:, None, None]
    knot = np.where(row < 96, row % 48 - 2, row % 8 + place - 2)
    b = np.where(row < 96, row // 48, (row - 96) // 8)
    slab = column // 16 % 4 * 8 + column // 64
    found = (knot == slab - 1 + column % 8) & (column % 8 < 4) & (column // 8 % 2 == b)
    t["sum_m"] = one_hot(found & (knot >= 0) & (knot < 33))
    return t


def dot(a, b):
    return jnp.dot(a, b, preferred_element_type=F32)


def dot_rows(a, b):
    return lax.dot_general(
        a, b, (((0,), (0,)), ((), ())), precision=HIGHEST, preferred_element_type=F32
    )


def parts(values):
    high = values.astype(BF16)
    return high, (values - high.astype(F32)).astype(BF16)


def dot3(a, right):
    high, low = parts(a)
    return dot(jnp.concatenate([high, high, low], axis=1), right)


def dot_wide(a, table):
    wide = dot(jnp.concatenate(parts(a), axis=1), table)
    return wide[:, 0:128] + wide[:, 128:256]


def dot_exact(table, b):
    wide = dot(table, jnp.concatenate(parts(b), axis=1))
    return wide[:, 0:128] + wide[:, 128:256]


def dot_gather(table, b):
    n = table.shape[0] // 2
    wide = dot(table, jnp.concatenate(parts(b), axis=1))
    return (wide[0:n, 0:128] + wide[0:n, 128:256]) + wide[n:, 0:128]


def stacked(column, n):
    high, low = parts(jnp.concatenate([column, jnp.zeros((32 - n, column.shape[1]), F32)], axis=0))
    return jnp.concatenate([high, low, high, jnp.zeros_like(low)], axis=0)


def from_lane(values, lane):
    return values if lane == 0 else pltpu.roll(values, 128 - lane, 1)


def shift_lanes(chunks, shift):
    amount = (128 - shift) & 127
    rolled = [pltpu.roll(chunk, amount, 1) for chunk in chunks]
    lane = lax.broadcasted_iota(jnp.int32, chunks[0].shape, 1)
    first = lane < jnp.maximum(-shift, 0)
    last = lane >= 128 - jnp.maximum(shift, 0)
    zero = jnp.zeros_like(chunks[0])
    padded = [zero, *rolled, zero]
    return [
        jnp.where(first, padded[j], jnp.where(last, padded[j + 2], padded[j + 1]))
        for j in range(len(chunks))
    ]


def fraction(exponent):
    grown = jnp.exp2(exponent)
    frac = pl.reciprocal(1.0 + grown, approx=True)
    return frac, frac * (grown * frac)


def weights(fixed, corner, step, fractions):
    (fz, gz), (fy, gy), (fx, gx) = fractions
    line = [[corner[z][y] + fx * step[z][y] for y in (0, 1)] for z in (0, 1)]
    rise = [line[z][1] - line[z][0] for z in (0, 1)]
    plane = [line[z][0] + fy * rise[z] for z in (0, 1)]
    slope_z = plane[1] - plane[0]
    residual = (plane[0] + fz * slope_z) - fixed
    slope_y = rise[0] + fz * (rise[1] - rise[0])
    along = [step[z][0] + fy * (step[z][1] - step[z][0]) for z in (0, 1)]
    slope_x = along[0] + fz * (along[1] - along[0])
    return [
        (residual * slope_z) * gz,
        (residual * slope_y) * gy,
        (residual * slope_x) * gx,
    ]


def greet(k, s):
    barrier = pltpu.get_barrier_semaphore()

    def signal(slab, sec):
        pl.semaphore_signal(barrier, inc=1, device_id=(slab, sec), device_id_type=MESH)

    for i in range(1, 4):
        signal((k + 8 * i) & (SLABS - 1), s)
    for i in range(1, 8):
        signal((k & 24) + ((k + i) & 7), s)
    signal((k + 1) & (SLABS - 1), s)
    signal((k + SLABS - 1) & (SLABS - 1), s)
    for i in range(1, SECS):
        other = (s + i) & (SECS - 1)
        signal(k, other)
        signal((k + 1) & (SLABS - 1), other)
        signal((k + SLABS - 1) & (SLABS - 1), other)
    return lambda: pl.semaphore_wait(barrier, 3 + 7 + 2 + 3 * (SECS - 1))


def gather_along_z(k, s, tile, buffer, sems):
    for i in (2, 1, 3):
        remote(tile, buffer.at[k & 7, k >> 3], sems.at[0], sems.at[1], ((k + 8 * i) & (SLABS - 1), s)).start()
    buffer[k & 7, k >> 3] = tile[...]


def gather_across(k, s, buffer, sems):
    part = buffer.at[0, pl.ds(0, 3)]
    pltpu.make_async_copy(part, part, sems.at[1]).wait()
    pltpu.make_async_copy(part, part, sems.at[0]).wait()
    row = buffer.at[k & 7]
    for i in (5, 4, 3, 6, 2, 7, 1):
        remote(row, row, sems.at[2], sems.at[3], ((k & 24) + ((k + i) & 7), s)).start()


def gathered(buffer, sems):
    part = buffer.at[pl.ds(0, 7)]
    pltpu.make_async_copy(part, part, sems.at[3]).wait()
    pltpu.make_async_copy(part, part, sems.at[2]).wait()


def remote(src, dst, send_sem, recv_sem, device):
    return pltpu.make_async_remote_copy(
        src_ref=src,
        dst_ref=dst,
        send_sem=send_sem,
        recv_sem=recv_sem,
        device_id=device,
        device_id_type=MESH,
    )


def around(k, s, source, buffer, send, recv, act):
    slabs = ((k + SLABS - 1) & (SLABS - 1), k, (k + 1) & (SLABS - 1))

    def one(dk, other):
        if act == "wait_recv":
            copy = remote(source, buffer.at[dk, other], send.at[dk, other], recv.at[dk, other], (k, other))
        else:
            copy = remote(
                source, buffer.at[2 - dk, s], send.at[dk, other], recv.at[2 - dk, s], (slabs[dk], other)
            )
        getattr(copy, act)()

    for dk in (0, 2):
        for other in range(SECS):
            one(dk, other)
    for i in range(1, SECS):
        one(1, (s + i) & (SECS - 1))


TABLES = {
    "px": None, "pz": None, "pcx": None, "pcz": None,
    "rows_m": "k", "rows_c": "q", "cspread": "r", "cgather": "r", "cbt": None, "cbx": None,
    "sum_c": "q", "mspread": "rs", "mgather": "rs", "mbt": None, "mbx": None,
    "spread": "rs", "gather": "s", "bt": None, "bx": None, "sum_m": "k",
}


def finish(result, fine_out, mid_out, coarse_out):
    for d in range(3):
        for b in range(5):
            row = 40 * d + 8 * b
            fine_out[d, b] = result[row : row + 4, 0:33]
        for a in range(9):
            for b in range(2):
                row = 120 + 48 * b + 16 * d + a
                mid_out[d, a, b : b + 1, :] = result[row : row + 1, 0:33]
        for a in range(3):
            row = 216 + 16 * d + a
            coarse_out[d, a] = result[row : row + 1, 0:9]


def kernel(
    moving, fixed, lat_fine, lat_mid, lat_coarse, off_fine, off_mid, off_coarse, *refs
):
    n = len(TABLES)
    stored, refs = refs[:n], refs[n:]
    result, *refs = refs
    t = dict(zip(TABLES, refs[:n]))
    (
        pad, fx, sums, zlo, zhi, z_bef, z_aft, y_bef, y_aft, corners,
        lf_own, lf_prev, lf_next, lf, mt, ct,
        pooled_m, pooled_f, pm_bef, pm_aft, pm_halo,
        piece, pieces, cv, cf, mm,
        c_tile, c_buf, m_part, m_parts, m_tile, m_buf,
        at, by, columns, field_a, field_b, split_a, split_b, adjoint, mixed,
        f_part, f_parts, f_tile, f_buf,
        load_sem, table_sem, send, recv, psend, precv, fsend, frecv, tsend, trecv, c_sem, m_sem, f_sem,
    ) = refs[n:]
    k, s = lax.axis_index("slab"), lax.axis_index("sec")
    nxt, prv = (k + 1) & (SLABS - 1), (k + SLABS - 1) & (SLABS - 1)
    q, r = k >> 2, k & 3
    has_prev, has_next = (k > 0).astype(F32), (k < SLABS - 1).astype(F32)
    up, down = s < SECS - 1, s > 0
    own_y, own_z = pl.ds(4, NY), pl.ds(8, NZ)

    load_moving = [
        pltpu.make_async_copy(
            moving.at[:, :, pl.ds(128 * c, 128)], pad.at[c, own_y, own_z], load_sem.at[c]
        )
        for c in range(CHUNKS)
    ]
    load_fixed = [
        pltpu.make_async_copy(
            fixed.at[:, :, pl.ds(128 * c, 128)], fx.at[c, :, pl.ds(0, NZ)], load_sem.at[CHUNKS + c]
        )
        for c in range(CHUNKS)
    ]
    place = {"k": k, "q": q, "r": r, "s": s, "rs": 4 * r + s}
    load_table = {}
    for i, (name, which) in enumerate(TABLES.items()):
        source = stored[i] if which is None else stored[i].at[place[which]]
        load_table[name] = pltpu.make_async_copy(source, t[name], table_sem.at[i])
    for copy in load_moving:
        copy.start()
    all_here = greet(k, s)
    for copy in (*load_fixed, *load_table.values()):
        copy.start()

    def table(name):
        load_table[name].wait()
        return t[name]

    lat_to_next = remote(lf_own, lf_prev, send.at[0], recv.at[0], (nxt, s))
    lat_to_prev = remote(lf_own, lf_next, send.at[1], recv.at[1], (prv, s))
    z_to_next = remote(zhi, z_bef, send.at[2], recv.at[2], (nxt, s))
    z_to_prev = remote(zlo, z_aft, send.at[3], recv.at[3], (prv, s))
    to_bef = remote(moving.at[pl.ds(16, 4)], y_bef, send.at[4], recv.at[4], (k, s + 1))
    to_aft = remote(moving.at[pl.ds(0, 4)], y_aft, send.at[5], recv.at[5], (k, s - 1))
    first, last = pl.ds(0, 2), pl.ds(8, 2)
    corner_up = [
        remote(zhi.at[:, last], corners.at[0], send.at[6], recv.at[6], (nxt, s + 1)),
        remote(zlo.at[:, last], corners.at[1], send.at[7], recv.at[7], (prv, s + 1)),
    ]
    corner_down = [
        remote(zhi.at[:, first], corners.at[2], send.at[8], recv.at[8], (nxt, s - 1)),
        remote(zlo.at[:, first], corners.at[3], send.at[9], recv.at[9], (prv, s - 1)),
    ]
    head, tail = pl.ds(0, 8), pl.ds(16, 8)
    mid_same = [
        remote(pooled_m.at[:, tail], pm_halo.at[0, 1], send.at[10], recv.at[10], (nxt, s)),
        remote(pooled_m.at[:, head], pm_halo.at[1, 1], send.at[11], recv.at[11], (prv, s)),
    ]
    mid_up = [
        remote(pooled_m, pm_bef, send.at[12], recv.at[12], (k, s + 1)),
        remote(pooled_m.at[:, tail], pm_halo.at[0, 0], send.at[13], recv.at[13], (nxt, s + 1)),
        remote(pooled_m.at[:, head], pm_halo.at[1, 0], send.at[14], recv.at[14], (prv, s + 1)),
    ]
    mid_down = [
        remote(pooled_m, pm_aft, send.at[15], recv.at[15], (k, s - 1)),
        remote(pooled_m.at[:, tail], pm_halo.at[0, 2], send.at[16], recv.at[16], (nxt, s - 1)),
        remote(pooled_m.at[:, head], pm_halo.at[1, 2], send.at[17], recv.at[17], (prv, s - 1)),
    ]

    def start(*copies):
        for copy in copies:
            copy.start()

    def start_if(condition, *copies):
        @pl.when(condition)
        def _():
            start(*copies)

    for ref in (lf_own, mt, ct, cv, mm):
        ref[...] = jnp.zeros_like(ref)
    for d in range(3):
        for b in range(5):
            lf_own[d, b, 0:4, 0:33] = lat_fine[d, b]
        for a in range(9):
            for b in range(2):
                row = 32 * d + 16 * b + a
                mt[row : row + 1, 0:33] = lat_mid[d, a, b : b + 1]
        for a in range(3):
            ct[16 * d + a : 16 * d + a + 1, 0:9] = lat_coarse[d, a]
    for c in range(CHUNKS):
        pad[c, :, 0:8, :] = jnp.zeros((28, 8, 128), F32)
        pad[c, :, 88:96, :] = jnp.zeros((28, 8, 128), F32)
        fx[c, :, 80:88, :] = jnp.zeros((NY, 8, 128), F32)
        for block in range(4):
            at[block, c, :, 24:32, :] = jnp.zeros((21, 8, 128), F32)
            by[block, c, :, 24:32, :] = jnp.zeros((21, 8, 128), F32)
    all_here()
    start_if(up, to_bef)
    start_if(down, to_aft)
    for c in range(CHUNKS):
        load_moving[c].wait()

        @pl.loop(0, NY // 2, unroll=5)
        def _(pair):
            for half in range(2):
                rows = slice(4 * half, 4 * half + 4)
                zlo[c, pair, rows, :] = pad[c, 2 * pair + half + 4, 8:12, :]
                zhi[c, pair, rows, :] = pad[c, 2 * pair + half + 4, 84:88, :]

    start(z_to_next, z_to_prev)
    start_if(up, *corner_up)
    start_if(down, *corner_down)

    px, pz = table("px"), table("pz")

    def pooled():
        high, low = parts(sums[...].reshape(400, NX))
        high, low = parts(dot(high, px[...]) + dot(low, px[...]))
        return ((dot(pz[...], high) + dot(pz[...], low)) * (1.0 / 64.0)).reshape(5, 24, 256)

    for c in range(CHUNKS):
        lanes = slice(128 * c, 128 * c + 128)

        @pl.loop(0, 5, unroll=5)
        def _(group):
            four = [pad[c, 4 * group + 4 + i, 8:88, :] for i in range(4)]
            sums[group, :, lanes] = (four[0] + four[1]) + (four[2] + four[3])

    pooled_m[...] = pooled()

    for c in range(CHUNKS):
        load_fixed[c].wait()
        lanes = slice(128 * c, 128 * c + 128)

        @pl.loop(0, 5, unroll=5)
        def _(group):
            four = [fx[c, 4 * group + i, 0:80, :] for i in range(4)]
            sums[group, :, lanes] = (four[0] + four[1]) + (four[2] + four[3])

    pooled_f[...] = pooled()

    halves = []
    for ref in (pooled_m, pooled_f):
        upper, lower = jnp.zeros((24, 256), F32), jnp.zeros((24, 256), F32)
        for i in range(5):
            keep = (i + s < 4).astype(F32)
            upper = upper + ref[i] * keep
            lower = lower + ref[i] * (1.0 - keep)
        halves.append(jnp.concatenate([upper, lower], axis=0))
    high, low = parts(jnp.concatenate(halves, axis=1))
    pcx, pcz = table("pcx")[...], table("pcz")[...]
    both = dot(high, pcx) + dot(low, pcx)
    piece[...] = (dot_exact(pcz, both) * (1.0 / 64.0)).reshape(2, 8, 128)
    around(k, s, piece, pieces, psend, precv, "start")
    pieces[1, s] = piece[...]
    start(*mid_same)
    start_if(up, *mid_up)
    start_if(down, *mid_down)

    start(lat_to_next, lat_to_prev)

    def pick_rows(name, ref):
        rows = table(name)[...]
        contract = (((1,), (1,)), ((), ()))
        high, low = parts(ref[...])
        return lax.dot_general(rows, high, contract, preferred_element_type=F32) + lax.dot_general(
            rows, low, contract, preferred_element_type=F32
        )

    rows_m, rows_c = pick_rows("rows_m", mt), pick_rows("rows_c", ct)
    cbt, cspread = table("cbt")[...], table("cspread")[...]
    column = dot3(jnp.concatenate([from_lane(rows_c[0:8], 16 * d) for d in range(3)], axis=0), cbt)
    column = jnp.concatenate([column[8 * d : 8 * d + 8] for d in range(3)], axis=1)
    exponent = dot(cspread, stacked(column, 8))[0:40]
    fractions_c = [fraction(exponent[:, 128 * d : 128 * d + 128]) for d in range(3)]
    cbx, cgather = table("cbx"), table("cgather")

    around(k, s, piece, pieces, psend, precv, "wait_recv")

    lane = lax.broadcasted_iota(jnp.int32, (5, 128), 1)
    for dk in range(3):
        scale = (has_prev, jnp.float32(1.0), has_next)[dk]
        rows = (slice(3, 8), slice(8, 13), slice(13, 18))[dk]
        for c in range(5):
            value = jnp.zeros((8, 128), F32)
            if c < 4:
                value = value + pieces[dk, c, 0]
            if c > 0:
                value = value + pieces[dk, c - 1, 1]
            cv[4 + c, rows, :] = jnp.where(lane < 40, value[0:5], 0.0) * scale
            if dk == 1:
                cf[c] = value
    fixed_c = pltpu.roll(cf[...].reshape(40, 128), 64, 1)

    oz, oy, ox = off_coarse[0, 0, q], off_coarse[1, 0, q], off_coarse[2, 0, q]
    a_z, b_z = [], []
    for e in (0, 1):
        window = cv[pl.ds(4 + oy, 6), pl.ds(8 + oz + e, 8), :].reshape(48, 128)
        here, there = shift_lanes([window], ox)[0], shift_lanes([window], ox + 1)[0]
        a_z.append(here)
        b_z.append(there - here)
    corner = [[a_z[z][8 * y : 8 * y + 40] for y in (0, 1)] for z in (0, 1)]
    step = [[b_z[z][8 * y : 8 * y + 40] for y in (0, 1)] for z in (0, 1)]
    total = jnp.concatenate(weights(fixed_c, corner, step, fractions_c), axis=1)
    total = dot_wide(jnp.concatenate([total, jnp.zeros((8, 384), F32)], axis=0), cbx[...])
    total = jnp.concatenate([total, jnp.zeros((80, 128), F32)], axis=0)
    c_tile[...] = dot_gather(cgather[...], total)[0:8]
    gather_along_z(k, s, c_tile, c_buf, c_sem)

    mbt, mspread, mbx, mgather = table("mbt"), table("mspread"), table("mbx"), table("mgather")
    own = [from_lane(rows_m[0:8], 32 * d + 16 * b) for d in range(3) for b in range(2)]
    own = dot3(jnp.concatenate(own, axis=0), mbt[0])
    coarse = dot3(jnp.concatenate([from_lane(rows_c[8:16], 16 * d) for d in range(3)], axis=0), mbt[1])
    column = [
        jnp.concatenate([own[16 * d : 16 * d + 16], coarse[8 * d : 8 * d + 8]], axis=0) for d in range(3)
    ]
    base_m = dot(mspread[...], stacked(jnp.concatenate(column, axis=1), 24))[0:120]
    sum_c = table("sum_c")
    gather_across(k, s, c_buf, c_sem)

    @pl.when(s == 0)
    def _():
        y_bef[...] = jnp.zeros_like(y_bef)
        corners[0:2] = jnp.zeros((2, CHUNKS, 2, 8, 128), F32)
        pm_bef[...] = jnp.zeros_like(pm_bef)
        pm_halo[:, 0] = jnp.zeros((2, 5, 8, 256), F32)

    @pl.when(s == SECS - 1)
    def _():
        y_aft[...] = jnp.zeros_like(y_aft)
        corners[2:4] = jnp.zeros((2, CHUNKS, 2, 8, 128), F32)
        pm_aft[...] = jnp.zeros_like(pm_aft)
        pm_halo[:, 2] = jnp.zeros((2, 5, 8, 256), F32)

    for copy in mid_same:
        copy.wait_recv()

    @pl.when(s > 0)
    def _():
        for copy in mid_up:
            copy.wait_recv()

    @pl.when(s < SECS - 1)
    def _():
        for copy in mid_down:
            copy.wait_recv()

    for c in range(2):
        lanes = slice(128 * c, 128 * c + 128)
        for e, whole in enumerate((pm_bef, pooled_m, pm_aft)):
            for y in range(5):
                mm[c, 5 * e + y, 4:8, :] = pm_halo[0, e, y, 0:4, lanes] * has_prev
                mm[c, 5 * e + y, 8:28, :] = whole[y, 0:20, lanes]
                mm[c, 5 * e + y, 28:32, :] = pm_halo[1, e, y, 0:4, lanes] * has_next

    oz, oy, ox = off_mid[0, 0, 0], off_mid[0, 0, 1], off_mid[0, 0, 2]
    a_z, b_z = [], []
    for e in (0, 1):
        window = [mm[c, pl.ds(5 + oy, 6), pl.ds(8 + oz + e, 24), :].reshape(144, 128) for c in range(2)]
        here, there = shift_lanes(window, ox), shift_lanes(window, ox + 1)
        a_z.append(here)
        b_z.append([there[c] - here[c] for c in range(2)])

    def make_window(block, oz, oy, ox, y):
        window = [pad[c, 4 + oy + y, pl.ds(20 * block + 8 + oz, 24), :] for c in range(CHUNKS)]
        here, there = shift_lanes(window, ox), shift_lanes(window, ox + 1)
        for c in range(CHUNKS):
            at[block, c, y, 0:24, :] = here[c]
            by[block, c, y, 0:24, :] = there[c] - here[c]

    def make_windows(blocks, ranges):
        @pl.loop(*blocks)
        def _(block):
            offsets = [off_fine[d, block, s] for d in range(3)]
            for first_y, last_y, unroll in ranges:
                pl.loop(first_y, last_y, unroll=unroll)(functools.partial(make_window, block, *offsets))

    make_windows((1, 3), ((4, 16, 3),))

    gathered(c_buf, c_sem)
    gradient = dot_exact(sum_c[...], c_buf[...].reshape(256, 128))
    near_c = gradient[16:24]
    gradient = gradient[0:16]
    inverse = lax.rsqrt(jnp.sum(gradient * gradient) * (1.0 / 81.0) + EPSILON)

    near = dot3(jnp.concatenate([from_lane(near_c, 16 * d) for d in range(3)], axis=0), mbt[1])
    near = jnp.concatenate([near[8 * d : 8 * d + 8] for d in range(3)], axis=1)
    near = dot(mspread[...], stacked(jnp.concatenate([jnp.zeros((16, 768), F32), near], axis=0), 24))
    exponent = base_m - (STEP_SIZE * inverse) * near[0:120]
    fixed_m = pooled_f[...].reshape(120, 256)
    found = []
    for c in range(2):
        lanes = slice(128 * c, 128 * c + 128)
        corner = [[a_z[z][c][24 * y : 24 * y + 120] for y in (0, 1)] for z in (0, 1)]
        step = [[b_z[z][c][24 * y : 24 * y + 120] for y in (0, 1)] for z in (0, 1)]
        fractions = [fraction(exponent[:, 256 * d + 128 * c : 256 * d + 128 * c + 128]) for d in range(3)]
        found.append(weights(fixed_m[:, lanes], corner, step, fractions))
    total = jnp.concatenate([found[c][d] for d in range(3) for c in range(2)], axis=1)
    total = dot_wide(jnp.concatenate([total, jnp.zeros((8, 768), F32)], axis=0), mbx[...])
    m_part[...] = dot_gather(mgather[...], total)

    def part_copies(act):
        for i in range(1, SECS):
            other = (s + i) & (SECS - 1)
            slot = other if act == "wait_recv" else s
            getattr(remote(m_part, m_parts.at[slot], tsend.at[other], trecv.at[slot], (k, other)), act)()

    part_copies("start")
    m_parts[s] = m_part[...]
    part_copies("wait_recv")
    m_tile[...] = (m_parts[0] + m_parts[1]) + (m_parts[2] + m_parts[3])
    gather_along_z(k, s, m_tile, m_buf, m_sem)

    gradient = gradient * inverse
    next_c = [
        from_lane(rows_c[8:16], 16 * d) - (STEP_SIZE * inverse) * from_lane(near_c, 16 * d) for d in range(3)
    ]
    turn_r = lax.broadcasted_iota(jnp.int32, (48, 128), 0)
    turn = jnp.where(turn_r == lax.broadcasted_iota(jnp.int32, (48, 128), 1) + 2, 1.0, 0.0)
    result[216:264, :] = dot_rows(gradient, turn[0:16])[0:48]

    for copy in (lat_to_next, lat_to_prev):
        copy.wait_recv()
    for d in range(3):
        for b in range(5):
            lf[d, 8 * b : 8 * b + 1, :] = lf_prev[d, b, 3:4, :] * has_prev
            lf[d, 8 * b + 1 : 8 * b + 5, :] = lf_own[d, b, 0:4, :]
            lf[d, 8 * b + 5 : 8 * b + 7, :] = lf_next[d, b, 0:2, :] * has_next
            lf[d, 8 * b + 7 : 8 * b + 8, :] = jnp.zeros((1, 128), F32)
    bt = table("bt")
    own = dot3(lf[...].reshape(120, 128), bt[0])
    mid = [from_lane(rows_m[8:16], 32 * d + 16 * b) for d in range(3) for b in range(2)]
    mid = dot3(jnp.concatenate(mid, axis=0), bt[1])
    coarse = dot3(jnp.concatenate(next_c, axis=0), bt[2])
    base_f = [
        jnp.concatenate(
            [own[40 * d : 40 * d + 40], mid[16 * d : 16 * d + 16], coarse[8 * d : 8 * d + 8]], axis=0
        )
        for d in range(3)
    ]
    base_f = jnp.concatenate(base_f, axis=1)
    gather_across(k, s, m_buf, m_sem)

    for copy in (z_to_next, z_to_prev):
        copy.wait_recv()

    @pl.when(s > 0)
    def _():
        for copy in (to_bef, *corner_up):
            copy.wait_recv()

    @pl.when(s < SECS - 1)
    def _():
        for copy in (to_aft, *corner_down):
            copy.wait_recv()

    for c in range(CHUNKS):
        lanes = slice(128 * c, 128 * c + 128)
        pad[c, 0:4, 8:88, :] = y_bef[:, :, lanes]
        pad[c, 24:28, 8:88, :] = y_aft[:, :, lanes]

    @pl.loop(0, NY // 2, unroll=2)
    def _(pair):
        for half in range(2):
            rows = slice(4 * half, 4 * half + 4)
            for c in range(CHUNKS):
                pad[c, 2 * pair + half + 4, 4:8, :] = z_bef[c, pair, rows, :] * has_prev
                pad[c, 2 * pair + half + 4, 88:92, :] = z_aft[c, pair, rows, :] * has_next

    for y in range(4):
        rows = slice(4 * (y % 2), 4 * (y % 2) + 4)
        for c in range(CHUNKS):
            for n in range(2):
                where = slice(4, 8) if n == 0 else slice(88, 92)
                keep = has_prev if n == 0 else has_next
                pad[c, y, where, :] = corners[n, c, y // 2, rows, :] * keep
                pad[c, 24 + y, where, :] = corners[2 + n, c, y // 2, rows, :] * keep

    make_windows((1, 3), ((0, 4, 2), (16, 21, 5)))
    make_windows((0, 1), ((0, 21, 3),))
    make_windows((3, 4), ((0, 21, 3),))

    spread, gather, bx, sum_m = table("spread"), table("gather"), table("bx"), table("sum_m")

    gathered(m_buf, m_sem)
    gradient = dot_exact(sum_m[...], m_buf[...].reshape(512, 128))
    near = gradient[96:112]
    gradient = gradient[0:96]
    inverse = lax.rsqrt(jnp.sum(gradient * gradient) * (1.0 / 1782.0) + EPSILON)

    near = dot3(jnp.concatenate([from_lane(near, 16 * d) for d in range(3)], axis=0), bt[1])
    near = jnp.concatenate([near[16 * d : 16 * d + 16] for d in range(3)], axis=1)
    near = jnp.concatenate([jnp.zeros((40, 3 * NX), F32), near, jnp.zeros((8, 3 * NX), F32)], axis=0)
    upper, lower = parts(base_f - (STEP_SIZE * inverse) * near)
    columns[0:64, :] = upper
    columns[64:128, :] = upper
    columns[128:192, :] = lower
    columns[192:256, :] = lower
    field_a[...] = dot(spread[0:480, :], columns[...])

    rows_z = (pl.ds(0, 24), pl.ds(jnp.minimum(k + 1, 1), 24))

    def fine_block(block, split, split_before, field, field_after):
        adjoint[...] = jnp.zeros_like(adjoint)
        after = pl.ds(pl.multiple_of(480 * jnp.minimum(block + 1, 3), 480), 480)

        @pl.loop(0, 5)
        def _(i):
            lanes = pl.ds(pl.multiple_of(384 * i, 384), 384)
            field_after[:, lanes] = dot(spread[after, :], columns[:, lanes])
            lanes = pl.ds(pl.multiple_of(768 * i, 768), 768)
            adjoint[...] += dot(split_before[:, lanes], bx[lanes, :])
            for pair in range(2):
                for c in range(CHUNKS):
                    found = []
                    for h in range(2):
                        y = 4 * i + 2 * pair + h
                        corner = [[at[block, c, y + e, z, :] for e in (0, 1)] for z in rows_z]
                        step = [[by[block, c, y + e, z, :] for e in (0, 1)] for z in rows_z]
                        rows = pl.ds(pl.multiple_of(24 * y, 8), 24)
                        fractions = [
                            fraction(field[rows, NX * d + 128 * c : NX * d + 128 * c + 128]) for d in range(3)
                        ]
                        atlas = fx[c, y, pl.ds(20 * block, 24), :]
                        found.append(weights(atlas, corner, step, fractions))
                    rows = pl.ds(pl.multiple_of(96 * i + 48 * pair, 48), 48)
                    for d in range(3):
                        upper, lower = parts(jnp.concatenate([found[0][d], found[1][d]], axis=0))
                        lane = 2 * NX * d + 128 * c
                        split[rows, lane : lane + 128] = upper
                        split[rows, lane + NX : lane + NX + 128] = lower

        before = pl.ds(pl.multiple_of(480 * jnp.maximum(block - 1, 0), 480), 480)
        mixed[before, :] = adjoint[:, 0:128] + adjoint[:, 128:256]

    @pl.loop(0, 2)
    def _(two):
        fine_block(2 * two, split_a, split_b, field_a, field_b)
        fine_block(2 * two + 1, split_b, split_a, field_b, field_a)

    wide = dot(split_b[...], bx[...])
    mixed[1440:1920, :] = wide[:, 0:128] + wide[:, 128:256]
    f_part[...] = dot_gather(gather[...], mixed[...])
    around(k, s, f_part, f_parts, fsend, frecv, "start")
    f_parts[1, s] = f_part[...]

    for b in range(2):
        turned = dot_rows(gradient[48 * b : 48 * b + 48] * inverse, turn)
        result[120 + 48 * b : 168 + 48 * b, :] = turned[0:48]
    row = lax.broadcasted_iota(jnp.int32, (40, 128), 0) & 7

    around(k, s, f_part, f_parts, fsend, frecv, "wait_recv")
    before, middle, after = ((f_parts[i, 0] + f_parts[i, 1]) + (f_parts[i, 2] + f_parts[i, 3]) for i in range(3))
    middle = middle + jnp.where((row == 1) | (row == 2), pltpu.roll(before * has_prev, 36, 0), 0.0)
    middle = middle + jnp.where(row == 4, pltpu.roll(after * has_next, 4, 0), 0.0)
    middle = jnp.where((row >= 1) & (row <= 4), middle, 0.0)
    f_tile[...] = jnp.full((8, 128), jnp.sum(middle * middle))
    gather_along_z(k, s, f_tile, f_buf, f_sem)
    gather_across(k, s, f_buf, f_sem)

    for copy in (lat_to_next, lat_to_prev, z_to_next, z_to_prev, *mid_same):
        copy.wait_send()

    @pl.when(up)
    def _():
        for copy in (to_bef, *corner_up, *mid_up):
            copy.wait_send()

    @pl.when(down)
    def _():
        for copy in (to_aft, *corner_down, *mid_down):
            copy.wait_send()

    around(k, s, piece, pieces, psend, precv, "wait_send")
    around(k, s, f_part, f_parts, fsend, frecv, "wait_send")
    part_copies("wait_send")
    middle = pltpu.roll(middle, 39, 0)
    thirds = [from_lane(middle, 40 * d) for d in range(3)]

    gathered(f_buf, f_sem)
    squares = jnp.sum(f_buf[...].reshape(SLABS, 8, 128), axis=0)[0:1, :]
    inverse = lax.rsqrt(squares * (1.0 / 63360.0) + EPSILON)
    for d in range(3):
        result[40 * d : 40 * d + 40, :] = thirds[d] * inverse


def body(
    fixed_image,
    moving_image,
    lattice_fine,
    lattice_mid,
    lattice_coarse,
    offset_fine,
    offset_mid,
    offset_coarse,
):
    t = tables()
    vmem, smem, hbm = (pl.BlockSpec(memory_space=m) for m in (pltpu.VMEM, pltpu.SMEM, pl.ANY))
    shape = lambda *dims: jax.ShapeDtypeStruct(dims, F32)
    buf = lambda *dims: pltpu.VMEM(dims, F32)
    half = lambda *dims: pltpu.VMEM(dims, BF16)
    dma = lambda *dims: pltpu.SemaphoreType.DMA(dims)
    result = pl.pallas_call(
        kernel,
        out_shape=shape(264, 128),
        in_specs=[hbm, hbm, vmem, vmem, vmem, smem, smem, smem] + [hbm] * len(TABLES),
        out_specs=vmem,
        scratch_shapes=[
            *[pltpu.VMEM(t[n].shape[which is not None :], t[n].dtype) for n, which in TABLES.items()],
            buf(CHUNKS, 28, 96, 128), buf(CHUNKS, NY, 88, 128), buf(5, NZ, NX),
            *[buf(CHUNKS, 10, 8, 128)] * 4, *[buf(4, NZ, NX)] * 2, buf(4, CHUNKS, 2, 8, 128),
            *[buf(3, 5, 8, 128)] * 3, buf(3, 40, 128), buf(128, 128), buf(128, 128),
            *[buf(5, 24, 256)] * 4, buf(2, 3, 5, 8, 256),
            buf(2, 8, 128), buf(3, SECS, 2, 8, 128), buf(14, 32, 128), buf(5, 8, 128), buf(2, 15, 40, 128),
            buf(8, 128), buf(8, 4, 8, 128), buf(16, 128), buf(SECS, 16, 128), buf(16, 128), buf(8, 4, 16, 128),
            *[buf(4, CHUNKS, 21, 32, 128)] * 2, half(256, 3 * NX),
            *[buf(480, 3 * NX)] * 2, *[half(480, 6 * NX)] * 2, buf(480, 256), buf(1920, 128),
            buf(40, 128), buf(3, SECS, 40, 128), buf(8, 128), buf(8, 4, 8, 128),
            dma(10), dma(len(TABLES)), dma(18), dma(18), *[dma(3, SECS)] * 4, dma(SECS), dma(SECS), dma(4), dma(4), dma(4),
        ],
        compiler_params=pltpu.CompilerParams(
            collective_id=0, has_side_effects=True, vmem_limit_bytes=VMEM_LIMIT
        ),
        name="mega",
    )(
        jnp.transpose(moving_image, (1, 0, 2)),
        jnp.transpose(fixed_image, (1, 0, 2)),
        jnp.transpose(lattice_fine, (0, 2, 1, 3)),
        jnp.transpose(lattice_mid, (0, 3, 2, 1)),
        jnp.transpose(lattice_coarse, (0, 3, 2, 1)),
        offset_fine,
        jnp.transpose(offset_mid, (1, 2, 0)),
        jnp.transpose(offset_coarse, (0, 2, 1)),
        *(t[n] for n in TABLES),
    )
    fine, mid, coarse = pl.pallas_call(
        finish,
        out_shape=[shape(3, 5, 4, 33), shape(3, 9, 2, 33), shape(3, 3, 1, 9)],
        in_specs=[vmem],
        out_specs=[vmem] * 3,
        name="finish",
    )(result)
    return (
        jnp.transpose(fine, (0, 2, 1, 3)),
        jnp.transpose(mid, (0, 3, 2, 1)),
        jnp.transpose(coarse, (0, 3, 2, 1)),
    )


def solution(mesh):
    placed = (
        P("slab", "sec", None),
        P("slab", "sec", None),
        P(None, "slab", None, None),
        P(),
        P(),
        P(None, "slab", None),
        P(None, "slab", None),
        P(),
    )
    return jax.shard_map(
        body,
        mesh=mesh,
        in_specs=placed,
        out_specs=(P(None, "slab", None, None), P(), P()),
        check_vma=False,
    )
```

```python
import functools

import jax
import jax.numpy as jnp
import ml_dtypes
import numpy as np
from jax import lax
from jax.experimental import pallas as pl
from jax.experimental.pallas import tpu as pltpu
from jax.sharding import PartitionSpec as P

SP = 20
EPSILON = 1e-06
STEP_SIZE = 0.5
HIGHEST = lax.Precision.HIGHEST
F32 = jnp.float32
BF16 = jnp.bfloat16
MESH = pl.DeviceIdType.MESH
SLABS = 32
SECS = 4
NZ, NY, NX = 80, 20, 640
CHUNKS = NX // 128
LOG2E = 1.4426950408889634
VMEM_LIMIT = 58 * 1024 * 1024


def basis(rows, knots, factor, coarse):
    rows, knots = np.asarray(rows, np.float64), np.asarray(knots, np.float64)
    position = factor * rows + 0.5 * (factor - 1)
    centre = SP * coarse * knots + 0.5 * (coarse - 1)
    distance = np.abs((position[:, None] - centre[None, :]) / (SP * coarse))
    near = 2.0 / 3.0 - distance**2 + 0.5 * distance**3
    far = np.maximum(2.0 - distance, 0.0) ** 3 / 6.0
    return np.where(distance < 1.0, near, far)


def two_parts(values):
    high = values.astype(ml_dtypes.bfloat16)
    low = (values - high.astype(np.float64)).astype(ml_dtypes.bfloat16)
    return high, low


def right_parts(values):
    high, low = two_parts(values)
    return np.concatenate([high, low, high], axis=-2)


def wide_parts(values):
    high, low = two_parts(values)
    zero = np.zeros_like(high)
    return np.concatenate([np.concatenate([high, low], 1), np.concatenate([high, zero], 1)], 0)


def one_hot(condition):
    return condition.astype(ml_dtypes.bfloat16)


@functools.cache
def tables():
    t = {}
    rz, ry = np.zeros((4, 4, 24, 64)), np.zeros((4, NY, 64))
    z, y, x = np.arange(NZ), np.arange(NY), np.arange(NX)
    for r in range(4):
        for block in range(4):
            rows = z[20 * block : 20 * block + 20]
            for a in range(7):
                rz[r, block, :20, a:40:8] = basis(rows, [a - 1], 1, 1)
            for a in range(5):
                rz[r, block, :20, 40 + a : 56 : 8] = basis(rows, [a - 2], 1, 4)
                rz[r, block, :20, 56 + a : 57 + a] = basis(rows + 80 * r, [a - 2], 1, 16)
    for s in range(4):
        for a in range(7):
            ry[s, :, a:40:8] = basis(y + 20 * s, range(5), 1, 1)
        for a in range(5):
            ry[s, :, 40 + a : 56 : 8] = basis(y + 20 * s, range(2), 1, 4)
            ry[s, :, 56 + a : 57 + a] = basis(y + 20 * s, [0], 1, 16)
    whole = rz[:, None, :, None] * ry[None, :, None, :, None, :]
    high, low = two_parts(whole.reshape(16, 1920, 64))
    t["spread"] = np.concatenate([high, low, high, low], axis=2)
    t["gather"] = np.concatenate([high[:4, :, :40], low[:4, :, :40]], axis=2).transpose(0, 2, 1)
    across = np.zeros((3, 128, NX))
    across[0, :33] = basis(x, range(33), 1, 1).T
    across[1, :9] = basis(x, range(9), 1, 4).T
    across[2, :3] = basis(x, range(3), 1, 16).T
    t["bt"] = right_parts(-LOG2E * across)
    along = np.zeros((3, NX, 128))
    for d in range(3):
        along[d, :, 40 * d : 40 * d + 33] = basis(x, range(33), 1, 1)
    t["bx"] = np.concatenate([wide_parts(along[d]) for d in range(3)], axis=0)
    rz, ry = np.zeros((4, 24, 32)), np.zeros((4, 5, 32))
    z, y, x = np.arange(20), np.arange(5), np.arange(160)
    for r in range(4):
        for a in range(4):
            rz[r, :20, a:16:8] = basis(z, [a - 1], 4, 4)
        for a in range(5):
            rz[r, :20, 16 + a : 17 + a] = basis(z + 20 * r, [a - 2], 4, 16)
    for s in range(4):
        for a in range(4):
            ry[s, :, a:16:8] = basis(y + 5 * s, range(2), 4, 4)
        for a in range(5):
            ry[s, :, 16 + a : 17 + a] = basis(y + 5 * s, [0], 4, 16)
    whole = np.zeros((16, 128, 32))
    whole[:, :120] = (rz[:, None, None] * ry[None, :, :, None]).reshape(16, 120, 32)
    high, low = two_parts(whole)
    t["mspread"] = np.concatenate([high, high, low, np.zeros_like(low)], axis=2)
    t["mgather"] = np.concatenate([high[:, :, :16], low[:, :, :16]], axis=2).transpose(0, 2, 1)
    across = np.zeros((2, 128, 256))
    across[0, :9, :160] = basis(x, range(9), 4, 4).T
    across[1, :3, :160] = basis(x, range(3), 4, 16).T
    t["mbt"] = right_parts(-LOG2E * across)
    along = np.zeros((3, 256, 128))
    for d in range(3):
        along[d, :160, 16 * d : 16 * d + 9] = basis(x, range(9), 4, 4)
    t["mbx"] = wide_parts(along.reshape(768, 128))
    rz = np.zeros((4, 8, 32))
    z, y, x = np.arange(5), np.arange(5), np.arange(40)
    for r in range(4):
        for a in range(4):
            rz[r, :5, a : a + 1] = basis(z + 5 * r, [a - 1], 16, 16)
    whole = np.zeros((4, 128, 32))
    whole[:, :40] = (rz[:, None] * basis(y, [0], 16, 16)[None, :, None]).reshape(4, 40, 32)
    high, low = two_parts(whole)
    t["cspread"] = np.concatenate([high, high, low, np.zeros_like(low)], axis=2)
    t["cgather"] = np.concatenate([high[:, :, :16], low[:, :, :16]], axis=2).transpose(0, 2, 1)
    across = np.zeros((128, 128))
    across[:3, :40] = basis(x, range(3), 16, 16).T
    t["cbt"] = right_parts(-LOG2E * across)
    along = np.zeros((3, 128, 128))
    for d in range(3):
        along[d, :40, 16 * d : 16 * d + 3] = basis(x, range(3), 16, 16)
    t["cbx"] = wide_parts(along.reshape(384, 128))
    row, column = np.arange(NX)[:, None], np.arange(256)[None, :]
    t["px"] = one_hot(row // 4 == column)
    row, column = np.arange(120)[:, None], np.arange(400)[None, :]
    t["pz"] = one_hot((row // 24 == column // 80) & (row % 24 == column % 80 // 4))
    row, column = np.arange(512)[:, None], np.arange(128)[None, :]
    t["pcx"] = one_hot((row % 256 < 160) & (row // 256 * 64 + row % 256 // 4 == column))
    row, column = np.arange(16)[:, None], np.arange(48)[None, :]
    t["pcz"] = one_hot((row // 8 == column // 24) & (column % 24 < 20) & (row % 8 == column % 24 // 4))
    row, column, place = np.arange(16)[:, None], np.arange(128)[None, :], np.arange(32)[:, None, None]
    knot = place - 1 - row // 8 + row % 8
    t["rows_m"] = one_hot((knot == column) & (column < 33))
    t["rows_c"] = one_hot((knot == column) & (column < 9))[:8]
    row, column, place = np.arange(24)[:, None], np.arange(256)[None, :], np.arange(8)[:, None, None]
    knot = np.where(row < 16, row - 2, row - 16 + place - 2)
    found = (knot == column // 32 - 1 + column % 8) & (column % 8 < 4) & (knot >= 0) & (knot < 9)
    t["sum_c"] = one_hot(found)
    row, column, place = np.arange(112)[:, None], np.arange(512)[None, :], np.arange(32)[:, None, None]
    knot = np.where(row < 96, row % 48 - 2, row % 8 + place - 2)
    b = np.where(row < 96, row // 48, (row - 96) // 8)
    found = (knot == column // 16 - 1 + column % 8) & (column % 8 < 4) & (column // 8 % 2 == b)
    t["sum_m"] = one_hot(found & (knot >= 0) & (knot < 33))
    return t


def dot(a, b):
    return jnp.dot(a, b, preferred_element_type=F32)


def dot_rows(a, b):
    return lax.dot_general(
        a, b, (((0,), (0,)), ((), ())), precision=HIGHEST, preferred_element_type=F32
    )


def parts(values):
    high = values.astype(BF16)
    return high, (values - high.astype(F32)).astype(BF16)


def dot3(a, right):
    high, low = parts(a)
    return dot(jnp.concatenate([high, high, low], axis=1), right)


def dot_wide(a, table):
    wide = dot(jnp.concatenate(parts(a), axis=1), table)
    return wide[:, 0:128] + wide[:, 128:256]


def dot_exact(table, b):
    wide = dot(table, jnp.concatenate(parts(b), axis=1))
    return wide[:, 0:128] + wide[:, 128:256]


def dot_gather(table, b):
    n = table.shape[0] // 2
    wide = dot(table, jnp.concatenate(parts(b), axis=1))
    return (wide[0:n, 0:128] + wide[0:n, 128:256]) + wide[n:, 0:128]


def stacked(column, n):
    high, low = parts(jnp.concatenate([column, jnp.zeros((32 - n, column.shape[1]), F32)], axis=0))
    return jnp.concatenate([high, low, high, jnp.zeros_like(low)], axis=0)


def from_lane(values, lane):
    return values if lane == 0 else pltpu.roll(values, 128 - lane, 1)


def shift_lanes(chunks, shift):
    amount = (128 - shift) & 127
    rolled = [pltpu.roll(chunk, amount, 1) for chunk in chunks]
    lane = lax.broadcasted_iota(jnp.int32, chunks[0].shape, 1)
    first = lane < jnp.maximum(-shift, 0)
    last = lane >= 128 - jnp.maximum(shift, 0)
    zero = jnp.zeros_like(chunks[0])
    padded = [zero, *rolled, zero]
    return [
        jnp.where(first, padded[j], jnp.where(last, padded[j + 2], padded[j + 1]))
        for j in range(len(chunks))
    ]


def fraction(exponent):
    grown = jnp.exp2(exponent)
    frac = pl.reciprocal(1.0 + grown, approx=True)
    return frac, frac * (grown * frac)


def weights(fixed, corner, step, fractions):
    (fz, gz), (fy, gy), (fx, gx) = fractions
    line = [[corner[z][y] + fx * step[z][y] for y in (0, 1)] for z in (0, 1)]
    rise = [line[z][1] - line[z][0] for z in (0, 1)]
    plane = [line[z][0] + fy * rise[z] for z in (0, 1)]
    slope_z = plane[1] - plane[0]
    residual = (plane[0] + fz * slope_z) - fixed
    slope_y = rise[0] + fz * (rise[1] - rise[0])
    along = [step[z][0] + fy * (step[z][1] - step[z][0]) for z in (0, 1)]
    slope_x = along[0] + fz * (along[1] - along[0])
    return [
        (residual * slope_z) * gz,
        (residual * slope_y) * gy,
        (residual * slope_x) * gx,
    ]


def greet(k, s):
    barrier = pltpu.get_barrier_semaphore()

    def signal(slab, sec):
        pl.semaphore_signal(barrier, inc=1, device_id=(slab, sec), device_id_type=MESH)

    @pl.loop(1, SLABS)
    def _(i):
        signal((k + i) & (SLABS - 1), s)

    for i in range(1, SECS):
        other = (s + i) & (SECS - 1)
        signal(k, other)
        signal((k + 1) & (SLABS - 1), other)
        signal((k + SLABS - 1) & (SLABS - 1), other)
    return lambda: pl.semaphore_wait(barrier, SLABS - 1 + 3 * (SECS - 1))


def broadcast_start(k, s, tile, buffer, send_sem, recv_sem):
    @pl.loop(0, SLABS - 1)
    def _(i):
        pltpu.make_async_remote_copy(
            src_ref=tile,
            dst_ref=buffer.at[k],
            send_sem=send_sem,
            recv_sem=recv_sem,
            device_id=((k + 16 + i + (i > 15).astype(jnp.int32)) & (SLABS - 1), s),
            device_id_type=MESH,
        ).start()


def broadcast_wait(buffer, send_sem, recv_sem):
    part = buffer.at[pl.ds(0, SLABS - 1)]
    pltpu.make_async_copy(part, part, recv_sem).wait()
    pltpu.make_async_copy(part, part, send_sem).wait()


def remote(src, dst, send_sem, recv_sem, device):
    return pltpu.make_async_remote_copy(
        src_ref=src,
        dst_ref=dst,
        send_sem=send_sem,
        recv_sem=recv_sem,
        device_id=device,
        device_id_type=MESH,
    )


def around(k, s, source, buffer, send, recv, act):
    slabs = ((k + SLABS - 1) & (SLABS - 1), k, (k + 1) & (SLABS - 1))

    def one(dk, other):
        if act == "wait_recv":
            copy = remote(source, buffer.at[dk, other], send.at[dk, other], recv.at[dk, other], (k, other))
        else:
            copy = remote(
                source, buffer.at[2 - dk, s], send.at[dk, other], recv.at[2 - dk, s], (slabs[dk], other)
            )
        getattr(copy, act)()

    for dk in (0, 2):
        for other in range(SECS):
            one(dk, other)
    for i in range(1, SECS):
        one(1, (s + i) & (SECS - 1))


TABLES = {
    "px": None, "pz": None, "pcx": None, "pcz": None,
    "rows_m": "k", "rows_c": "q", "cspread": "r", "cgather": "r", "cbt": None, "cbx": None,
    "sum_c": "q", "mspread": "rs", "mgather": "rs", "mbt": None, "mbx": None,
    "spread": "rs", "gather": "s", "bt": None, "bx": None, "sum_m": "k",
}


def finish(result, fine_out, mid_out, coarse_out):
    for d in range(3):
        for b in range(5):
            row = 40 * d + 8 * b
            fine_out[d, b] = result[row : row + 4, 0:33]
        for a in range(9):
            for b in range(2):
                row = 120 + 48 * b + 16 * d + a
                mid_out[d, a, b : b + 1, :] = result[row : row + 1, 0:33]
        for a in range(3):
            row = 216 + 16 * d + a
            coarse_out[d, a] = result[row : row + 1, 0:9]


def kernel(
    moving, fixed, lat_fine, lat_mid, lat_coarse, off_fine, off_mid, off_coarse, *refs
):
    n = len(TABLES)
    stored, refs = refs[:n], refs[n:]
    result, *refs = refs
    t = dict(zip(TABLES, refs[:n]))
    (
        pad, fx, sums, zlo, zhi, z_bef, z_aft, y_bef, y_aft, corners,
        lf_own, lf_prev, lf_next, lf, mt, ct,
        pooled_m, pooled_f, pm_bef, pm_aft, pm_halo,
        piece, pieces, cv, cf, mm,
        c_tile, c_buf, m_part, m_parts, m_tile, m_buf,
        at, by, columns, field_a, field_b, split_a, split_b, adjoint, mixed,
        f_part, f_parts, f_tile, f_buf,
        load_sem, table_sem, send, recv, psend, precv, fsend, frecv, tsend, trecv, bsem,
    ) = refs[n:]
    k, s = lax.axis_index("slab"), lax.axis_index("sec")
    nxt, prv = (k + 1) & (SLABS - 1), (k + SLABS - 1) & (SLABS - 1)
    q, r = k >> 2, k & 3
    has_prev, has_next = (k > 0).astype(F32), (k < SLABS - 1).astype(F32)
    up, down = s < SECS - 1, s > 0
    own_y, own_z = pl.ds(4, NY), pl.ds(8, NZ)

    load_moving = [
        pltpu.make_async_copy(
            moving.at[:, :, pl.ds(128 * c, 128)], pad.at[c, own_y, own_z], load_sem.at[c]
        )
        for c in range(CHUNKS)
    ]
    load_fixed = [
        pltpu.make_async_copy(
            fixed.at[:, :, pl.ds(128 * c, 128)], fx.at[c, :, pl.ds(0, NZ)], load_sem.at[CHUNKS + c]
        )
        for c in range(CHUNKS)
    ]
    place = {"k": k, "q": q, "r": r, "s": s, "rs": 4 * r + s}
    load_table = {}
    for i, (name, which) in enumerate(TABLES.items()):
        source = stored[i] if which is None else stored[i].at[place[which]]
        load_table[name] = pltpu.make_async_copy(source, t[name], table_sem.at[i])
    for copy in load_moving:
        copy.start()
    all_here = greet(k, s)
    for copy in (*load_fixed, *load_table.values()):
        copy.start()

    def table(name):
        load_table[name].wait()
        return t[name]

    lat_to_next = remote(lf_own, lf_prev, send.at[0], recv.at[0], (nxt, s))
    lat_to_prev = remote(lf_own, lf_next, send.at[1], recv.at[1], (prv, s))
    z_to_next = remote(zhi, z_bef, send.at[2], recv.at[2], (nxt, s))
    z_to_prev = remote(zlo, z_aft, send.at[3], recv.at[3], (prv, s))
    to_bef = remote(moving.at[pl.ds(16, 4)], y_bef, send.at[4], recv.at[4], (k, s + 1))
    to_aft = remote(moving.at[pl.ds(0, 4)], y_aft, send.at[5], recv.at[5], (k, s - 1))
    first, last = pl.ds(0, 2), pl.ds(8, 2)
    corner_up = [
        remote(zhi.at[:, last], corners.at[0], send.at[6], recv.at[6], (nxt, s + 1)),
        remote(zlo.at[:, last], corners.at[1], send.at[7], recv.at[7], (prv, s + 1)),
    ]
    corner_down = [
        remote(zhi.at[:, first], corners.at[2], send.at[8], recv.at[8], (nxt, s - 1)),
        remote(zlo.at[:, first], corners.at[3], send.at[9], recv.at[9], (prv, s - 1)),
    ]
    head, tail = pl.ds(0, 8), pl.ds(16, 8)
    mid_same = [
        remote(pooled_m.at[:, tail], pm_halo.at[0, 1], send.at[10], recv.at[10], (nxt, s)),
        remote(pooled_m.at[:, head], pm_halo.at[1, 1], send.at[11], recv.at[11], (prv, s)),
    ]
    mid_up = [
        remote(pooled_m, pm_bef, send.at[12], recv.at[12], (k, s + 1)),
        remote(pooled_m.at[:, tail], pm_halo.at[0, 0], send.at[13], recv.at[13], (nxt, s + 1)),
        remote(pooled_m.at[:, head], pm_halo.at[1, 0], send.at[14], recv.at[14], (prv, s + 1)),
    ]
    mid_down = [
        remote(pooled_m, pm_aft, send.at[15], recv.at[15], (k, s - 1)),
        remote(pooled_m.at[:, tail], pm_halo.at[0, 2], send.at[16], recv.at[16], (nxt, s - 1)),
        remote(pooled_m.at[:, head], pm_halo.at[1, 2], send.at[17], recv.at[17], (prv, s - 1)),
    ]

    def start_y_halos(*parts_of_z):
        rows = [pl.ds(16 * part, 16) for part in parts_of_z]

        @pl.when(up)
        def _():
            for z in rows:
                remote(moving.at[pl.ds(16, 4), z], y_bef.at[:, z], send.at[4], recv.at[4], (k, s + 1)).start()

        @pl.when(down)
        def _():
            for z in rows:
                remote(moving.at[pl.ds(0, 4), z], y_aft.at[:, z], send.at[5], recv.at[5], (k, s - 1)).start()

    def start(*copies):
        for copy in copies:
            copy.start()

    def start_if(condition, *copies):
        @pl.when(condition)
        def _():
            start(*copies)

    for c in range(CHUNKS):
        pad[c, :, 0:8, :] = jnp.zeros((28, 8, 128), F32)
        pad[c, :, 88:96, :] = jnp.zeros((28, 8, 128), F32)
        fx[c, :, 80:88, :] = jnp.zeros((NY, 8, 128), F32)
        for block in range(4):
            at[block, c, :, 24:32, :] = jnp.zeros((21, 8, 128), F32)
            by[block, c, :, 24:32, :] = jnp.zeros((21, 8, 128), F32)
    all_here()
    start_y_halos(0, 1)
    for c in range(CHUNKS):
        load_moving[c].wait()

        @pl.loop(0, NY // 2, unroll=5)
        def _(pair):
            for half in range(2):
                rows = slice(4 * half, 4 * half + 4)
                zlo[c, pair, rows, :] = pad[c, 2 * pair + half + 4, 8:12, :]
                zhi[c, pair, rows, :] = pad[c, 2 * pair + half + 4, 84:88, :]

    px, pz = table("px"), table("pz")

    def pooled():
        high, low = parts(sums[...].reshape(400, NX))
        high, low = parts(dot(high, px[...]) + dot(low, px[...]))
        return ((dot(pz[...], high) + dot(pz[...], low)) * (1.0 / 64.0)).reshape(5, 24, 256)

    for c in range(CHUNKS):
        lanes = slice(128 * c, 128 * c + 128)

        @pl.loop(0, 5, unroll=5)
        def _(group):
            four = [pad[c, 4 * group + 4 + i, 8:88, :] for i in range(4)]
            sums[group, :, lanes] = (four[0] + four[1]) + (four[2] + four[3])

    pooled_m[...] = pooled()

    for c in range(CHUNKS):
        load_fixed[c].wait()
        lanes = slice(128 * c, 128 * c + 128)

        @pl.loop(0, 5, unroll=5)
        def _(group):
            four = [fx[c, 4 * group + i, 0:80, :] for i in range(4)]
            sums[group, :, lanes] = (four[0] + four[1]) + (four[2] + four[3])

    pooled_f[...] = pooled()

    halves = []
    for ref in (pooled_m, pooled_f):
        upper, lower = jnp.zeros((24, 256), F32), jnp.zeros((24, 256), F32)
        for i in range(5):
            keep = (i + s < 4).astype(F32)
            upper = upper + ref[i] * keep
            lower = lower + ref[i] * (1.0 - keep)
        halves.append(jnp.concatenate([upper, lower], axis=0))
    high, low = parts(jnp.concatenate(halves, axis=1))
    pcx, pcz = table("pcx")[...], table("pcz")[...]
    both = dot(high, pcx) + dot(low, pcx)
    piece[...] = (dot_exact(pcz, both) * (1.0 / 64.0)).reshape(2, 8, 128)
    around(k, s, piece, pieces, psend, precv, "start")
    pieces[1, s] = piece[...]
    start(*mid_same)
    start_if(up, *mid_up)
    start_if(down, *mid_down)

    for ref in (lf_own, mt, ct, cv, mm):
        ref[...] = jnp.zeros_like(ref)
    for d in range(3):
        for b in range(5):
            lf_own[d, b, 0:4, 0:33] = lat_fine[d, b]
        for a in range(9):
            for b in range(2):
                row = 32 * d + 16 * b + a
                mt[row : row + 1, 0:33] = lat_mid[d, a, b : b + 1]
        for a in range(3):
            ct[16 * d + a : 16 * d + a + 1, 0:9] = lat_coarse[d, a]
    start(lat_to_next, lat_to_prev, z_to_next)

    def pick_rows(name, ref):
        rows = table(name)[...]
        contract = (((1,), (1,)), ((), ()))
        high, low = parts(ref[...])
        return lax.dot_general(rows, high, contract, preferred_element_type=F32) + lax.dot_general(
            rows, low, contract, preferred_element_type=F32
        )

    rows_m, rows_c = pick_rows("rows_m", mt), pick_rows("rows_c", ct)
    cbt, cspread = table("cbt")[...], table("cspread")[...]
    column = dot3(jnp.concatenate([from_lane(rows_c[0:8], 16 * d) for d in range(3)], axis=0), cbt)
    column = jnp.concatenate([column[8 * d : 8 * d + 8] for d in range(3)], axis=1)
    exponent = dot(cspread, stacked(column, 8))[0:40]
    fractions_c = [fraction(exponent[:, 128 * d : 128 * d + 128]) for d in range(3)]
    cbx, cgather = table("cbx"), table("cgather")

    around(k, s, piece, pieces, psend, precv, "wait_recv")

    lane = lax.broadcasted_iota(jnp.int32, (5, 128), 1)
    for dk in range(3):
        scale = (has_prev, jnp.float32(1.0), has_next)[dk]
        rows = (slice(3, 8), slice(8, 13), slice(13, 18))[dk]
        for c in range(5):
            value = jnp.zeros((8, 128), F32)
            if c < 4:
                value = value + pieces[dk, c, 0]
            if c > 0:
                value = value + pieces[dk, c - 1, 1]
            cv[4 + c, rows, :] = jnp.where(lane < 40, value[0:5], 0.0) * scale
            if dk == 1:
                cf[c] = value
    fixed_c = pltpu.roll(cf[...].reshape(40, 128), 64, 1)

    oz, oy, ox = off_coarse[0, 0, q], off_coarse[1, 0, q], off_coarse[2, 0, q]
    a_z, b_z = [], []
    for e in (0, 1):
        window = cv[pl.ds(4 + oy, 6), pl.ds(8 + oz + e, 8), :].reshape(48, 128)
        here, there = shift_lanes([window], ox)[0], shift_lanes([window], ox + 1)[0]
        a_z.append(here)
        b_z.append(there - here)
    corner = [[a_z[z][8 * y : 8 * y + 40] for y in (0, 1)] for z in (0, 1)]
    step = [[b_z[z][8 * y : 8 * y + 40] for y in (0, 1)] for z in (0, 1)]
    total = jnp.concatenate(weights(fixed_c, corner, step, fractions_c), axis=1)
    total = dot_wide(jnp.concatenate([total, jnp.zeros((8, 384), F32)], axis=0), cbx[...])
    total = jnp.concatenate([total, jnp.zeros((80, 128), F32)], axis=0)
    c_tile[...] = dot_gather(cgather[...], total)[0:8]
    broadcast_start(k, s, c_tile, c_buf, bsem.at[0], bsem.at[1])
    c_buf[k] = c_tile[...]
    start_y_halos(2, 3)
    start(z_to_prev)
    start_if(up, *corner_up)
    start_if(down, *corner_down)

    mbt, mspread, mbx, mgather = table("mbt"), table("mspread"), table("mbx"), table("mgather")
    own = [from_lane(rows_m[0:8], 32 * d + 16 * b) for d in range(3) for b in range(2)]
    own = dot3(jnp.concatenate(own, axis=0), mbt[0])
    coarse = dot3(jnp.concatenate([from_lane(rows_c[8:16], 16 * d) for d in range(3)], axis=0), mbt[1])
    column = [
        jnp.concatenate([own[16 * d : 16 * d + 16], coarse[8 * d : 8 * d + 8]], axis=0) for d in range(3)
    ]
    base_m = dot(mspread[...], stacked(jnp.concatenate(column, axis=1), 24))[0:120]
    sum_c = table("sum_c")

    @pl.when(s == 0)
    def _():
        y_bef[...] = jnp.zeros_like(y_bef)
        corners[0:2] = jnp.zeros((2, CHUNKS, 2, 8, 128), F32)
        pm_bef[...] = jnp.zeros_like(pm_bef)
        pm_halo[:, 0] = jnp.zeros((2, 5, 8, 256), F32)

    @pl.when(s == SECS - 1)
    def _():
        y_aft[...] = jnp.zeros_like(y_aft)
        corners[2:4] = jnp.zeros((2, CHUNKS, 2, 8, 128), F32)
        pm_aft[...] = jnp.zeros_like(pm_aft)
        pm_halo[:, 2] = jnp.zeros((2, 5, 8, 256), F32)

    for copy in mid_same:
        copy.wait_recv()

    @pl.when(s > 0)
    def _():
        for copy in mid_up:
            copy.wait_recv()

    @pl.when(s < SECS - 1)
    def _():
        for copy in mid_down:
            copy.wait_recv()

    for c in range(2):
        lanes = slice(128 * c, 128 * c + 128)
        for e, whole in enumerate((pm_bef, pooled_m, pm_aft)):
            for y in range(5):
                mm[c, 5 * e + y, 4:8, :] = pm_halo[0, e, y, 0:4, lanes] * has_prev
                mm[c, 5 * e + y, 8:28, :] = whole[y, 0:20, lanes]
                mm[c, 5 * e + y, 28:32, :] = pm_halo[1, e, y, 0:4, lanes] * has_next

    oz, oy, ox = off_mid[0, 0, 0], off_mid[0, 0, 1], off_mid[0, 0, 2]
    a_z, b_z = [], []
    for e in (0, 1):
        window = [mm[c, pl.ds(5 + oy, 6), pl.ds(8 + oz + e, 24), :].reshape(144, 128) for c in range(2)]
        here, there = shift_lanes(window, ox), shift_lanes(window, ox + 1)
        a_z.append(here)
        b_z.append([there[c] - here[c] for c in range(2)])

    def make_window(block, oz, oy, ox, y):
        window = [pad[c, 4 + oy + y, pl.ds(20 * block + 8 + oz, 24), :] for c in range(CHUNKS)]
        here, there = shift_lanes(window, ox), shift_lanes(window, ox + 1)
        for c in range(CHUNKS):
            at[block, c, y, 0:24, :] = here[c]
            by[block, c, y, 0:24, :] = there[c] - here[c]

    def make_windows(blocks, ranges):
        @pl.loop(*blocks)
        def _(block):
            offsets = [off_fine[d, block, s] for d in range(3)]
            for first_y, last_y, unroll in ranges:
                pl.loop(first_y, last_y, unroll=unroll)(functools.partial(make_window, block, *offsets))

    make_windows((1, 3), ((4, 16, 3),))

    broadcast_wait(c_buf, bsem.at[0], bsem.at[1])
    gradient = dot_exact(sum_c[...], c_buf[...].reshape(256, 128))
    near_c = gradient[16:24]
    gradient = gradient[0:16]
    inverse = lax.rsqrt(jnp.sum(gradient * gradient) * (1.0 / 81.0) + EPSILON)

    near = dot3(jnp.concatenate([from_lane(near_c, 16 * d) for d in range(3)], axis=0), mbt[1])
    near = jnp.concatenate([near[8 * d : 8 * d + 8] for d in range(3)], axis=1)
    near = dot(mspread[...], stacked(jnp.concatenate([jnp.zeros((16, 768), F32), near], axis=0), 24))
    exponent = base_m - (STEP_SIZE * inverse) * near[0:120]
    fixed_m = pooled_f[...].reshape(120, 256)
    found = []
    for c in range(2):
        lanes = slice(128 * c, 128 * c + 128)
        corner = [[a_z[z][c][24 * y : 24 * y + 120] for y in (0, 1)] for z in (0, 1)]
        step = [[b_z[z][c][24 * y : 24 * y + 120] for y in (0, 1)] for z in (0, 1)]
        fractions = [fraction(exponent[:, 256 * d + 128 * c : 256 * d + 128 * c + 128]) for d in range(3)]
        found.append(weights(fixed_m[:, lanes], corner, step, fractions))
    total = jnp.concatenate([found[c][d] for d in range(3) for c in range(2)], axis=1)
    total = dot_wide(jnp.concatenate([total, jnp.zeros((8, 768), F32)], axis=0), mbx[...])
    m_part[...] = dot_gather(mgather[...], total)

    def part_copies(act):
        for i in range(1, SECS):
            other = (s + i) & (SECS - 1)
            slot = other if act == "wait_recv" else s
            getattr(remote(m_part, m_parts.at[slot], tsend.at[other], trecv.at[slot], (k, other)), act)()

    part_copies("start")
    start_y_halos(4)
    m_parts[s] = m_part[...]
    part_copies("wait_recv")
    m_tile[...] = (m_parts[0] + m_parts[1]) + (m_parts[2] + m_parts[3])
    broadcast_start(k, s, m_tile, m_buf, bsem.at[2], bsem.at[3])
    m_buf[k] = m_tile[...]

    gradient = gradient * inverse
    next_c = [
        from_lane(rows_c[8:16], 16 * d) - (STEP_SIZE * inverse) * from_lane(near_c, 16 * d) for d in range(3)
    ]
    turn_r = lax.broadcasted_iota(jnp.int32, (48, 128), 0)
    turn = jnp.where(turn_r == lax.broadcasted_iota(jnp.int32, (48, 128), 1) + 2, 1.0, 0.0)
    result[216:264, :] = dot_rows(gradient, turn[0:16])[0:48]

    for copy in (lat_to_next, lat_to_prev):
        copy.wait_recv()
    for d in range(3):
        for b in range(5):
            lf[d, 8 * b : 8 * b + 1, :] = lf_prev[d, b, 3:4, :] * has_prev
            lf[d, 8 * b + 1 : 8 * b + 5, :] = lf_own[d, b, 0:4, :]
            lf[d, 8 * b + 5 : 8 * b + 7, :] = lf_next[d, b, 0:2, :] * has_next
            lf[d, 8 * b + 7 : 8 * b + 8, :] = jnp.zeros((1, 128), F32)
    bt = table("bt")
    own = dot3(lf[...].reshape(120, 128), bt[0])
    mid = [from_lane(rows_m[8:16], 32 * d + 16 * b) for d in range(3) for b in range(2)]
    mid = dot3(jnp.concatenate(mid, axis=0), bt[1])
    coarse = dot3(jnp.concatenate(next_c, axis=0), bt[2])
    base_f = [
        jnp.concatenate(
            [own[40 * d : 40 * d + 40], mid[16 * d : 16 * d + 16], coarse[8 * d : 8 * d + 8]], axis=0
        )
        for d in range(3)
    ]
    base_f = jnp.concatenate(base_f, axis=1)

    for copy in (z_to_next, z_to_prev):
        copy.wait_recv()

    @pl.when(s > 0)
    def _():
        for copy in (to_bef, *corner_up):
            copy.wait_recv()

    @pl.when(s < SECS - 1)
    def _():
        for copy in (to_aft, *corner_down):
            copy.wait_recv()

    for c in range(CHUNKS):
        lanes = slice(128 * c, 128 * c + 128)
        pad[c, 0:4, 8:88, :] = y_bef[:, :, lanes]
        pad[c, 24:28, 8:88, :] = y_aft[:, :, lanes]

    @pl.loop(0, NY // 2, unroll=2)
    def _(pair):
        for half in range(2):
            rows = slice(4 * half, 4 * half + 4)
            for c in range(CHUNKS):
                pad[c, 2 * pair + half + 4, 4:8, :] = z_bef[c, pair, rows, :] * has_prev
                pad[c, 2 * pair + half + 4, 88:92, :] = z_aft[c, pair, rows, :] * has_next

    for y in range(4):
        rows = slice(4 * (y % 2), 4 * (y % 2) + 4)
        for c in range(CHUNKS):
            for n in range(2):
                where = slice(4, 8) if n == 0 else slice(88, 92)
                keep = has_prev if n == 0 else has_next
                pad[c, y, where, :] = corners[n, c, y // 2, rows, :] * keep
                pad[c, 24 + y, where, :] = corners[2 + n, c, y // 2, rows, :] * keep

    make_windows((1, 3), ((0, 4, 2), (16, 21, 5)))
    make_windows((0, 1), ((0, 21, 3),))
    make_windows((3, 4), ((0, 21, 3),))

    spread, gather, bx, sum_m = table("spread"), table("gather"), table("bx"), table("sum_m")

    broadcast_wait(m_buf, bsem.at[2], bsem.at[3])
    gradient = dot_exact(sum_m[...], m_buf[...].reshape(512, 128))
    near = gradient[96:112]
    gradient = gradient[0:96]
    inverse = lax.rsqrt(jnp.sum(gradient * gradient) * (1.0 / 1782.0) + EPSILON)

    near = dot3(jnp.concatenate([from_lane(near, 16 * d) for d in range(3)], axis=0), bt[1])
    near = jnp.concatenate([near[16 * d : 16 * d + 16] for d in range(3)], axis=1)
    near = jnp.concatenate([jnp.zeros((40, 3 * NX), F32), near, jnp.zeros((8, 3 * NX), F32)], axis=0)
    upper, lower = parts(base_f - (STEP_SIZE * inverse) * near)
    columns[0:64, :] = upper
    columns[64:128, :] = upper
    columns[128:192, :] = lower
    columns[192:256, :] = lower
    field_a[...] = dot(spread[0:480, :], columns[...])

    rows_z = (pl.ds(0, 24), pl.ds(jnp.minimum(k + 1, 1), 24))

    def fine_block(block, split, split_before, field, field_after):
        adjoint[...] = jnp.zeros_like(adjoint)
        after = pl.ds(pl.multiple_of(480 * jnp.minimum(block + 1, 3), 480), 480)

        @pl.loop(0, 5)
        def _(i):
            lanes = pl.ds(pl.multiple_of(384 * i, 384), 384)
            field_after[:, lanes] = dot(spread[after, :], columns[:, lanes])
            lanes = pl.ds(pl.multiple_of(768 * i, 768), 768)
            adjoint[...] += dot(split_before[:, lanes], bx[lanes, :])
            for pair in range(2):
                for c in range(CHUNKS):
                    found = []
                    for h in range(2):
                        y = 4 * i + 2 * pair + h
                        corner = [[at[block, c, y + e, z, :] for e in (0, 1)] for z in rows_z]
                        step = [[by[block, c, y + e, z, :] for e in (0, 1)] for z in rows_z]
                        rows = pl.ds(pl.multiple_of(24 * y, 8), 24)
                        fractions = [
                            fraction(field[rows, NX * d + 128 * c : NX * d + 128 * c + 128]) for d in range(3)
                        ]
                        atlas = fx[c, y, pl.ds(20 * block, 24), :]
                        found.append(weights(atlas, corner, step, fractions))
                    rows = pl.ds(pl.multiple_of(96 * i + 48 * pair, 48), 48)
                    for d in range(3):
                        upper, lower = parts(jnp.concatenate([found[0][d], found[1][d]], axis=0))
                        lane = 2 * NX * d + 128 * c
                        split[rows, lane : lane + 128] = upper
                        split[rows, lane + NX : lane + NX + 128] = lower

        before = pl.ds(pl.multiple_of(480 * jnp.maximum(block - 1, 0), 480), 480)
        mixed[before, :] = adjoint[:, 0:128] + adjoint[:, 128:256]

    @pl.loop(0, 2)
    def _(two):
        fine_block(2 * two, split_a, split_b, field_a, field_b)
        fine_block(2 * two + 1, split_b, split_a, field_b, field_a)

    wide = dot(split_b[...], bx[...])
    mixed[1440:1920, :] = wide[:, 0:128] + wide[:, 128:256]
    f_part[...] = dot_gather(gather[...], mixed[...])
    around(k, s, f_part, f_parts, fsend, frecv, "start")
    f_parts[1, s] = f_part[...]

    for b in range(2):
        turned = dot_rows(gradient[48 * b : 48 * b + 48] * inverse, turn)
        result[120 + 48 * b : 168 + 48 * b, :] = turned[0:48]
    row = lax.broadcasted_iota(jnp.int32, (40, 128), 0) & 7

    around(k, s, f_part, f_parts, fsend, frecv, "wait_recv")
    before, middle, after = ((f_parts[i, 0] + f_parts[i, 1]) + (f_parts[i, 2] + f_parts[i, 3]) for i in range(3))
    middle = middle + jnp.where((row == 1) | (row == 2), pltpu.roll(before * has_prev, 36, 0), 0.0)
    middle = middle + jnp.where(row == 4, pltpu.roll(after * has_next, 4, 0), 0.0)
    middle = jnp.where((row >= 1) & (row <= 4), middle, 0.0)
    f_tile[...] = jnp.full((8, 128), jnp.sum(middle * middle))
    broadcast_start(k, s, f_tile, f_buf, bsem.at[4], bsem.at[5])
    f_buf[k] = f_tile[...]

    for copy in (lat_to_next, lat_to_prev, z_to_next, z_to_prev, *mid_same):
        copy.wait_send()

    @pl.when(up)
    def _():
        for copy in (to_bef, *corner_up, *mid_up):
            copy.wait_send()

    @pl.when(down)
    def _():
        for copy in (to_aft, *corner_down, *mid_down):
            copy.wait_send()

    around(k, s, piece, pieces, psend, precv, "wait_send")
    around(k, s, f_part, f_parts, fsend, frecv, "wait_send")
    part_copies("wait_send")
    middle = pltpu.roll(middle, 39, 0)
    thirds = [from_lane(middle, 40 * d) for d in range(3)]

    broadcast_wait(f_buf, bsem.at[4], bsem.at[5])
    squares = jnp.sum(f_buf[...], axis=0)[0:1, :]
    inverse = lax.rsqrt(squares * (1.0 / 63360.0) + EPSILON)
    for d in range(3):
        result[40 * d : 40 * d + 40, :] = thirds[d] * inverse


def body(
    fixed_image,
    moving_image,
    lattice_fine,
    lattice_mid,
    lattice_coarse,
    offset_fine,
    offset_mid,
    offset_coarse,
):
    t = tables()
    vmem, smem, hbm = (pl.BlockSpec(memory_space=m) for m in (pltpu.VMEM, pltpu.SMEM, pl.ANY))
    shape = lambda *dims: jax.ShapeDtypeStruct(dims, F32)
    buf = lambda *dims: pltpu.VMEM(dims, F32)
    half = lambda *dims: pltpu.VMEM(dims, BF16)
    dma = lambda *dims: pltpu.SemaphoreType.DMA(dims)
    result = pl.pallas_call(
        kernel,
        out_shape=shape(264, 128),
        in_specs=[hbm, hbm, vmem, vmem, vmem, smem, smem, smem] + [hbm] * len(TABLES),
        out_specs=vmem,
        scratch_shapes=[
            *[pltpu.VMEM(t[n].shape[which is not None :], t[n].dtype) for n, which in TABLES.items()],
            buf(CHUNKS, 28, 96, 128), buf(CHUNKS, NY, 88, 128), buf(5, NZ, NX),
            *[buf(CHUNKS, 10, 8, 128)] * 4, *[buf(4, NZ, NX)] * 2, buf(4, CHUNKS, 2, 8, 128),
            *[buf(3, 5, 8, 128)] * 3, buf(3, 40, 128), buf(128, 128), buf(128, 128),
            *[buf(5, 24, 256)] * 4, buf(2, 3, 5, 8, 256),
            buf(2, 8, 128), buf(3, SECS, 2, 8, 128), buf(14, 32, 128), buf(5, 8, 128), buf(2, 15, 40, 128),
            buf(8, 128), buf(SLABS, 8, 128), buf(16, 128), buf(SECS, 16, 128), buf(16, 128), buf(SLABS, 16, 128),
            *[buf(4, CHUNKS, 21, 32, 128)] * 2, half(256, 3 * NX),
            *[buf(480, 3 * NX)] * 2, *[half(480, 6 * NX)] * 2, buf(480, 256), buf(1920, 128),
            buf(40, 128), buf(3, SECS, 40, 128), buf(8, 128), buf(SLABS, 8, 128),
            dma(10), dma(len(TABLES)), dma(18), dma(18), *[dma(3, SECS)] * 4, dma(SECS), dma(SECS), dma(6),
        ],
        compiler_params=pltpu.CompilerParams(
            collective_id=0, has_side_effects=True, vmem_limit_bytes=VMEM_LIMIT
        ),
        name="mega",
    )(
        jnp.transpose(moving_image, (1, 0, 2)),
        jnp.transpose(fixed_image, (1, 0, 2)),
        jnp.transpose(lattice_fine, (0, 2, 1, 3)),
        jnp.transpose(lattice_mid, (0, 3, 2, 1)),
        jnp.transpose(lattice_coarse, (0, 3, 2, 1)),
        offset_fine,
        jnp.transpose(offset_mid, (1, 2, 0)),
        jnp.transpose(offset_coarse, (0, 2, 1)),
        *(t[n] for n in TABLES),
    )
    fine, mid, coarse = pl.pallas_call(
        finish,
        out_shape=[shape(3, 5, 4, 33), shape(3, 9, 2, 33), shape(3, 3, 1, 9)],
        in_specs=[vmem],
        out_specs=[vmem] * 3,
        name="finish",
    )(result)
    return (
        jnp.transpose(fine, (0, 2, 1, 3)),
        jnp.transpose(mid, (0, 3, 2, 1)),
        jnp.transpose(coarse, (0, 3, 2, 1)),
    )


def solution(mesh):
    placed = (
        P("slab", "sec", None),
        P("slab", "sec", None),
        P(None, "slab", None, None),
        P(),
        P(),
        P(None, "slab", None),
        P(None, "slab", None),
        P(),
    )
    return jax.shard_map(
        body,
        mesh=mesh,
        in_specs=placed,
        out_specs=(P(None, "slab", None, None), P(), P()),
        check_vma=False,
    )
```

```python
import functools

import jax
import jax.numpy as jnp
import ml_dtypes
import numpy as np
from jax import lax
from jax.experimental import pallas as pl
from jax.experimental.pallas import tpu as pltpu
from jax.sharding import PartitionSpec as P

SP = 20
EPSILON = 1e-06
STEP_SIZE = 0.5
HIGHEST = lax.Precision.HIGHEST
F32 = jnp.float32
BF16 = jnp.bfloat16
MESH = pl.DeviceIdType.MESH
SLABS = 32
SECS = 4
NZ, NY, NX = 80, 20, 640
CHUNKS = NX // 128
LOG2E = 1.4426950408889634
VMEM_LIMIT = 58 * 1024 * 1024


def basis(rows, knots, factor, coarse):
    rows, knots = np.asarray(rows, np.float64), np.asarray(knots, np.float64)
    position = factor * rows + 0.5 * (factor - 1)
    centre = SP * coarse * knots + 0.5 * (coarse - 1)
    distance = np.abs((position[:, None] - centre[None, :]) / (SP * coarse))
    near = 2.0 / 3.0 - distance**2 + 0.5 * distance**3
    far = np.maximum(2.0 - distance, 0.0) ** 3 / 6.0
    return np.where(distance < 1.0, near, far)


def two_parts(values):
    high = values.astype(ml_dtypes.bfloat16)
    low = (values - high.astype(np.float64)).astype(ml_dtypes.bfloat16)
    return high, low


def right_parts(values):
    high, low = two_parts(values)
    return np.concatenate([high, low, high], axis=-2)


def wide_parts(values):
    high, low = two_parts(values)
    zero = np.zeros_like(high)
    return np.concatenate([np.concatenate([high, low], 1), np.concatenate([high, zero], 1)], 0)


def one_hot(condition):
    return condition.astype(ml_dtypes.bfloat16)


@functools.cache
def tables():
    t = {}
    rz, ry = np.zeros((4, 4, 24, 64)), np.zeros((4, NY, 64))
    z, y, x = np.arange(NZ), np.arange(NY), np.arange(NX)
    for r in range(4):
        for block in range(4):
            rows = z[20 * block : 20 * block + 20]
            for a in range(7):
                rz[r, block, :20, a:40:8] = basis(rows, [a - 1], 1, 1)
            for a in range(5):
                rz[r, block, :20, 40 + a : 56 : 8] = basis(rows, [a - 2], 1, 4)
                rz[r, block, :20, 56 + a : 57 + a] = basis(rows + 80 * r, [a - 2], 1, 16)
    for s in range(4):
        for a in range(7):
            ry[s, :, a:40:8] = basis(y + 20 * s, range(5), 1, 1)
        for a in range(5):
            ry[s, :, 40 + a : 56 : 8] = basis(y + 20 * s, range(2), 1, 4)
            ry[s, :, 56 + a : 57 + a] = basis(y + 20 * s, [0], 1, 16)
    whole = rz[:, None, :, None] * ry[None, :, None, :, None, :]
    high, low = two_parts(whole.reshape(16, 1920, 64))
    t["spread"] = np.concatenate([high, low, high, low], axis=2)
    t["gather"] = np.concatenate([high[:4, :, :40], low[:4, :, :40]], axis=2).transpose(0, 2, 1)
    across = np.zeros((3, 128, NX))
    across[0, :33] = basis(x, range(33), 1, 1).T
    across[1, :9] = basis(x, range(9), 1, 4).T
    across[2, :3] = basis(x, range(3), 1, 16).T
    t["bt"] = right_parts(-LOG2E * across)
    along = np.zeros((3, NX, 128))
    for d in range(3):
        along[d, :, 40 * d : 40 * d + 33] = basis(x, range(33), 1, 1)
    t["bx"] = np.concatenate([wide_parts(along[d]) for d in range(3)], axis=0)
    rz, ry = np.zeros((4, 24, 32)), np.zeros((4, 5, 32))
    z, y, x = np.arange(20), np.arange(5), np.arange(160)
    for r in range(4):
        for a in range(4):
            rz[r, :20, a:16:8] = basis(z, [a - 1], 4, 4)
        for a in range(5):
            rz[r, :20, 16 + a : 17 + a] = basis(z + 20 * r, [a - 2], 4, 16)
    for s in range(4):
        for a in range(4):
            ry[s, :, a:16:8] = basis(y + 5 * s, range(2), 4, 4)
        for a in range(5):
            ry[s, :, 16 + a : 17 + a] = basis(y + 5 * s, [0], 4, 16)
    whole = np.zeros((16, 128, 32))
    whole[:, :120] = (rz[:, None, None] * ry[None, :, :, None]).reshape(16, 120, 32)
    high, low = two_parts(whole)
    t["mspread"] = np.concatenate([high, high, low, np.zeros_like(low)], axis=2)
    t["mgather"] = np.concatenate([high[:, :, :16], low[:, :, :16]], axis=2).transpose(0, 2, 1)
    across = np.zeros((2, 128, 256))
    across[0, :9, :160] = basis(x, range(9), 4, 4).T
    across[1, :3, :160] = basis(x, range(3), 4, 16).T
    t["mbt"] = right_parts(-LOG2E * across)
    along = np.zeros((3, 256, 128))
    for d in range(3):
        along[d, :160, 16 * d : 16 * d + 9] = basis(x, range(9), 4, 4)
    t["mbx"] = wide_parts(along.reshape(768, 128))
    rz = np.zeros((4, 8, 32))
    z, y, x = np.arange(5), np.arange(5), np.arange(40)
    for r in range(4):
        for a in range(4):
            rz[r, :5, a : a + 1] = basis(z + 5 * r, [a - 1], 16, 16)
    whole = np.zeros((4, 128, 32))
    whole[:, :40] = (rz[:, None] * basis(y, [0], 16, 16)[None, :, None]).reshape(4, 40, 32)
    high, low = two_parts(whole)
    t["cspread"] = np.concatenate([high, high, low, np.zeros_like(low)], axis=2)
    t["cgather"] = np.concatenate([high[:, :, :16], low[:, :, :16]], axis=2).transpose(0, 2, 1)
    across = np.zeros((128, 128))
    across[:3, :40] = basis(x, range(3), 16, 16).T
    t["cbt"] = right_parts(-LOG2E * across)
    along = np.zeros((3, 128, 128))
    for d in range(3):
        along[d, :40, 16 * d : 16 * d + 3] = basis(x, range(3), 16, 16)
    t["cbx"] = wide_parts(along.reshape(384, 128))
    row, column = np.arange(NX)[:, None], np.arange(256)[None, :]
    t["px"] = one_hot(row // 4 == column)
    row, column = np.arange(120)[:, None], np.arange(400)[None, :]
    t["pz"] = one_hot((row // 24 == column // 80) & (row % 24 == column % 80 // 4))
    row, column = np.arange(512)[:, None], np.arange(128)[None, :]
    t["pcx"] = one_hot((row % 256 < 160) & (row // 256 * 64 + row % 256 // 4 == column))
    row, column = np.arange(16)[:, None], np.arange(48)[None, :]
    t["pcz"] = one_hot((row // 8 == column // 24) & (column % 24 < 20) & (row % 8 == column % 24 // 4))
    row, column, place = np.arange(16)[:, None], np.arange(128)[None, :], np.arange(32)[:, None, None]
    knot = place - 1 - row // 8 + row % 8
    t["rows_m"] = one_hot((knot == column) & (column < 33))
    t["rows_c"] = one_hot((knot == column) & (column < 9))[:8]
    row, column, place = np.arange(24)[:, None], np.arange(256)[None, :], np.arange(8)[:, None, None]
    knot = np.where(row < 16, row - 2, row - 16 + place - 2)
    found = (knot == column // 32 - 1 + column % 8) & (column % 8 < 4) & (knot >= 0) & (knot < 9)
    t["sum_c"] = one_hot(found)
    row, column, place = np.arange(112)[:, None], np.arange(512)[None, :], np.arange(32)[:, None, None]
    knot = np.where(row < 96, row % 48 - 2, row % 8 + place - 2)
    b = np.where(row < 96, row // 48, (row - 96) // 8)
    found = (knot == column // 16 - 1 + column % 8) & (column % 8 < 4) & (column // 8 % 2 == b)
    t["sum_m"] = one_hot(found & (knot >= 0) & (knot < 33))
    return t


def dot(a, b):
    return jnp.dot(a, b, preferred_element_type=F32)


def dot_rows(a, b):
    return lax.dot_general(
        a, b, (((0,), (0,)), ((), ())), precision=HIGHEST, preferred_element_type=F32
    )


def parts(values):
    high = values.astype(BF16)
    return high, (values - high.astype(F32)).astype(BF16)


def dot3(a, right):
    high, low = parts(a)
    return dot(jnp.concatenate([high, high, low], axis=1), right)


def dot_wide(a, table):
    wide = dot(jnp.concatenate(parts(a), axis=1), table)
    return wide[:, 0:128] + wide[:, 128:256]


def dot_exact(table, b):
    wide = dot(table, jnp.concatenate(parts(b), axis=1))
    return wide[:, 0:128] + wide[:, 128:256]


def dot_gather(table, b):
    n = table.shape[0] // 2
    wide = dot(table, jnp.concatenate(parts(b), axis=1))
    return (wide[0:n, 0:128] + wide[0:n, 128:256]) + wide[n:, 0:128]


def stacked(column, n):
    high, low = parts(jnp.concatenate([column, jnp.zeros((32 - n, column.shape[1]), F32)], axis=0))
    return jnp.concatenate([high, low, high, jnp.zeros_like(low)], axis=0)


def from_lane(values, lane):
    return values if lane == 0 else pltpu.roll(values, 128 - lane, 1)


def shift_lanes(chunks, shift):
    amount = (128 - shift) & 127
    rolled = [pltpu.roll(chunk, amount, 1) for chunk in chunks]
    lane = lax.broadcasted_iota(jnp.int32, chunks[0].shape, 1)
    first = lane < jnp.maximum(-shift, 0)
    last = lane >= 128 - jnp.maximum(shift, 0)
    zero = jnp.zeros_like(chunks[0])
    padded = [zero, *rolled, zero]
    return [
        jnp.where(first, padded[j], jnp.where(last, padded[j + 2], padded[j + 1]))
        for j in range(len(chunks))
    ]


def fraction(exponent):
    grown = jnp.exp2(exponent)
    frac = pl.reciprocal(1.0 + grown, approx=True)
    return frac, frac * (grown * frac)


def weights(fixed, corner, step, fractions):
    (fz, gz), (fy, gy), (fx, gx) = fractions
    line = [[corner[z][y] + fx * step[z][y] for y in (0, 1)] for z in (0, 1)]
    rise = [line[z][1] - line[z][0] for z in (0, 1)]
    plane = [line[z][0] + fy * rise[z] for z in (0, 1)]
    slope_z = plane[1] - plane[0]
    residual = (plane[0] + fz * slope_z) - fixed
    slope_y = rise[0] + fz * (rise[1] - rise[0])
    along = [step[z][0] + fy * (step[z][1] - step[z][0]) for z in (0, 1)]
    slope_x = along[0] + fz * (along[1] - along[0])
    return [
        (residual * slope_z) * gz,
        (residual * slope_y) * gy,
        (residual * slope_x) * gx,
    ]


def greet(k, s):
    barrier = pltpu.get_barrier_semaphore()

    def signal(slab, sec):
        pl.semaphore_signal(barrier, inc=1, device_id=(slab, sec), device_id_type=MESH)

    @pl.loop(1, SLABS)
    def _(i):
        signal((k + i) & (SLABS - 1), s)

    for i in range(1, SECS):
        other = (s + i) & (SECS - 1)
        signal(k, other)
        signal((k + 1) & (SLABS - 1), other)
        signal((k + SLABS - 1) & (SLABS - 1), other)
    return lambda: pl.semaphore_wait(barrier, SLABS - 1 + 3 * (SECS - 1))


def broadcast_start(k, s, tile, buffer, send_sem, recv_sem):
    @pl.loop(0, SLABS - 1)
    def _(i):
        pltpu.make_async_remote_copy(
            src_ref=tile,
            dst_ref=buffer.at[k],
            send_sem=send_sem,
            recv_sem=recv_sem,
            device_id=((k + 16 + i + (i > 15).astype(jnp.int32)) & (SLABS - 1), s),
            device_id_type=MESH,
        ).start()


def broadcast_wait(buffer, send_sem, recv_sem):
    part = buffer.at[pl.ds(0, SLABS - 1)]
    pltpu.make_async_copy(part, part, recv_sem).wait()
    pltpu.make_async_copy(part, part, send_sem).wait()


def remote(src, dst, send_sem, recv_sem, device):
    return pltpu.make_async_remote_copy(
        src_ref=src,
        dst_ref=dst,
        send_sem=send_sem,
        recv_sem=recv_sem,
        device_id=device,
        device_id_type=MESH,
    )


def around(k, s, source, buffer, send, recv, act):
    slabs = ((k + SLABS - 1) & (SLABS - 1), k, (k + 1) & (SLABS - 1))

    def one(dk, other):
        if act == "wait_recv":
            copy = remote(source, buffer.at[dk, other], send.at[dk, other], recv.at[dk, other], (k, other))
        else:
            copy = remote(
                source, buffer.at[2 - dk, s], send.at[dk, other], recv.at[2 - dk, s], (slabs[dk], other)
            )
        getattr(copy, act)()

    for dk in (0, 2):
        for other in range(SECS):
            one(dk, other)
    for i in range(1, SECS):
        one(1, (s + i) & (SECS - 1))


TABLES = {
    "px": None, "pz": None, "pcx": None, "pcz": None,
    "rows_m": "k", "rows_c": "q", "cspread": "r", "cgather": "r", "cbt": None, "cbx": None,
    "sum_c": "q", "mspread": "rs", "mgather": "rs", "mbt": None, "mbx": None,
    "spread": "rs", "gather": "s", "bt": None, "bx": None, "sum_m": "k",
}


def finish(result, fine_out, mid_out, coarse_out):
    for d in range(3):
        for b in range(5):
            row = 40 * d + 8 * b
            fine_out[d, b] = result[row : row + 4, 0:33]
        for a in range(9):
            for b in range(2):
                row = 120 + 48 * b + 16 * d + a
                mid_out[d, a, b : b + 1, :] = result[row : row + 1, 0:33]
        for a in range(3):
            row = 216 + 16 * d + a
            coarse_out[d, a] = result[row : row + 1, 0:9]


def kernel(
    moving, fixed, lat_fine, lat_mid, lat_coarse, off_fine, off_mid, off_coarse, *refs
):
    n = len(TABLES)
    stored, refs = refs[:n], refs[n:]
    result, *refs = refs
    t = dict(zip(TABLES, refs[:n]))
    (
        pad, fx, sums, zlo, zhi, z_bef, z_aft, y_bef, y_aft, corners,
        lf_own, lf_up, lf_down, lf_prev, lf_next, lf, mt, ct,
        pooled_m, pooled_f, pack_up, pack_down, pm_bef, pm_aft, pm_halo, pm_same,
        piece, pieces, cv, cf, mm,
        c_tile, c_buf, m_part, m_parts, m_tile, m_buf,
        at, by, columns, field_a, field_b, split_a, split_b, adjoint, mixed,
        f_part, f_parts, f_tile, f_buf,
        load_sem, table_sem, send, recv, psend, precv, fsend, frecv, tsend, trecv, bsem,
    ) = refs[n:]
    k, s = lax.axis_index("slab"), lax.axis_index("sec")
    nxt, prv = (k + 1) & (SLABS - 1), (k + SLABS - 1) & (SLABS - 1)
    q, r = k >> 2, k & 3
    has_prev, has_next = (k > 0).astype(F32), (k < SLABS - 1).astype(F32)
    up, down = s < SECS - 1, s > 0
    own_y, own_z = pl.ds(4, NY), pl.ds(8, NZ)

    load_moving = [
        pltpu.make_async_copy(
            moving.at[:, :, pl.ds(128 * c, 128)], pad.at[c, own_y, own_z], load_sem.at[c]
        )
        for c in range(CHUNKS)
    ]
    load_fixed = [
        pltpu.make_async_copy(
            fixed.at[:, :, pl.ds(128 * c, 128)], fx.at[c, :, pl.ds(0, NZ)], load_sem.at[CHUNKS + c]
        )
        for c in range(CHUNKS)
    ]
    place = {"k": k, "q": q, "r": r, "s": s, "rs": 4 * r + s}
    load_table = {}
    for i, (name, which) in enumerate(TABLES.items()):
        source = stored[i] if which is None else stored[i].at[place[which]]
        load_table[name] = pltpu.make_async_copy(source, t[name], table_sem.at[i])
    for copy in load_moving:
        copy.start()
    all_here = greet(k, s)
    for copy in (*load_fixed, *load_table.values()):
        copy.start()

    def table(name):
        load_table[name].wait()
        return t[name]

    lat_to_next = remote(lf_up, lf_prev, send.at[0], recv.at[0], (nxt, s))
    lat_to_prev = remote(lf_down, lf_next, send.at[1], recv.at[1], (prv, s))
    z_to_next = remote(zhi, z_bef, send.at[2], recv.at[2], (nxt, s))
    z_to_prev = remote(zlo, z_aft, send.at[3], recv.at[3], (prv, s))
    to_bef = remote(moving.at[pl.ds(16, 4)], y_bef, send.at[4], recv.at[4], (k, s + 1))
    to_aft = remote(moving.at[pl.ds(0, 4)], y_aft, send.at[5], recv.at[5], (k, s - 1))
    first, last = pl.ds(0, 2), pl.ds(8, 2)
    corner_up = [
        remote(zhi.at[:, last], corners.at[0], send.at[6], recv.at[6], (nxt, s + 1)),
        remote(zlo.at[:, last], corners.at[1], send.at[7], recv.at[7], (prv, s + 1)),
    ]
    corner_down = [
        remote(zhi.at[:, first], corners.at[2], send.at[8], recv.at[8], (nxt, s - 1)),
        remote(zlo.at[:, first], corners.at[3], send.at[9], recv.at[9], (prv, s - 1)),
    ]
    head, tail = pl.ds(0, 8), pl.ds(16, 8)
    mid_same = [
        remote(pooled_m.at[:, tail], pm_same.at[0], send.at[10], recv.at[10], (nxt, s)),
        remote(pooled_m.at[:, head], pm_same.at[1], send.at[11], recv.at[11], (prv, s)),
    ]
    mid_up = [
        remote(pack_up, pm_bef, send.at[12], recv.at[12], (k, s + 1)),
        remote(pack_up.at[:, tail], pm_halo.at[0, 0], send.at[13], recv.at[13], (nxt, s + 1)),
        remote(pack_up.at[:, head], pm_halo.at[1, 0], send.at[14], recv.at[14], (prv, s + 1)),
    ]
    mid_down = [
        remote(pack_down, pm_aft, send.at[15], recv.at[15], (k, s - 1)),
        remote(pack_down.at[:, tail], pm_halo.at[0, 1], send.at[16], recv.at[16], (nxt, s - 1)),
        remote(pack_down.at[:, head], pm_halo.at[1, 1], send.at[17], recv.at[17], (prv, s - 1)),
    ]

    def start_y_halos(*parts_of_z):
        rows = [pl.ds(16 * part, 16) for part in parts_of_z]

        @pl.when(up)
        def _():
            for z in rows:
                remote(moving.at[pl.ds(16, 4), z], y_bef.at[:, z], send.at[4], recv.at[4], (k, s + 1)).start()

        @pl.when(down)
        def _():
            for z in rows:
                remote(moving.at[pl.ds(0, 4), z], y_aft.at[:, z], send.at[5], recv.at[5], (k, s - 1)).start()

    def start(*copies):
        for copy in copies:
            copy.start()

    def start_if(condition, *copies):
        @pl.when(condition)
        def _():
            start(*copies)

    for c in range(CHUNKS):
        pad[c, :, 0:8, :] = jnp.zeros((28, 8, 128), F32)
        pad[c, :, 88:96, :] = jnp.zeros((28, 8, 128), F32)
        fx[c, :, 80:88, :] = jnp.zeros((NY, 8, 128), F32)
        for block in range(4):
            at[block, c, :, 24:32, :] = jnp.zeros((21, 8, 128), F32)
            by[block, c, :, 24:32, :] = jnp.zeros((21, 8, 128), F32)
    all_here()
    start_y_halos(0, 1)
    for c in range(CHUNKS):
        load_moving[c].wait()

        @pl.loop(0, NY // 2, unroll=5)
        def _(pair):
            for half in range(2):
                rows = slice(4 * half, 4 * half + 4)
                zlo[c, pair, rows, :] = pad[c, 2 * pair + half + 4, 8:12, :]
                zhi[c, pair, rows, :] = pad[c, 2 * pair + half + 4, 84:88, :]

    px, pz = table("px"), table("pz")

    def pooled():
        high, low = parts(sums[...].reshape(400, NX))
        high, low = parts(dot(high, px[...]) + dot(low, px[...]))
        return ((dot(pz[...], high) + dot(pz[...], low)) * (1.0 / 64.0)).reshape(5, 24, 256)

    for c in range(CHUNKS):
        lanes = slice(128 * c, 128 * c + 128)

        @pl.loop(0, 5, unroll=5)
        def _(group):
            four = [pad[c, 4 * group + 4 + i, 8:88, :] for i in range(4)]
            sums[group, :, lanes] = (four[0] + four[1]) + (four[2] + four[3])

    pooled_m[...] = pooled()

    for c in range(CHUNKS):
        load_fixed[c].wait()
        lanes = slice(128 * c, 128 * c + 128)

        @pl.loop(0, 5, unroll=5)
        def _(group):
            four = [fx[c, 4 * group + i, 0:80, :] for i in range(4)]
            sums[group, :, lanes] = (four[0] + four[1]) + (four[2] + four[3])

    pooled_f[...] = pooled()

    halves = []
    for ref in (pooled_m, pooled_f):
        upper, lower = jnp.zeros((24, 256), F32), jnp.zeros((24, 256), F32)
        for i in range(5):
            keep = (i + s < 4).astype(F32)
            upper = upper + ref[i] * keep
            lower = lower + ref[i] * (1.0 - keep)
        halves.append(jnp.concatenate([upper, lower], axis=0))
    high, low = parts(jnp.concatenate(halves, axis=1))
    pcx, pcz = table("pcx")[...], table("pcz")[...]
    both = dot(high, pcx) + dot(low, pcx)
    piece[...] = (dot_exact(pcz, both) * (1.0 / 64.0)).reshape(2, 8, 128)
    around(k, s, piece, pieces, psend, precv, "start")
    pieces[1, s] = piece[...]
    for ref, first_y in ((pack_up, 1), (pack_down, 0)):
        ref[0:4] = pooled_m[first_y : first_y + 4, :, 0:128]
        others = [pooled_m[first_y + i, :, 128:256] for i in range(4)]
        ref[4] = (others[0] + pltpu.roll(others[1], 32, 1)) + (
            pltpu.roll(others[2], 64, 1) + pltpu.roll(others[3], 96, 1)
        )
    start(*mid_same)
    start_if(up, *mid_up)
    start_if(down, *mid_down)

    for ref in (lf_own, mt, ct, cv, mm):
        ref[...] = jnp.zeros_like(ref)
    for d in range(3):
        for b in range(5):
            lf_own[d, b, 0:4, 0:33] = lat_fine[d, b]
        for a in range(9):
            for b in range(2):
                row = 32 * d + 16 * b + a
                mt[row : row + 1, 0:33] = lat_mid[d, a, b : b + 1]
        for a in range(3):
            ct[16 * d + a : 16 * d + a + 1, 0:9] = lat_coarse[d, a]
    for d in range(3):
        for b in range(5):
            row = 5 * d + b
            lf_up[row : row + 1, :] = lf_own[d, b, 3:4, :]
            lf_down[2 * row : 2 * row + 2, :] = lf_own[d, b, 0:2, :]
    start(lat_to_next, lat_to_prev)

    def pick_rows(name, ref):
        rows = table(name)[...]
        contract = (((1,), (1,)), ((), ()))
        high, low = parts(ref[...])
        return lax.dot_general(rows, high, contract, preferred_element_type=F32) + lax.dot_general(
            rows, low, contract, preferred_element_type=F32
        )

    rows_m, rows_c = pick_rows("rows_m", mt), pick_rows("rows_c", ct)
    cbt, cspread = table("cbt")[...], table("cspread")[...]
    column = dot3(jnp.concatenate([from_lane(rows_c[0:8], 16 * d) for d in range(3)], axis=0), cbt)
    column = jnp.concatenate([column[8 * d : 8 * d + 8] for d in range(3)], axis=1)
    exponent = dot(cspread, stacked(column, 8))[0:40]
    fractions_c = [fraction(exponent[:, 128 * d : 128 * d + 128]) for d in range(3)]
    cbx, cgather = table("cbx"), table("cgather")

    around(k, s, piece, pieces, psend, precv, "wait_recv")

    lane = lax.broadcasted_iota(jnp.int32, (5, 128), 1)
    for dk in range(3):
        scale = (has_prev, jnp.float32(1.0), has_next)[dk]
        rows = (slice(3, 8), slice(8, 13), slice(13, 18))[dk]
        for c in range(5):
            value = jnp.zeros((8, 128), F32)
            if c < 4:
                value = value + pieces[dk, c, 0]
            if c > 0:
                value = value + pieces[dk, c - 1, 1]
            cv[4 + c, rows, :] = jnp.where(lane < 40, value[0:5], 0.0) * scale
            if dk == 1:
                cf[c] = value
    fixed_c = pltpu.roll(cf[...].reshape(40, 128), 64, 1)

    oz, oy, ox = off_coarse[0, 0, q], off_coarse[1, 0, q], off_coarse[2, 0, q]
    a_z, b_z = [], []
    for e in (0, 1):
        window = cv[pl.ds(4 + oy, 6), pl.ds(8 + oz + e, 8), :].reshape(48, 128)
        here, there = shift_lanes([window], ox)[0], shift_lanes([window], ox + 1)[0]
        a_z.append(here)
        b_z.append(there - here)
    corner = [[a_z[z][8 * y : 8 * y + 40] for y in (0, 1)] for z in (0, 1)]
    step = [[b_z[z][8 * y : 8 * y + 40] for y in (0, 1)] for z in (0, 1)]
    total = jnp.concatenate(weights(fixed_c, corner, step, fractions_c), axis=1)
    total = dot_wide(jnp.concatenate([total, jnp.zeros((8, 384), F32)], axis=0), cbx[...])
    total = jnp.concatenate([total, jnp.zeros((80, 128), F32)], axis=0)
    c_tile[...] = dot_gather(cgather[...], total)[0:8]
    broadcast_start(k, s, c_tile, c_buf, bsem.at[0], bsem.at[1])
    c_buf[k] = c_tile[...]
    start_y_halos(2, 3)
    start(z_to_next, z_to_prev)
    start_if(up, *corner_up)
    start_if(down, *corner_down)

    mbt, mspread, mbx, mgather = table("mbt"), table("mspread"), table("mbx"), table("mgather")
    own = [from_lane(rows_m[0:8], 32 * d + 16 * b) for d in range(3) for b in range(2)]
    own = dot3(jnp.concatenate(own, axis=0), mbt[0])
    coarse = dot3(jnp.concatenate([from_lane(rows_c[8:16], 16 * d) for d in range(3)], axis=0), mbt[1])
    column = [
        jnp.concatenate([own[16 * d : 16 * d + 16], coarse[8 * d : 8 * d + 8]], axis=0) for d in range(3)
    ]
    base_m = dot(mspread[...], stacked(jnp.concatenate(column, axis=1), 24))[0:120]
    sum_c = table("sum_c")

    @pl.when(s == 0)
    def _():
        y_bef[...] = jnp.zeros_like(y_bef)
        corners[0:2] = jnp.zeros((2, CHUNKS, 2, 8, 128), F32)
        pm_bef[...] = jnp.zeros_like(pm_bef)
        pm_halo[:, 0] = jnp.zeros((2, 5, 8, 128), F32)

    @pl.when(s == SECS - 1)
    def _():
        y_aft[...] = jnp.zeros_like(y_aft)
        corners[2:4] = jnp.zeros((2, CHUNKS, 2, 8, 128), F32)
        pm_aft[...] = jnp.zeros_like(pm_aft)
        pm_halo[:, 1] = jnp.zeros((2, 5, 8, 128), F32)

    for copy in mid_same:
        copy.wait_recv()

    @pl.when(s > 0)
    def _():
        for copy in mid_up:
            copy.wait_recv()

    @pl.when(s < SECS - 1)
    def _():
        for copy in mid_down:
            copy.wait_recv()

    for c in range(2):
        lanes = slice(128 * c, 128 * c + 128)
        for y in range(5):
            mm[c, 5 + y, 4:8, :] = pm_same[0, y, 0:4, lanes] * has_prev
            mm[c, 5 + y, 8:28, :] = pooled_m[y, 0:20, lanes]
            mm[c, 5 + y, 28:32, :] = pm_same[1, y, 0:4, lanes] * has_next
    few = lax.broadcasted_iota(jnp.int32, (24, 128), 1) < 32
    for e, (whole, first_y) in enumerate(((pm_bef, 1), (pm_aft, 10))):
        for y in range(4):
            for c in range(2):

                def row(ref):
                    value = ref[y] if c == 0 else from_lane(ref[4], 32 * y)
                    return value if c == 0 else jnp.where(few[0 : value.shape[0]], value, 0.0)

                mm[c, first_y + y, 4:8, :] = row(pm_halo.at[0, e])[0:4] * has_prev
                mm[c, first_y + y, 8:28, :] = row(whole)[0:20]
                mm[c, first_y + y, 28:32, :] = row(pm_halo.at[1, e])[0:4] * has_next

    oz, oy, ox = off_mid[0, 0, 0], off_mid[0, 0, 1], off_mid[0, 0, 2]
    a_z, b_z = [], []
    for e in (0, 1):
        window = [mm[c, pl.ds(5 + oy, 6), pl.ds(8 + oz + e, 24), :].reshape(144, 128) for c in range(2)]
        here, there = shift_lanes(window, ox), shift_lanes(window, ox + 1)
        a_z.append(here)
        b_z.append([there[c] - here[c] for c in range(2)])

    def make_window(block, oz, oy, ox, y):
        window = [pad[c, 4 + oy + y, pl.ds(20 * block + 8 + oz, 24), :] for c in range(CHUNKS)]
        here, there = shift_lanes(window, ox), shift_lanes(window, ox + 1)
        for c in range(CHUNKS):
            at[block, c, y, 0:24, :] = here[c]
            by[block, c, y, 0:24, :] = there[c] - here[c]

    def make_windows(blocks, ranges):
        @pl.loop(*blocks)
        def _(block):
            offsets = [off_fine[d, block, s] for d in range(3)]
            for first_y, last_y, unroll in ranges:
                pl.loop(first_y, last_y, unroll=unroll)(functools.partial(make_window, block, *offsets))

    make_windows((1, 3), ((4, 16, 3),))

    broadcast_wait(c_buf, bsem.at[0], bsem.at[1])
    gradient = dot_exact(sum_c[...], c_buf[...].reshape(256, 128))
    near_c = gradient[16:24]
    gradient = gradient[0:16]
    inverse = lax.rsqrt(jnp.sum(gradient * gradient) * (1.0 / 81.0) + EPSILON)

    near = dot3(jnp.concatenate([from_lane(near_c, 16 * d) for d in range(3)], axis=0), mbt[1])
    near = jnp.concatenate([near[8 * d : 8 * d + 8] for d in range(3)], axis=1)
    near = dot(mspread[...], stacked(jnp.concatenate([jnp.zeros((16, 768), F32), near], axis=0), 24))
    exponent = base_m - (STEP_SIZE * inverse) * near[0:120]
    fixed_m = pooled_f[...].reshape(120, 256)
    found = []
    for c in range(2):
        lanes = slice(128 * c, 128 * c + 128)
        corner = [[a_z[z][c][24 * y : 24 * y + 120] for y in (0, 1)] for z in (0, 1)]
        step = [[b_z[z][c][24 * y : 24 * y + 120] for y in (0, 1)] for z in (0, 1)]
        fractions = [fraction(exponent[:, 256 * d + 128 * c : 256 * d + 128 * c + 128]) for d in range(3)]
        found.append(weights(fixed_m[:, lanes], corner, step, fractions))
    total = jnp.concatenate([found[c][d] for d in range(3) for c in range(2)], axis=1)
    total = dot_wide(jnp.concatenate([total, jnp.zeros((8, 768), F32)], axis=0), mbx[...])
    m_part[...] = dot_gather(mgather[...], total)

    def part_copies(act):
        for i in range(1, SECS):
            other = (s + i) & (SECS - 1)
            slot = other if act == "wait_recv" else s
            getattr(remote(m_part, m_parts.at[slot], tsend.at[other], trecv.at[slot], (k, other)), act)()

    part_copies("start")
    start_y_halos(4)
    m_parts[s] = m_part[...]
    part_copies("wait_recv")
    m_tile[...] = (m_parts[0] + m_parts[1]) + (m_parts[2] + m_parts[3])
    broadcast_start(k, s, m_tile, m_buf, bsem.at[2], bsem.at[3])
    m_buf[k] = m_tile[...]

    gradient = gradient * inverse
    next_c = [
        from_lane(rows_c[8:16], 16 * d) - (STEP_SIZE * inverse) * from_lane(near_c, 16 * d) for d in range(3)
    ]
    turn_r = lax.broadcasted_iota(jnp.int32, (48, 128), 0)
    turn = jnp.where(turn_r == lax.broadcasted_iota(jnp.int32, (48, 128), 1) + 2, 1.0, 0.0)
    result[216:264, :] = dot_rows(gradient, turn[0:16])[0:48]

    for copy in (lat_to_next, lat_to_prev):
        copy.wait_recv()
    for d in range(3):
        for b in range(5):
            lf[d, 8 * b : 8 * b + 1, :] = lf_prev[5 * d + b : 5 * d + b + 1, :] * has_prev
            lf[d, 8 * b + 1 : 8 * b + 5, :] = lf_own[d, b, 0:4, :]
            lf[d, 8 * b + 5 : 8 * b + 7, :] = lf_next[10 * d + 2 * b : 10 * d + 2 * b + 2, :] * has_next
            lf[d, 8 * b + 7 : 8 * b + 8, :] = jnp.zeros((1, 128), F32)
    bt = table("bt")
    own = dot3(lf[...].reshape(120, 128), bt[0])
    mid = [from_lane(rows_m[8:16], 32 * d + 16 * b) for d in range(3) for b in range(2)]
    mid = dot3(jnp.concatenate(mid, axis=0), bt[1])
    coarse = dot3(jnp.concatenate(next_c, axis=0), bt[2])
    base_f = [
        jnp.concatenate(
            [own[40 * d : 40 * d + 40], mid[16 * d : 16 * d + 16], coarse[8 * d : 8 * d + 8]], axis=0
        )
        for d in range(3)
    ]
    base_f = jnp.concatenate(base_f, axis=1)

    for copy in (z_to_next, z_to_prev):
        copy.wait_recv()

    @pl.when(s > 0)
    def _():
        for copy in (to_bef, *corner_up):
            copy.wait_recv()

    @pl.when(s < SECS - 1)
    def _():
        for copy in (to_aft, *corner_down):
            copy.wait_recv()

    for c in range(CHUNKS):
        lanes = slice(128 * c, 128 * c + 128)
        pad[c, 0:4, 8:88, :] = y_bef[:, :, lanes]
        pad[c, 24:28, 8:88, :] = y_aft[:, :, lanes]

    @pl.loop(0, NY // 2, unroll=2)
    def _(pair):
        for half in range(2):
            rows = slice(4 * half, 4 * half + 4)
            for c in range(CHUNKS):
                pad[c, 2 * pair + half + 4, 4:8, :] = z_bef[c, pair, rows, :] * has_prev
                pad[c, 2 * pair + half + 4, 88:92, :] = z_aft[c, pair, rows, :] * has_next

    for y in range(4):
        rows = slice(4 * (y % 2), 4 * (y % 2) + 4)
        for c in range(CHUNKS):
            for n in range(2):
                where = slice(4, 8) if n == 0 else slice(88, 92)
                keep = has_prev if n == 0 else has_next
                pad[c, y, where, :] = corners[n, c, y // 2, rows, :] * keep
                pad[c, 24 + y, where, :] = corners[2 + n, c, y // 2, rows, :] * keep

    make_windows((1, 3), ((0, 4, 2), (16, 21, 5)))
    make_windows((0, 1), ((0, 21, 3),))
    make_windows((3, 4), ((0, 21, 3),))

    spread, gather, bx, sum_m = table("spread"), table("gather"), table("bx"), table("sum_m")

    broadcast_wait(m_buf, bsem.at[2], bsem.at[3])
    gradient = dot_exact(sum_m[...], m_buf[...].reshape(512, 128))
    near = gradient[96:112]
    gradient = gradient[0:96]
    inverse = lax.rsqrt(jnp.sum(gradient * gradient) * (1.0 / 1782.0) + EPSILON)

    near = dot3(jnp.concatenate([from_lane(near, 16 * d) for d in range(3)], axis=0), bt[1])
    near = jnp.concatenate([near[16 * d : 16 * d + 16] for d in range(3)], axis=1)
    near = jnp.concatenate([jnp.zeros((40, 3 * NX), F32), near, jnp.zeros((8, 3 * NX), F32)], axis=0)
    upper, lower = parts(base_f - (STEP_SIZE * inverse) * near)
    columns[0:64, :] = upper
    columns[64:128, :] = upper
    columns[128:192, :] = lower
    columns[192:256, :] = lower
    field_a[...] = dot(spread[0:480, :], columns[...])

    rows_z = (pl.ds(0, 24), pl.ds(jnp.minimum(k + 1, 1), 24))

    def fine_block(block, split, split_before, field, field_after):
        adjoint[...] = jnp.zeros_like(adjoint)
        after = pl.ds(pl.multiple_of(480 * jnp.minimum(block + 1, 3), 480), 480)

        @pl.loop(0, 5)
        def _(i):
            lanes = pl.ds(pl.multiple_of(384 * i, 384), 384)
            field_after[:, lanes] = dot(spread[after, :], columns[:, lanes])
            lanes = pl.ds(pl.multiple_of(768 * i, 768), 768)
            adjoint[...] += dot(split_before[:, lanes], bx[lanes, :])
            for pair in range(2):
                for c in range(CHUNKS):
                    found = []
                    for h in range(2):
                        y = 4 * i + 2 * pair + h
                        corner = [[at[block, c, y + e, z, :] for e in (0, 1)] for z in rows_z]
                        step = [[by[block, c, y + e, z, :] for e in (0, 1)] for z in rows_z]
                        rows = pl.ds(pl.multiple_of(24 * y, 8), 24)
                        fractions = [
                            fraction(field[rows, NX * d + 128 * c : NX * d + 128 * c + 128]) for d in range(3)
                        ]
                        atlas = fx[c, y, pl.ds(20 * block, 24), :]
                        found.append(weights(atlas, corner, step, fractions))
                    rows = pl.ds(pl.multiple_of(96 * i + 48 * pair, 48), 48)
                    for d in range(3):
                        upper, lower = parts(jnp.concatenate([found[0][d], found[1][d]], axis=0))
                        lane = 2 * NX * d + 128 * c
                        split[rows, lane : lane + 128] = upper
                        split[rows, lane + NX : lane + NX + 128] = lower

        before = pl.ds(pl.multiple_of(480 * jnp.maximum(block - 1, 0), 480), 480)
        mixed[before, :] = adjoint[:, 0:128] + adjoint[:, 128:256]

    @pl.loop(0, 2)
    def _(two):
        fine_block(2 * two, split_a, split_b, field_a, field_b)
        fine_block(2 * two + 1, split_b, split_a, field_b, field_a)

    wide = dot(split_b[...], bx[...])
    mixed[1440:1920, :] = wide[:, 0:128] + wide[:, 128:256]
    f_part[...] = dot_gather(gather[...], mixed[...])
    around(k, s, f_part, f_parts, fsend, frecv, "start")
    f_parts[1, s] = f_part[...]

    for b in range(2):
        turned = dot_rows(gradient[48 * b : 48 * b + 48] * inverse, turn)
        result[120 + 48 * b : 168 + 48 * b, :] = turned[0:48]
    row = lax.broadcasted_iota(jnp.int32, (40, 128), 0) & 7

    around(k, s, f_part, f_parts, fsend, frecv, "wait_recv")
    before, middle, after = ((f_parts[i, 0] + f_parts[i, 1]) + (f_parts[i, 2] + f_parts[i, 3]) for i in range(3))
    middle = middle + jnp.where((row == 1) | (row == 2), pltpu.roll(before * has_prev, 36, 0), 0.0)
    middle = middle + jnp.where(row == 4, pltpu.roll(after * has_next, 4, 0), 0.0)
    middle = jnp.where((row >= 1) & (row <= 4), middle, 0.0)
    f_tile[...] = jnp.full((8, 128), jnp.sum(middle * middle))
    broadcast_start(k, s, f_tile, f_buf, bsem.at[4], bsem.at[5])
    f_buf[k] = f_tile[...]

    for copy in (lat_to_next, lat_to_prev, z_to_next, z_to_prev, *mid_same):
        copy.wait_send()

    @pl.when(up)
    def _():
        for copy in (to_bef, *corner_up, *mid_up):
            copy.wait_send()

    @pl.when(down)
    def _():
        for copy in (to_aft, *corner_down, *mid_down):
            copy.wait_send()

    around(k, s, piece, pieces, psend, precv, "wait_send")
    around(k, s, f_part, f_parts, fsend, frecv, "wait_send")
    part_copies("wait_send")
    middle = pltpu.roll(middle, 39, 0)
    thirds = [from_lane(middle, 40 * d) for d in range(3)]

    broadcast_wait(f_buf, bsem.at[4], bsem.at[5])
    squares = jnp.sum(f_buf[...], axis=0)[0:1, :]
    inverse = lax.rsqrt(squares * (1.0 / 63360.0) + EPSILON)
    for d in range(3):
        result[40 * d : 40 * d + 40, :] = thirds[d] * inverse


def body(
    fixed_image,
    moving_image,
    lattice_fine,
    lattice_mid,
    lattice_coarse,
    offset_fine,
    offset_mid,
    offset_coarse,
):
    t = tables()
    vmem, smem, hbm = (pl.BlockSpec(memory_space=m) for m in (pltpu.VMEM, pltpu.SMEM, pl.ANY))
    shape = lambda *dims: jax.ShapeDtypeStruct(dims, F32)
    buf = lambda *dims: pltpu.VMEM(dims, F32)
    half = lambda *dims: pltpu.VMEM(dims, BF16)
    dma = lambda *dims: pltpu.SemaphoreType.DMA(dims)
    result = pl.pallas_call(
        kernel,
        out_shape=shape(264, 128),
        in_specs=[hbm, hbm, vmem, vmem, vmem, smem, smem, smem] + [hbm] * len(TABLES),
        out_specs=vmem,
        scratch_shapes=[
            *[pltpu.VMEM(t[n].shape[which is not None :], t[n].dtype) for n, which in TABLES.items()],
            buf(CHUNKS, 28, 96, 128), buf(CHUNKS, NY, 88, 128), buf(5, NZ, NX),
            *[buf(CHUNKS, 10, 8, 128)] * 4, *[buf(4, NZ, NX)] * 2, buf(4, CHUNKS, 2, 8, 128),
            buf(3, 5, 8, 128), *[buf(16, 128), buf(32, 128)] * 2, buf(3, 40, 128), buf(128, 128), buf(128, 128),
            *[buf(5, 24, 256)] * 2, *[buf(5, 24, 128)] * 4, buf(2, 2, 5, 8, 128), buf(2, 5, 8, 256),
            buf(2, 8, 128), buf(3, SECS, 2, 8, 128), buf(14, 32, 128), buf(5, 8, 128), buf(2, 15, 40, 128),
            buf(8, 128), buf(SLABS, 8, 128), buf(16, 128), buf(SECS, 16, 128), buf(16, 128), buf(SLABS, 16, 128),
            *[buf(4, CHUNKS, 21, 32, 128)] * 2, half(256, 3 * NX),
            *[buf(480, 3 * NX)] * 2, *[half(480, 6 * NX)] * 2, buf(480, 256), buf(1920, 128),
            buf(40, 128), buf(3, SECS, 40, 128), buf(8, 128), buf(SLABS, 8, 128),
            dma(10), dma(len(TABLES)), dma(18), dma(18), *[dma(3, SECS)] * 4, dma(SECS), dma(SECS), dma(6),
        ],
        compiler_params=pltpu.CompilerParams(
            collective_id=0, has_side_effects=True, vmem_limit_bytes=VMEM_LIMIT
        ),
        name="mega",
    )(
        jnp.transpose(moving_image, (1, 0, 2)),
        jnp.transpose(fixed_image, (1, 0, 2)),
        jnp.transpose(lattice_fine, (0, 2, 1, 3)),
        jnp.transpose(lattice_mid, (0, 3, 2, 1)),
        jnp.transpose(lattice_coarse, (0, 3, 2, 1)),
        offset_fine,
        jnp.transpose(offset_mid, (1, 2, 0)),
        jnp.transpose(offset_coarse, (0, 2, 1)),
        *(t[n] for n in TABLES),
    )
    fine, mid, coarse = pl.pallas_call(
        finish,
        out_shape=[shape(3, 5, 4, 33), shape(3, 9, 2, 33), shape(3, 3, 1, 9)],
        in_specs=[vmem],
        out_specs=[vmem] * 3,
        name="finish",
    )(result)
    return (
        jnp.transpose(fine, (0, 2, 1, 3)),
        jnp.transpose(mid, (0, 3, 2, 1)),
        jnp.transpose(coarse, (0, 3, 2, 1)),
    )


def solution(mesh):
    placed = (
        P("slab", "sec", None),
        P("slab", "sec", None),
        P(None, "slab", None, None),
        P(),
        P(),
        P(None, "slab", None),
        P(None, "slab", None),
        P(),
    )
    return jax.shard_map(
        body,
        mesh=mesh,
        in_specs=placed,
        out_specs=(P(None, "slab", None, None), P(), P()),
        check_vma=False,
    )
```

```python
import functools

import jax
import jax.numpy as jnp
import ml_dtypes
import numpy as np
from jax import lax
from jax.experimental import pallas as pl
from jax.experimental.pallas import tpu as pltpu
from jax.sharding import PartitionSpec as P

SP = 20
EPSILON = 1e-06
STEP_SIZE = 0.5
HIGHEST = lax.Precision.HIGHEST
F32 = jnp.float32
BF16 = jnp.bfloat16
MESH = pl.DeviceIdType.MESH
SLABS = 32
SECS = 4
NZ, NY, NX = 80, 20, 640
CHUNKS = NX // 128
LOG2E = 1.4426950408889634
VMEM_LIMIT = 58 * 1024 * 1024


def basis(rows, knots, factor, coarse):
    rows, knots = np.asarray(rows, np.float64), np.asarray(knots, np.float64)
    position = factor * rows + 0.5 * (factor - 1)
    centre = SP * coarse * knots + 0.5 * (coarse - 1)
    distance = np.abs((position[:, None] - centre[None, :]) / (SP * coarse))
    near = 2.0 / 3.0 - distance**2 + 0.5 * distance**3
    far = np.maximum(2.0 - distance, 0.0) ** 3 / 6.0
    return np.where(distance < 1.0, near, far)


def two_parts(values):
    high = values.astype(ml_dtypes.bfloat16)
    low = (values - high.astype(np.float64)).astype(ml_dtypes.bfloat16)
    return high, low


def right_parts(values):
    high, low = two_parts(values)
    return np.concatenate([high, low, high], axis=-2)


def wide_parts(values):
    high, low = two_parts(values)
    zero = np.zeros_like(high)
    return np.concatenate([np.concatenate([high, low], 1), np.concatenate([high, zero], 1)], 0)


def one_hot(condition):
    return condition.astype(ml_dtypes.bfloat16)


@functools.cache
def tables():
    t = {}
    rz, ry = np.zeros((4, 4, 24, 64)), np.zeros((4, NY, 64))
    z, y, x = np.arange(NZ), np.arange(NY), np.arange(NX)
    for r in range(4):
        for block in range(4):
            rows = z[20 * block : 20 * block + 20]
            for a in range(7):
                rz[r, block, :20, a:40:8] = basis(rows, [a - 1], 1, 1)
            for a in range(5):
                rz[r, block, :20, 40 + a : 56 : 8] = basis(rows, [a - 2], 1, 4)
                rz[r, block, :20, 56 + a : 57 + a] = basis(rows + 80 * r, [a - 2], 1, 16)
    for s in range(4):
        for a in range(7):
            ry[s, :, a:40:8] = basis(y + 20 * s, range(5), 1, 1)
        for a in range(5):
            ry[s, :, 40 + a : 56 : 8] = basis(y + 20 * s, range(2), 1, 4)
            ry[s, :, 56 + a : 57 + a] = basis(y + 20 * s, [0], 1, 16)
    whole = rz[:, None, :, None] * ry[None, :, None, :, None, :]
    high, low = two_parts(whole.reshape(16, 1920, 64))
    t["spread"] = np.concatenate([high, low, high, low], axis=2)
    t["gather"] = np.concatenate([high[:4, :, :40], low[:4, :, :40]], axis=2).transpose(0, 2, 1)
    across = np.zeros((3, 128, NX))
    across[0, :33] = basis(x, range(33), 1, 1).T
    across[1, :9] = basis(x, range(9), 1, 4).T
    across[2, :3] = basis(x, range(3), 1, 16).T
    t["bt"] = right_parts(-LOG2E * across)
    along = np.zeros((3, NX, 128))
    for d in range(3):
        along[d, :, 40 * d : 40 * d + 33] = basis(x, range(33), 1, 1)
    t["bx"] = np.concatenate([wide_parts(along[d]) for d in range(3)], axis=0)
    rz, ry = np.zeros((4, 24, 32)), np.zeros((4, 5, 32))
    z, y, x = np.arange(20), np.arange(5), np.arange(160)
    for r in range(4):
        for a in range(4):
            rz[r, :20, a:16:8] = basis(z, [a - 1], 4, 4)
        for a in range(5):
            rz[r, :20, 16 + a : 17 + a] = basis(z + 20 * r, [a - 2], 4, 16)
    for s in range(4):
        for a in range(4):
            ry[s, :, a:16:8] = basis(y + 5 * s, range(2), 4, 4)
        for a in range(5):
            ry[s, :, 16 + a : 17 + a] = basis(y + 5 * s, [0], 4, 16)
    whole = np.zeros((16, 128, 32))
    whole[:, :120] = (rz[:, None, None] * ry[None, :, :, None]).reshape(16, 120, 32)
    high, low = two_parts(whole)
    t["mspread"] = np.concatenate([high, high, low, np.zeros_like(low)], axis=2)
    t["mgather"] = np.concatenate([high[:, :, :16], low[:, :, :16]], axis=2).transpose(0, 2, 1)
    across = np.zeros((2, 128, 256))
    across[0, :9, :160] = basis(x, range(9), 4, 4).T
    across[1, :3, :160] = basis(x, range(3), 4, 16).T
    t["mbt"] = right_parts(-LOG2E * across)
    along = np.zeros((3, 256, 128))
    for d in range(3):
        along[d, :160, 16 * d : 16 * d + 9] = basis(x, range(9), 4, 4)
    t["mbx"] = wide_parts(along.reshape(768, 128))
    rz = np.zeros((4, 8, 32))
    z, y, x = np.arange(5), np.arange(5), np.arange(40)
    for r in range(4):
        for a in range(4):
            rz[r, :5, a : a + 1] = basis(z + 5 * r, [a - 1], 16, 16)
    whole = np.zeros((4, 128, 32))
    whole[:, :40] = (rz[:, None] * basis(y, [0], 16, 16)[None, :, None]).reshape(4, 40, 32)
    high, low = two_parts(whole)
    t["cspread"] = np.concatenate([high, high, low, np.zeros_like(low)], axis=2)
    t["cgather"] = np.concatenate([high[:, :, :16], low[:, :, :16]], axis=2).transpose(0, 2, 1)
    across = np.zeros((128, 128))
    across[:3, :40] = basis(x, range(3), 16, 16).T
    t["cbt"] = right_parts(-LOG2E * across)
    along = np.zeros((3, 128, 128))
    for d in range(3):
        along[d, :40, 16 * d : 16 * d + 3] = basis(x, range(3), 16, 16)
    t["cbx"] = wide_parts(along.reshape(384, 128))
    row, column = np.arange(NX)[:, None], np.arange(256)[None, :]
    t["px"] = one_hot(row // 4 == column)
    row, column = np.arange(120)[:, None], np.arange(400)[None, :]
    t["pz"] = one_hot((row // 24 == column // 80) & (row % 24 == column % 80 // 4))
    row, column = np.arange(512)[:, None], np.arange(128)[None, :]
    t["pcx"] = one_hot((row % 256 < 160) & (row // 256 * 64 + row % 256 // 4 == column))
    row, column = np.arange(16)[:, None], np.arange(48)[None, :]
    t["pcz"] = one_hot((row // 8 == column // 24) & (column % 24 < 20) & (row % 8 == column % 24 // 4))
    row, column, place = np.arange(16)[:, None], np.arange(128)[None, :], np.arange(32)[:, None, None]
    knot = place - 1 - row // 8 + row % 8
    t["rows_m"] = one_hot((knot == column) & (column < 33))
    t["rows_c"] = one_hot((knot == column) & (column < 9))[:8]
    row, column, place = np.arange(24)[:, None], np.arange(256)[None, :], np.arange(8)[:, None, None]
    knot = np.where(row < 16, row - 2, row - 16 + place - 2)
    found = (knot == column // 32 - 1 + column % 8) & (column % 8 < 4) & (knot >= 0) & (knot < 9)
    t["sum_c"] = one_hot(found)
    row, column, place = np.arange(112)[:, None], np.arange(512)[None, :], np.arange(32)[:, None, None]
    knot = np.where(row < 96, row % 48 - 2, row % 8 + place - 2)
    b = np.where(row < 96, row // 48, (row - 96) // 8)
    found = (knot == column // 16 - 1 + column % 8) & (column % 8 < 4) & (column // 8 % 2 == b)
    t["sum_m"] = one_hot(found & (knot >= 0) & (knot < 33))
    return t


def dot(a, b):
    return jnp.dot(a, b, preferred_element_type=F32)


def dot_rows(a, b):
    return lax.dot_general(
        a, b, (((0,), (0,)), ((), ())), precision=HIGHEST, preferred_element_type=F32
    )


def parts(values):
    high = values.astype(BF16)
    return high, (values - high.astype(F32)).astype(BF16)


def dot3(a, right):
    high, low = parts(a)
    return dot(jnp.concatenate([high, high, low], axis=1), right)


def dot_wide(a, table):
    wide = dot(jnp.concatenate(parts(a), axis=1), table)
    return wide[:, 0:128] + wide[:, 128:256]


def dot_exact(table, b):
    wide = dot(table, jnp.concatenate(parts(b), axis=1))
    return wide[:, 0:128] + wide[:, 128:256]


def dot_gather(table, b):
    n = table.shape[0] // 2
    wide = dot(table, jnp.concatenate(parts(b), axis=1))
    return (wide[0:n, 0:128] + wide[0:n, 128:256]) + wide[n:, 0:128]


def stacked(column, n):
    high, low = parts(jnp.concatenate([column, jnp.zeros((32 - n, column.shape[1]), F32)], axis=0))
    return jnp.concatenate([high, low, high, jnp.zeros_like(low)], axis=0)


def from_lane(values, lane):
    return values if lane == 0 else pltpu.roll(values, 128 - lane, 1)


def shift_lanes(chunks, shift):
    amount = (128 - shift) & 127
    rolled = [pltpu.roll(chunk, amount, 1) for chunk in chunks]
    lane = lax.broadcasted_iota(jnp.int32, chunks[0].shape, 1)
    first = lane < jnp.maximum(-shift, 0)
    last = lane >= 128 - jnp.maximum(shift, 0)
    zero = jnp.zeros_like(chunks[0])
    padded = [zero, *rolled, zero]
    return [
        jnp.where(first, padded[j], jnp.where(last, padded[j + 2], padded[j + 1]))
        for j in range(len(chunks))
    ]


def fraction(exponent):
    grown = jnp.exp2(exponent)
    frac = pl.reciprocal(1.0 + grown, approx=True)
    return frac, frac * (grown * frac)


def weights(fixed, corner, step, fractions):
    (fz, gz), (fy, gy), (fx, gx) = fractions
    line = [[corner[z][y] + fx * step[z][y] for y in (0, 1)] for z in (0, 1)]
    rise = [line[z][1] - line[z][0] for z in (0, 1)]
    plane = [line[z][0] + fy * rise[z] for z in (0, 1)]
    slope_z = plane[1] - plane[0]
    residual = (plane[0] + fz * slope_z) - fixed
    slope_y = rise[0] + fz * (rise[1] - rise[0])
    along = [step[z][0] + fy * (step[z][1] - step[z][0]) for z in (0, 1)]
    slope_x = along[0] + fz * (along[1] - along[0])
    return [
        (residual * slope_z) * gz,
        (residual * slope_y) * gy,
        (residual * slope_x) * gx,
    ]


def greet(k, s):
    barrier = pltpu.get_barrier_semaphore()

    def signal(slab, sec):
        pl.semaphore_signal(barrier, inc=1, device_id=(slab, sec), device_id_type=MESH)

    @pl.loop(1, SLABS)
    def _(i):
        signal((k + i) & (SLABS - 1), s)

    for i in range(1, SECS):
        other = (s + i) & (SECS - 1)
        signal(k, other)
        signal((k + 1) & (SLABS - 1), other)
        signal((k + SLABS - 1) & (SLABS - 1), other)
    return lambda: pl.semaphore_wait(barrier, SLABS - 1 + 3 * (SECS - 1))


def broadcast_start(k, s, tile, buffer, send_sem, recv_sem):
    @pl.loop(0, SLABS - 1)
    def _(i):
        pltpu.make_async_remote_copy(
            src_ref=tile,
            dst_ref=buffer.at[k],
            send_sem=send_sem,
            recv_sem=recv_sem,
            device_id=((k + 16 + i + (i > 15).astype(jnp.int32)) & (SLABS - 1), s),
            device_id_type=MESH,
        ).start()


def broadcast_wait(buffer, send_sem, recv_sem):
    part = buffer.at[pl.ds(0, SLABS - 1)]
    pltpu.make_async_copy(part, part, recv_sem).wait()
    pltpu.make_async_copy(part, part, send_sem).wait()


def remote(src, dst, send_sem, recv_sem, device):
    return pltpu.make_async_remote_copy(
        src_ref=src,
        dst_ref=dst,
        send_sem=send_sem,
        recv_sem=recv_sem,
        device_id=device,
        device_id_type=MESH,
    )


def around(k, s, source, buffer, send, recv, act):
    slabs = ((k + SLABS - 1) & (SLABS - 1), k, (k + 1) & (SLABS - 1))

    def one(dk, other):
        if act == "wait_recv":
            copy = remote(source, buffer.at[dk, other], send.at[dk, other], recv.at[dk, other], (k, other))
        else:
            copy = remote(
                source, buffer.at[2 - dk, s], send.at[dk, other], recv.at[2 - dk, s], (slabs[dk], other)
            )
        getattr(copy, act)()

    for dk in (0, 2):
        for other in range(SECS):
            one(dk, other)
    for i in range(1, SECS):
        one(1, (s + i) & (SECS - 1))


TABLES = {
    "px": None, "pz": None, "pcx": None, "pcz": None,
    "rows_m": "k", "rows_c": "q", "cspread": "r", "cgather": "r", "cbt": None, "cbx": None,
    "sum_c": "q", "mspread": "rs", "mgather": "rs", "mbt": None, "mbx": None,
    "spread": "rs", "gather": "s", "bt": None, "bx": None, "sum_m": "k",
}


def finish(result, fine_out, mid_out, coarse_out):
    for d in range(3):
        for b in range(5):
            row = 40 * d + 8 * b
            fine_out[d, b] = result[row : row + 4, 0:33]
        for a in range(9):
            for b in range(2):
                row = 120 + 48 * b + 16 * d + a
                mid_out[d, a, b : b + 1, :] = result[row : row + 1, 0:33]
        for a in range(3):
            row = 216 + 16 * d + a
            coarse_out[d, a] = result[row : row + 1, 0:9]


def kernel(
    moving, fixed, lat_fine, lat_mid, lat_coarse, off_fine, off_mid, off_coarse, *refs
):
    n = len(TABLES)
    stored, refs = refs[:n], refs[n:]
    result, *refs = refs
    t = dict(zip(TABLES, refs[:n]))
    (
        pad, fx, sums, zlo, zhi, z_bef, z_aft, y_bef, y_aft, corners,
        lf_own, lf_up, lf_down, lf_prev, lf_next, lf, mt, ct,
        pooled_m, pooled_f, pack_up, pack_down, pm_bef, pm_aft, pm_halo, pm_same,
        piece, pieces, cv, cf, mm,
        c_tile, c_buf, m_part, m_parts, m_tile, m_buf,
        at, by, columns, field_a, field_b, split_a, split_b, adjoint, mixed,
        f_part, f_parts, f_tile, f_buf,
        load_sem, table_sem, send, recv, psend, precv, fsend, frecv, tsend, trecv, bsem,
    ) = refs[n:]
    k, s = lax.axis_index("slab"), lax.axis_index("sec")
    nxt, prv = (k + 1) & (SLABS - 1), (k + SLABS - 1) & (SLABS - 1)
    q, r = k >> 2, k & 3
    has_prev, has_next = (k > 0).astype(F32), (k < SLABS - 1).astype(F32)
    up, down = s < SECS - 1, s > 0
    own_y, own_z = pl.ds(4, NY), pl.ds(8, NZ)

    load_moving = [
        pltpu.make_async_copy(
            moving.at[:, :, pl.ds(128 * c, 128)], pad.at[c, own_y, own_z], load_sem.at[c]
        )
        for c in range(CHUNKS)
    ]
    load_fixed = [
        pltpu.make_async_copy(
            fixed.at[:, :, pl.ds(128 * c, 128)], fx.at[c, :, pl.ds(0, NZ)], load_sem.at[CHUNKS + c]
        )
        for c in range(CHUNKS)
    ]
    place = {"k": k, "q": q, "r": r, "s": s, "rs": 4 * r + s}
    load_table = {}
    for i, (name, which) in enumerate(TABLES.items()):
        source = stored[i] if which is None else stored[i].at[place[which]]
        load_table[name] = pltpu.make_async_copy(source, t[name], table_sem.at[i])
    for copy in load_moving:
        copy.start()
    all_here = greet(k, s)
    for copy in (*load_fixed, *load_table.values()):
        copy.start()

    def table(name):
        load_table[name].wait()
        return t[name]

    lat_to_next = remote(lf_up, lf_prev, send.at[0], recv.at[0], (nxt, s))
    lat_to_prev = remote(lf_down, lf_next, send.at[1], recv.at[1], (prv, s))
    z_to_next = remote(zhi, z_bef, send.at[2], recv.at[2], (nxt, s))
    z_to_prev = remote(zlo, z_aft, send.at[3], recv.at[3], (prv, s))
    to_bef = remote(moving.at[pl.ds(16, 4)], y_bef, send.at[4], recv.at[4], (k, s + 1))
    to_aft = remote(moving.at[pl.ds(0, 4)], y_aft, send.at[5], recv.at[5], (k, s - 1))
    first, last = pl.ds(0, 2), pl.ds(8, 2)
    corner_up = [
        remote(zhi.at[:, last], corners.at[0], send.at[6], recv.at[6], (nxt, s + 1)),
        remote(zlo.at[:, last], corners.at[1], send.at[7], recv.at[7], (prv, s + 1)),
    ]
    corner_down = [
        remote(zhi.at[:, first], corners.at[2], send.at[8], recv.at[8], (nxt, s - 1)),
        remote(zlo.at[:, first], corners.at[3], send.at[9], recv.at[9], (prv, s - 1)),
    ]
    head, tail = pl.ds(0, 8), pl.ds(16, 8)
    mid_same = [
        remote(pooled_m.at[:, tail], pm_same.at[0], send.at[10], recv.at[10], (nxt, s)),
        remote(pooled_m.at[:, head], pm_same.at[1], send.at[11], recv.at[11], (prv, s)),
    ]
    mid_up = [
        remote(pack_up, pm_bef, send.at[12], recv.at[12], (k, s + 1)),
        remote(pack_up.at[:, tail], pm_halo.at[0, 0], send.at[13], recv.at[13], (nxt, s + 1)),
        remote(pack_up.at[:, head], pm_halo.at[1, 0], send.at[14], recv.at[14], (prv, s + 1)),
    ]
    mid_down = [
        remote(pack_down, pm_aft, send.at[15], recv.at[15], (k, s - 1)),
        remote(pack_down.at[:, tail], pm_halo.at[0, 1], send.at[16], recv.at[16], (nxt, s - 1)),
        remote(pack_down.at[:, head], pm_halo.at[1, 1], send.at[17], recv.at[17], (prv, s - 1)),
    ]

    def start_y_halos(*parts_of_z):
        rows = [pl.ds(16 * part, 16) for part in parts_of_z]

        @pl.when(up)
        def _():
            for z in rows:
                remote(moving.at[pl.ds(16, 4), z], y_bef.at[:, z], send.at[4], recv.at[4], (k, s + 1)).start()

        @pl.when(down)
        def _():
            for z in rows:
                remote(moving.at[pl.ds(0, 4), z], y_aft.at[:, z], send.at[5], recv.at[5], (k, s - 1)).start()

    def start(*copies):
        for copy in copies:
            copy.start()

    def start_if(condition, *copies):
        @pl.when(condition)
        def _():
            start(*copies)

    for c in range(CHUNKS):
        pad[c, :, 0:8, :] = jnp.zeros((28, 8, 128), F32)
        pad[c, :, 88:96, :] = jnp.zeros((28, 8, 128), F32)
        fx[c, :, 80:88, :] = jnp.zeros((NY, 8, 128), F32)
        for block in range(4):
            at[block, c, :, 24:32, :] = jnp.zeros((21, 8, 128), F32)
            by[block, c, :, 24:32, :] = jnp.zeros((21, 8, 128), F32)
    all_here()
    start_y_halos(0, 1)
    for c in range(CHUNKS):
        load_moving[c].wait()

        @pl.loop(0, NY // 2, unroll=5)
        def _(pair):
            for half in range(2):
                rows = slice(4 * half, 4 * half + 4)
                zlo[c, pair, rows, :] = pad[c, 2 * pair + half + 4, 8:12, :]
                zhi[c, pair, rows, :] = pad[c, 2 * pair + half + 4, 84:88, :]

    start(z_to_next)

    px, pz = table("px"), table("pz")

    def pooled():
        high, low = parts(sums[...].reshape(400, NX))
        high, low = parts(dot(high, px[...]) + dot(low, px[...]))
        return ((dot(pz[...], high) + dot(pz[...], low)) * (1.0 / 64.0)).reshape(5, 24, 256)

    for c in range(CHUNKS):
        lanes = slice(128 * c, 128 * c + 128)

        @pl.loop(0, 5, unroll=5)
        def _(group):
            four = [pad[c, 4 * group + 4 + i, 8:88, :] for i in range(4)]
            sums[group, :, lanes] = (four[0] + four[1]) + (four[2] + four[3])

    pooled_m[...] = pooled()

    for c in range(CHUNKS):
        load_fixed[c].wait()
        lanes = slice(128 * c, 128 * c + 128)

        @pl.loop(0, 5, unroll=5)
        def _(group):
            four = [fx[c, 4 * group + i, 0:80, :] for i in range(4)]
            sums[group, :, lanes] = (four[0] + four[1]) + (four[2] + four[3])

    pooled_f[...] = pooled()

    halves = []
    for ref in (pooled_m, pooled_f):
        upper, lower = jnp.zeros((24, 256), F32), jnp.zeros((24, 256), F32)
        for i in range(5):
            keep = (i + s < 4).astype(F32)
            upper = upper + ref[i] * keep
            lower = lower + ref[i] * (1.0 - keep)
        halves.append(jnp.concatenate([upper, lower], axis=0))
    high, low = parts(jnp.concatenate(halves, axis=1))
    pcx, pcz = table("pcx")[...], table("pcz")[...]
    both = dot(high, pcx) + dot(low, pcx)
    piece[...] = (dot_exact(pcz, both) * (1.0 / 64.0)).reshape(2, 8, 128)
    around(k, s, piece, pieces, psend, precv, "start")
    pieces[1, s] = piece[...]
    for ref, first_y in ((pack_up, 1), (pack_down, 0)):
        ref[0:4] = pooled_m[first_y : first_y + 4, :, 0:128]
        others = [pooled_m[first_y + i, :, 128:256] for i in range(4)]
        ref[4] = (others[0] + pltpu.roll(others[1], 32, 1)) + (
            pltpu.roll(others[2], 64, 1) + pltpu.roll(others[3], 96, 1)
        )
    start(*mid_same)
    start_if(up, *mid_up)
    start_if(down, *mid_down)

    for ref in (lf_own, mt, ct, cv, mm):
        ref[...] = jnp.zeros_like(ref)
    for d in range(3):
        for b in range(5):
            lf_own[d, b, 0:4, 0:33] = lat_fine[d, b]
        for a in range(9):
            for b in range(2):
                row = 32 * d + 16 * b + a
                mt[row : row + 1, 0:33] = lat_mid[d, a, b : b + 1]
        for a in range(3):
            ct[16 * d + a : 16 * d + a + 1, 0:9] = lat_coarse[d, a]
    for d in range(3):
        for b in range(5):
            row = 5 * d + b
            lf_up[row : row + 1, :] = lf_own[d, b, 3:4, :]
            lf_down[2 * row : 2 * row + 2, :] = lf_own[d, b, 0:2, :]
    start(lat_to_next, lat_to_prev)

    def pick_rows(name, ref):
        rows = table(name)[...]
        contract = (((1,), (1,)), ((), ()))
        high, low = parts(ref[...])
        return lax.dot_general(rows, high, contract, preferred_element_type=F32) + lax.dot_general(
            rows, low, contract, preferred_element_type=F32
        )

    rows_m, rows_c = pick_rows("rows_m", mt), pick_rows("rows_c", ct)
    cbt, cspread = table("cbt")[...], table("cspread")[...]
    column = dot3(jnp.concatenate([from_lane(rows_c[0:8], 16 * d) for d in range(3)], axis=0), cbt)
    column = jnp.concatenate([column[8 * d : 8 * d + 8] for d in range(3)], axis=1)
    exponent = dot(cspread, stacked(column, 8))[0:40]
    fractions_c = [fraction(exponent[:, 128 * d : 128 * d + 128]) for d in range(3)]
    cbx, cgather = table("cbx"), table("cgather")

    around(k, s, piece, pieces, psend, precv, "wait_recv")

    lane = lax.broadcasted_iota(jnp.int32, (5, 128), 1)
    for dk in range(3):
        scale = (has_prev, jnp.float32(1.0), has_next)[dk]
        rows = (slice(3, 8), slice(8, 13), slice(13, 18))[dk]
        for c in range(5):
            value = jnp.zeros((8, 128), F32)
            if c < 4:
                value = value + pieces[dk, c, 0]
            if c > 0:
                value = value + pieces[dk, c - 1, 1]
            cv[4 + c, rows, :] = jnp.where(lane < 40, value[0:5], 0.0) * scale
            if dk == 1:
                cf[c] = value
    fixed_c = pltpu.roll(cf[...].reshape(40, 128), 64, 1)

    oz, oy, ox = off_coarse[0, 0, q], off_coarse[1, 0, q], off_coarse[2, 0, q]
    a_z, b_z = [], []
    for e in (0, 1):
        window = cv[pl.ds(4 + oy, 6), pl.ds(8 + oz + e, 8), :].reshape(48, 128)
        here, there = shift_lanes([window], ox)[0], shift_lanes([window], ox + 1)[0]
        a_z.append(here)
        b_z.append(there - here)
    corner = [[a_z[z][8 * y : 8 * y + 40] for y in (0, 1)] for z in (0, 1)]
    step = [[b_z[z][8 * y : 8 * y + 40] for y in (0, 1)] for z in (0, 1)]
    total = jnp.concatenate(weights(fixed_c, corner, step, fractions_c), axis=1)
    total = dot_wide(jnp.concatenate([total, jnp.zeros((8, 384), F32)], axis=0), cbx[...])
    total = jnp.concatenate([total, jnp.zeros((80, 128), F32)], axis=0)
    c_tile[...] = dot_gather(cgather[...], total)[0:8]
    broadcast_start(k, s, c_tile, c_buf, bsem.at[0], bsem.at[1])
    c_buf[k] = c_tile[...]
    start_y_halos(2, 3)
    start(z_to_prev)

    mbt, mspread, mbx, mgather = table("mbt"), table("mspread"), table("mbx"), table("mgather")
    own = [from_lane(rows_m[0:8], 32 * d + 16 * b) for d in range(3) for b in range(2)]
    own = dot3(jnp.concatenate(own, axis=0), mbt[0])
    coarse = dot3(jnp.concatenate([from_lane(rows_c[8:16], 16 * d) for d in range(3)], axis=0), mbt[1])
    column = [
        jnp.concatenate([own[16 * d : 16 * d + 16], coarse[8 * d : 8 * d + 8]], axis=0) for d in range(3)
    ]
    base_m = dot(mspread[...], stacked(jnp.concatenate(column, axis=1), 24))[0:120]
    sum_c = table("sum_c")

    @pl.when(s == 0)
    def _():
        y_bef[...] = jnp.zeros_like(y_bef)
        corners[0:2] = jnp.zeros((2, CHUNKS, 2, 8, 128), F32)
        pm_bef[...] = jnp.zeros_like(pm_bef)
        pm_halo[:, 0] = jnp.zeros((2, 5, 8, 128), F32)

    @pl.when(s == SECS - 1)
    def _():
        y_aft[...] = jnp.zeros_like(y_aft)
        corners[2:4] = jnp.zeros((2, CHUNKS, 2, 8, 128), F32)
        pm_aft[...] = jnp.zeros_like(pm_aft)
        pm_halo[:, 1] = jnp.zeros((2, 5, 8, 128), F32)

    for copy in mid_same:
        copy.wait_recv()

    @pl.when(s > 0)
    def _():
        for copy in mid_up:
            copy.wait_recv()

    @pl.when(s < SECS - 1)
    def _():
        for copy in mid_down:
            copy.wait_recv()

    for c in range(2):
        lanes = slice(128 * c, 128 * c + 128)
        for y in range(5):
            mm[c, 5 + y, 4:8, :] = pm_same[0, y, 0:4, lanes] * has_prev
            mm[c, 5 + y, 8:28, :] = pooled_m[y, 0:20, lanes]
            mm[c, 5 + y, 28:32, :] = pm_same[1, y, 0:4, lanes] * has_next
    few = lax.broadcasted_iota(jnp.int32, (24, 128), 1) < 32
    for e, (whole, first_y) in enumerate(((pm_bef, 1), (pm_aft, 10))):
        for y in range(4):
            for c in range(2):

                def row(ref):
                    value = ref[y] if c == 0 else from_lane(ref[4], 32 * y)
                    return value if c == 0 else jnp.where(few[0 : value.shape[0]], value, 0.0)

                mm[c, first_y + y, 4:8, :] = row(pm_halo.at[0, e])[0:4] * has_prev
                mm[c, first_y + y, 8:28, :] = row(whole)[0:20]
                mm[c, first_y + y, 28:32, :] = row(pm_halo.at[1, e])[0:4] * has_next

    oz, oy, ox = off_mid[0, 0, 0], off_mid[0, 0, 1], off_mid[0, 0, 2]
    a_z, b_z = [], []
    for e in (0, 1):
        window = [mm[c, pl.ds(5 + oy, 6), pl.ds(8 + oz + e, 24), :].reshape(144, 128) for c in range(2)]
        here, there = shift_lanes(window, ox), shift_lanes(window, ox + 1)
        a_z.append(here)
        b_z.append([there[c] - here[c] for c in range(2)])

    def make_window(block, oz, oy, ox, y):
        window = [pad[c, 4 + oy + y, pl.ds(20 * block + 8 + oz, 24), :] for c in range(CHUNKS)]
        here, there = shift_lanes(window, ox), shift_lanes(window, ox + 1)
        for c in range(CHUNKS):
            at[block, c, y, 0:24, :] = here[c]
            by[block, c, y, 0:24, :] = there[c] - here[c]

    def make_windows(blocks, ranges):
        @pl.loop(*blocks)
        def _(block):
            offsets = [off_fine[d, block, s] for d in range(3)]
            for first_y, last_y, unroll in ranges:
                pl.loop(first_y, last_y, unroll=unroll)(functools.partial(make_window, block, *offsets))

    broadcast_wait(c_buf, bsem.at[0], bsem.at[1])
    gradient = dot_exact(sum_c[...], c_buf[...].reshape(256, 128))
    near_c = gradient[16:24]
    gradient = gradient[0:16]
    inverse = lax.rsqrt(jnp.sum(gradient * gradient) * (1.0 / 81.0) + EPSILON)

    near = dot3(jnp.concatenate([from_lane(near_c, 16 * d) for d in range(3)], axis=0), mbt[1])
    near = jnp.concatenate([near[8 * d : 8 * d + 8] for d in range(3)], axis=1)
    near = dot(mspread[...], stacked(jnp.concatenate([jnp.zeros((16, 768), F32), near], axis=0), 24))
    exponent = base_m - (STEP_SIZE * inverse) * near[0:120]
    fixed_m = pooled_f[...].reshape(120, 256)
    found = []
    for c in range(2):
        lanes = slice(128 * c, 128 * c + 128)
        corner = [[a_z[z][c][24 * y : 24 * y + 120] for y in (0, 1)] for z in (0, 1)]
        step = [[b_z[z][c][24 * y : 24 * y + 120] for y in (0, 1)] for z in (0, 1)]
        fractions = [fraction(exponent[:, 256 * d + 128 * c : 256 * d + 128 * c + 128]) for d in range(3)]
        found.append(weights(fixed_m[:, lanes], corner, step, fractions))
    total = jnp.concatenate([found[c][d] for d in range(3) for c in range(2)], axis=1)
    total = dot_wide(jnp.concatenate([total, jnp.zeros((8, 768), F32)], axis=0), mbx[...])
    m_part[...] = dot_gather(mgather[...], total)

    def part_copies(act):
        for i in range(1, SECS):
            other = (s + i) & (SECS - 1)
            slot = other if act == "wait_recv" else s
            getattr(remote(m_part, m_parts.at[slot], tsend.at[other], trecv.at[slot], (k, other)), act)()

    part_copies("start")
    start_y_halos(4)
    start_if(up, *corner_up)
    start_if(down, *corner_down)
    m_parts[s] = m_part[...]

    gradient = gradient * inverse
    next_c = [
        from_lane(rows_c[8:16], 16 * d) - (STEP_SIZE * inverse) * from_lane(near_c, 16 * d) for d in range(3)
    ]
    for copy in (lat_to_next, lat_to_prev):
        copy.wait_recv()
    for d in range(3):
        for b in range(5):
            lf[d, 8 * b : 8 * b + 1, :] = lf_prev[5 * d + b : 5 * d + b + 1, :] * has_prev
            lf[d, 8 * b + 1 : 8 * b + 5, :] = lf_own[d, b, 0:4, :]
            lf[d, 8 * b + 5 : 8 * b + 7, :] = lf_next[10 * d + 2 * b : 10 * d + 2 * b + 2, :] * has_next
            lf[d, 8 * b + 7 : 8 * b + 8, :] = jnp.zeros((1, 128), F32)
    bt = table("bt")
    own = dot3(lf[...].reshape(120, 128), bt[0])
    mid = [from_lane(rows_m[8:16], 32 * d + 16 * b) for d in range(3) for b in range(2)]
    mid = dot3(jnp.concatenate(mid, axis=0), bt[1])
    coarse = dot3(jnp.concatenate(next_c, axis=0), bt[2])
    base_f = [
        jnp.concatenate(
            [own[40 * d : 40 * d + 40], mid[16 * d : 16 * d + 16], coarse[8 * d : 8 * d + 8]], axis=0
        )
        for d in range(3)
    ]
    base_f = jnp.concatenate(base_f, axis=1)

    make_windows((1, 3), ((4, 16, 3),))
    part_copies("wait_recv")
    m_tile[...] = (m_parts[0] + m_parts[1]) + (m_parts[2] + m_parts[3])
    broadcast_start(k, s, m_tile, m_buf, bsem.at[2], bsem.at[3])
    m_buf[k] = m_tile[...]

    turn_r = lax.broadcasted_iota(jnp.int32, (48, 128), 0)
    turn = jnp.where(turn_r == lax.broadcasted_iota(jnp.int32, (48, 128), 1) + 2, 1.0, 0.0)
    result[216:264, :] = dot_rows(gradient, turn[0:16])[0:48]

    for copy in (z_to_next, z_to_prev):
        copy.wait_recv()

    @pl.when(s > 0)
    def _():
        for copy in (to_bef, *corner_up):
            copy.wait_recv()

    @pl.when(s < SECS - 1)
    def _():
        for copy in (to_aft, *corner_down):
            copy.wait_recv()

    for c in range(CHUNKS):
        lanes = slice(128 * c, 128 * c + 128)
        pad[c, 0:4, 8:88, :] = y_bef[:, :, lanes]
        pad[c, 24:28, 8:88, :] = y_aft[:, :, lanes]

    @pl.loop(0, NY // 2, unroll=2)
    def _(pair):
        for half in range(2):
            rows = slice(4 * half, 4 * half + 4)
            for c in range(CHUNKS):
                pad[c, 2 * pair + half + 4, 4:8, :] = z_bef[c, pair, rows, :] * has_prev
                pad[c, 2 * pair + half + 4, 88:92, :] = z_aft[c, pair, rows, :] * has_next

    for y in range(4):
        rows = slice(4 * (y % 2), 4 * (y % 2) + 4)
        for c in range(CHUNKS):
            for n in range(2):
                where = slice(4, 8) if n == 0 else slice(88, 92)
                keep = has_prev if n == 0 else has_next
                pad[c, y, where, :] = corners[n, c, y // 2, rows, :] * keep
                pad[c, 24 + y, where, :] = corners[2 + n, c, y // 2, rows, :] * keep

    make_windows((1, 3), ((0, 4, 2), (16, 21, 5)))
    make_windows((0, 1), ((0, 21, 3),))
    make_windows((3, 4), ((0, 21, 3),))

    spread, gather, bx, sum_m = table("spread"), table("gather"), table("bx"), table("sum_m")

    broadcast_wait(m_buf, bsem.at[2], bsem.at[3])
    gradient = dot_exact(sum_m[...], m_buf[...].reshape(512, 128))
    near = gradient[96:112]
    gradient = gradient[0:96]
    inverse = lax.rsqrt(jnp.sum(gradient * gradient) * (1.0 / 1782.0) + EPSILON)

    near = dot3(jnp.concatenate([from_lane(near, 16 * d) for d in range(3)], axis=0), bt[1])
    near = jnp.concatenate([near[16 * d : 16 * d + 16] for d in range(3)], axis=1)
    near = jnp.concatenate([jnp.zeros((40, 3 * NX), F32), near, jnp.zeros((8, 3 * NX), F32)], axis=0)
    upper, lower = parts(base_f - (STEP_SIZE * inverse) * near)
    columns[0:64, :] = upper
    columns[64:128, :] = upper
    columns[128:192, :] = lower
    columns[192:256, :] = lower
    field_a[...] = dot(spread[0:480, :], columns[...])

    rows_z = (pl.ds(0, 24), pl.ds(jnp.minimum(k + 1, 1), 24))

    def fine_block(block, split, split_before, field, field_after):
        adjoint[...] = jnp.zeros_like(adjoint)
        after = pl.ds(pl.multiple_of(480 * jnp.minimum(block + 1, 3), 480), 480)

        @pl.loop(0, 5)
        def _(i):
            lanes = pl.ds(pl.multiple_of(384 * i, 384), 384)
            field_after[:, lanes] = dot(spread[after, :], columns[:, lanes])
            lanes = pl.ds(pl.multiple_of(768 * i, 768), 768)
            adjoint[...] += dot(split_before[:, lanes], bx[lanes, :])
            for pair in range(2):
                for c in range(CHUNKS):
                    found = []
                    for h in range(2):
                        y = 4 * i + 2 * pair + h
                        corner = [[at[block, c, y + e, z, :] for e in (0, 1)] for z in rows_z]
                        step = [[by[block, c, y + e, z, :] for e in (0, 1)] for z in rows_z]
                        rows = pl.ds(pl.multiple_of(24 * y, 8), 24)
                        fractions = [
                            fraction(field[rows, NX * d + 128 * c : NX * d + 128 * c + 128]) for d in range(3)
                        ]
                        atlas = fx[c, y, pl.ds(20 * block, 24), :]
                        found.append(weights(atlas, corner, step, fractions))
                    rows = pl.ds(pl.multiple_of(96 * i + 48 * pair, 48), 48)
                    for d in range(3):
                        upper, lower = parts(jnp.concatenate([found[0][d], found[1][d]], axis=0))
                        lane = 2 * NX * d + 128 * c
                        split[rows, lane : lane + 128] = upper
                        split[rows, lane + NX : lane + NX + 128] = lower

        before = pl.ds(pl.multiple_of(480 * jnp.maximum(block - 1, 0), 480), 480)
        mixed[before, :] = adjoint[:, 0:128] + adjoint[:, 128:256]

    @pl.loop(0, 2)
    def _(two):
        fine_block(2 * two, split_a, split_b, field_a, field_b)
        fine_block(2 * two + 1, split_b, split_a, field_b, field_a)

    wide = dot(split_b[...], bx[...])
    mixed[1440:1920, :] = wide[:, 0:128] + wide[:, 128:256]
    f_part[...] = dot_gather(gather[...], mixed[...])
    around(k, s, f_part, f_parts, fsend, frecv, "start")
    f_parts[1, s] = f_part[...]

    for b in range(2):
        turned = dot_rows(gradient[48 * b : 48 * b + 48] * inverse, turn)
        result[120 + 48 * b : 168 + 48 * b, :] = turned[0:48]
    row = lax.broadcasted_iota(jnp.int32, (40, 128), 0) & 7

    around(k, s, f_part, f_parts, fsend, frecv, "wait_recv")
    before, middle, after = ((f_parts[i, 0] + f_parts[i, 1]) + (f_parts[i, 2] + f_parts[i, 3]) for i in range(3))
    middle = middle + jnp.where((row == 1) | (row == 2), pltpu.roll(before * has_prev, 36, 0), 0.0)
    middle = middle + jnp.where(row == 4, pltpu.roll(after * has_next, 4, 0), 0.0)
    middle = jnp.where((row >= 1) & (row <= 4), middle, 0.0)
    f_tile[...] = jnp.full((8, 128), jnp.sum(middle * middle))
    broadcast_start(k, s, f_tile, f_buf, bsem.at[4], bsem.at[5])
    f_buf[k] = f_tile[...]

    for copy in (lat_to_next, lat_to_prev, z_to_next, z_to_prev, *mid_same):
        copy.wait_send()

    @pl.when(up)
    def _():
        for copy in (to_bef, *corner_up, *mid_up):
            copy.wait_send()

    @pl.when(down)
    def _():
        for copy in (to_aft, *corner_down, *mid_down):
            copy.wait_send()

    around(k, s, piece, pieces, psend, precv, "wait_send")
    around(k, s, f_part, f_parts, fsend, frecv, "wait_send")
    part_copies("wait_send")
    middle = pltpu.roll(middle, 39, 0)
    thirds = [from_lane(middle, 40 * d) for d in range(3)]

    broadcast_wait(f_buf, bsem.at[4], bsem.at[5])
    squares = jnp.sum(f_buf[...], axis=0)[0:1, :]
    inverse = lax.rsqrt(squares * (1.0 / 63360.0) + EPSILON)
    for d in range(3):
        result[40 * d : 40 * d + 40, :] = thirds[d] * inverse


def body(
    fixed_image,
    moving_image,
    lattice_fine,
    lattice_mid,
    lattice_coarse,
    offset_fine,
    offset_mid,
    offset_coarse,
):
    t = tables()
    vmem, smem, hbm = (pl.BlockSpec(memory_space=m) for m in (pltpu.VMEM, pltpu.SMEM, pl.ANY))
    shape = lambda *dims: jax.ShapeDtypeStruct(dims, F32)
    buf = lambda *dims: pltpu.VMEM(dims, F32)
    half = lambda *dims: pltpu.VMEM(dims, BF16)
    dma = lambda *dims: pltpu.SemaphoreType.DMA(dims)
    result = pl.pallas_call(
        kernel,
        out_shape=shape(264, 128),
        in_specs=[hbm, hbm, vmem, vmem, vmem, smem, smem, smem] + [hbm] * len(TABLES),
        out_specs=vmem,
        scratch_shapes=[
            *[pltpu.VMEM(t[n].shape[which is not None :], t[n].dtype) for n, which in TABLES.items()],
            buf(CHUNKS, 28, 96, 128), buf(CHUNKS, NY, 88, 128), buf(5, NZ, NX),
            *[buf(CHUNKS, 10, 8, 128)] * 4, *[buf(4, NZ, NX)] * 2, buf(4, CHUNKS, 2, 8, 128),
            buf(3, 5, 8, 128), *[buf(16, 128), buf(32, 128)] * 2, buf(3, 40, 128), buf(128, 128), buf(128, 128),
            *[buf(5, 24, 256)] * 2, *[buf(5, 24, 128)] * 4, buf(2, 2, 5, 8, 128), buf(2, 5, 8, 256),
            buf(2, 8, 128), buf(3, SECS, 2, 8, 128), buf(14, 32, 128), buf(5, 8, 128), buf(2, 15, 40, 128),
            buf(8, 128), buf(SLABS, 8, 128), buf(16, 128), buf(SECS, 16, 128), buf(16, 128), buf(SLABS, 16, 128),
            *[buf(4, CHUNKS, 21, 32, 128)] * 2, half(256, 3 * NX),
            *[buf(480, 3 * NX)] * 2, *[half(480, 6 * NX)] * 2, buf(480, 256), buf(1920, 128),
            buf(40, 128), buf(3, SECS, 40, 128), buf(8, 128), buf(SLABS, 8, 128),
            dma(10), dma(len(TABLES)), dma(18), dma(18), *[dma(3, SECS)] * 4, dma(SECS), dma(SECS), dma(6),
        ],
        compiler_params=pltpu.CompilerParams(
            collective_id=0, has_side_effects=True, vmem_limit_bytes=VMEM_LIMIT
        ),
        name="mega",
    )(
        jnp.transpose(moving_image, (1, 0, 2)),
        jnp.transpose(fixed_image, (1, 0, 2)),
        jnp.transpose(lattice_fine, (0, 2, 1, 3)),
        jnp.transpose(lattice_mid, (0, 3, 2, 1)),
        jnp.transpose(lattice_coarse, (0, 3, 2, 1)),
        offset_fine,
        jnp.transpose(offset_mid, (1, 2, 0)),
        jnp.transpose(offset_coarse, (0, 2, 1)),
        *(t[n] for n in TABLES),
    )
    fine, mid, coarse = pl.pallas_call(
        finish,
        out_shape=[shape(3, 5, 4, 33), shape(3, 9, 2, 33), shape(3, 3, 1, 9)],
        in_specs=[vmem],
        out_specs=[vmem] * 3,
        name="finish",
    )(result)
    return (
        jnp.transpose(fine, (0, 2, 1, 3)),
        jnp.transpose(mid, (0, 3, 2, 1)),
        jnp.transpose(coarse, (0, 3, 2, 1)),
    )


def solution(mesh):
    placed = (
        P("slab", "sec", None),
        P("slab", "sec", None),
        P(None, "slab", None, None),
        P(),
        P(),
        P(None, "slab", None),
        P(None, "slab", None),
        P(),
    )
    return jax.shard_map(
        body,
        mesh=mesh,
        in_specs=placed,
        out_specs=(P(None, "slab", None, None), P(), P()),
        check_vma=False,
    )
```

```python
import functools

import jax
import jax.numpy as jnp
import ml_dtypes
import numpy as np
from jax import lax
from jax.experimental import pallas as pl
from jax.experimental.pallas import tpu as pltpu
from jax.sharding import PartitionSpec as P

SP = 20
EPSILON = 1e-06
STEP_SIZE = 0.5
HIGHEST = lax.Precision.HIGHEST
F32 = jnp.float32
BF16 = jnp.bfloat16
MESH = pl.DeviceIdType.MESH
SLABS = 32
SECS = 4
NZ, NY, NX = 80, 20, 640
CHUNKS = NX // 128
LOG2E = 1.4426950408889634
VMEM_LIMIT = 58 * 1024 * 1024


def basis(rows, knots, factor, coarse):
    rows, knots = np.asarray(rows, np.float64), np.asarray(knots, np.float64)
    position = factor * rows + 0.5 * (factor - 1)
    centre = SP * coarse * knots + 0.5 * (coarse - 1)
    distance = np.abs((position[:, None] - centre[None, :]) / (SP * coarse))
    near = 2.0 / 3.0 - distance**2 + 0.5 * distance**3
    far = np.maximum(2.0 - distance, 0.0) ** 3 / 6.0
    return np.where(distance < 1.0, near, far)


def two_parts(values):
    high = values.astype(ml_dtypes.bfloat16)
    low = (values - high.astype(np.float64)).astype(ml_dtypes.bfloat16)
    return high, low


def right_parts(values):
    high, low = two_parts(values)
    return np.concatenate([high, low, high], axis=-2)


def wide_parts(values):
    high, low = two_parts(values)
    zero = np.zeros_like(high)
    return np.concatenate([np.concatenate([high, low], 1), np.concatenate([high, zero], 1)], 0)


def one_hot(condition):
    return condition.astype(ml_dtypes.bfloat16)


@functools.cache
def tables():
    t = {}
    rz, ry = np.zeros((4, 4, 20, 64)), np.zeros((4, NY, 64))
    z, y, x = np.arange(NZ), np.arange(NY), np.arange(NX)
    for r in range(4):
        for block in range(4):
            rows = z[20 * block : 20 * block + 20]
            for a in range(7):
                rz[r, block, :, a:40:8] = basis(rows, [a - 1], 1, 1)
            for a in range(5):
                rz[r, block, :, 40 + a : 56 : 8] = basis(rows, [a - 2], 1, 4)
                rz[r, block, :, 56 + a : 57 + a] = basis(rows + 80 * r, [a - 2], 1, 16)
    for s in range(4):
        for a in range(7):
            ry[s, :, a:40:8] = basis(y + 20 * s, range(5), 1, 1)
        for a in range(5):
            ry[s, :, 40 + a : 56 : 8] = basis(y + 20 * s, range(2), 1, 4)
            ry[s, :, 56 + a : 57 + a] = basis(y + 20 * s, [0], 1, 16)
    rz = rz.reshape(4, 2, 40, 64)
    whole = rz[:, None, :, None] * ry[None, :, None, :, None, :]
    high, low = two_parts(whole.reshape(16, 1600, 64))
    t["spread"] = np.concatenate([high, low, high, low], axis=2)
    t["gather"] = np.concatenate([high[:4, :, :40], low[:4, :, :40]], axis=2).transpose(0, 2, 1)
    across = np.zeros((3, 128, NX))
    across[0, :33] = basis(x, range(33), 1, 1).T
    across[1, :9] = basis(x, range(9), 1, 4).T
    across[2, :3] = basis(x, range(3), 1, 16).T
    t["bt"] = right_parts(-LOG2E * across)
    along = np.zeros((3, NX, 128))
    for d in range(3):
        along[d, :, 40 * d : 40 * d + 33] = basis(x, range(33), 1, 1)
    t["bx"] = np.concatenate([wide_parts(along[d]) for d in range(3)], axis=0)
    rz, ry = np.zeros((4, 24, 32)), np.zeros((4, 5, 32))
    z, y, x = np.arange(20), np.arange(5), np.arange(160)
    for r in range(4):
        for a in range(4):
            rz[r, :20, a:16:8] = basis(z, [a - 1], 4, 4)
        for a in range(5):
            rz[r, :20, 16 + a : 17 + a] = basis(z + 20 * r, [a - 2], 4, 16)
    for s in range(4):
        for a in range(4):
            ry[s, :, a:16:8] = basis(y + 5 * s, range(2), 4, 4)
        for a in range(5):
            ry[s, :, 16 + a : 17 + a] = basis(y + 5 * s, [0], 4, 16)
    whole = np.zeros((16, 128, 32))
    whole[:, :120] = (rz[:, None, None] * ry[None, :, :, None]).reshape(16, 120, 32)
    high, low = two_parts(whole)
    t["mspread"] = np.concatenate([high, high, low, np.zeros_like(low)], axis=2)
    t["mgather"] = np.concatenate([high[:, :, :16], low[:, :, :16]], axis=2).transpose(0, 2, 1)
    across = np.zeros((2, 128, 256))
    across[0, :9, :160] = basis(x, range(9), 4, 4).T
    across[1, :3, :160] = basis(x, range(3), 4, 16).T
    t["mbt"] = right_parts(-LOG2E * across)
    along = np.zeros((3, 256, 128))
    for d in range(3):
        along[d, :160, 16 * d : 16 * d + 9] = basis(x, range(9), 4, 4)
    t["mbx"] = wide_parts(along.reshape(768, 128))
    rz = np.zeros((4, 8, 32))
    z, y, x = np.arange(5), np.arange(5), np.arange(40)
    for r in range(4):
        for a in range(4):
            rz[r, :5, a : a + 1] = basis(z + 5 * r, [a - 1], 16, 16)
    whole = np.zeros((4, 128, 32))
    whole[:, :40] = (rz[:, None] * basis(y, [0], 16, 16)[None, :, None]).reshape(4, 40, 32)
    high, low = two_parts(whole)
    t["cspread"] = np.concatenate([high, high, low, np.zeros_like(low)], axis=2)
    t["cgather"] = np.concatenate([high[:, :, :16], low[:, :, :16]], axis=2).transpose(0, 2, 1)
    across = np.zeros((128, 128))
    across[:3, :40] = basis(x, range(3), 16, 16).T
    t["cbt"] = right_parts(-LOG2E * across)
    along = np.zeros((3, 128, 128))
    for d in range(3):
        along[d, :40, 16 * d : 16 * d + 3] = basis(x, range(3), 16, 16)
    t["cbx"] = wide_parts(along.reshape(384, 128))
    row, column = np.arange(NX)[:, None], np.arange(256)[None, :]
    t["px"] = one_hot(row // 4 == column)
    row, column = np.arange(120)[:, None], np.arange(400)[None, :]
    t["pz"] = one_hot((row // 24 == column // 80) & (row % 24 == column % 80 // 4))
    row, column = np.arange(512)[:, None], np.arange(128)[None, :]
    t["pcx"] = one_hot((row % 256 < 160) & (row // 256 * 64 + row % 256 // 4 == column))
    row, column = np.arange(16)[:, None], np.arange(48)[None, :]
    t["pcz"] = one_hot((row // 8 == column // 24) & (column % 24 < 20) & (row % 8 == column % 24 // 4))
    row, column, place = np.arange(16)[:, None], np.arange(128)[None, :], np.arange(32)[:, None, None]
    knot = place - 1 - row // 8 + row % 8
    t["rows_m"] = one_hot((knot == column) & (column < 33))
    t["rows_c"] = one_hot((knot == column) & (column < 9))[:8]
    row, column, place = np.arange(24)[:, None], np.arange(256)[None, :], np.arange(8)[:, None, None]
    knot = np.where(row < 16, row - 2, row - 16 + place - 2)
    found = (knot == column // 32 - 1 + column % 8) & (column % 8 < 4) & (knot >= 0) & (knot < 9)
    t["sum_c"] = one_hot(found)
    row, column, place = np.arange(112)[:, None], np.arange(512)[None, :], np.arange(32)[:, None, None]
    knot = np.where(row < 96, row % 48 - 2, row % 8 + place - 2)
    b = np.where(row < 96, row // 48, (row - 96) // 8)
    found = (knot == column // 16 - 1 + column % 8) & (column % 8 < 4) & (column // 8 % 2 == b)
    t["sum_m"] = one_hot(found & (knot >= 0) & (knot < 33))
    return t


def dot(a, b):
    return jnp.dot(a, b, preferred_element_type=F32)


def dot_rows(a, b):
    return lax.dot_general(
        a, b, (((0,), (0,)), ((), ())), precision=HIGHEST, preferred_element_type=F32
    )


def parts(values):
    high = values.astype(BF16)
    return high, (values - high.astype(F32)).astype(BF16)


def dot3(a, right):
    high, low = parts(a)
    return dot(jnp.concatenate([high, high, low], axis=1), right)


def dot_wide(a, table):
    wide = dot(jnp.concatenate(parts(a), axis=1), table)
    return wide[:, 0:128] + wide[:, 128:256]


def dot_exact(table, b):
    wide = dot(table, jnp.concatenate(parts(b), axis=1))
    return wide[:, 0:128] + wide[:, 128:256]


def dot_gather(table, b):
    n = table.shape[0] // 2
    wide = dot(table, jnp.concatenate(parts(b), axis=1))
    return (wide[0:n, 0:128] + wide[0:n, 128:256]) + wide[n:, 0:128]


def stacked(column, n):
    high, low = parts(jnp.concatenate([column, jnp.zeros((32 - n, column.shape[1]), F32)], axis=0))
    return jnp.concatenate([high, low, high, jnp.zeros_like(low)], axis=0)


def from_lane(values, lane):
    return values if lane == 0 else pltpu.roll(values, 128 - lane, 1)


def shift_lanes(chunks, shift):
    amount = (128 - shift) & 127
    rolled = [pltpu.roll(chunk, amount, 1) for chunk in chunks]
    lane = lax.broadcasted_iota(jnp.int32, chunks[0].shape, 1)
    first = lane < jnp.maximum(-shift, 0)
    last = lane >= 128 - jnp.maximum(shift, 0)
    zero = jnp.zeros_like(chunks[0])
    padded = [zero, *rolled, zero]
    return [
        jnp.where(first, padded[j], jnp.where(last, padded[j + 2], padded[j + 1]))
        for j in range(len(chunks))
    ]


def fraction(exponent):
    grown = jnp.exp2(exponent)
    frac = pl.reciprocal(1.0 + grown, approx=True)
    return frac, frac * (grown * frac)


def weights(fixed, corner, step, fractions):
    (fz, gz), (fy, gy), (fx, gx) = fractions
    line = [[corner[z][y] + fx * step[z][y] for y in (0, 1)] for z in (0, 1)]
    rise = [line[z][1] - line[z][0] for z in (0, 1)]
    plane = [line[z][0] + fy * rise[z] for z in (0, 1)]
    slope_z = plane[1] - plane[0]
    residual = (plane[0] + fz * slope_z) - fixed
    slope_y = rise[0] + fz * (rise[1] - rise[0])
    along = [step[z][0] + fy * (step[z][1] - step[z][0]) for z in (0, 1)]
    slope_x = along[0] + fz * (along[1] - along[0])
    return [
        (residual * slope_z) * gz,
        (residual * slope_y) * gy,
        (residual * slope_x) * gx,
    ]


def greet(k, s):
    barrier = pltpu.get_barrier_semaphore()

    def signal(slab, sec):
        pl.semaphore_signal(barrier, inc=1, device_id=(slab, sec), device_id_type=MESH)

    @pl.loop(1, SLABS)
    def _(i):
        signal((k + i) & (SLABS - 1), s)

    for i in range(1, SECS):
        other = (s + i) & (SECS - 1)
        signal(k, other)
        signal((k + 1) & (SLABS - 1), other)
        signal((k + SLABS - 1) & (SLABS - 1), other)
    return lambda: pl.semaphore_wait(barrier, SLABS - 1 + 3 * (SECS - 1))


def broadcast_start(k, s, tile, buffer, send_sem, recv_sem):
    @pl.loop(0, SLABS - 1)
    def _(i):
        pltpu.make_async_remote_copy(
            src_ref=tile,
            dst_ref=buffer.at[k],
            send_sem=send_sem,
            recv_sem=recv_sem,
            device_id=((k + 16 + i + (i > 15).astype(jnp.int32)) & (SLABS - 1), s),
            device_id_type=MESH,
        ).start()


def broadcast_wait(buffer, send_sem, recv_sem):
    part = buffer.at[pl.ds(0, SLABS - 1)]
    pltpu.make_async_copy(part, part, recv_sem).wait()
    pltpu.make_async_copy(part, part, send_sem).wait()


def remote(src, dst, send_sem, recv_sem, device):
    return pltpu.make_async_remote_copy(
        src_ref=src,
        dst_ref=dst,
        send_sem=send_sem,
        recv_sem=recv_sem,
        device_id=device,
        device_id_type=MESH,
    )


def around(k, s, source, buffer, send, recv, act):
    slabs = ((k + SLABS - 1) & (SLABS - 1), k, (k + 1) & (SLABS - 1))

    def one(dk, other):
        if act == "wait_recv":
            copy = remote(source, buffer.at[dk, other], send.at[dk, other], recv.at[dk, other], (k, other))
        else:
            copy = remote(
                source, buffer.at[2 - dk, s], send.at[dk, other], recv.at[2 - dk, s], (slabs[dk], other)
            )
        getattr(copy, act)()

    for dk in (0, 2):
        for other in range(SECS):
            one(dk, other)
    for i in range(1, SECS):
        one(1, (s + i) & (SECS - 1))


TABLES = {
    "px": None, "pz": None, "pcx": None, "pcz": None,
    "rows_m": "k", "rows_c": "q", "cspread": "r", "cgather": "r", "cbt": None, "cbx": None,
    "sum_c": "q", "mspread": "rs", "mgather": "rs", "mbt": None, "mbx": None,
    "spread": "rs", "gather": "s", "bt": None, "bx": None, "sum_m": "k",
}


def finish(result, fine_out, mid_out, coarse_out):
    for d in range(3):
        for b in range(5):
            row = 40 * d + 8 * b
            fine_out[d, b] = result[row : row + 4, 0:33]
        for a in range(9):
            for b in range(2):
                row = 120 + 48 * b + 16 * d + a
                mid_out[d, a, b : b + 1, :] = result[row : row + 1, 0:33]
        for a in range(3):
            row = 216 + 16 * d + a
            coarse_out[d, a] = result[row : row + 1, 0:9]


def kernel(
    moving, fixed, lat_fine, lat_mid, lat_coarse, off_fine, off_mid, off_coarse, *refs
):
    n = len(TABLES)
    stored, refs = refs[:n], refs[n:]
    result, *refs = refs
    t = dict(zip(TABLES, refs[:n]))
    (
        pad, fx, sums, zlo, zhi, z_bef, z_aft, y_bef, y_aft, corners,
        lf_own, lf_up, lf_down, lf_prev, lf_next, lf, mt, ct,
        pooled_m, pooled_f, pack_up, pack_down, pm_bef, pm_aft, pm_halo, pm_same,
        piece, pieces, cv, cf, mm,
        c_tile, c_buf, m_part, m_parts, m_tile, m_buf,
        at, by, columns, field_a, field_b, split_a, split_b, adjoint, mixed,
        f_part, f_parts, f_tile, f_buf,
        load_sem, table_sem, send, recv, psend, precv, fsend, frecv, tsend, trecv, bsem,
    ) = refs[n:]
    k, s = lax.axis_index("slab"), lax.axis_index("sec")
    nxt, prv = (k + 1) & (SLABS - 1), (k + SLABS - 1) & (SLABS - 1)
    q, r = k >> 2, k & 3
    has_prev, has_next = (k > 0).astype(F32), (k < SLABS - 1).astype(F32)
    up, down = s < SECS - 1, s > 0
    own_y, own_z = pl.ds(4, NY), pl.ds(8, NZ)

    load_moving = [
        pltpu.make_async_copy(
            moving.at[:, :, pl.ds(128 * c, 128)], pad.at[c, own_y, own_z], load_sem.at[c]
        )
        for c in range(CHUNKS)
    ]
    load_fixed = [
        pltpu.make_async_copy(
            fixed.at[:, :, pl.ds(128 * c, 128)], fx.at[c], load_sem.at[CHUNKS + c]
        )
        for c in range(CHUNKS)
    ]
    place = {"k": k, "q": q, "r": r, "s": s, "rs": 4 * r + s}
    load_table = {}
    for i, (name, which) in enumerate(TABLES.items()):
        source = stored[i] if which is None else stored[i].at[place[which]]
        load_table[name] = pltpu.make_async_copy(source, t[name], table_sem.at[i])
    for copy in load_moving:
        copy.start()
    all_here = greet(k, s)
    for copy in (*load_fixed, *load_table.values()):
        copy.start()

    def table(name):
        load_table[name].wait()
        return t[name]

    lat_to_next = remote(lf_up, lf_prev, send.at[0], recv.at[0], (nxt, s))
    lat_to_prev = remote(lf_down, lf_next, send.at[1], recv.at[1], (prv, s))
    z_to_next = remote(zhi, z_bef, send.at[2], recv.at[2], (nxt, s))
    z_to_prev = remote(zlo, z_aft, send.at[3], recv.at[3], (prv, s))
    to_bef = remote(moving.at[pl.ds(16, 4)], y_bef, send.at[4], recv.at[4], (k, s + 1))
    to_aft = remote(moving.at[pl.ds(0, 4)], y_aft, send.at[5], recv.at[5], (k, s - 1))
    first, last = pl.ds(0, 2), pl.ds(8, 2)
    corner_up = [
        remote(zhi.at[:, last], corners.at[0], send.at[6], recv.at[6], (nxt, s + 1)),
        remote(zlo.at[:, last], corners.at[1], send.at[7], recv.at[7], (prv, s + 1)),
    ]
    corner_down = [
        remote(zhi.at[:, first], corners.at[2], send.at[8], recv.at[8], (nxt, s - 1)),
        remote(zlo.at[:, first], corners.at[3], send.at[9], recv.at[9], (prv, s - 1)),
    ]
    head, tail = pl.ds(0, 8), pl.ds(16, 8)
    mid_same = [
        remote(pooled_m.at[:, tail], pm_same.at[0], send.at[10], recv.at[10], (nxt, s)),
        remote(pooled_m.at[:, head], pm_same.at[1], send.at[11], recv.at[11], (prv, s)),
    ]
    mid_up = [
        remote(pack_up, pm_bef, send.at[12], recv.at[12], (k, s + 1)),
        remote(pack_up.at[:, tail], pm_halo.at[0, 0], send.at[13], recv.at[13], (nxt, s + 1)),
        remote(pack_up.at[:, head], pm_halo.at[1, 0], send.at[14], recv.at[14], (prv, s + 1)),
    ]
    mid_down = [
        remote(pack_down, pm_aft, send.at[15], recv.at[15], (k, s - 1)),
        remote(pack_down.at[:, tail], pm_halo.at[0, 1], send.at[16], recv.at[16], (nxt, s - 1)),
        remote(pack_down.at[:, head], pm_halo.at[1, 1], send.at[17], recv.at[17], (prv, s - 1)),
    ]

    def start_y_halos(*parts_of_z):
        rows = [pl.ds(16 * part, 16) for part in parts_of_z]

        @pl.when(up)
        def _():
            for z in rows:
                remote(moving.at[pl.ds(16, 4), z], y_bef.at[:, z], send.at[4], recv.at[4], (k, s + 1)).start()

        @pl.when(down)
        def _():
            for z in rows:
                remote(moving.at[pl.ds(0, 4), z], y_aft.at[:, z], send.at[5], recv.at[5], (k, s - 1)).start()

    def start(*copies):
        for copy in copies:
            copy.start()

    def start_if(condition, *copies):
        @pl.when(condition)
        def _():
            start(*copies)

    for c in range(CHUNKS):
        pad[c, :, 0:8, :] = jnp.zeros((28, 8, 128), F32)
        pad[c, :, 88:96, :] = jnp.zeros((28, 8, 128), F32)
    all_here()
    start_y_halos(0, 1)
    for c in range(CHUNKS):
        load_moving[c].wait()

        @pl.loop(0, NY // 2, unroll=5)
        def _(pair):
            for half in range(2):
                rows = slice(4 * half, 4 * half + 4)
                zlo[c, pair, rows, :] = pad[c, 2 * pair + half + 4, 8:12, :]
                zhi[c, pair, rows, :] = pad[c, 2 * pair + half + 4, 84:88, :]

    start(z_to_next)

    px, pz = table("px"), table("pz")

    def pooled():
        high, low = parts(sums[...].reshape(400, NX))
        high, low = parts(dot(high, px[...]) + dot(low, px[...]))
        return ((dot(pz[...], high) + dot(pz[...], low)) * (1.0 / 64.0)).reshape(5, 24, 256)

    for c in range(CHUNKS):
        lanes = slice(128 * c, 128 * c + 128)

        @pl.loop(0, 5, unroll=5)
        def _(group):
            four = [pad[c, 4 * group + 4 + i, 8:88, :] for i in range(4)]
            sums[group, :, lanes] = (four[0] + four[1]) + (four[2] + four[3])

    pooled_m[...] = pooled()

    for c in range(CHUNKS):
        load_fixed[c].wait()
        lanes = slice(128 * c, 128 * c + 128)

        @pl.loop(0, 5, unroll=5)
        def _(group):
            four = [fx[c, 4 * group + i] for i in range(4)]
            sums[group, :, lanes] = (four[0] + four[1]) + (four[2] + four[3])

    pooled_f[...] = pooled()

    halves = []
    for ref in (pooled_m, pooled_f):
        upper, lower = jnp.zeros((24, 256), F32), jnp.zeros((24, 256), F32)
        for i in range(5):
            keep = (i + s < 4).astype(F32)
            upper = upper + ref[i] * keep
            lower = lower + ref[i] * (1.0 - keep)
        halves.append(jnp.concatenate([upper, lower], axis=0))
    high, low = parts(jnp.concatenate(halves, axis=1))
    pcx, pcz = table("pcx")[...], table("pcz")[...]
    both = dot(high, pcx) + dot(low, pcx)
    piece[...] = (dot_exact(pcz, both) * (1.0 / 64.0)).reshape(2, 8, 128)
    around(k, s, piece, pieces, psend, precv, "start")
    pieces[1, s] = piece[...]
    for ref, first_y in ((pack_up, 1), (pack_down, 0)):
        ref[0:4] = pooled_m[first_y : first_y + 4, :, 0:128]
        others = [pooled_m[first_y + i, :, 128:256] for i in range(4)]
        ref[4] = (others[0] + pltpu.roll(others[1], 32, 1)) + (
            pltpu.roll(others[2], 64, 1) + pltpu.roll(others[3], 96, 1)
        )
    start(*mid_same)
    start_if(up, *mid_up)
    start_if(down, *mid_down)

    for ref in (lf_own, mt, ct, cv, mm):
        ref[...] = jnp.zeros_like(ref)
    for d in range(3):
        for b in range(5):
            lf_own[d, b, 0:4, 0:33] = lat_fine[d, b]
        for a in range(9):
            for b in range(2):
                row = 32 * d + 16 * b + a
                mt[row : row + 1, 0:33] = lat_mid[d, a, b : b + 1]
        for a in range(3):
            ct[16 * d + a : 16 * d + a + 1, 0:9] = lat_coarse[d, a]
    for d in range(3):
        for b in range(5):
            row = 5 * d + b
            lf_up[row : row + 1, :] = lf_own[d, b, 3:4, :]
            lf_down[2 * row : 2 * row + 2, :] = lf_own[d, b, 0:2, :]
    start(lat_to_next, lat_to_prev)

    def pick_rows(name, ref):
        rows = table(name)[...]
        contract = (((1,), (1,)), ((), ()))
        high, low = parts(ref[...])
        return lax.dot_general(rows, high, contract, preferred_element_type=F32) + lax.dot_general(
            rows, low, contract, preferred_element_type=F32
        )

    rows_m, rows_c = pick_rows("rows_m", mt), pick_rows("rows_c", ct)
    cbt, cspread = table("cbt")[...], table("cspread")[...]
    column = dot3(jnp.concatenate([from_lane(rows_c[0:8], 16 * d) for d in range(3)], axis=0), cbt)
    column = jnp.concatenate([column[8 * d : 8 * d + 8] for d in range(3)], axis=1)
    exponent = dot(cspread, stacked(column, 8))[0:40]
    fractions_c = [fraction(exponent[:, 128 * d : 128 * d + 128]) for d in range(3)]
    cbx, cgather = table("cbx"), table("cgather")

    around(k, s, piece, pieces, psend, precv, "wait_recv")

    lane = lax.broadcasted_iota(jnp.int32, (5, 128), 1)
    for dk in range(3):
        scale = (has_prev, jnp.float32(1.0), has_next)[dk]
        rows = (slice(3, 8), slice(8, 13), slice(13, 18))[dk]
        for c in range(5):
            value = jnp.zeros((8, 128), F32)
            if c < 4:
                value = value + pieces[dk, c, 0]
            if c > 0:
                value = value + pieces[dk, c - 1, 1]
            cv[4 + c, rows, :] = jnp.where(lane < 40, value[0:5], 0.0) * scale
            if dk == 1:
                cf[c] = value
    fixed_c = pltpu.roll(cf[...].reshape(40, 128), 64, 1)

    oz, oy, ox = off_coarse[0, 0, q], off_coarse[1, 0, q], off_coarse[2, 0, q]
    a_z, b_z = [], []
    for e in (0, 1):
        window = cv[pl.ds(4 + oy, 6), pl.ds(8 + oz + e, 8), :].reshape(48, 128)
        here, there = shift_lanes([window], ox)[0], shift_lanes([window], ox + 1)[0]
        a_z.append(here)
        b_z.append(there - here)
    corner = [[a_z[z][8 * y : 8 * y + 40] for y in (0, 1)] for z in (0, 1)]
    step = [[b_z[z][8 * y : 8 * y + 40] for y in (0, 1)] for z in (0, 1)]
    total = jnp.concatenate(weights(fixed_c, corner, step, fractions_c), axis=1)
    total = dot_wide(jnp.concatenate([total, jnp.zeros((8, 384), F32)], axis=0), cbx[...])
    total = jnp.concatenate([total, jnp.zeros((80, 128), F32)], axis=0)
    c_tile[...] = dot_gather(cgather[...], total)[0:8]
    broadcast_start(k, s, c_tile, c_buf, bsem.at[0], bsem.at[1])
    c_buf[k] = c_tile[...]
    start_y_halos(2, 3)
    start(z_to_prev)

    mbt, mspread, mbx, mgather = table("mbt"), table("mspread"), table("mbx"), table("mgather")
    own = [from_lane(rows_m[0:8], 32 * d + 16 * b) for d in range(3) for b in range(2)]
    own = dot3(jnp.concatenate(own, axis=0), mbt[0])
    coarse = dot3(jnp.concatenate([from_lane(rows_c[8:16], 16 * d) for d in range(3)], axis=0), mbt[1])
    column = [
        jnp.concatenate([own[16 * d : 16 * d + 16], coarse[8 * d : 8 * d + 8]], axis=0) for d in range(3)
    ]
    base_m = dot(mspread[...], stacked(jnp.concatenate(column, axis=1), 24))[0:120]
    sum_c = table("sum_c")

    @pl.when(s == 0)
    def _():
        y_bef[...] = jnp.zeros_like(y_bef)
        corners[0:2] = jnp.zeros((2, CHUNKS, 2, 8, 128), F32)
        pm_bef[...] = jnp.zeros_like(pm_bef)
        pm_halo[:, 0] = jnp.zeros((2, 5, 8, 128), F32)

    @pl.when(s == SECS - 1)
    def _():
        y_aft[...] = jnp.zeros_like(y_aft)
        corners[2:4] = jnp.zeros((2, CHUNKS, 2, 8, 128), F32)
        pm_aft[...] = jnp.zeros_like(pm_aft)
        pm_halo[:, 1] = jnp.zeros((2, 5, 8, 128), F32)

    for copy in mid_same:
        copy.wait_recv()

    @pl.when(s > 0)
    def _():
        for copy in mid_up:
            copy.wait_recv()

    @pl.when(s < SECS - 1)
    def _():
        for copy in mid_down:
            copy.wait_recv()

    for c in range(2):
        lanes = slice(128 * c, 128 * c + 128)
        for y in range(5):
            mm[c, 5 + y, 4:8, :] = pm_same[0, y, 0:4, lanes] * has_prev
            mm[c, 5 + y, 8:28, :] = pooled_m[y, 0:20, lanes]
            mm[c, 5 + y, 28:32, :] = pm_same[1, y, 0:4, lanes] * has_next
    few = lax.broadcasted_iota(jnp.int32, (24, 128), 1) < 32
    for e, (whole, first_y) in enumerate(((pm_bef, 1), (pm_aft, 10))):
        for y in range(4):
            for c in range(2):

                def row(ref):
                    value = ref[y] if c == 0 else from_lane(ref[4], 32 * y)
                    return value if c == 0 else jnp.where(few[0 : value.shape[0]], value, 0.0)

                mm[c, first_y + y, 4:8, :] = row(pm_halo.at[0, e])[0:4] * has_prev
                mm[c, first_y + y, 8:28, :] = row(whole)[0:20]
                mm[c, first_y + y, 28:32, :] = row(pm_halo.at[1, e])[0:4] * has_next

    oz, oy, ox = off_mid[0, 0, 0], off_mid[0, 0, 1], off_mid[0, 0, 2]
    a_z, b_z = [], []
    for e in (0, 1):
        window = [mm[c, pl.ds(5 + oy, 6), pl.ds(8 + oz + e, 24), :].reshape(144, 128) for c in range(2)]
        here, there = shift_lanes(window, ox), shift_lanes(window, ox + 1)
        a_z.append(here)
        b_z.append([there[c] - here[c] for c in range(2)])

    def make_window(block, oz, oy, ox, y):
        window = [pad[c, 4 + oy + y, pl.ds(20 * block + 8 + oz, 24), :] for c in range(CHUNKS)]
        here, there = shift_lanes(window, ox), shift_lanes(window, ox + 1)
        for c in range(CHUNKS):
            at[block, c, y, 8:32, :] = here[c]
            by[block, c, y, 8:32, :] = there[c] - here[c]

    def make_windows(blocks, ranges):
        @pl.loop(*blocks)
        def _(block):
            offsets = [off_fine[d, block, s] for d in range(3)]
            for first_y, last_y, unroll in ranges:
                pl.loop(first_y, last_y, unroll=unroll)(functools.partial(make_window, block, *offsets))

    broadcast_wait(c_buf, bsem.at[0], bsem.at[1])
    gradient = dot_exact(sum_c[...], c_buf[...].reshape(256, 128))
    near_c = gradient[16:24]
    gradient = gradient[0:16]
    inverse = lax.rsqrt(jnp.sum(gradient * gradient) * (1.0 / 81.0) + EPSILON)

    near = dot3(jnp.concatenate([from_lane(near_c, 16 * d) for d in range(3)], axis=0), mbt[1])
    near = jnp.concatenate([near[8 * d : 8 * d + 8] for d in range(3)], axis=1)
    near = dot(mspread[...], stacked(jnp.concatenate([jnp.zeros((16, 768), F32), near], axis=0), 24))
    exponent = base_m - (STEP_SIZE * inverse) * near[0:120]
    fixed_m = pooled_f[...].reshape(120, 256)
    found = []
    for c in range(2):
        lanes = slice(128 * c, 128 * c + 128)
        corner = [[a_z[z][c][24 * y : 24 * y + 120] for y in (0, 1)] for z in (0, 1)]
        step = [[b_z[z][c][24 * y : 24 * y + 120] for y in (0, 1)] for z in (0, 1)]
        fractions = [fraction(exponent[:, 256 * d + 128 * c : 256 * d + 128 * c + 128]) for d in range(3)]
        found.append(weights(fixed_m[:, lanes], corner, step, fractions))
    total = jnp.concatenate([found[c][d] for d in range(3) for c in range(2)], axis=1)
    total = dot_wide(jnp.concatenate([total, jnp.zeros((8, 768), F32)], axis=0), mbx[...])
    m_part[...] = dot_gather(mgather[...], total)

    def part_copies(act):
        for i in range(1, SECS):
            other = (s + i) & (SECS - 1)
            slot = other if act == "wait_recv" else s
            getattr(remote(m_part, m_parts.at[slot], tsend.at[other], trecv.at[slot], (k, other)), act)()

    part_copies("start")
    start_y_halos(4)
    start_if(up, *corner_up)
    start_if(down, *corner_down)
    m_parts[s] = m_part[...]

    gradient = gradient * inverse
    next_c = [
        from_lane(rows_c[8:16], 16 * d) - (STEP_SIZE * inverse) * from_lane(near_c, 16 * d) for d in range(3)
    ]
    for copy in (lat_to_next, lat_to_prev):
        copy.wait_recv()
    for d in range(3):
        for b in range(5):
            lf[d, 8 * b : 8 * b + 1, :] = lf_prev[5 * d + b : 5 * d + b + 1, :] * has_prev
            lf[d, 8 * b + 1 : 8 * b + 5, :] = lf_own[d, b, 0:4, :]
            lf[d, 8 * b + 5 : 8 * b + 7, :] = lf_next[10 * d + 2 * b : 10 * d + 2 * b + 2, :] * has_next
            lf[d, 8 * b + 7 : 8 * b + 8, :] = jnp.zeros((1, 128), F32)
    bt = table("bt")
    own = dot3(lf[...].reshape(120, 128), bt[0])
    mid = [from_lane(rows_m[8:16], 32 * d + 16 * b) for d in range(3) for b in range(2)]
    mid = dot3(jnp.concatenate(mid, axis=0), bt[1])
    coarse = dot3(jnp.concatenate(next_c, axis=0), bt[2])
    base_f = [
        jnp.concatenate(
            [own[40 * d : 40 * d + 40], mid[16 * d : 16 * d + 16], coarse[8 * d : 8 * d + 8]], axis=0
        )
        for d in range(3)
    ]
    base_f = jnp.concatenate(base_f, axis=1)

    make_windows((1, 3), ((4, 16, 3),))
    part_copies("wait_recv")
    m_tile[...] = (m_parts[0] + m_parts[1]) + (m_parts[2] + m_parts[3])
    broadcast_start(k, s, m_tile, m_buf, bsem.at[2], bsem.at[3])
    m_buf[k] = m_tile[...]

    turn_r = lax.broadcasted_iota(jnp.int32, (48, 128), 0)
    turn = jnp.where(turn_r == lax.broadcasted_iota(jnp.int32, (48, 128), 1) + 2, 1.0, 0.0)
    result[216:264, :] = dot_rows(gradient, turn[0:16])[0:48]

    for copy in (z_to_next, z_to_prev):
        copy.wait_recv()

    @pl.when(s > 0)
    def _():
        for copy in (to_bef, *corner_up):
            copy.wait_recv()

    @pl.when(s < SECS - 1)
    def _():
        for copy in (to_aft, *corner_down):
            copy.wait_recv()

    for c in range(CHUNKS):
        lanes = slice(128 * c, 128 * c + 128)
        pad[c, 0:4, 8:88, :] = y_bef[:, :, lanes]
        pad[c, 24:28, 8:88, :] = y_aft[:, :, lanes]

    @pl.loop(0, NY // 2, unroll=2)
    def _(pair):
        for half in range(2):
            rows = slice(4 * half, 4 * half + 4)
            for c in range(CHUNKS):
                pad[c, 2 * pair + half + 4, 4:8, :] = z_bef[c, pair, rows, :] * has_prev
                pad[c, 2 * pair + half + 4, 88:92, :] = z_aft[c, pair, rows, :] * has_next

    for y in range(4):
        rows = slice(4 * (y % 2), 4 * (y % 2) + 4)
        for c in range(CHUNKS):
            for n in range(2):
                where = slice(4, 8) if n == 0 else slice(88, 92)
                keep = has_prev if n == 0 else has_next
                pad[c, y, where, :] = corners[n, c, y // 2, rows, :] * keep
                pad[c, 24 + y, where, :] = corners[2 + n, c, y // 2, rows, :] * keep

    make_windows((1, 3), ((0, 4, 2), (16, 21, 5)))
    make_windows((0, 1), ((0, 21, 3),))
    make_windows((3, 4), ((0, 21, 3),))

    spread, gather, bx, sum_m = table("spread"), table("gather"), table("bx"), table("sum_m")

    broadcast_wait(m_buf, bsem.at[2], bsem.at[3])
    gradient = dot_exact(sum_m[...], m_buf[...].reshape(512, 128))
    near = gradient[96:112]
    gradient = gradient[0:96]
    inverse = lax.rsqrt(jnp.sum(gradient * gradient) * (1.0 / 1782.0) + EPSILON)

    near = dot3(jnp.concatenate([from_lane(near, 16 * d) for d in range(3)], axis=0), bt[1])
    near = jnp.concatenate([near[16 * d : 16 * d + 16] for d in range(3)], axis=1)
    near = jnp.concatenate([jnp.zeros((40, 3 * NX), F32), near, jnp.zeros((8, 3 * NX), F32)], axis=0)
    upper, lower = parts(base_f - (STEP_SIZE * inverse) * near)
    columns[0:64, :] = upper
    columns[64:128, :] = upper
    columns[128:192, :] = lower
    columns[192:256, :] = lower
    field_a[...] = dot(spread[0:400, :], columns[...])

    first_rows = lax.broadcasted_iota(jnp.int32, (8, 128), 0) < 4
    steps_z = (jnp.minimum(k, 0), jnp.minimum(k + 1, 1))

    def planes(ref, pair, c, y, z):
        a, b = 2 * pair, 2 * pair + 1
        middle = jnp.where(
            first_rows, ref[a, c, y, pl.ds(24 + z, 8), :], ref[b, c, y, pl.ds(4 + z, 8), :]
        )
        return jnp.concatenate(
            [ref[a, c, y, pl.ds(8 + z, 16), :], middle, ref[b, c, y, pl.ds(12 + z, 16), :]], axis=0
        )

    def fine_stage(stage, split, split_before, field, field_after):
        adjoint[...] = jnp.zeros_like(adjoint)
        pair, y_first = stage >> 1, 10 * (stage & 1)
        after = pl.ds(pl.multiple_of(400 * jnp.minimum(stage + 1, 3), 400), 400)

        @pl.loop(0, 5)
        def _(i):
            lanes = pl.ds(pl.multiple_of(384 * i, 384), 384)
            field_after[:, lanes] = dot(spread[after, :], columns[:, lanes])
            lanes = pl.ds(pl.multiple_of(768 * i, 768), 768)
            adjoint[...] += dot(split_before[:, lanes], bx[lanes, :])
            for c in range(CHUNKS):
                found = []
                for h in range(2):
                    y = y_first + 2 * i + h
                    corner = [[planes(at, pair, c, y + e, z) for e in (0, 1)] for z in steps_z]
                    step = [[planes(by, pair, c, y + e, z) for e in (0, 1)] for z in steps_z]
                    rows = pl.ds(pl.multiple_of(80 * i + 40 * h, 8), 40)
                    fractions = [
                        fraction(field[rows, NX * d + 128 * c : NX * d + 128 * c + 128]) for d in range(3)
                    ]
                    atlas = fx[c, y, pl.ds(pl.multiple_of(40 * pair, 8), 40), :]
                    found.append(weights(atlas, corner, step, fractions))
                rows = pl.ds(pl.multiple_of(80 * i, 80), 80)
                for d in range(3):
                    upper, lower = parts(jnp.concatenate([found[0][d], found[1][d]], axis=0))
                    lane = 2 * NX * d + 128 * c
                    split[rows, lane : lane + 128] = upper
                    split[rows, lane + NX : lane + NX + 128] = lower

        before = pl.ds(pl.multiple_of(400 * jnp.maximum(stage - 1, 0), 400), 400)
        mixed[before, :] = adjoint[:, 0:128] + adjoint[:, 128:256]

    @pl.loop(0, 2)
    def _(two):
        fine_stage(2 * two, split_a, split_b, field_a, field_b)
        fine_stage(2 * two + 1, split_b, split_a, field_b, field_a)

    wide = dot(split_b[...], bx[...])
    mixed[1200:1600, :] = wide[:, 0:128] + wide[:, 128:256]
    f_part[...] = dot_gather(gather[...], mixed[...])
    around(k, s, f_part, f_parts, fsend, frecv, "start")
    f_parts[1, s] = f_part[...]

    for b in range(2):
        turned = dot_rows(gradient[48 * b : 48 * b + 48] * inverse, turn)
        result[120 + 48 * b : 168 + 48 * b, :] = turned[0:48]
    row = lax.broadcasted_iota(jnp.int32, (40, 128), 0) & 7

    around(k, s, f_part, f_parts, fsend, frecv, "wait_recv")
    before, middle, after = ((f_parts[i, 0] + f_parts[i, 1]) + (f_parts[i, 2] + f_parts[i, 3]) for i in range(3))
    middle = middle + jnp.where((row == 1) | (row == 2), pltpu.roll(before * has_prev, 36, 0), 0.0)
    middle = middle + jnp.where(row == 4, pltpu.roll(after * has_next, 4, 0), 0.0)
    middle = jnp.where((row >= 1) & (row <= 4), middle, 0.0)
    f_tile[...] = jnp.full((8, 128), jnp.sum(middle * middle))
    broadcast_start(k, s, f_tile, f_buf, bsem.at[4], bsem.at[5])
    f_buf[k] = f_tile[...]

    for copy in (lat_to_next, lat_to_prev, z_to_next, z_to_prev, *mid_same):
        copy.wait_send()

    @pl.when(up)
    def _():
        for copy in (to_bef, *corner_up, *mid_up):
            copy.wait_send()

    @pl.when(down)
    def _():
        for copy in (to_aft, *corner_down, *mid_down):
            copy.wait_send()

    around(k, s, piece, pieces, psend, precv, "wait_send")
    around(k, s, f_part, f_parts, fsend, frecv, "wait_send")
    part_copies("wait_send")
    middle = pltpu.roll(middle, 39, 0)
    thirds = [from_lane(middle, 40 * d) for d in range(3)]

    broadcast_wait(f_buf, bsem.at[4], bsem.at[5])
    squares = jnp.sum(f_buf[...], axis=0)[0:1, :]
    inverse = lax.rsqrt(squares * (1.0 / 63360.0) + EPSILON)
    for d in range(3):
        result[40 * d : 40 * d + 40, :] = thirds[d] * inverse


def body(
    fixed_image,
    moving_image,
    lattice_fine,
    lattice_mid,
    lattice_coarse,
    offset_fine,
    offset_mid,
    offset_coarse,
):
    t = tables()
    vmem, smem, hbm = (pl.BlockSpec(memory_space=m) for m in (pltpu.VMEM, pltpu.SMEM, pl.ANY))
    shape = lambda *dims: jax.ShapeDtypeStruct(dims, F32)
    buf = lambda *dims: pltpu.VMEM(dims, F32)
    half = lambda *dims: pltpu.VMEM(dims, BF16)
    dma = lambda *dims: pltpu.SemaphoreType.DMA(dims)
    result = pl.pallas_call(
        kernel,
        out_shape=shape(264, 128),
        in_specs=[hbm, hbm, vmem, vmem, vmem, smem, smem, smem] + [hbm] * len(TABLES),
        out_specs=vmem,
        scratch_shapes=[
            *[pltpu.VMEM(t[n].shape[which is not None :], t[n].dtype) for n, which in TABLES.items()],
            buf(CHUNKS, 28, 96, 128), buf(CHUNKS, NY, NZ, 128), buf(5, NZ, NX),
            *[buf(CHUNKS, 10, 8, 128)] * 4, *[buf(4, NZ, NX)] * 2, buf(4, CHUNKS, 2, 8, 128),
            buf(3, 5, 8, 128), *[buf(16, 128), buf(32, 128)] * 2, buf(3, 40, 128), buf(128, 128), buf(128, 128),
            *[buf(5, 24, 256)] * 2, *[buf(5, 24, 128)] * 4, buf(2, 2, 5, 8, 128), buf(2, 5, 8, 256),
            buf(2, 8, 128), buf(3, SECS, 2, 8, 128), buf(14, 32, 128), buf(5, 8, 128), buf(2, 15, 40, 128),
            buf(8, 128), buf(SLABS, 8, 128), buf(16, 128), buf(SECS, 16, 128), buf(16, 128), buf(SLABS, 16, 128),
            *[buf(4, CHUNKS, 21, 40, 128)] * 2, half(256, 3 * NX),
            *[buf(400, 3 * NX)] * 2, *[half(400, 6 * NX)] * 2, buf(400, 256), buf(1600, 128),
            buf(40, 128), buf(3, SECS, 40, 128), buf(8, 128), buf(SLABS, 8, 128),
            dma(10), dma(len(TABLES)), dma(18), dma(18), *[dma(3, SECS)] * 4, dma(SECS), dma(SECS), dma(6),
        ],
        compiler_params=pltpu.CompilerParams(
            collective_id=0, has_side_effects=True, vmem_limit_bytes=VMEM_LIMIT
        ),
        name="mega",
    )(
        jnp.transpose(moving_image, (1, 0, 2)),
        jnp.transpose(fixed_image, (1, 0, 2)),
        jnp.transpose(lattice_fine, (0, 2, 1, 3)),
        jnp.transpose(lattice_mid, (0, 3, 2, 1)),
        jnp.transpose(lattice_coarse, (0, 3, 2, 1)),
        offset_fine,
        jnp.transpose(offset_mid, (1, 2, 0)),
        jnp.transpose(offset_coarse, (0, 2, 1)),
        *(t[n] for n in TABLES),
    )
    fine, mid, coarse = pl.pallas_call(
        finish,
        out_shape=[shape(3, 5, 4, 33), shape(3, 9, 2, 33), shape(3, 3, 1, 9)],
        in_specs=[vmem],
        out_specs=[vmem] * 3,
        name="finish",
    )(result)
    return (
        jnp.transpose(fine, (0, 2, 1, 3)),
        jnp.transpose(mid, (0, 3, 2, 1)),
        jnp.transpose(coarse, (0, 3, 2, 1)),
    )


def solution(mesh):
    placed = (
        P("slab", "sec", None),
        P("slab", "sec", None),
        P(None, "slab", None, None),
        P(),
        P(),
        P(None, "slab", None),
        P(None, "slab", None),
        P(),
    )
    return jax.shard_map(
        body,
        mesh=mesh,
        in_specs=placed,
        out_specs=(P(None, "slab", None, None), P(), P()),
        check_vma=False,
    )
```

```python
import functools

import jax
import jax.numpy as jnp
import ml_dtypes
import numpy as np
from jax import lax
from jax.experimental import pallas as pl
from jax.experimental.pallas import tpu as pltpu
from jax.sharding import PartitionSpec as P

SP = 20
EPSILON = 1e-06
STEP_SIZE = 0.5
HIGHEST = lax.Precision.HIGHEST
F32 = jnp.float32
BF16 = jnp.bfloat16
MESH = pl.DeviceIdType.MESH
SLABS = 32
SECS = 4
NZ, NY, NX = 80, 20, 640
CHUNKS = NX // 128
LOG2E = 1.4426950408889634
VMEM_LIMIT = 58 * 1024 * 1024


def basis(rows, knots, factor, coarse):
    rows, knots = np.asarray(rows, np.float64), np.asarray(knots, np.float64)
    position = factor * rows + 0.5 * (factor - 1)
    centre = SP * coarse * knots + 0.5 * (coarse - 1)
    distance = np.abs((position[:, None] - centre[None, :]) / (SP * coarse))
    near = 2.0 / 3.0 - distance**2 + 0.5 * distance**3
    far = np.maximum(2.0 - distance, 0.0) ** 3 / 6.0
    return np.where(distance < 1.0, near, far)


def two_parts(values):
    high = values.astype(ml_dtypes.bfloat16)
    low = (values - high.astype(np.float64)).astype(ml_dtypes.bfloat16)
    return high, low


def right_parts(values):
    high, low = two_parts(values)
    return np.concatenate([high, low, high], axis=-2)


def wide_parts(values):
    high, low = two_parts(values)
    zero = np.zeros_like(high)
    return np.concatenate([np.concatenate([high, low], 1), np.concatenate([high, zero], 1)], 0)


def one_hot(condition):
    return condition.astype(ml_dtypes.bfloat16)


@functools.cache
def tables():
    t = {}
    rz, ry = np.zeros((4, 4, 20, 64)), np.zeros((4, NY, 64))
    z, y, x = np.arange(NZ), np.arange(NY), np.arange(NX)
    for r in range(4):
        for block in range(4):
            rows = z[20 * block : 20 * block + 20]
            for a in range(7):
                rz[r, block, :, a:40:8] = basis(rows, [a - 1], 1, 1)
            for a in range(5):
                rz[r, block, :, 40 + a : 56 : 8] = basis(rows, [a - 2], 1, 4)
                rz[r, block, :, 56 + a : 57 + a] = basis(rows + 80 * r, [a - 2], 1, 16)
    for s in range(4):
        for a in range(7):
            ry[s, :, a:40:8] = basis(y + 20 * s, range(5), 1, 1)
        for a in range(5):
            ry[s, :, 40 + a : 56 : 8] = basis(y + 20 * s, range(2), 1, 4)
            ry[s, :, 56 + a : 57 + a] = basis(y + 20 * s, [0], 1, 16)
    rz = rz.reshape(4, 2, 40, 64)
    whole = rz[:, None, :, None] * ry[None, :, None, :, None, :]
    high, low = two_parts(whole.reshape(16, 1600, 64))
    t["spread"] = np.concatenate([high, low, high, low], axis=2)
    t["gather"] = np.concatenate([high[:4, :, :40], low[:4, :, :40]], axis=2).transpose(0, 2, 1)
    across = np.zeros((3, 128, NX))
    across[0, :33] = basis(x, range(33), 1, 1).T
    across[1, :9] = basis(x, range(9), 1, 4).T
    across[2, :3] = basis(x, range(3), 1, 16).T
    t["bt"] = right_parts(-LOG2E * across)
    along = np.zeros((3, NX, 128))
    for d in range(3):
        along[d, :, 40 * d : 40 * d + 33] = basis(x, range(33), 1, 1)
    t["bx"] = np.concatenate([wide_parts(along[d]) for d in range(3)], axis=0)
    rz, ry = np.zeros((4, 24, 32)), np.zeros((4, 5, 32))
    z, y, x = np.arange(20), np.arange(5), np.arange(160)
    for r in range(4):
        for a in range(4):
            rz[r, :20, a:16:8] = basis(z, [a - 1], 4, 4)
        for a in range(5):
            rz[r, :20, 16 + a : 17 + a] = basis(z + 20 * r, [a - 2], 4, 16)
    for s in range(4):
        for a in range(4):
            ry[s, :, a:16:8] = basis(y + 5 * s, range(2), 4, 4)
        for a in range(5):
            ry[s, :, 16 + a : 17 + a] = basis(y + 5 * s, [0], 4, 16)
    whole = np.zeros((16, 128, 32))
    whole[:, :120] = (rz[:, None, None] * ry[None, :, :, None]).reshape(16, 120, 32)
    high, low = two_parts(whole)
    t["mspread"] = np.concatenate([high, high, low, np.zeros_like(low)], axis=2)
    t["mgather"] = np.concatenate([high[:, :, :16], low[:, :, :16]], axis=2).transpose(0, 2, 1)
    across = np.zeros((2, 128, 256))
    across[0, :9, :160] = basis(x, range(9), 4, 4).T
    across[1, :3, :160] = basis(x, range(3), 4, 16).T
    t["mbt"] = right_parts(-LOG2E * across)
    along = np.zeros((3, 256, 128))
    for d in range(3):
        along[d, :160, 16 * d : 16 * d + 9] = basis(x, range(9), 4, 4)
    t["mbx"] = wide_parts(along.reshape(768, 128))
    rz = np.zeros((4, 8, 32))
    z, y, x = np.arange(5), np.arange(5), np.arange(40)
    for r in range(4):
        for a in range(4):
            rz[r, :5, a : a + 1] = basis(z + 5 * r, [a - 1], 16, 16)
    whole = np.zeros((4, 128, 32))
    whole[:, :40] = (rz[:, None] * basis(y, [0], 16, 16)[None, :, None]).reshape(4, 40, 32)
    high, low = two_parts(whole)
    t["cspread"] = np.concatenate([high, high, low, np.zeros_like(low)], axis=2)
    t["cgather"] = np.concatenate([high[:, :, :16], low[:, :, :16]], axis=2).transpose(0, 2, 1)
    across = np.zeros((128, 128))
    across[:3, :40] = basis(x, range(3), 16, 16).T
    t["cbt"] = right_parts(-LOG2E * across)
    along = np.zeros((3, 128, 128))
    for d in range(3):
        along[d, :40, 16 * d : 16 * d + 3] = basis(x, range(3), 16, 16)
    t["cbx"] = wide_parts(along.reshape(384, 128))
    row, column = np.arange(NX)[:, None], np.arange(256)[None, :]
    t["px"] = one_hot(row // 4 == column)
    row, column = np.arange(120)[:, None], np.arange(400)[None, :]
    t["pz"] = one_hot((row // 24 == column // 80) & (row % 24 == column % 80 // 4))
    row, column = np.arange(512)[:, None], np.arange(128)[None, :]
    t["pcx"] = one_hot((row % 256 < 160) & (row // 256 * 64 + row % 256 // 4 == column))
    row, column = np.arange(16)[:, None], np.arange(48)[None, :]
    t["pcz"] = one_hot((row // 8 == column // 24) & (column % 24 < 20) & (row % 8 == column % 24 // 4))
    row, column, place = np.arange(16)[:, None], np.arange(128)[None, :], np.arange(32)[:, None, None]
    knot = place - 1 - row // 8 + row % 8
    t["rows_m"] = one_hot((knot == column) & (column < 33))
    t["rows_c"] = one_hot((knot == column) & (column < 9))[:8]
    row, column, place = np.arange(24)[:, None], np.arange(256)[None, :], np.arange(8)[:, None, None]
    knot = np.where(row < 16, row - 2, row - 16 + place - 2)
    found = (knot == column // 32 - 1 + column % 8) & (column % 8 < 4) & (knot >= 0) & (knot < 9)
    t["sum_c"] = one_hot(found)
    row, column, place = np.arange(112)[:, None], np.arange(512)[None, :], np.arange(32)[:, None, None]
    knot = np.where(row < 96, row % 48 - 2, row % 8 + place - 2)
    b = np.where(row < 96, row // 48, (row - 96) // 8)
    found = (knot == column // 16 - 1 + column % 8) & (column % 8 < 4) & (column // 8 % 2 == b)
    t["sum_m"] = one_hot(found & (knot >= 0) & (knot < 33))
    return t


def dot(a, b):
    return jnp.dot(a, b, preferred_element_type=F32)


def dot_rows(a, b):
    return lax.dot_general(
        a, b, (((0,), (0,)), ((), ())), precision=HIGHEST, preferred_element_type=F32
    )


def parts(values):
    high = values.astype(BF16)
    return high, (values - high.astype(F32)).astype(BF16)


def dot3(a, right):
    high, low = parts(a)
    return dot(jnp.concatenate([high, high, low], axis=1), right)


def dot_wide(a, table):
    wide = dot(jnp.concatenate(parts(a), axis=1), table)
    return wide[:, 0:128] + wide[:, 128:256]


def dot_exact(table, b):
    wide = dot(table, jnp.concatenate(parts(b), axis=1))
    return wide[:, 0:128] + wide[:, 128:256]


def dot_gather(table, b):
    n = table.shape[0] // 2
    wide = dot(table, jnp.concatenate(parts(b), axis=1))
    return (wide[0:n, 0:128] + wide[0:n, 128:256]) + wide[n:, 0:128]


def stacked(column, n):
    high, low = parts(jnp.concatenate([column, jnp.zeros((32 - n, column.shape[1]), F32)], axis=0))
    return jnp.concatenate([high, low, high, jnp.zeros_like(low)], axis=0)


def from_lane(values, lane):
    return values if lane == 0 else pltpu.roll(values, 128 - lane, 1)


def shift_lanes(chunks, shift):
    amount = (128 - shift) & 127
    rolled = [pltpu.roll(chunk, amount, 1) for chunk in chunks]
    lane = lax.broadcasted_iota(jnp.int32, chunks[0].shape, 1)
    first = lane < jnp.maximum(-shift, 0)
    last = lane >= 128 - jnp.maximum(shift, 0)
    zero = jnp.zeros_like(chunks[0])
    padded = [zero, *rolled, zero]
    return [
        jnp.where(first, padded[j], jnp.where(last, padded[j + 2], padded[j + 1]))
        for j in range(len(chunks))
    ]


def fraction(exponent):
    grown = jnp.exp2(exponent)
    frac = pl.reciprocal(1.0 + grown, approx=True)
    return frac, frac * (grown * frac)


def weights(fixed, corner, step, fractions):
    (fz, gz), (fy, gy), (fx, gx) = fractions
    line = [[corner[z][y] + fx * step[z][y] for y in (0, 1)] for z in (0, 1)]
    rise = [line[z][1] - line[z][0] for z in (0, 1)]
    plane = [line[z][0] + fy * rise[z] for z in (0, 1)]
    slope_z = plane[1] - plane[0]
    residual = (plane[0] + fz * slope_z) - fixed
    slope_y = rise[0] + fz * (rise[1] - rise[0])
    along = [step[z][0] + fy * (step[z][1] - step[z][0]) for z in (0, 1)]
    slope_x = along[0] + fz * (along[1] - along[0])
    return [
        (residual * slope_z) * gz,
        (residual * slope_y) * gy,
        (residual * slope_x) * gx,
    ]


def greet(k, s):
    barrier = pltpu.get_barrier_semaphore()

    def signal(slab, sec):
        pl.semaphore_signal(barrier, inc=1, device_id=(slab, sec), device_id_type=MESH)

    @pl.loop(1, SLABS)
    def _(i):
        signal((k + i) & (SLABS - 1), s)

    for i in range(1, SECS):
        other = (s + i) & (SECS - 1)
        signal(k, other)
        signal((k + 1) & (SLABS - 1), other)
        signal((k + SLABS - 1) & (SLABS - 1), other)
    return lambda: pl.semaphore_wait(barrier, SLABS - 1 + 3 * (SECS - 1))


def broadcast_start(k, s, tile, buffer, send_sem, recv_sem):
    @pl.loop(0, SLABS - 1)
    def _(i):
        pltpu.make_async_remote_copy(
            src_ref=tile,
            dst_ref=buffer.at[k],
            send_sem=send_sem,
            recv_sem=recv_sem,
            device_id=((k + 16 + i + (i > 15).astype(jnp.int32)) & (SLABS - 1), s),
            device_id_type=MESH,
        ).start()


def broadcast_wait(buffer, send_sem, recv_sem):
    part = buffer.at[pl.ds(0, SLABS - 1)]
    pltpu.make_async_copy(part, part, recv_sem).wait()
    pltpu.make_async_copy(part, part, send_sem).wait()


def remote(src, dst, send_sem, recv_sem, device):
    return pltpu.make_async_remote_copy(
        src_ref=src,
        dst_ref=dst,
        send_sem=send_sem,
        recv_sem=recv_sem,
        device_id=device,
        device_id_type=MESH,
    )


def around(k, s, source, buffer, send, recv, act):
    slabs = ((k + SLABS - 1) & (SLABS - 1), k, (k + 1) & (SLABS - 1))

    def one(dk, other):
        if act == "wait_recv":
            copy = remote(source, buffer.at[dk, other], send.at[dk, other], recv.at[dk, other], (k, other))
        else:
            copy = remote(
                source, buffer.at[2 - dk, s], send.at[dk, other], recv.at[2 - dk, s], (slabs[dk], other)
            )
        getattr(copy, act)()

    for dk in (0, 2):
        for other in range(SECS):
            one(dk, other)
    for i in range(1, SECS):
        one(1, (s + i) & (SECS - 1))


TABLES = {
    "px": None, "pz": None, "pcx": None, "pcz": None,
    "rows_m": "k", "rows_c": "q", "cspread": "r", "cgather": "r", "cbt": None, "cbx": None,
    "sum_c": "q", "mspread": "rs", "mgather": "rs", "mbt": None, "mbx": None,
    "spread": "rs", "gather": "s", "bt": None, "bx": None, "sum_m": "k",
}


def finish(result, fine_out, mid_out, coarse_out):
    for d in range(3):
        for b in range(5):
            row = 40 * d + 8 * b
            fine_out[d, b] = result[row : row + 4, 0:33]
        for a in range(9):
            for b in range(2):
                row = 120 + 48 * b + 16 * d + a
                mid_out[d, a, b : b + 1, :] = result[row : row + 1, 0:33]
        for a in range(3):
            row = 216 + 16 * d + a
            coarse_out[d, a] = result[row : row + 1, 0:9]


def kernel(
    moving, fixed, lat_fine, lat_mid, lat_coarse, off_fine, off_mid, off_coarse, *refs
):
    n = len(TABLES)
    stored, refs = refs[:n], refs[n:]
    result, *refs = refs
    t = dict(zip(TABLES, refs[:n]))
    (
        pad, fx, sums, zlo, zhi, z_bef, z_aft, y_bef, y_aft, corners,
        lf_own, lf_up, lf_down, lf_prev, lf_next, lf, mt, ct,
        pooled_m, pooled_f, pack_up, pack_down, pm_bef, pm_aft, pm_halo, pm_same,
        piece, pieces, cv, cf, mm,
        c_tile, c_buf, m_part, m_parts, m_tile, m_buf,
        at, by, columns, field_a, field_b, split_a, split_b, adjoint, mixed,
        f_part, f_parts, f_tile, f_buf,
        load_sem, table_sem, send, recv, psend, precv, fsend, frecv, tsend, trecv, bsem,
    ) = refs[n:]
    k, s = lax.axis_index("slab"), lax.axis_index("sec")
    nxt, prv = (k + 1) & (SLABS - 1), (k + SLABS - 1) & (SLABS - 1)
    q, r = k >> 2, k & 3
    has_prev, has_next = (k > 0).astype(F32), (k < SLABS - 1).astype(F32)
    up, down = s < SECS - 1, s > 0
    own_y, own_z = pl.ds(4, NY), pl.ds(8, NZ)

    load_moving = [
        pltpu.make_async_copy(
            moving.at[:, :, pl.ds(128 * c, 128)], pad.at[c, own_y, own_z], load_sem.at[c]
        )
        for c in range(CHUNKS)
    ]
    load_fixed = [
        pltpu.make_async_copy(
            fixed.at[:, :, pl.ds(128 * c, 128)], fx.at[c], load_sem.at[CHUNKS + c]
        )
        for c in range(CHUNKS)
    ]
    place = {"k": k, "q": q, "r": r, "s": s, "rs": 4 * r + s}
    load_table = {}
    for i, (name, which) in enumerate(TABLES.items()):
        source = stored[i] if which is None else stored[i].at[place[which]]
        load_table[name] = pltpu.make_async_copy(source, t[name], table_sem.at[i])
    for copy in load_moving:
        copy.start()
    all_here = greet(k, s)
    for copy in (*load_fixed, *load_table.values()):
        copy.start()

    def table(name):
        load_table[name].wait()
        return t[name]

    lat_to_next = remote(lf_up, lf_prev, send.at[0], recv.at[0], (nxt, s))
    lat_to_prev = remote(lf_down, lf_next, send.at[1], recv.at[1], (prv, s))
    z_to_next = remote(zhi, z_bef, send.at[2], recv.at[2], (nxt, s))
    z_to_prev = remote(zlo, z_aft, send.at[3], recv.at[3], (prv, s))
    to_bef = remote(moving.at[pl.ds(16, 4)], y_bef, send.at[4], recv.at[4], (k, s + 1))
    to_aft = remote(moving.at[pl.ds(0, 4)], y_aft, send.at[5], recv.at[5], (k, s - 1))
    first, last = pl.ds(0, 2), pl.ds(8, 2)
    corner_up = [
        remote(zhi.at[:, last], corners.at[0], send.at[6], recv.at[6], (nxt, s + 1)),
        remote(zlo.at[:, last], corners.at[1], send.at[7], recv.at[7], (prv, s + 1)),
    ]
    corner_down = [
        remote(zhi.at[:, first], corners.at[2], send.at[8], recv.at[8], (nxt, s - 1)),
        remote(zlo.at[:, first], corners.at[3], send.at[9], recv.at[9], (prv, s - 1)),
    ]
    head, tail = pl.ds(0, 8), pl.ds(16, 8)
    mid_same = [
        remote(pooled_m.at[:, tail], pm_same.at[0], send.at[10], recv.at[10], (nxt, s)),
        remote(pooled_m.at[:, head], pm_same.at[1], send.at[11], recv.at[11], (prv, s)),
    ]
    mid_up = [
        remote(pack_up, pm_bef, send.at[12], recv.at[12], (k, s + 1)),
        remote(pack_up.at[:, tail], pm_halo.at[0, 0], send.at[13], recv.at[13], (nxt, s + 1)),
        remote(pack_up.at[:, head], pm_halo.at[1, 0], send.at[14], recv.at[14], (prv, s + 1)),
    ]
    mid_down = [
        remote(pack_down, pm_aft, send.at[15], recv.at[15], (k, s - 1)),
        remote(pack_down.at[:, tail], pm_halo.at[0, 1], send.at[16], recv.at[16], (nxt, s - 1)),
        remote(pack_down.at[:, head], pm_halo.at[1, 1], send.at[17], recv.at[17], (prv, s - 1)),
    ]

    def start_y_halos(*parts_of_z):
        rows = [pl.ds(16 * part, 16) for part in parts_of_z]

        @pl.when(up)
        def _():
            for z in rows:
                remote(moving.at[pl.ds(16, 4), z], y_bef.at[:, z], send.at[4], recv.at[4], (k, s + 1)).start()

        @pl.when(down)
        def _():
            for z in rows:
                remote(moving.at[pl.ds(0, 4), z], y_aft.at[:, z], send.at[5], recv.at[5], (k, s - 1)).start()

    def start(*copies):
        for copy in copies:
            copy.start()

    def start_if(condition, *copies):
        @pl.when(condition)
        def _():
            start(*copies)

    for c in range(CHUNKS):
        pad[c, :, 0:8, :] = jnp.zeros((28, 8, 128), F32)
        pad[c, :, 88:96, :] = jnp.zeros((28, 8, 128), F32)
    all_here()
    start_y_halos(0, 1)
    for c in range(CHUNKS):
        load_moving[c].wait()

        @pl.loop(0, NY // 2, unroll=5)
        def _(pair):
            for half in range(2):
                rows = slice(4 * half, 4 * half + 4)
                zlo[c, pair, rows, :] = pad[c, 2 * pair + half + 4, 8:12, :]
                zhi[c, pair, rows, :] = pad[c, 2 * pair + half + 4, 84:88, :]

    start(z_to_next)

    px, pz = table("px"), table("pz")

    def pooled():
        high, low = parts(sums[...].reshape(400, NX))
        high, low = parts(dot(high, px[...]) + dot(low, px[...]))
        return ((dot(pz[...], high) + dot(pz[...], low)) * (1.0 / 64.0)).reshape(5, 24, 256)

    for c in range(CHUNKS):
        lanes = slice(128 * c, 128 * c + 128)

        @pl.loop(0, 5, unroll=5)
        def _(group):
            four = [pad[c, 4 * group + 4 + i, 8:88, :] for i in range(4)]
            sums[group, :, lanes] = (four[0] + four[1]) + (four[2] + four[3])

    pooled_m[...] = pooled()

    for c in range(CHUNKS):
        load_fixed[c].wait()
        lanes = slice(128 * c, 128 * c + 128)

        @pl.loop(0, 5, unroll=5)
        def _(group):
            four = [fx[c, 4 * group + i] for i in range(4)]
            sums[group, :, lanes] = (four[0] + four[1]) + (four[2] + four[3])

    pooled_f[...] = pooled()

    halves = []
    for ref in (pooled_m, pooled_f):
        upper, lower = jnp.zeros((24, 256), F32), jnp.zeros((24, 256), F32)
        for i in range(5):
            keep = (i + s < 4).astype(F32)
            upper = upper + ref[i] * keep
            lower = lower + ref[i] * (1.0 - keep)
        halves.append(jnp.concatenate([upper, lower], axis=0))
    high, low = parts(jnp.concatenate(halves, axis=1))
    pcx, pcz = table("pcx")[...], table("pcz")[...]
    both = dot(high, pcx) + dot(low, pcx)
    piece[...] = (dot_exact(pcz, both) * (1.0 / 64.0)).reshape(2, 8, 128)
    around(k, s, piece, pieces, psend, precv, "start")
    pieces[1, s] = piece[...]
    for ref, first_y in ((pack_up, 1), (pack_down, 0)):
        ref[0:4] = pooled_m[first_y : first_y + 4, :, 0:128]
        others = [pooled_m[first_y + i, :, 128:256] for i in range(4)]
        ref[4] = (others[0] + pltpu.roll(others[1], 32, 1)) + (
            pltpu.roll(others[2], 64, 1) + pltpu.roll(others[3], 96, 1)
        )
    start(*mid_same)
    start_if(up, *mid_up)
    start_if(down, *mid_down)
    start_y_halos(2)

    for ref in (lf_own, mt, ct, cv, mm):
        ref[...] = jnp.zeros_like(ref)
    for d in range(3):
        for b in range(5):
            lf_own[d, b, 0:4, 0:33] = lat_fine[d, b]
        for a in range(9):
            for b in range(2):
                row = 32 * d + 16 * b + a
                mt[row : row + 1, 0:33] = lat_mid[d, a, b : b + 1]
        for a in range(3):
            ct[16 * d + a : 16 * d + a + 1, 0:9] = lat_coarse[d, a]
    for d in range(3):
        for b in range(5):
            row = 5 * d + b
            lf_up[row : row + 1, :] = lf_own[d, b, 3:4, :]
            lf_down[2 * row : 2 * row + 2, :] = lf_own[d, b, 0:2, :]
    start(lat_to_next, lat_to_prev)

    def pick_rows(name, ref):
        rows = table(name)[...]
        contract = (((1,), (1,)), ((), ()))
        high, low = parts(ref[...])
        return lax.dot_general(rows, high, contract, preferred_element_type=F32) + lax.dot_general(
            rows, low, contract, preferred_element_type=F32
        )

    rows_m, rows_c = pick_rows("rows_m", mt), pick_rows("rows_c", ct)
    cbt, cspread = table("cbt")[...], table("cspread")[...]
    column = dot3(jnp.concatenate([from_lane(rows_c[0:8], 16 * d) for d in range(3)], axis=0), cbt)
    column = jnp.concatenate([column[8 * d : 8 * d + 8] for d in range(3)], axis=1)
    exponent = dot(cspread, stacked(column, 8))[0:40]
    fractions_c = [fraction(exponent[:, 128 * d : 128 * d + 128]) for d in range(3)]
    cbx, cgather = table("cbx"), table("cgather")

    around(k, s, piece, pieces, psend, precv, "wait_recv")

    lane = lax.broadcasted_iota(jnp.int32, (5, 128), 1)
    for dk in range(3):
        scale = (has_prev, jnp.float32(1.0), has_next)[dk]
        rows = (slice(3, 8), slice(8, 13), slice(13, 18))[dk]
        for c in range(5):
            value = jnp.zeros((8, 128), F32)
            if c < 4:
                value = value + pieces[dk, c, 0]
            if c > 0:
                value = value + pieces[dk, c - 1, 1]
            cv[4 + c, rows, :] = jnp.where(lane < 40, value[0:5], 0.0) * scale
            if dk == 1:
                cf[c] = value
    fixed_c = pltpu.roll(cf[...].reshape(40, 128), 64, 1)

    oz, oy, ox = off_coarse[0, 0, q], off_coarse[1, 0, q], off_coarse[2, 0, q]
    a_z, b_z = [], []
    for e in (0, 1):
        window = cv[pl.ds(4 + oy, 6), pl.ds(8 + oz + e, 8), :].reshape(48, 128)
        here, there = shift_lanes([window], ox)[0], shift_lanes([window], ox + 1)[0]
        a_z.append(here)
        b_z.append(there - here)
    corner = [[a_z[z][8 * y : 8 * y + 40] for y in (0, 1)] for z in (0, 1)]
    step = [[b_z[z][8 * y : 8 * y + 40] for y in (0, 1)] for z in (0, 1)]
    total = jnp.concatenate(weights(fixed_c, corner, step, fractions_c), axis=1)
    total = dot_wide(jnp.concatenate([total, jnp.zeros((8, 384), F32)], axis=0), cbx[...])
    total = jnp.concatenate([total, jnp.zeros((80, 128), F32)], axis=0)
    c_tile[...] = dot_gather(cgather[...], total)[0:8]
    broadcast_start(k, s, c_tile, c_buf, bsem.at[0], bsem.at[1])
    c_buf[k] = c_tile[...]
    start_y_halos(3, 4)
    start(z_to_prev)

    mbt, mspread, mbx, mgather = table("mbt"), table("mspread"), table("mbx"), table("mgather")
    own = [from_lane(rows_m[0:8], 32 * d + 16 * b) for d in range(3) for b in range(2)]
    own = dot3(jnp.concatenate(own, axis=0), mbt[0])
    coarse = dot3(jnp.concatenate([from_lane(rows_c[8:16], 16 * d) for d in range(3)], axis=0), mbt[1])
    column = [
        jnp.concatenate([own[16 * d : 16 * d + 16], coarse[8 * d : 8 * d + 8]], axis=0) for d in range(3)
    ]
    base_m = dot(mspread[...], stacked(jnp.concatenate(column, axis=1), 24))[0:120]
    sum_c = table("sum_c")

    @pl.when(s == 0)
    def _():
        y_bef[...] = jnp.zeros_like(y_bef)
        corners[0:2] = jnp.zeros((2, CHUNKS, 2, 8, 128), F32)
        pm_bef[...] = jnp.zeros_like(pm_bef)
        pm_halo[:, 0] = jnp.zeros((2, 5, 8, 128), F32)

    @pl.when(s == SECS - 1)
    def _():
        y_aft[...] = jnp.zeros_like(y_aft)
        corners[2:4] = jnp.zeros((2, CHUNKS, 2, 8, 128), F32)
        pm_aft[...] = jnp.zeros_like(pm_aft)
        pm_halo[:, 1] = jnp.zeros((2, 5, 8, 128), F32)

    for copy in mid_same:
        copy.wait_recv()

    @pl.when(s > 0)
    def _():
        for copy in mid_up:
            copy.wait_recv()

    @pl.when(s < SECS - 1)
    def _():
        for copy in mid_down:
            copy.wait_recv()

    for c in range(2):
        lanes = slice(128 * c, 128 * c + 128)
        for y in range(5):
            mm[c, 5 + y, 4:8, :] = pm_same[0, y, 0:4, lanes] * has_prev
            mm[c, 5 + y, 8:28, :] = pooled_m[y, 0:20, lanes]
            mm[c, 5 + y, 28:32, :] = pm_same[1, y, 0:4, lanes] * has_next
    few = lax.broadcasted_iota(jnp.int32, (24, 128), 1) < 32
    for e, (whole, first_y) in enumerate(((pm_bef, 1), (pm_aft, 10))):
        for y in range(4):
            for c in range(2):

                def row(ref):
                    value = ref[y] if c == 0 else from_lane(ref[4], 32 * y)
                    return value if c == 0 else jnp.where(few[0 : value.shape[0]], value, 0.0)

                mm[c, first_y + y, 4:8, :] = row(pm_halo.at[0, e])[0:4] * has_prev
                mm[c, first_y + y, 8:28, :] = row(whole)[0:20]
                mm[c, first_y + y, 28:32, :] = row(pm_halo.at[1, e])[0:4] * has_next

    oz, oy, ox = off_mid[0, 0, 0], off_mid[0, 0, 1], off_mid[0, 0, 2]
    a_z, b_z = [], []
    for e in (0, 1):
        window = [mm[c, pl.ds(5 + oy, 6), pl.ds(8 + oz + e, 24), :].reshape(144, 128) for c in range(2)]
        here, there = shift_lanes(window, ox), shift_lanes(window, ox + 1)
        a_z.append(here)
        b_z.append([there[c] - here[c] for c in range(2)])

    def make_window(block, oz, oy, ox, y):
        window = [pad[c, 4 + oy + y, pl.ds(20 * block + 8 + oz, 24), :] for c in range(CHUNKS)]
        here, there = shift_lanes(window, ox), shift_lanes(window, ox + 1)
        for c in range(CHUNKS):
            at[block, c, y, 8:32, :] = here[c]
            by[block, c, y, 8:32, :] = there[c] - here[c]

    def make_windows(blocks, ranges):
        @pl.loop(*blocks)
        def _(block):
            offsets = [off_fine[d, block, s] for d in range(3)]
            for first_y, last_y, unroll in ranges:
                pl.loop(first_y, last_y, unroll=unroll)(functools.partial(make_window, block, *offsets))

    broadcast_wait(c_buf, bsem.at[0], bsem.at[1])
    gradient = dot_exact(sum_c[...], c_buf[...].reshape(256, 128))
    near_c = gradient[16:24]
    gradient = gradient[0:16]
    inverse = lax.rsqrt(jnp.sum(gradient * gradient) * (1.0 / 81.0) + EPSILON)

    near = dot3(jnp.concatenate([from_lane(near_c, 16 * d) for d in range(3)], axis=0), mbt[1])
    near = jnp.concatenate([near[8 * d : 8 * d + 8] for d in range(3)], axis=1)
    near = dot(mspread[...], stacked(jnp.concatenate([jnp.zeros((16, 768), F32), near], axis=0), 24))
    exponent = base_m - (STEP_SIZE * inverse) * near[0:120]
    fixed_m = pooled_f[...].reshape(120, 256)
    found = []
    for c in range(2):
        lanes = slice(128 * c, 128 * c + 128)
        corner = [[a_z[z][c][24 * y : 24 * y + 120] for y in (0, 1)] for z in (0, 1)]
        step = [[b_z[z][c][24 * y : 24 * y + 120] for y in (0, 1)] for z in (0, 1)]
        fractions = [fraction(exponent[:, 256 * d + 128 * c : 256 * d + 128 * c + 128]) for d in range(3)]
        found.append(weights(fixed_m[:, lanes], corner, step, fractions))
    total = jnp.concatenate([found[c][d] for d in range(3) for c in range(2)], axis=1)
    total = dot_wide(jnp.concatenate([total, jnp.zeros((8, 768), F32)], axis=0), mbx[...])
    m_part[...] = dot_gather(mgather[...], total)

    def part_copies(act):
        for i in range(1, SECS):
            other = (s + i) & (SECS - 1)
            slot = other if act == "wait_recv" else s
            getattr(remote(m_part, m_parts.at[slot], tsend.at[other], trecv.at[slot], (k, other)), act)()

    part_copies("start")
    start_if(up, *corner_up)
    start_if(down, *corner_down)
    m_parts[s] = m_part[...]

    gradient = gradient * inverse
    next_c = [
        from_lane(rows_c[8:16], 16 * d) - (STEP_SIZE * inverse) * from_lane(near_c, 16 * d) for d in range(3)
    ]
    for copy in (lat_to_next, lat_to_prev):
        copy.wait_recv()
    for d in range(3):
        for b in range(5):
            lf[d, 8 * b : 8 * b + 1, :] = lf_prev[5 * d + b : 5 * d + b + 1, :] * has_prev
            lf[d, 8 * b + 1 : 8 * b + 5, :] = lf_own[d, b, 0:4, :]
            lf[d, 8 * b + 5 : 8 * b + 7, :] = lf_next[10 * d + 2 * b : 10 * d + 2 * b + 2, :] * has_next
            lf[d, 8 * b + 7 : 8 * b + 8, :] = jnp.zeros((1, 128), F32)
    bt = table("bt")
    own = dot3(lf[...].reshape(120, 128), bt[0])
    mid = [from_lane(rows_m[8:16], 32 * d + 16 * b) for d in range(3) for b in range(2)]
    mid = dot3(jnp.concatenate(mid, axis=0), bt[1])
    coarse = dot3(jnp.concatenate(next_c, axis=0), bt[2])
    base_f = [
        jnp.concatenate(
            [own[40 * d : 40 * d + 40], mid[16 * d : 16 * d + 16], coarse[8 * d : 8 * d + 8]], axis=0
        )
        for d in range(3)
    ]
    base_f = jnp.concatenate(base_f, axis=1)

    make_windows((1, 3), ((4, 16, 3),))
    part_copies("wait_recv")
    m_tile[...] = (m_parts[0] + m_parts[1]) + (m_parts[2] + m_parts[3])
    broadcast_start(k, s, m_tile, m_buf, bsem.at[2], bsem.at[3])
    m_buf[k] = m_tile[...]

    turn_r = lax.broadcasted_iota(jnp.int32, (48, 128), 0)
    turn = jnp.where(turn_r == lax.broadcasted_iota(jnp.int32, (48, 128), 1) + 2, 1.0, 0.0)
    result[216:264, :] = dot_rows(gradient, turn[0:16])[0:48]

    for copy in (z_to_next, z_to_prev):
        copy.wait_recv()

    @pl.loop(0, NY // 2, unroll=2)
    def _(pair):
        for half in range(2):
            rows = slice(4 * half, 4 * half + 4)
            for c in range(CHUNKS):
                pad[c, 2 * pair + half + 4, 4:8, :] = z_bef[c, pair, rows, :] * has_prev
                pad[c, 2 * pair + half + 4, 88:92, :] = z_aft[c, pair, rows, :] * has_next

    make_windows((0, 1), ((4, 16, 3),))
    make_windows((3, 4), ((4, 16, 3),))

    @pl.when(s > 0)
    def _():
        for copy in (to_bef, *corner_up):
            copy.wait_recv()

    @pl.when(s < SECS - 1)
    def _():
        for copy in (to_aft, *corner_down):
            copy.wait_recv()

    for c in range(CHUNKS):
        lanes = slice(128 * c, 128 * c + 128)
        pad[c, 0:4, 8:88, :] = y_bef[:, :, lanes]
        pad[c, 24:28, 8:88, :] = y_aft[:, :, lanes]
    for y in range(4):
        rows = slice(4 * (y % 2), 4 * (y % 2) + 4)
        for c in range(CHUNKS):
            for n in range(2):
                where = slice(4, 8) if n == 0 else slice(88, 92)
                keep = has_prev if n == 0 else has_next
                pad[c, y, where, :] = corners[n, c, y // 2, rows, :] * keep
                pad[c, 24 + y, where, :] = corners[2 + n, c, y // 2, rows, :] * keep

    make_windows((0, 4), ((0, 4, 2), (16, 21, 5)))

    spread, gather, bx, sum_m = table("spread"), table("gather"), table("bx"), table("sum_m")

    broadcast_wait(m_buf, bsem.at[2], bsem.at[3])
    gradient = dot_exact(sum_m[...], m_buf[...].reshape(512, 128))
    near = gradient[96:112]
    gradient = gradient[0:96]
    inverse = lax.rsqrt(jnp.sum(gradient * gradient) * (1.0 / 1782.0) + EPSILON)

    near = dot3(jnp.concatenate([from_lane(near, 16 * d) for d in range(3)], axis=0), bt[1])
    near = jnp.concatenate([near[16 * d : 16 * d + 16] for d in range(3)], axis=1)
    near = jnp.concatenate([jnp.zeros((40, 3 * NX), F32), near, jnp.zeros((8, 3 * NX), F32)], axis=0)
    upper, lower = parts(base_f - (STEP_SIZE * inverse) * near)
    columns[0:64, :] = upper
    columns[64:128, :] = upper
    columns[128:192, :] = lower
    columns[192:256, :] = lower
    field_a[...] = dot(spread[0:400, :], columns[...])

    first_rows = lax.broadcasted_iota(jnp.int32, (8, 128), 0) < 4
    steps_z = (jnp.minimum(k, 0), jnp.minimum(k + 1, 1))

    def planes(ref, pair, c, y, z):
        a, b = 2 * pair, 2 * pair + 1
        middle = jnp.where(
            first_rows, ref[a, c, y, pl.ds(24 + z, 8), :], ref[b, c, y, pl.ds(4 + z, 8), :]
        )
        return jnp.concatenate(
            [ref[a, c, y, pl.ds(8 + z, 16), :], middle, ref[b, c, y, pl.ds(12 + z, 16), :]], axis=0
        )

    def fine_stage(stage, split, split_before, field, field_after):
        adjoint[...] = jnp.zeros_like(adjoint)
        pair, y_first = stage >> 1, 10 * (stage & 1)
        after = pl.ds(pl.multiple_of(400 * jnp.minimum(stage + 1, 3), 400), 400)

        @pl.loop(0, 5)
        def _(i):
            lanes = pl.ds(pl.multiple_of(384 * i, 384), 384)
            field_after[:, lanes] = dot(spread[after, :], columns[:, lanes])
            lanes = pl.ds(pl.multiple_of(768 * i, 768), 768)
            adjoint[...] += dot(split_before[:, lanes], bx[lanes, :])
            for c in range(CHUNKS):
                found = []
                for h in range(2):
                    y = y_first + 2 * i + h
                    corner = [[planes(at, pair, c, y + e, z) for e in (0, 1)] for z in steps_z]
                    step = [[planes(by, pair, c, y + e, z) for e in (0, 1)] for z in steps_z]
                    rows = pl.ds(pl.multiple_of(80 * i + 40 * h, 8), 40)
                    fractions = [
                        fraction(field[rows, NX * d + 128 * c : NX * d + 128 * c + 128]) for d in range(3)
                    ]
                    atlas = fx[c, y, pl.ds(pl.multiple_of(40 * pair, 8), 40), :]
                    found.append(weights(atlas, corner, step, fractions))
                rows = pl.ds(pl.multiple_of(80 * i, 80), 80)
                for d in range(3):
                    upper, lower = parts(jnp.concatenate([found[0][d], found[1][d]], axis=0))
                    lane = 2 * NX * d + 128 * c
                    split[rows, lane : lane + 128] = upper
                    split[rows, lane + NX : lane + NX + 128] = lower

        before = pl.ds(pl.multiple_of(400 * jnp.maximum(stage - 1, 0), 400), 400)
        mixed[before, :] = adjoint[:, 0:128] + adjoint[:, 128:256]

    @pl.loop(0, 2)
    def _(two):
        fine_stage(2 * two, split_a, split_b, field_a, field_b)
        fine_stage(2 * two + 1, split_b, split_a, field_b, field_a)

    wide = dot(split_b[...], bx[...])
    mixed[1200:1600, :] = wide[:, 0:128] + wide[:, 128:256]
    f_part[...] = dot_gather(gather[...], mixed[...])
    around(k, s, f_part, f_parts, fsend, frecv, "start")
    f_parts[1, s] = f_part[...]

    for b in range(2):
        turned = dot_rows(gradient[48 * b : 48 * b + 48] * inverse, turn)
        result[120 + 48 * b : 168 + 48 * b, :] = turned[0:48]
    row = lax.broadcasted_iota(jnp.int32, (40, 128), 0) & 7

    around(k, s, f_part, f_parts, fsend, frecv, "wait_recv")
    before, middle, after = ((f_parts[i, 0] + f_parts[i, 1]) + (f_parts[i, 2] + f_parts[i, 3]) for i in range(3))
    middle = middle + jnp.where((row == 1) | (row == 2), pltpu.roll(before * has_prev, 36, 0), 0.0)
    middle = middle + jnp.where(row == 4, pltpu.roll(after * has_next, 4, 0), 0.0)
    middle = jnp.where((row >= 1) & (row <= 4), middle, 0.0)
    f_tile[...] = jnp.full((8, 128), jnp.sum(middle * middle))
    broadcast_start(k, s, f_tile, f_buf, bsem.at[4], bsem.at[5])
    f_buf[k] = f_tile[...]

    for copy in (lat_to_next, lat_to_prev, z_to_next, z_to_prev, *mid_same):
        copy.wait_send()

    @pl.when(up)
    def _():
        for copy in (to_bef, *corner_up, *mid_up):
            copy.wait_send()

    @pl.when(down)
    def _():
        for copy in (to_aft, *corner_down, *mid_down):
            copy.wait_send()

    around(k, s, piece, pieces, psend, precv, "wait_send")
    around(k, s, f_part, f_parts, fsend, frecv, "wait_send")
    part_copies("wait_send")
    middle = pltpu.roll(middle, 39, 0)
    thirds = [from_lane(middle, 40 * d) for d in range(3)]

    broadcast_wait(f_buf, bsem.at[4], bsem.at[5])
    squares = jnp.sum(f_buf[...], axis=0)[0:1, :]
    inverse = lax.rsqrt(squares * (1.0 / 63360.0) + EPSILON)
    for d in range(3):
        result[40 * d : 40 * d + 40, :] = thirds[d] * inverse


def body(
    fixed_image,
    moving_image,
    lattice_fine,
    lattice_mid,
    lattice_coarse,
    offset_fine,
    offset_mid,
    offset_coarse,
):
    t = tables()
    vmem, smem, hbm = (pl.BlockSpec(memory_space=m) for m in (pltpu.VMEM, pltpu.SMEM, pl.ANY))
    shape = lambda *dims: jax.ShapeDtypeStruct(dims, F32)
    buf = lambda *dims: pltpu.VMEM(dims, F32)
    half = lambda *dims: pltpu.VMEM(dims, BF16)
    dma = lambda *dims: pltpu.SemaphoreType.DMA(dims)
    result = pl.pallas_call(
        kernel,
        out_shape=shape(264, 128),
        in_specs=[hbm, hbm, vmem, vmem, vmem, smem, smem, smem] + [hbm] * len(TABLES),
        out_specs=vmem,
        scratch_shapes=[
            *[pltpu.VMEM(t[n].shape[which is not None :], t[n].dtype) for n, which in TABLES.items()],
            buf(CHUNKS, 28, 96, 128), buf(CHUNKS, NY, NZ, 128), buf(5, NZ, NX),
            *[buf(CHUNKS, 10, 8, 128)] * 4, *[buf(4, NZ, NX)] * 2, buf(4, CHUNKS, 2, 8, 128),
            buf(3, 5, 8, 128), *[buf(16, 128), buf(32, 128)] * 2, buf(3, 40, 128), buf(128, 128), buf(128, 128),
            *[buf(5, 24, 256)] * 2, *[buf(5, 24, 128)] * 4, buf(2, 2, 5, 8, 128), buf(2, 5, 8, 256),
            buf(2, 8, 128), buf(3, SECS, 2, 8, 128), buf(14, 32, 128), buf(5, 8, 128), buf(2, 15, 40, 128),
            buf(8, 128), buf(SLABS, 8, 128), buf(16, 128), buf(SECS, 16, 128), buf(16, 128), buf(SLABS, 16, 128),
            *[buf(4, CHUNKS, 21, 40, 128)] * 2, half(256, 3 * NX),
            *[buf(400, 3 * NX)] * 2, *[half(400, 6 * NX)] * 2, buf(400, 256), buf(1600, 128),
            buf(40, 128), buf(3, SECS, 40, 128), buf(8, 128), buf(SLABS, 8, 128),
            dma(10), dma(len(TABLES)), dma(18), dma(18), *[dma(3, SECS)] * 4, dma(SECS), dma(SECS), dma(6),
        ],
        compiler_params=pltpu.CompilerParams(
            collective_id=0, has_side_effects=True, vmem_limit_bytes=VMEM_LIMIT
        ),
        name="mega",
    )(
        jnp.transpose(moving_image, (1, 0, 2)),
        jnp.transpose(fixed_image, (1, 0, 2)),
        jnp.transpose(lattice_fine, (0, 2, 1, 3)),
        jnp.transpose(lattice_mid, (0, 3, 2, 1)),
        jnp.transpose(lattice_coarse, (0, 3, 2, 1)),
        offset_fine,
        jnp.transpose(offset_mid, (1, 2, 0)),
        jnp.transpose(offset_coarse, (0, 2, 1)),
        *(t[n] for n in TABLES),
    )
    fine, mid, coarse = pl.pallas_call(
        finish,
        out_shape=[shape(3, 5, 4, 33), shape(3, 9, 2, 33), shape(3, 3, 1, 9)],
        in_specs=[vmem],
        out_specs=[vmem] * 3,
        name="finish",
    )(result)
    return (
        jnp.transpose(fine, (0, 2, 1, 3)),
        jnp.transpose(mid, (0, 3, 2, 1)),
        jnp.transpose(coarse, (0, 3, 2, 1)),
    )


def solution(mesh):
    placed = (
        P("slab", "sec", None),
        P("slab", "sec", None),
        P(None, "slab", None, None),
        P(),
        P(),
        P(None, "slab", None),
        P(None, "slab", None),
        P(),
    )
    return jax.shard_map(
        body,
        mesh=mesh,
        in_specs=placed,
        out_specs=(P(None, "slab", None, None), P(), P()),
        check_vma=False,
    )
```

```python
import functools

import jax
import jax.numpy as jnp
import ml_dtypes
import numpy as np
from jax import lax
from jax.experimental import pallas as pl
from jax.experimental.pallas import tpu as pltpu
from jax.sharding import PartitionSpec as P

SP = 20
EPSILON = 1e-06
STEP_SIZE = 0.5
HIGHEST = lax.Precision.HIGHEST
F32 = jnp.float32
BF16 = jnp.bfloat16
MESH = pl.DeviceIdType.MESH
SLABS = 32
SECS = 4
NZ, NY, NX = 80, 20, 640
CHUNKS = NX // 128
LOG2E = 1.4426950408889634
VMEM_LIMIT = 58 * 1024 * 1024


def basis(rows, knots, factor, coarse):
    rows, knots = np.asarray(rows, np.float64), np.asarray(knots, np.float64)
    position = factor * rows + 0.5 * (factor - 1)
    centre = SP * coarse * knots + 0.5 * (coarse - 1)
    distance = np.abs((position[:, None] - centre[None, :]) / (SP * coarse))
    near = 2.0 / 3.0 - distance**2 + 0.5 * distance**3
    far = np.maximum(2.0 - distance, 0.0) ** 3 / 6.0
    return np.where(distance < 1.0, near, far)


def two_parts(values):
    high = values.astype(ml_dtypes.bfloat16)
    low = (values - high.astype(np.float64)).astype(ml_dtypes.bfloat16)
    return high, low


def right_parts(values):
    high, low = two_parts(values)
    return np.concatenate([high, low, high], axis=-2)


def wide_parts(values):
    high, low = two_parts(values)
    zero = np.zeros_like(high)
    return np.concatenate([np.concatenate([high, low], 1), np.concatenate([high, zero], 1)], 0)


def one_hot(condition):
    return condition.astype(ml_dtypes.bfloat16)


@functools.cache
def tables():
    t = {}
    rz, ry = np.zeros((4, 4, 20, 64)), np.zeros((4, NY, 64))
    z, y, x = np.arange(NZ), np.arange(NY), np.arange(NX)
    for r in range(4):
        for block in range(4):
            rows = z[20 * block : 20 * block + 20]
            for a in range(7):
                rz[r, block, :, a:40:8] = basis(rows, [a - 1], 1, 1)
            for a in range(5):
                rz[r, block, :, 40 + a : 56 : 8] = basis(rows, [a - 2], 1, 4)
                rz[r, block, :, 56 + a : 57 + a] = basis(rows + 80 * r, [a - 2], 1, 16)
    for s in range(4):
        for a in range(7):
            ry[s, :, a:40:8] = basis(y + 20 * s, range(5), 1, 1)
        for a in range(5):
            ry[s, :, 40 + a : 56 : 8] = basis(y + 20 * s, range(2), 1, 4)
            ry[s, :, 56 + a : 57 + a] = basis(y + 20 * s, [0], 1, 16)
    rz = rz.reshape(4, 2, 40, 64)
    whole = rz[:, None, :, None] * ry[None, :, None, :, None, :]
    high, low = two_parts(whole.reshape(16, 1600, 64))
    t["spread"] = np.concatenate([high, low, high, low], axis=2)
    t["gather"] = np.concatenate([high[:4, :, :40], low[:4, :, :40]], axis=2).transpose(0, 2, 1)
    across = np.zeros((3, 128, NX))
    across[0, :33] = basis(x, range(33), 1, 1).T
    across[1, :9] = basis(x, range(9), 1, 4).T
    across[2, :3] = basis(x, range(3), 1, 16).T
    t["bt"] = right_parts(-LOG2E * across)
    along = np.zeros((3, NX, 128))
    for d in range(3):
        along[d, :, 40 * d : 40 * d + 33] = basis(x, range(33), 1, 1)
    t["bx"] = np.concatenate([wide_parts(along[d]) for d in range(3)], axis=0)
    rz, ry = np.zeros((4, 24, 32)), np.zeros((4, 5, 32))
    z, y, x = np.arange(20), np.arange(5), np.arange(160)
    for r in range(4):
        for a in range(4):
            rz[r, :20, a:16:8] = basis(z, [a - 1], 4, 4)
        for a in range(5):
            rz[r, :20, 16 + a : 17 + a] = basis(z + 20 * r, [a - 2], 4, 16)
    for s in range(4):
        for a in range(4):
            ry[s, :, a:16:8] = basis(y + 5 * s, range(2), 4, 4)
        for a in range(5):
            ry[s, :, 16 + a : 17 + a] = basis(y + 5 * s, [0], 4, 16)
    whole = np.zeros((16, 128, 32))
    whole[:, :120] = (rz[:, None, None] * ry[None, :, :, None]).reshape(16, 120, 32)
    high, low = two_parts(whole)
    t["mspread"] = np.concatenate([high, high, low, np.zeros_like(low)], axis=2)
    t["mgather"] = np.concatenate([high[:, :, :16], low[:, :, :16]], axis=2).transpose(0, 2, 1)
    across = np.zeros((2, 128, 256))
    across[0, :9, :160] = basis(x, range(9), 4, 4).T
    across[1, :3, :160] = basis(x, range(3), 4, 16).T
    t["mbt"] = right_parts(-LOG2E * across)
    along = np.zeros((3, 256, 128))
    for d in range(3):
        along[d, :160, 16 * d : 16 * d + 9] = basis(x, range(9), 4, 4)
    t["mbx"] = wide_parts(along.reshape(768, 128))
    rz = np.zeros((4, 8, 32))
    z, y, x = np.arange(5), np.arange(5), np.arange(40)
    for r in range(4):
        for a in range(4):
            rz[r, :5, a : a + 1] = basis(z + 5 * r, [a - 1], 16, 16)
    whole = np.zeros((4, 128, 32))
    whole[:, :40] = (rz[:, None] * basis(y, [0], 16, 16)[None, :, None]).reshape(4, 40, 32)
    high, low = two_parts(whole)
    t["cspread"] = np.concatenate([high, high, low, np.zeros_like(low)], axis=2)
    t["cgather"] = np.concatenate([high[:, :, :16], low[:, :, :16]], axis=2).transpose(0, 2, 1)
    across = np.zeros((128, 128))
    across[:3, :40] = basis(x, range(3), 16, 16).T
    t["cbt"] = right_parts(-LOG2E * across)
    along = np.zeros((3, 128, 128))
    for d in range(3):
        along[d, :40, 16 * d : 16 * d + 3] = basis(x, range(3), 16, 16)
    t["cbx"] = wide_parts(along.reshape(384, 128))
    row, column = np.arange(NX)[:, None], np.arange(256)[None, :]
    t["px"] = one_hot(row // 4 == column)
    row, column = np.arange(120)[:, None], np.arange(400)[None, :]
    t["pz"] = one_hot((row // 24 == column // 80) & (row % 24 == column % 80 // 4))
    row, column = np.arange(512)[:, None], np.arange(128)[None, :]
    t["pcx"] = one_hot((row % 256 < 160) & (row // 256 * 64 + row % 256 // 4 == column))
    row, column = np.arange(16)[:, None], np.arange(48)[None, :]
    t["pcz"] = one_hot((row // 8 == column // 24) & (column % 24 < 20) & (row % 8 == column % 24 // 4))
    row, column, place = np.arange(16)[:, None], np.arange(128)[None, :], np.arange(32)[:, None, None]
    knot = place - 1 - row // 8 + row % 8
    t["rows_m"] = one_hot((knot == column) & (column < 33))
    t["rows_c"] = one_hot((knot == column) & (column < 9))[:8]
    row, column, place = np.arange(24)[:, None], np.arange(256)[None, :], np.arange(8)[:, None, None]
    knot = np.where(row < 16, row - 2, row - 16 + place - 2)
    found = (knot == column // 32 - 1 + column % 8) & (column % 8 < 4) & (knot >= 0) & (knot < 9)
    t["sum_c"] = one_hot(found)
    row, column, place = np.arange(112)[:, None], np.arange(512)[None, :], np.arange(32)[:, None, None]
    knot = np.where(row < 96, row % 48 - 2, row % 8 + place - 2)
    b = np.where(row < 96, row // 48, (row - 96) // 8)
    found = (knot == column // 16 - 1 + column % 8) & (column % 8 < 4) & (column // 8 % 2 == b)
    t["sum_m"] = one_hot(found & (knot >= 0) & (knot < 33))
    return t


def dot(a, b):
    return jnp.dot(a, b, preferred_element_type=F32)


def dot_rows(a, b):
    return lax.dot_general(
        a, b, (((0,), (0,)), ((), ())), precision=HIGHEST, preferred_element_type=F32
    )


def parts(values):
    high = values.astype(BF16)
    return high, (values - high.astype(F32)).astype(BF16)


def dot3(a, right):
    high, low = parts(a)
    return dot(jnp.concatenate([high, high, low], axis=1), right)


def dot_wide(a, table):
    wide = dot(jnp.concatenate(parts(a), axis=1), table)
    return wide[:, 0:128] + wide[:, 128:256]


def dot_exact(table, b):
    wide = dot(table, jnp.concatenate(parts(b), axis=1))
    return wide[:, 0:128] + wide[:, 128:256]


def dot_gather(table, b):
    n = table.shape[0] // 2
    wide = dot(table, jnp.concatenate(parts(b), axis=1))
    return (wide[0:n, 0:128] + wide[0:n, 128:256]) + wide[n:, 0:128]


def stacked(column, n):
    high, low = parts(jnp.concatenate([column, jnp.zeros((32 - n, column.shape[1]), F32)], axis=0))
    return jnp.concatenate([high, low, high, jnp.zeros_like(low)], axis=0)


def from_lane(values, lane):
    return values if lane == 0 else pltpu.roll(values, 128 - lane, 1)


def shift_lanes(chunks, shift):
    amount = (128 - shift) & 127
    rolled = [pltpu.roll(chunk, amount, 1) for chunk in chunks]
    lane = lax.broadcasted_iota(jnp.int32, chunks[0].shape, 1)
    first = lane < jnp.maximum(-shift, 0)
    last = lane >= 128 - jnp.maximum(shift, 0)
    zero = jnp.zeros_like(chunks[0])
    padded = [zero, *rolled, zero]
    return [
        jnp.where(first, padded[j], jnp.where(last, padded[j + 2], padded[j + 1]))
        for j in range(len(chunks))
    ]


def fraction(exponent):
    grown = jnp.exp2(exponent)
    frac = pl.reciprocal(1.0 + grown, approx=True)
    return frac, frac * (grown * frac)


def weights(fixed, corner, step, fractions):
    (fz, gz), (fy, gy), (fx, gx) = fractions
    line = [[corner[z][y] + fx * step[z][y] for y in (0, 1)] for z in (0, 1)]
    rise = [line[z][1] - line[z][0] for z in (0, 1)]
    plane = [line[z][0] + fy * rise[z] for z in (0, 1)]
    slope_z = plane[1] - plane[0]
    residual = (plane[0] + fz * slope_z) - fixed
    slope_y = rise[0] + fz * (rise[1] - rise[0])
    along = [step[z][0] + fy * (step[z][1] - step[z][0]) for z in (0, 1)]
    slope_x = along[0] + fz * (along[1] - along[0])
    return [
        (residual * slope_z) * gz,
        (residual * slope_y) * gy,
        (residual * slope_x) * gx,
    ]


def greet(k, s):
    barrier = pltpu.get_barrier_semaphore()

    def signal(slab, sec):
        pl.semaphore_signal(barrier, inc=1, device_id=(slab, sec), device_id_type=MESH)

    @pl.loop(1, SLABS)
    def _(i):
        signal((k + i) & (SLABS - 1), s)

    for i in range(1, SECS):
        other = (s + i) & (SECS - 1)
        signal(k, other)
        signal((k + 1) & (SLABS - 1), other)
        signal((k + SLABS - 1) & (SLABS - 1), other)
    return lambda: pl.semaphore_wait(barrier, SLABS - 1 + 3 * (SECS - 1))


def broadcast_start(k, s, tile, buffer, send_sem, recv_sem):
    @pl.loop(0, SLABS - 1)
    def _(i):
        pltpu.make_async_remote_copy(
            src_ref=tile,
            dst_ref=buffer.at[k],
            send_sem=send_sem,
            recv_sem=recv_sem,
            device_id=((k + 16 + i + (i > 15).astype(jnp.int32)) & (SLABS - 1), s),
            device_id_type=MESH,
        ).start()


def broadcast_wait(buffer, send_sem, recv_sem):
    part = buffer.at[pl.ds(0, SLABS - 1)]
    pltpu.make_async_copy(part, part, recv_sem).wait()
    pltpu.make_async_copy(part, part, send_sem).wait()


def remote(src, dst, send_sem, recv_sem, device):
    return pltpu.make_async_remote_copy(
        src_ref=src,
        dst_ref=dst,
        send_sem=send_sem,
        recv_sem=recv_sem,
        device_id=device,
        device_id_type=MESH,
    )


def around(k, s, source, buffer, send, recv, act):
    slabs = ((k + SLABS - 1) & (SLABS - 1), k, (k + 1) & (SLABS - 1))

    def one(dk, other):
        if act == "wait_recv":
            copy = remote(source, buffer.at[dk, other], send.at[dk, other], recv.at[dk, other], (k, other))
        else:
            copy = remote(
                source, buffer.at[2 - dk, s], send.at[dk, other], recv.at[2 - dk, s], (slabs[dk], other)
            )
        getattr(copy, act)()

    for dk in (0, 2):
        for other in range(SECS):
            one(dk, other)
    for i in range(1, SECS):
        one(1, (s + i) & (SECS - 1))


TABLES = {
    "px": None, "pz": None, "pcx": None, "pcz": None,
    "rows_m": "k", "rows_c": "q", "cspread": "r", "cgather": "r", "cbt": None, "cbx": None,
    "sum_c": "q", "mspread": "rs", "mgather": "rs", "mbt": None, "mbx": None,
    "spread": "rs", "gather": "s", "bt": None, "bx": None, "sum_m": "k",
}


def finish(result, fine_out, mid_out, coarse_out):
    for d in range(3):
        for b in range(5):
            row = 40 * d + 8 * b
            fine_out[d, b] = result[row : row + 4, 0:33]
        for a in range(9):
            for b in range(2):
                row = 120 + 48 * b + 16 * d + a
                mid_out[d, a, b : b + 1, :] = result[row : row + 1, 0:33]
        for a in range(3):
            row = 216 + 16 * d + a
            coarse_out[d, a] = result[row : row + 1, 0:9]


def kernel(
    moving, fixed, lat_fine, lat_mid, lat_coarse, off_fine, off_mid, off_coarse, *refs
):
    n = len(TABLES)
    stored, refs = refs[:n], refs[n:]
    result, *refs = refs
    t = dict(zip(TABLES, refs[:n]))
    (
        pad, fx, sums, zlo, zhi, z_bef, z_aft, y_bef, y_aft, corners,
        lf_own, lf_up, lf_down, lf_prev, lf_next, lf, mt, ct,
        pooled_m, pooled_f, pack_up, pack_down, pm_bef, pm_aft, pm_halo, pm_same,
        piece, pieces, cv, cf, mm,
        c_tile, c_buf, m_part, m_parts, m_tile, m_buf,
        at, by, columns, field_a, field_b, split_a, split_b, adjoint, mixed,
        f_part, f_parts, f_tile, f_buf,
        load_sem, table_sem, send, recv, psend, precv, fsend, frecv, tsend, trecv, bsem,
    ) = refs[n:]
    k, s = lax.axis_index("slab"), lax.axis_index("sec")
    nxt, prv = (k + 1) & (SLABS - 1), (k + SLABS - 1) & (SLABS - 1)
    q, r = k >> 2, k & 3
    has_prev, has_next = (k > 0).astype(F32), (k < SLABS - 1).astype(F32)
    up, down = s < SECS - 1, s > 0
    own_y, own_z = pl.ds(4, NY), pl.ds(8, NZ)

    load_moving = [
        pltpu.make_async_copy(
            moving.at[:, :, pl.ds(128 * c, 128)], pad.at[c, own_y, own_z], load_sem.at[c]
        )
        for c in range(CHUNKS)
    ]
    load_fixed = [
        pltpu.make_async_copy(
            fixed.at[:, :, pl.ds(128 * c, 128)], fx.at[c], load_sem.at[CHUNKS + c]
        )
        for c in range(CHUNKS)
    ]
    place = {"k": k, "q": q, "r": r, "s": s, "rs": 4 * r + s}
    load_table = {}
    for i, (name, which) in enumerate(TABLES.items()):
        source = stored[i] if which is None else stored[i].at[place[which]]
        load_table[name] = pltpu.make_async_copy(source, t[name], table_sem.at[i])
    for copy in load_moving:
        copy.start()
    all_here = greet(k, s)
    for copy in (*load_fixed, *load_table.values()):
        copy.start()

    def table(name):
        load_table[name].wait()
        return t[name]

    lat_to_next = remote(lf_up, lf_prev, send.at[0], recv.at[0], (nxt, s))
    lat_to_prev = remote(lf_down, lf_next, send.at[1], recv.at[1], (prv, s))
    z_to_next = remote(zhi, z_bef, send.at[2], recv.at[2], (nxt, s))
    z_to_prev = remote(zlo, z_aft, send.at[3], recv.at[3], (prv, s))
    to_bef = remote(moving.at[pl.ds(16, 4)], y_bef, send.at[4], recv.at[4], (k, s + 1))
    to_aft = remote(moving.at[pl.ds(0, 4)], y_aft, send.at[5], recv.at[5], (k, s - 1))
    first, last = pl.ds(0, 2), pl.ds(8, 2)
    corner_up = [
        remote(zhi.at[:, last], corners.at[0], send.at[6], recv.at[6], (nxt, s + 1)),
        remote(zlo.at[:, last], corners.at[1], send.at[7], recv.at[7], (prv, s + 1)),
    ]
    corner_down = [
        remote(zhi.at[:, first], corners.at[2], send.at[8], recv.at[8], (nxt, s - 1)),
        remote(zlo.at[:, first], corners.at[3], send.at[9], recv.at[9], (prv, s - 1)),
    ]
    head, tail = pl.ds(0, 8), pl.ds(16, 8)
    mid_same = [
        remote(pooled_m.at[:, tail], pm_same.at[0], send.at[10], recv.at[10], (nxt, s)),
        remote(pooled_m.at[:, head], pm_same.at[1], send.at[11], recv.at[11], (prv, s)),
    ]
    mid_up = [
        remote(pack_up, pm_bef, send.at[12], recv.at[12], (k, s + 1)),
        remote(pack_up.at[:, tail], pm_halo.at[0, 0], send.at[13], recv.at[13], (nxt, s + 1)),
        remote(pack_up.at[:, head], pm_halo.at[1, 0], send.at[14], recv.at[14], (prv, s + 1)),
    ]
    mid_down = [
        remote(pack_down, pm_aft, send.at[15], recv.at[15], (k, s - 1)),
        remote(pack_down.at[:, tail], pm_halo.at[0, 1], send.at[16], recv.at[16], (nxt, s - 1)),
        remote(pack_down.at[:, head], pm_halo.at[1, 1], send.at[17], recv.at[17], (prv, s - 1)),
    ]

    def start_y_halos(*parts_of_z):
        rows = [pl.ds(16 * part, 16) for part in parts_of_z]

        @pl.when(up)
        def _():
            for z in rows:
                remote(moving.at[pl.ds(16, 4), z], y_bef.at[:, z], send.at[4], recv.at[4], (k, s + 1)).start()

        @pl.when(down)
        def _():
            for z in rows:
                remote(moving.at[pl.ds(0, 4), z], y_aft.at[:, z], send.at[5], recv.at[5], (k, s - 1)).start()

    def start(*copies):
        for copy in copies:
            copy.start()

    def start_if(condition, *copies):
        @pl.when(condition)
        def _():
            start(*copies)

    for c in range(CHUNKS):
        pad[c, :, 0:8, :] = jnp.zeros((28, 8, 128), F32)
        pad[c, :, 88:96, :] = jnp.zeros((28, 8, 128), F32)
    all_here()
    start_y_halos(0, 1, 2)
    for c in range(CHUNKS):
        load_moving[c].wait()

    px, pz = table("px"), table("pz")

    def pooled():
        high, low = parts(sums[...].reshape(400, NX))
        high, low = parts(dot(high, px[...]) + dot(low, px[...]))
        return ((dot(pz[...], high) + dot(pz[...], low)) * (1.0 / 64.0)).reshape(5, 24, 256)

    for c in range(CHUNKS):
        lanes = slice(128 * c, 128 * c + 128)

        @pl.loop(0, 5, unroll=5)
        def _(group):
            four = [pad[c, 4 * group + 4 + i, 8:88, :] for i in range(4)]
            sums[group, :, lanes] = (four[0] + four[1]) + (four[2] + four[3])

    pooled_m[...] = pooled()

    for c in range(CHUNKS):
        load_fixed[c].wait()
        lanes = slice(128 * c, 128 * c + 128)

        @pl.loop(0, 5, unroll=5)
        def _(group):
            four = [fx[c, 4 * group + i] for i in range(4)]
            sums[group, :, lanes] = (four[0] + four[1]) + (four[2] + four[3])

    pooled_f[...] = pooled()

    halves = []
    for ref in (pooled_m, pooled_f):
        upper, lower = jnp.zeros((24, 256), F32), jnp.zeros((24, 256), F32)
        for i in range(5):
            keep = (i + s < 4).astype(F32)
            upper = upper + ref[i] * keep
            lower = lower + ref[i] * (1.0 - keep)
        halves.append(jnp.concatenate([upper, lower], axis=0))
    high, low = parts(jnp.concatenate(halves, axis=1))
    pcx, pcz = table("pcx")[...], table("pcz")[...]
    both = dot(high, pcx) + dot(low, pcx)
    piece[...] = (dot_exact(pcz, both) * (1.0 / 64.0)).reshape(2, 8, 128)
    around(k, s, piece, pieces, psend, precv, "start")
    pieces[1, s] = piece[...]
    for ref, first_y in ((pack_up, 1), (pack_down, 0)):
        ref[0:4] = pooled_m[first_y : first_y + 4, :, 0:128]
        others = [pooled_m[first_y + i, :, 128:256] for i in range(4)]
        ref[4] = (others[0] + pltpu.roll(others[1], 32, 1)) + (
            pltpu.roll(others[2], 64, 1) + pltpu.roll(others[3], 96, 1)
        )
    start(*mid_same)
    start_if(up, *mid_up)
    start_if(down, *mid_down)
    for c in range(CHUNKS):

        @pl.loop(0, NY // 2, unroll=5)
        def _(pair):
            for half in range(2):
                rows = slice(4 * half, 4 * half + 4)
                zlo[c, pair, rows, :] = pad[c, 2 * pair + half + 4, 8:12, :]
                zhi[c, pair, rows, :] = pad[c, 2 * pair + half + 4, 84:88, :]

    start(z_to_next)

    for ref in (lf_own, mt, ct, cv, mm):
        ref[...] = jnp.zeros_like(ref)
    for d in range(3):
        for b in range(5):
            lf_own[d, b, 0:4, 0:33] = lat_fine[d, b]
        for a in range(9):
            for b in range(2):
                row = 32 * d + 16 * b + a
                mt[row : row + 1, 0:33] = lat_mid[d, a, b : b + 1]
        for a in range(3):
            ct[16 * d + a : 16 * d + a + 1, 0:9] = lat_coarse[d, a]
    for d in range(3):
        for b in range(5):
            row = 5 * d + b
            lf_up[row : row + 1, :] = lf_own[d, b, 3:4, :]
            lf_down[2 * row : 2 * row + 2, :] = lf_own[d, b, 0:2, :]
    start(lat_to_next, lat_to_prev)

    def pick_rows(name, ref):
        rows = table(name)[...]
        contract = (((1,), (1,)), ((), ()))
        high, low = parts(ref[...])
        return lax.dot_general(rows, high, contract, preferred_element_type=F32) + lax.dot_general(
            rows, low, contract, preferred_element_type=F32
        )

    rows_m, rows_c = pick_rows("rows_m", mt), pick_rows("rows_c", ct)
    cbt, cspread = table("cbt")[...], table("cspread")[...]
    column = dot3(jnp.concatenate([from_lane(rows_c[0:8], 16 * d) for d in range(3)], axis=0), cbt)
    column = jnp.concatenate([column[8 * d : 8 * d + 8] for d in range(3)], axis=1)
    exponent = dot(cspread, stacked(column, 8))[0:40]
    fractions_c = [fraction(exponent[:, 128 * d : 128 * d + 128]) for d in range(3)]
    cbx, cgather = table("cbx"), table("cgather")

    around(k, s, piece, pieces, psend, precv, "wait_recv")

    lane = lax.broadcasted_iota(jnp.int32, (5, 128), 1)
    for dk in range(3):
        scale = (has_prev, jnp.float32(1.0), has_next)[dk]
        rows = (slice(3, 8), slice(8, 13), slice(13, 18))[dk]
        for c in range(5):
            value = jnp.zeros((8, 128), F32)
            if c < 4:
                value = value + pieces[dk, c, 0]
            if c > 0:
                value = value + pieces[dk, c - 1, 1]
            cv[4 + c, rows, :] = jnp.where(lane < 40, value[0:5], 0.0) * scale
            if dk == 1:
                cf[c] = value
    fixed_c = pltpu.roll(cf[...].reshape(40, 128), 64, 1)

    oz, oy, ox = off_coarse[0, 0, q], off_coarse[1, 0, q], off_coarse[2, 0, q]
    a_z, b_z = [], []
    for e in (0, 1):
        window = cv[pl.ds(4 + oy, 6), pl.ds(8 + oz + e, 8), :].reshape(48, 128)
        here, there = shift_lanes([window], ox)[0], shift_lanes([window], ox + 1)[0]
        a_z.append(here)
        b_z.append(there - here)
    corner = [[a_z[z][8 * y : 8 * y + 40] for y in (0, 1)] for z in (0, 1)]
    step = [[b_z[z][8 * y : 8 * y + 40] for y in (0, 1)] for z in (0, 1)]
    total = jnp.concatenate(weights(fixed_c, corner, step, fractions_c), axis=1)
    total = dot_wide(jnp.concatenate([total, jnp.zeros((8, 384), F32)], axis=0), cbx[...])
    total = jnp.concatenate([total, jnp.zeros((80, 128), F32)], axis=0)
    c_tile[...] = dot_gather(cgather[...], total)[0:8]
    broadcast_start(k, s, c_tile, c_buf, bsem.at[0], bsem.at[1])
    c_buf[k] = c_tile[...]
    start_y_halos(3, 4)
    start(z_to_prev)

    mbt, mspread, mbx, mgather = table("mbt"), table("mspread"), table("mbx"), table("mgather")
    own = [from_lane(rows_m[0:8], 32 * d + 16 * b) for d in range(3) for b in range(2)]
    own = dot3(jnp.concatenate(own, axis=0), mbt[0])
    coarse = dot3(jnp.concatenate([from_lane(rows_c[8:16], 16 * d) for d in range(3)], axis=0), mbt[1])
    column = [
        jnp.concatenate([own[16 * d : 16 * d + 16], coarse[8 * d : 8 * d + 8]], axis=0) for d in range(3)
    ]
    base_m = dot(mspread[...], stacked(jnp.concatenate(column, axis=1), 24))[0:120]
    sum_c = table("sum_c")

    @pl.when(s == 0)
    def _():
        y_bef[...] = jnp.zeros_like(y_bef)
        corners[0:2] = jnp.zeros((2, CHUNKS, 2, 8, 128), F32)
        pm_bef[...] = jnp.zeros_like(pm_bef)
        pm_halo[:, 0] = jnp.zeros((2, 5, 8, 128), F32)

    @pl.when(s == SECS - 1)
    def _():
        y_aft[...] = jnp.zeros_like(y_aft)
        corners[2:4] = jnp.zeros((2, CHUNKS, 2, 8, 128), F32)
        pm_aft[...] = jnp.zeros_like(pm_aft)
        pm_halo[:, 1] = jnp.zeros((2, 5, 8, 128), F32)

    for copy in mid_same:
        copy.wait_recv()

    @pl.when(s > 0)
    def _():
        for copy in mid_up:
            copy.wait_recv()

    @pl.when(s < SECS - 1)
    def _():
        for copy in mid_down:
            copy.wait_recv()

    for c in range(2):
        lanes = slice(128 * c, 128 * c + 128)
        for y in range(5):
            mm[c, 5 + y, 4:8, :] = pm_same[0, y, 0:4, lanes] * has_prev
            mm[c, 5 + y, 8:28, :] = pooled_m[y, 0:20, lanes]
            mm[c, 5 + y, 28:32, :] = pm_same[1, y, 0:4, lanes] * has_next
    few = lax.broadcasted_iota(jnp.int32, (24, 128), 1) < 32
    for e, (whole, first_y) in enumerate(((pm_bef, 1), (pm_aft, 10))):
        for y in range(4):
            for c in range(2):

                def row(ref):
                    value = ref[y] if c == 0 else from_lane(ref[4], 32 * y)
                    return value if c == 0 else jnp.where(few[0 : value.shape[0]], value, 0.0)

                mm[c, first_y + y, 4:8, :] = row(pm_halo.at[0, e])[0:4] * has_prev
                mm[c, first_y + y, 8:28, :] = row(whole)[0:20]
                mm[c, first_y + y, 28:32, :] = row(pm_halo.at[1, e])[0:4] * has_next

    oz, oy, ox = off_mid[0, 0, 0], off_mid[0, 0, 1], off_mid[0, 0, 2]
    a_z, b_z = [], []
    for e in (0, 1):
        window = [mm[c, pl.ds(5 + oy, 6), pl.ds(8 + oz + e, 24), :].reshape(144, 128) for c in range(2)]
        here, there = shift_lanes(window, ox), shift_lanes(window, ox + 1)
        a_z.append(here)
        b_z.append([there[c] - here[c] for c in range(2)])

    def make_window(block, oz, oy, ox, y):
        window = [pad[c, 4 + oy + y, pl.ds(20 * block + 8 + oz, 24), :] for c in range(CHUNKS)]
        here, there = shift_lanes(window, ox), shift_lanes(window, ox + 1)
        for c in range(CHUNKS):
            at[block, c, y, 8:32, :] = here[c]
            by[block, c, y, 8:32, :] = there[c] - here[c]

    def make_windows(blocks, ranges):
        @pl.loop(*blocks)
        def _(block):
            offsets = [off_fine[d, block, s] for d in range(3)]
            for first_y, last_y, unroll in ranges:
                pl.loop(first_y, last_y, unroll=unroll)(functools.partial(make_window, block, *offsets))

    broadcast_wait(c_buf, bsem.at[0], bsem.at[1])
    gradient = dot_exact(sum_c[...], c_buf[...].reshape(256, 128))
    near_c = gradient[16:24]
    gradient = gradient[0:16]
    inverse = lax.rsqrt(jnp.sum(gradient * gradient) * (1.0 / 81.0) + EPSILON)

    near = dot3(jnp.concatenate([from_lane(near_c, 16 * d) for d in range(3)], axis=0), mbt[1])
    near = jnp.concatenate([near[8 * d : 8 * d + 8] for d in range(3)], axis=1)
    near = dot(mspread[...], stacked(jnp.concatenate([jnp.zeros((16, 768), F32), near], axis=0), 24))
    exponent = base_m - (STEP_SIZE * inverse) * near[0:120]
    fixed_m = pooled_f[...].reshape(120, 256)
    found = []
    for c in range(2):
        lanes = slice(128 * c, 128 * c + 128)
        corner = [[a_z[z][c][24 * y : 24 * y + 120] for y in (0, 1)] for z in (0, 1)]
        step = [[b_z[z][c][24 * y : 24 * y + 120] for y in (0, 1)] for z in (0, 1)]
        fractions = [fraction(exponent[:, 256 * d + 128 * c : 256 * d + 128 * c + 128]) for d in range(3)]
        found.append(weights(fixed_m[:, lanes], corner, step, fractions))
    total = jnp.concatenate([found[c][d] for d in range(3) for c in range(2)], axis=1)
    total = dot_wide(jnp.concatenate([total, jnp.zeros((8, 768), F32)], axis=0), mbx[...])
    m_part[...] = dot_gather(mgather[...], total)

    def part_copies(act):
        for i in range(1, SECS):
            other = (s + i) & (SECS - 1)
            slot = other if act == "wait_recv" else s
            getattr(remote(m_part, m_parts.at[slot], tsend.at[other], trecv.at[slot], (k, other)), act)()

    part_copies("start")
    start_if(up, *corner_up)
    start_if(down, *corner_down)
    m_parts[s] = m_part[...]

    gradient = gradient * inverse
    next_c = [
        from_lane(rows_c[8:16], 16 * d) - (STEP_SIZE * inverse) * from_lane(near_c, 16 * d) for d in range(3)
    ]
    for copy in (lat_to_next, lat_to_prev):
        copy.wait_recv()
    for d in range(3):
        for b in range(5):
            lf[d, 8 * b : 8 * b + 1, :] = lf_prev[5 * d + b : 5 * d + b + 1, :] * has_prev
            lf[d, 8 * b + 1 : 8 * b + 5, :] = lf_own[d, b, 0:4, :]
            lf[d, 8 * b + 5 : 8 * b + 7, :] = lf_next[10 * d + 2 * b : 10 * d + 2 * b + 2, :] * has_next
            lf[d, 8 * b + 7 : 8 * b + 8, :] = jnp.zeros((1, 128), F32)
    bt = table("bt")
    own = dot3(lf[...].reshape(120, 128), bt[0])
    mid = [from_lane(rows_m[8:16], 32 * d + 16 * b) for d in range(3) for b in range(2)]
    mid = dot3(jnp.concatenate(mid, axis=0), bt[1])
    coarse = dot3(jnp.concatenate(next_c, axis=0), bt[2])
    base_f = [
        jnp.concatenate(
            [own[40 * d : 40 * d + 40], mid[16 * d : 16 * d + 16], coarse[8 * d : 8 * d + 8]], axis=0
        )
        for d in range(3)
    ]
    base_f = jnp.concatenate(base_f, axis=1)

    make_windows((1, 3), ((4, 16, 3),))
    part_copies("wait_recv")
    m_tile[...] = (m_parts[0] + m_parts[1]) + (m_parts[2] + m_parts[3])
    broadcast_start(k, s, m_tile, m_buf, bsem.at[2], bsem.at[3])
    m_buf[k] = m_tile[...]

    turn_r = lax.broadcasted_iota(jnp.int32, (48, 128), 0)
    turn = jnp.where(turn_r == lax.broadcasted_iota(jnp.int32, (48, 128), 1) + 2, 1.0, 0.0)
    result[216:264, :] = dot_rows(gradient, turn[0:16])[0:48]

    for copy in (z_to_next, z_to_prev):
        copy.wait_recv()

    @pl.loop(0, NY // 2, unroll=2)
    def _(pair):
        for half in range(2):
            rows = slice(4 * half, 4 * half + 4)
            for c in range(CHUNKS):
                pad[c, 2 * pair + half + 4, 4:8, :] = z_bef[c, pair, rows, :] * has_prev
                pad[c, 2 * pair + half + 4, 88:92, :] = z_aft[c, pair, rows, :] * has_next

    make_windows((0, 1), ((4, 16, 3),))
    make_windows((3, 4), ((4, 16, 3),))

    @pl.when(s > 0)
    def _():
        for copy in (to_bef, *corner_up):
            copy.wait_recv()

    @pl.when(s < SECS - 1)
    def _():
        for copy in (to_aft, *corner_down):
            copy.wait_recv()

    for c in range(CHUNKS):
        lanes = slice(128 * c, 128 * c + 128)
        pad[c, 0:4, 8:88, :] = y_bef[:, :, lanes]
        pad[c, 24:28, 8:88, :] = y_aft[:, :, lanes]
    for y in range(4):
        rows = slice(4 * (y % 2), 4 * (y % 2) + 4)
        for c in range(CHUNKS):
            for n in range(2):
                where = slice(4, 8) if n == 0 else slice(88, 92)
                keep = has_prev if n == 0 else has_next
                pad[c, y, where, :] = corners[n, c, y // 2, rows, :] * keep
                pad[c, 24 + y, where, :] = corners[2 + n, c, y // 2, rows, :] * keep

    make_windows((0, 4), ((0, 4, 2), (16, 21, 5)))

    spread, gather, bx, sum_m = table("spread"), table("gather"), table("bx"), table("sum_m")

    broadcast_wait(m_buf, bsem.at[2], bsem.at[3])
    gradient = dot_exact(sum_m[...], m_buf[...].reshape(512, 128))
    near = gradient[96:112]
    gradient = gradient[0:96]
    inverse = lax.rsqrt(jnp.sum(gradient * gradient) * (1.0 / 1782.0) + EPSILON)

    near = dot3(jnp.concatenate([from_lane(near, 16 * d) for d in range(3)], axis=0), bt[1])
    near = jnp.concatenate([near[16 * d : 16 * d + 16] for d in range(3)], axis=1)
    near = jnp.concatenate([jnp.zeros((40, 3 * NX), F32), near, jnp.zeros((8, 3 * NX), F32)], axis=0)
    upper, lower = parts(base_f - (STEP_SIZE * inverse) * near)
    columns[0:64, :] = upper
    columns[64:128, :] = upper
    columns[128:192, :] = lower
    columns[192:256, :] = lower
    field_a[...] = dot(spread[0:400, :], columns[...])

    first_rows = lax.broadcasted_iota(jnp.int32, (8, 128), 0) < 4
    steps_z = (jnp.minimum(k, 0), jnp.minimum(k + 1, 1))

    def planes(ref, pair, c, y, z):
        a, b = 2 * pair, 2 * pair + 1
        middle = jnp.where(
            first_rows, ref[a, c, y, pl.ds(24 + z, 8), :], ref[b, c, y, pl.ds(4 + z, 8), :]
        )
        return jnp.concatenate(
            [ref[a, c, y, pl.ds(8 + z, 16), :], middle, ref[b, c, y, pl.ds(12 + z, 16), :]], axis=0
        )

    def fine_stage(stage, split, split_before, field, field_after):
        adjoint[...] = jnp.zeros_like(adjoint)
        pair, y_first = stage >> 1, 10 * (stage & 1)
        after = pl.ds(pl.multiple_of(400 * jnp.minimum(stage + 1, 3), 400), 400)

        @pl.loop(0, 5)
        def _(i):
            lanes = pl.ds(pl.multiple_of(384 * i, 384), 384)
            field_after[:, lanes] = dot(spread[after, :], columns[:, lanes])
            lanes = pl.ds(pl.multiple_of(768 * i, 768), 768)
            adjoint[...] += dot(split_before[:, lanes], bx[lanes, :])
            for c in range(CHUNKS):
                found = []
                for h in range(2):
                    y = y_first + 2 * i + h
                    corner = [[planes(at, pair, c, y + e, z) for e in (0, 1)] for z in steps_z]
                    step = [[planes(by, pair, c, y + e, z) for e in (0, 1)] for z in steps_z]
                    rows = pl.ds(pl.multiple_of(80 * i + 40 * h, 8), 40)
                    fractions = [
                        fraction(field[rows, NX * d + 128 * c : NX * d + 128 * c + 128]) for d in range(3)
                    ]
                    atlas = fx[c, y, pl.ds(pl.multiple_of(40 * pair, 8), 40), :]
                    found.append(weights(atlas, corner, step, fractions))
                rows = pl.ds(pl.multiple_of(80 * i, 80), 80)
                for d in range(3):
                    upper, lower = parts(jnp.concatenate([found[0][d], found[1][d]], axis=0))
                    lane = 2 * NX * d + 128 * c
                    split[rows, lane : lane + 128] = upper
                    split[rows, lane + NX : lane + NX + 128] = lower

        before = pl.ds(pl.multiple_of(400 * jnp.maximum(stage - 1, 0), 400), 400)
        mixed[before, :] = adjoint[:, 0:128] + adjoint[:, 128:256]

    @pl.loop(0, 2)
    def _(two):
        fine_stage(2 * two, split_a, split_b, field_a, field_b)
        fine_stage(2 * two + 1, split_b, split_a, field_b, field_a)

    wide = dot(split_b[...], bx[...])
    mixed[1200:1600, :] = wide[:, 0:128] + wide[:, 128:256]
    f_part[...] = dot_gather(gather[...], mixed[...])
    around(k, s, f_part, f_parts, fsend, frecv, "start")
    f_parts[1, s] = f_part[...]

    for b in range(2):
        turned = dot_rows(gradient[48 * b : 48 * b + 48] * inverse, turn)
        result[120 + 48 * b : 168 + 48 * b, :] = turned[0:48]
    row = lax.broadcasted_iota(jnp.int32, (40, 128), 0) & 7

    around(k, s, f_part, f_parts, fsend, frecv, "wait_recv")
    before, middle, after = ((f_parts[i, 0] + f_parts[i, 1]) + (f_parts[i, 2] + f_parts[i, 3]) for i in range(3))
    middle = middle + jnp.where((row == 1) | (row == 2), pltpu.roll(before * has_prev, 36, 0), 0.0)
    middle = middle + jnp.where(row == 4, pltpu.roll(after * has_next, 4, 0), 0.0)
    middle = jnp.where((row >= 1) & (row <= 4), middle, 0.0)
    f_tile[...] = jnp.full((8, 128), jnp.sum(middle * middle))
    broadcast_start(k, s, f_tile, f_buf, bsem.at[4], bsem.at[5])
    f_buf[k] = f_tile[...]

    for copy in (lat_to_next, lat_to_prev, z_to_next, z_to_prev, *mid_same):
        copy.wait_send()

    @pl.when(up)
    def _():
        for copy in (to_bef, *corner_up, *mid_up):
            copy.wait_send()

    @pl.when(down)
    def _():
        for copy in (to_aft, *corner_down, *mid_down):
            copy.wait_send()

    around(k, s, piece, pieces, psend, precv, "wait_send")
    around(k, s, f_part, f_parts, fsend, frecv, "wait_send")
    part_copies("wait_send")
    middle = pltpu.roll(middle, 39, 0)
    thirds = [from_lane(middle, 40 * d) for d in range(3)]

    broadcast_wait(f_buf, bsem.at[4], bsem.at[5])
    squares = jnp.sum(f_buf[...], axis=0)[0:1, :]
    inverse = lax.rsqrt(squares * (1.0 / 63360.0) + EPSILON)
    for d in range(3):
        result[40 * d : 40 * d + 40, :] = thirds[d] * inverse


def body(
    fixed_image,
    moving_image,
    lattice_fine,
    lattice_mid,
    lattice_coarse,
    offset_fine,
    offset_mid,
    offset_coarse,
):
    t = tables()
    vmem, smem, hbm = (pl.BlockSpec(memory_space=m) for m in (pltpu.VMEM, pltpu.SMEM, pl.ANY))
    shape = lambda *dims: jax.ShapeDtypeStruct(dims, F32)
    buf = lambda *dims: pltpu.VMEM(dims, F32)
    half = lambda *dims: pltpu.VMEM(dims, BF16)
    dma = lambda *dims: pltpu.SemaphoreType.DMA(dims)
    result = pl.pallas_call(
        kernel,
        out_shape=shape(264, 128),
        in_specs=[hbm, hbm, vmem, vmem, vmem, smem, smem, smem] + [hbm] * len(TABLES),
        out_specs=vmem,
        scratch_shapes=[
            *[pltpu.VMEM(t[n].shape[which is not None :], t[n].dtype) for n, which in TABLES.items()],
            buf(CHUNKS, 28, 96, 128), buf(CHUNKS, NY, NZ, 128), buf(5, NZ, NX),
            *[buf(CHUNKS, 10, 8, 128)] * 4, *[buf(4, NZ, NX)] * 2, buf(4, CHUNKS, 2, 8, 128),
            buf(3, 5, 8, 128), *[buf(16, 128), buf(32, 128)] * 2, buf(3, 40, 128), buf(128, 128), buf(128, 128),
            *[buf(5, 24, 256)] * 2, *[buf(5, 24, 128)] * 4, buf(2, 2, 5, 8, 128), buf(2, 5, 8, 256),
            buf(2, 8, 128), buf(3, SECS, 2, 8, 128), buf(14, 32, 128), buf(5, 8, 128), buf(2, 15, 40, 128),
            buf(8, 128), buf(SLABS, 8, 128), buf(16, 128), buf(SECS, 16, 128), buf(16, 128), buf(SLABS, 16, 128),
            *[buf(4, CHUNKS, 21, 40, 128)] * 2, half(256, 3 * NX),
            *[buf(400, 3 * NX)] * 2, *[half(400, 6 * NX)] * 2, buf(400, 256), buf(1600, 128),
            buf(40, 128), buf(3, SECS, 40, 128), buf(8, 128), buf(SLABS, 8, 128),
            dma(10), dma(len(TABLES)), dma(18), dma(18), *[dma(3, SECS)] * 4, dma(SECS), dma(SECS), dma(6),
        ],
        compiler_params=pltpu.CompilerParams(
            collective_id=0, has_side_effects=True, vmem_limit_bytes=VMEM_LIMIT
        ),
        name="mega",
    )(
        jnp.transpose(moving_image, (1, 0, 2)),
        jnp.transpose(fixed_image, (1, 0, 2)),
        jnp.transpose(lattice_fine, (0, 2, 1, 3)),
        jnp.transpose(lattice_mid, (0, 3, 2, 1)),
        jnp.transpose(lattice_coarse, (0, 3, 2, 1)),
        offset_fine,
        jnp.transpose(offset_mid, (1, 2, 0)),
        jnp.transpose(offset_coarse, (0, 2, 1)),
        *(t[n] for n in TABLES),
    )
    fine, mid, coarse = pl.pallas_call(
        finish,
        out_shape=[shape(3, 5, 4, 33), shape(3, 9, 2, 33), shape(3, 3, 1, 9)],
        in_specs=[vmem],
        out_specs=[vmem] * 3,
        name="finish",
    )(result)
    return (
        jnp.transpose(fine, (0, 2, 1, 3)),
        jnp.transpose(mid, (0, 3, 2, 1)),
        jnp.transpose(coarse, (0, 3, 2, 1)),
    )


def solution(mesh):
    placed = (
        P("slab", "sec", None),
        P("slab", "sec", None),
        P(None, "slab", None, None),
        P(),
        P(),
        P(None, "slab", None),
        P(None, "slab", None),
        P(),
    )
    return jax.shard_map(
        body,
        mesh=mesh,
        in_specs=placed,
        out_specs=(P(None, "slab", None, None), P(), P()),
        check_vma=False,
    )
```
